32 devices in a mesh: seq: 4 (over y, core), blk: 8 (over z, x).
Axes of the slice: x: 2, y: 2, z: 4, core: 2. Of those that a mesh axis runs over, the one named last changes fastest.
Arguments:
- tokens: bfloat16 [4, 2048, 1024], P('seq', 'blk'), may hold values from -20 to 20
- lengths: int32 [4, 1], P('seq'), may hold values from 768 to 1536, as said below
- attend_weight: bfloat16 [1024, 3072], replicated, may hold values from -0.1875 to 0.1875
- merge_weight: bfloat16 [1024, 1024], replicated, may hold values from -4 to 4
- expand_weight: bfloat16 [1024, 4096], replicated, may hold values from -0.1875 to 0.1875
- contract_weight: bfloat16 [4096, 1024], replicated, may hold values from -0.09375 to 0.09375
- gain_first: float32 [1024], replicated, may hold values from 0.1 to 1.9
- shift_first: float32 [1024], replicated, may hold values from -3 to 3
- gain_second: float32 [1024], replicated, may hold values from 0.1 to 1.9
- shift_second: float32 [1024], replicated, may hold values from -3 to 3
- bias_table: float32 [32, 16], replicated, may hold values from -4 to 4
- cotangent: bfloat16 [4, 2048, 1024], P('seq', 'blk'), may hold values from -6 to 6
Outputs:
- output: bfloat16 [4, 2048, 1024], P('seq', 'blk')
- tokens_grad: float32 [4, 2048, 1024], P('seq', 'blk')
- attend_grad: float32 [1024, 3072], P('blk')
- merge_grad: float32 [1024, 1024], P('blk')
- expand_grad: float32 [1024, 4096], P('blk')
- contract_grad: float32 [4096, 1024], P('blk')
- gain_first_grad: float32 [1024], P('blk')
- shift_first_grad: float32 [1024], P('blk')
- gain_second_grad: float32 [1024], P('blk')
- shift_second_grad: float32 [1024], P('blk')
- table_grad: float32 [32, 16], replicated
The draws below stay inside these ranges and needn't reach their ends.
Inputs may be any that keep to these rules, and one draw needn't show every extreme that they name: Row s holds the lengths of the 1 items packed in order from the start of sequence s, one of them exactly 1536; the tokens after the last item are padding.
All inputs are finite; a program needn't handle non-finite values.
Results may differ from the reference program's by a relative error of at most 0.013.
Values may be sent and summed in bfloat16 or wider, within the bound.
No kernel may reach another device: no remote copies, remote signals or barrier semaphores. Data moves between devices by JAX's collectives and lax.ppermute only.
A program may use at most 256 MiB of HBM per device.

```python
import math
import jax
import jax.numpy as jnp
from jax import lax

D = 1024
HEADS = 16
FF = 4096
BUCKETS = 32
MAXLEN = 1536
MINLEN = 768
SEQLEN = 2048
SEQS = 4
ITEMS = 1


def draw_tokens(key, part):
    key = jax.random.fold_in(key, 11)
    base_key, row_key, col_key = jax.random.split(key, 3)
    row_scale = jnp.exp(jax.random.uniform(row_key, (SEQS, SEQLEN, 1), jnp.float32, math.log(0.5), math.log(2.0)))
    col_scale = jnp.exp(jax.random.uniform(col_key, (1, 1, D), jnp.float32, math.log(0.5), math.log(2.5)))
    base = jnp.clip(jax.random.normal(base_key, (SEQS, SEQLEN, D), jnp.float32), -4.0, 4.0)
    return (base * row_scale * col_scale).astype(jnp.bfloat16)


def draw_lengths(key, part):
    key = jax.random.fold_in(key, 5)
    size_key, pick_key = jax.random.split(key)
    drawn = jax.random.randint(size_key, (SEQS, ITEMS), MINLEN, MAXLEN + 1, dtype=jnp.int32)
    picked = jax.random.randint(pick_key, (SEQS, 1), 0, ITEMS, dtype=jnp.int32)
    slots = jnp.arange(ITEMS, dtype=jnp.int32)[None, :]
    return jnp.where(slots == picked, MAXLEN, drawn).astype(jnp.int32)


def spiked(values, key, source, target, shards_of, factor):
    def block_of(dim):
        return (jnp.arange(values.shape[dim]) // (values.shape[dim] // shards_of)).reshape((-1,) + (1,) * (values.ndim - 1 - dim))

    near = jax.random.permutation(key, shards_of)[block_of(target)]
    far = (block_of(target) + shards_of // 2) % shards_of
    return jnp.where((block_of(source) == near) | (block_of(source) == far), factor * values, values)


def block_scale(key, extent, cuts, least, high):
    def one(dim, parts):
        steps = jax.random.uniform(jax.random.fold_in(jax.random.fold_in(key, 6), dim), (parts,), jnp.float32, least / len(cuts), high / len(cuts))
        return jnp.repeat(jnp.exp(steps), extent[dim] // parts).reshape((-1,) + (1,) * (len(extent) - dim - 1))

    level = one(*cuts[0])
    for cut in cuts[1:]:
        level = level * one(*cut)
    return level


def scatter_about(own_key, dims, scale, most, cuts=(), held_as=jnp.bfloat16):
    values = jax.random.normal(own_key, dims, jnp.float32) * scale
    if len(cuts) > 0:
        values = block_scale(own_key, dims, cuts, -0.22, 0.18) * values
    return jnp.clip(values, min=-most, max=most).astype(held_as)


def bell_draw_with(rng, dims, deviation, limit, pieces, heavy, kind=jnp.bfloat16):
    array = deviation * jax.random.normal(rng, dims, jnp.float32)
    if pieces:
        array = array * block_scale(rng, dims, pieces, -0.22, 0.18)
    return jnp.clip(spiked(array, jax.random.fold_in(rng, 3), *heavy), -limit, limit).astype(kind)


def setup_inputs(seed: int = 0) -> dict:
    streams_of = jax.random.split(jax.random.key(seed), 13)
    return {
        "tokens": draw_tokens(jax.random.fold_in(streams_of[12], 71), 0),
        "lengths": draw_lengths(jax.random.fold_in(streams_of[12], 71), 0),
        "attend_weight": scatter_about(streams_of[2], (D, 3 * D), D ** -0.5, 0.1875),
        "merge_weight": scatter_about(streams_of[3], (D, D), (4 * D // MAXLEN) ** -0.5, 4.0),
        "expand_weight": scatter_about(streams_of[4], (D, FF), D ** -0.5, 0.1875),
        "contract_weight": scatter_about(streams_of[5], (FF, D), FF ** -0.5, 0.09375),
        "gain_first": jnp.clip(1.0 + 0.18 * jax.random.normal(streams_of[6], (D,), jnp.float32), 0.1, 1.9),
        "shift_first": scatter_about(streams_of[7], (D,), 0.5, 3.0, (), jnp.float32),
        "gain_second": jnp.clip(1.0 + 0.18 * jax.random.normal(streams_of[8], (D,), jnp.float32), 0.1, 1.9),
        "shift_second": scatter_about(streams_of[9], (D,), 0.5, 3.0, (), jnp.float32),
        "bias_table": scatter_about(streams_of[10], (BUCKETS, HEADS), 1.0, 4.0, (), jnp.float32),
        "cotangent": bell_draw_with(streams_of[11], (SEQS, SEQLEN, D), 1.0, 6.0, ((0, 4), (1, 8)), (1, 2, 8, 2.0)),
    }


epsilon = 1e-05
masked_score = -1e+30
highest = lax.Precision.HIGHEST
bucket_edges = [math.ceil(16 * 8 ** (t / 16)) for t in range(1, 16)]

@jax.custom_vjp
def low(v):
    return lax.optimization_barrier(v.astype(jnp.bfloat16)).astype(jnp.float32)

@jax.custom_vjp
def low_back(v):
    return v

def low_keep(v):
    return (low(v), None)

def low_pass(kept, grad):
    return (grad,)

def back_keep(v):
    return (v, None)

def back_low(kept, grad):
    return (low(grad),)
low.defvjp(low_keep, low_pass)
low_back.defvjp(back_keep, back_low)

def bucket_of(distance):
    total = jnp.minimum(jnp.maximum(distance, 0), 16).astype(jnp.int32)
    for edge in bucket_edges:
        total = total + (distance >= edge).astype(jnp.int32)
    return total

def segment_of(position, ends):
    return lax.optimization_barrier(jnp.sum((position[:, None] >= ends[None, :]).astype(jnp.int32), axis=1)).astype(jnp.int32)

def layer_norm(value, gain, shift):
    mean = lax.optimization_barrier(jnp.mean(value, axis=-1, keepdims=True))
    centred = value - mean
    variance = lax.optimization_barrier(jnp.mean(centred * centred, axis=-1, keepdims=True))
    return centred * lax.rsqrt(variance + epsilon) * gain + shift

def forward(params, residual, lengths_row):
    attend_weight, merge_weight, expand_weight, contract_weight, gain_first, shift_first, gain_second, shift_second, bias_table = params
    count = residual.shape[0]
    width = residual.shape[1]
    heads = bias_table.shape[1]
    head_size = width // heads
    items = lengths_row.shape[0]
    block_rows = math.gcd(count, 512)
    ends = jnp.cumsum(lengths_row).astype(jnp.int32)
    act_first = low(layer_norm(residual, gain_first, shift_first))
    projected = jnp.dot(act_first, attend_weight, precision=highest)
    query = low(low_back(projected[:, :width])).reshape(count, heads, head_size)
    key = low(low_back(projected[:, width:2 * width])).reshape(count, heads, head_size)
    value = low(low_back(projected[:, 2 * width:])).reshape(count, heads, head_size)
    key_pad = jnp.pad(key, ((MAXLEN, 0), (0, 0), (0, 0)))
    value_pad = jnp.pad(value, ((MAXLEN, 0), (0, 0), (0, 0)))

    def attend(begin):
        query_pos = begin + jnp.arange(block_rows, dtype=jnp.int32)
        key_pos = begin - MAXLEN + jnp.arange(block_rows + MAXLEN, dtype=jnp.int32)
        query_seg = segment_of(query_pos, ends)
        key_seg = segment_of(key_pos, ends)
        key_valid = (key_pos >= 0) & (key_seg < items)
        same = key_pos[None, :] == query_pos[:, None]
        allowed = (query_seg[:, None] == key_seg[None, :]) & (key_pos[None, :] <= query_pos[:, None]) & (key_valid[None, :] | same)
        query_block = lax.dynamic_slice_in_dim(query, begin, block_rows, 0)
        key_block = lax.dynamic_slice_in_dim(key_pad, begin, block_rows + MAXLEN, 0)
        value_block = lax.dynamic_slice_in_dim(value_pad, begin, block_rows + MAXLEN, 0)
        bias = jnp.transpose(bias_table[bucket_of(query_pos[:, None] - key_pos[None, :])], (2, 0, 1))
        raw = jnp.einsum('qhe,khe->hqk', query_block, key_block, precision=highest) * 0.125 + bias
        scores = jnp.where(allowed[None], low_back(raw), masked_score)
        weights = low(jax.nn.softmax(scores, axis=-1))
        mixed = jnp.einsum('hqk,khe->qhe', weights, value_block, precision=highest)
        return mixed.reshape(block_rows, width)
    begins = jnp.arange(0, count, block_rows, dtype=jnp.int32)
    attended = lax.map(jax.checkpoint(attend), begins).reshape(count, width)
    attn_low = low(low_back(attended))
    branch = low_back(jnp.dot(attn_low, merge_weight, precision=highest))
    middle = residual + branch
    act_second = low(layer_norm(middle, gain_second, shift_second))
    hidden_pre = low_back(jnp.dot(act_second, expand_weight, precision=highest))
    hidden_low = low(jax.nn.gelu(hidden_pre, approximate=False))
    return middle + jnp.dot(hidden_low, contract_weight, precision=highest)

def reference(tokens, lengths, attend_weight, merge_weight, expand_weight, contract_weight, gain_first, shift_first, gain_second, shift_second, bias_table, cotangent):
    params = tuple((a.astype(jnp.float32) for a in (attend_weight, merge_weight, expand_weight, contract_weight, gain_first, shift_first, gain_second, shift_second, bias_table)))

    def one_sequence(carry, inputs):
        token_rows, length_row, grad_rows = inputs
        result, pull = jax.vjp(lambda p, v: forward(p, v, length_row), params, token_rows.astype(jnp.float32))
        param_grads, input_grad = pull(grad_rows.astype(jnp.float32))
        carry = tuple((a + b for a, b in zip(carry, param_grads)))
        return (carry, (result.astype(jnp.bfloat16), input_grad))
    zeros = tuple((jnp.zeros_like(p) for p in params))
    sums, (outputs, input_grads) = lax.scan(one_sequence, zeros, (tokens, lengths, cotangent))
    return (outputs, input_grads, sums[0], sums[1], sums[2], sums[3], sums[4], sums[5], sums[6], sums[7], sums[8])
```

```python
from functools import partial
import math

import jax
import jax.numpy as jnp
from jax import lax
from jax.experimental import pallas as pl
from jax.experimental.pallas import tpu as pltpu
from jax.sharding import PartitionSpec as P

HOPS = 6


epsilon = 1e-05
masked_score = -1e30
highest = lax.Precision.HIGHEST
bucket_edges = [math.ceil(16 * 8 ** (t / 16)) for t in range(1, 16)]


def shifted(array, axis, by):
    peers = lax.axis_size(axis)
    pairs = [(i, i + by) for i in range(peers) if 0 <= i + by < peers]
    return lax.ppermute(array, axis, pairs)


def shortened(array):

    def short(part):
        return part.astype(jnp.bfloat16) if part.dtype == jnp.float32 else part

    return jax.tree.map(short, array)


def bucket_of(distance):
    total = jnp.minimum(jnp.maximum(distance, 0), 16)
    for edge in bucket_edges:
        total = total + (distance >= edge).astype(jnp.int32)
    return total


def segment_of(position, ends):
    return jnp.sum((position[:, None] >= ends[None, :]).astype(jnp.int32), axis=1)


def layer_norm(value, gain, shift):
    mean = jnp.mean(value, axis=-1, keepdims=True)
    centred = value - mean
    variance = jnp.mean(centred * centred, axis=-1, keepdims=True)
    return centred * lax.rsqrt(variance + epsilon) * gain + shift


def diagonal_sums(grid, count):
    heads = grid.shape[0]
    padded = jnp.pad(jnp.flip(grid, axis=-1), ((0, 0), (0, 0), (0, count)))
    flat = padded.reshape(heads, 2 * count * count)[:, : count * (2 * count - 1)]
    return jnp.sum(flat.reshape(heads, count, 2 * count - 1), axis=1)


def band_matrix(line, count):
    heads = line.shape[0]
    flipped = jnp.flip(line, axis=-1)
    tiled = jnp.tile(flipped, (1, count))
    window = tiled[:, count - 1 : count - 1 + count * (2 * count - 2)]
    return window.reshape(heads, count, 2 * count - 2)[:, :, :count]


def fetch_earlier(block):
    earlier = []
    moving = block
    for hop in range(HOPS):
        moving = shifted(moving, "blk", 1)
        earlier.append(moving)
    return earlier


def return_parts(parts):
    carried = jnp.zeros_like(parts[0])
    for hop in range(HOPS, 0, -1):
        carried = shifted(shortened(carried + parts[hop - 1]), "blk", -1)
    return carried


def local_by_runs(
    tokens,
    lengths,
    attend_weight,
    merge_weight,
    expand_weight,
    contract_weight,
    gain_first,
    shift_first,
    gain_second,
    shift_second,
    bias_table,
    cotangent,
):
    rows = tokens.shape[1]
    width = tokens.shape[2]
    heads = bias_table.shape[1]
    buckets = bias_table.shape[0]
    head_size = width // heads
    items = lengths.shape[1]
    start = lax.axis_index("blk") * rows
    query_pos = start + jnp.arange(rows, dtype=jnp.int32)
    ends = jnp.cumsum(lengths[0])
    query_seg = segment_of(query_pos, ends)
    band = jnp.arange(2 * rows - 1, dtype=jnp.int32) - (rows - 1)
    bucket_ids = jnp.arange(buckets, dtype=jnp.int32)

    def pair_setup(hop):
        key_pos = query_pos - hop * rows
        key_seg = segment_of(key_pos, ends)
        key_valid = (key_pos >= 0) & (key_seg < items)
        same = key_pos[None, :] == query_pos[:, None]
        allowed = (
            (query_seg[:, None] == key_seg[None, :])
            & (key_pos[None, :] <= query_pos[:, None])
            & (key_valid[None, :] | same)
        )
        onehot = (bucket_of(hop * rows + band)[:, None] == bucket_ids[None, :]).astype(jnp.float32)
        band_bias = jnp.dot(onehot, bias_table, precision=highest).T
        bias = band_matrix(band_bias, rows)
        additive = jnp.where(allowed[None], bias, masked_score)
        return (jnp.any(allowed), onehot, additive)

    pairs = [pair_setup(hop) for hop in range(HOPS + 1)]
    residual = tokens[0].astype(jnp.float32)
    normed_first, norm_first_pull = jax.vjp(layer_norm, residual, gain_first, shift_first)
    act_first = normed_first.astype(jnp.bfloat16)
    projected = jnp.dot(act_first, attend_weight, preferred_element_type=jnp.float32).astype(
        jnp.bfloat16
    )
    query = projected[:, :width].reshape(rows, heads, head_size)
    keys_values = jnp.stack([projected[:, width : 2 * width], projected[:, 2 * width :]])
    blocks = [keys_values] + fetch_earlier(keys_values)

    def scores_of(block, pair):
        key = block[0].reshape(rows, heads, head_size)
        raw = jnp.einsum("qhe,khe->hqk", query, key, preferred_element_type=jnp.float32) * 0.125
        return raw + pair[2]

    def empty_total():
        return jnp.full((heads, rows), masked_score, jnp.float32)

    def empty_scores():
        return jnp.full((heads, rows, rows), masked_score, jnp.float32)

    log_total = empty_total()
    kept_scores = []
    for block, pair in zip(blocks, pairs):

        def part_total(block=block, pair=pair):
            scores = scores_of(block, pair)
            peak = jnp.max(scores, axis=-1)
            return (peak + jnp.log(jnp.sum(jnp.exp(scores - peak[..., None]), axis=-1)), scores)

        def skip_total():
            return (empty_total(), empty_scores())

        part_log, scores = lax.cond(pair[0], part_total, skip_total)
        log_total = jnp.logaddexp(log_total, part_log)
        kept_scores.append(scores)

    def empty_heads():
        return jnp.zeros((rows, heads, head_size), jnp.float32)

    attended = empty_heads()
    for block, pair, scores in zip(blocks, pairs, kept_scores):

        def part_mix(block=block, scores=scores):
            weights = jnp.exp(scores - log_total[..., None]).astype(jnp.bfloat16)
            value = block[1].reshape(rows, heads, head_size)
            return jnp.einsum("hqk,khe->qhe", weights, value, preferred_element_type=jnp.float32)

        attended = attended + lax.cond(pair[0], part_mix, empty_heads)
    attn_low = attended.reshape(rows, width).astype(jnp.bfloat16)
    middle = residual + jnp.dot(attn_low, merge_weight, preferred_element_type=jnp.float32)
    normed_second, norm_second_pull = jax.vjp(layer_norm, middle, gain_second, shift_second)
    act_second = normed_second.astype(jnp.bfloat16)
    hidden_pre = jnp.dot(act_second, expand_weight, preferred_element_type=jnp.float32)
    hidden, gelu_pull = jax.vjp(partial(jax.nn.gelu, approximate=False), hidden_pre)
    hidden_low = hidden.astype(jnp.bfloat16)
    output = (
        middle + jnp.dot(hidden_low, contract_weight, preferred_element_type=jnp.float32)
    ).astype(jnp.bfloat16)
    grad_out = cotangent[0]
    contract_grad = jnp.einsum(
        "tf,td->fd", hidden_low, grad_out, preferred_element_type=jnp.float32
    )
    grad_hidden = jnp.einsum(
        "td,fd->tf", grad_out, contract_weight, preferred_element_type=jnp.float32
    )
    grad_pre = gelu_pull(grad_hidden)[0].astype(jnp.bfloat16)
    expand_grad = jnp.einsum("td,tf->df", act_second, grad_pre, preferred_element_type=jnp.float32)
    grad_second = jnp.einsum(
        "tf,df->td", grad_pre, expand_weight, preferred_element_type=jnp.float32
    )
    grad_middle_norm, gain_second_grad, shift_second_grad = norm_second_pull(grad_second)
    grad_middle = grad_out.astype(jnp.float32) + grad_middle_norm
    grad_middle_low = grad_middle.astype(jnp.bfloat16)
    merge_grad = jnp.einsum(
        "td,te->de", attn_low, grad_middle_low, preferred_element_type=jnp.float32
    )
    grad_heads = (
        jnp.einsum("te,de->td", grad_middle_low, merge_weight, preferred_element_type=jnp.float32)
        .astype(jnp.bfloat16)
        .reshape(rows, heads, head_size)
    )
    row_dot = jnp.sum(grad_heads.astype(jnp.float32) * attended, axis=-1).T
    back_blocks = [keys_values] + fetch_earlier(keys_values)

    def empty_grads():
        return (
            empty_heads(),
            jnp.zeros((2, rows, width), jnp.float32),
            jnp.zeros((buckets, heads), jnp.float32),
        )

    grad_query = empty_heads()
    table_local = jnp.zeros((buckets, heads), jnp.float32)
    parts = []
    for block, pair in zip(back_blocks, pairs):

        def part_grads(block=block, pair=pair):
            key = block[0].reshape(rows, heads, head_size)
            value = block[1].reshape(rows, heads, head_size)
            weights = jnp.exp(scores_of(block, pair) - log_total[..., None])
            weights_low = weights.astype(jnp.bfloat16)
            grad_weights = jnp.einsum(
                "qhe,khe->hqk", grad_heads, value, preferred_element_type=jnp.float32
            )
            grad_scores = (weights * (grad_weights - row_dot[..., None])).astype(jnp.bfloat16)
            query_part = (
                jnp.einsum("hqk,khe->qhe", grad_scores, key, preferred_element_type=jnp.float32)
                * 0.125
            )
            key_part = (
                jnp.einsum("hqk,qhe->khe", grad_scores, query, preferred_element_type=jnp.float32)
                * 0.125
            )
            value_part = jnp.einsum(
                "hqk,qhe->khe", weights_low, grad_heads, preferred_element_type=jnp.float32
            )
            line_grad = diagonal_sums(grad_scores.astype(jnp.float32), rows)
            table_part = jnp.dot(pair[1].T, line_grad.T, precision=highest)
            return (
                query_part,
                jnp.stack([key_part.reshape(rows, width), value_part.reshape(rows, width)]),
                table_part,
            )

        query_part, pair_part, table_part = lax.cond(pair[0], part_grads, empty_grads)
        grad_query = grad_query + query_part
        table_local = table_local + table_part
        parts.append(pair_part)
    owned = (parts[0] + return_parts(parts[1:])).astype(jnp.bfloat16)
    grad_project = jnp.concatenate(
        [grad_query.reshape(rows, width).astype(jnp.bfloat16), owned[0], owned[1]], axis=1
    )
    attend_grad = jnp.einsum(
        "td,te->de", act_first, grad_project, preferred_element_type=jnp.float32
    )
    grad_first = jnp.einsum(
        "te,de->td", grad_project, attend_weight, preferred_element_type=jnp.float32
    )
    grad_input_norm, gain_first_grad, shift_first_grad = norm_first_pull(grad_first)
    tokens_grad = grad_middle + grad_input_norm
    results = (
        lax.psum_scatter(attend_grad, "blk", scatter_dimension=0, tiled=True),
        lax.psum_scatter(merge_grad, "blk", scatter_dimension=0, tiled=True),
        lax.psum_scatter(expand_grad, "blk", scatter_dimension=0, tiled=True),
        lax.psum_scatter(contract_grad, "blk", scatter_dimension=0, tiled=True),
        lax.psum_scatter(gain_first_grad, "blk", scatter_dimension=0, tiled=True),
        lax.psum_scatter(shift_first_grad, "blk", scatter_dimension=0, tiled=True),
        lax.psum_scatter(gain_second_grad, "blk", scatter_dimension=0, tiled=True),
        lax.psum_scatter(shift_second_grad, "blk", scatter_dimension=0, tiled=True),
    )
    results = (
        lax.psum(results[0].astype(jnp.bfloat16), "seq").astype(jnp.float32),
        lax.psum(results[1].astype(jnp.bfloat16), "seq").astype(jnp.float32),
        lax.psum(results[2].astype(jnp.bfloat16), "seq").astype(jnp.float32),
        lax.psum(results[3].astype(jnp.bfloat16), "seq").astype(jnp.float32),
        lax.psum(results[4].astype(jnp.bfloat16), "seq").astype(jnp.float32),
        lax.psum(results[5].astype(jnp.bfloat16), "seq").astype(jnp.float32),
        lax.psum(results[6].astype(jnp.bfloat16), "seq").astype(jnp.float32),
        lax.psum(results[7].astype(jnp.bfloat16), "seq").astype(jnp.float32),
    )
    table_grad = lax.psum(table_local, ("seq", "blk"))
    return (
        output[None],
        tokens_grad[None],
        results[0],
        results[1],
        results[2],
        results[3],
        results[4],
        results[5],
        results[6],
        results[7],
        table_grad,
    )


def _segments(position, meta_ref, first, items):
    total = jnp.zeros(position.shape, jnp.int32)
    for item in range(items):
        total = total + (position >= meta_ref[first + item]).astype(jnp.int32)
    return total

def _allowed(meta_ref, peers, items, rows, i, j, diagonal):
    first = 1 + 2 * peers
    q_seg = _segments(i * rows + lax.broadcasted_iota(jnp.int32, (1, rows), 1), meta_ref, first, items)
    k_seg = _segments(j * rows + lax.broadcasted_iota(jnp.int32, (rows, 1), 0), meta_ref, first, items)
    k_seg = jnp.where(k_seg < items, k_seg, -1)
    same = q_seg == k_seg
    if diagonal:
        key = lax.broadcasted_iota(jnp.int32, (rows, rows), 0)
        query = lax.broadcasted_iota(jnp.int32, (rows, rows), 1)
        return (same & (key < query)) | (key == query)
    return same

def _dot(a, b, dims):
    return lax.dot_general(a, b, (dims, ((), ())), preferred_element_type=jnp.float32)

def _turned(array):
    return jnp.transpose(array.astype(jnp.float32))

def _split(array, axis=1):
    wide = array.astype(jnp.float32)
    left = lax.broadcasted_iota(jnp.int32, array.shape, axis) < 64
    return jnp.where(left, wide, 0.0).astype(jnp.bfloat16), jnp.where(left, 0.0, wide).astype(jnp.bfloat16)

def _fold(value, op):
    while value.shape[0] > 8:
        half = value.shape[0] // 2
        value = op(value[:half], value[half:])
    return value

def _put_bias(bias, line_ref, rows):
    for head in range(2):
        line = jnp.broadcast_to(line_ref[head:head + 1, :], (rows, 2 * rows))
        bias[head] = pltpu.roll(line, 0, 1, stride=1, stride_axis=0)

def _biased(raw, bias, far_ref, head, which, rows):
    if which == 0:
        return raw + bias[head, :, :rows]
    if which == 1:
        return raw + bias[head, :, rows:]
    return raw + far_ref[head]

def attend_kernel(peers, items, rows, meta_ref, far_ref, line_ref, *refs):
    parts = refs[:peers]
    outs = refs[peers:2 * peers]
    wide_ref, log_ref = refs[2 * peers:2 * peers + 2]
    qkv, turned, bias, scores, mixed = refs[2 * peers + 2:]
    me = meta_ref[0]
    for slot in range(peers):
        qkv[me ^ slot] = parts[slot][...]
        turned[me ^ slot] = _turned(parts[slot][2]).astype(jnp.bfloat16)
    _put_bias(bias, line_ref, rows)
    upper = lax.broadcasted_iota(jnp.int32, (128, rows), 0) < 64

    def one_row(i, _):
        low = meta_ref[1 + i]
        whole = jnp.minimum(meta_ref[1 + peers + i], i - 1)
        queries = _split(qkv[i, 0].astype(jnp.float32) * 0.125)

        def put(j, which, masked, peaks):
            key = qkv[j, 1]
            if masked:
                allowed = _allowed(meta_ref, peers, items, rows, i, j, which == 0)
            new = []
            for head in range(2):
                raw = _biased(_dot(key, queries[head], ((1,), (1,))), bias, far_ref, head, which, rows)
                if masked:
                    raw = jnp.where(allowed, raw, masked_score)
                scores[head, j] = raw
                new.append(jnp.maximum(peaks[head], _fold(raw, jnp.maximum)))
            return tuple(new)

        start = jnp.full((8, rows), masked_score, jnp.float32)
        peaks = put(i, 0, True, (start, start))
        peaks = lax.cond(low < i, lambda p: put(i - 1, 1, True, p), lambda p: p, peaks)
        peaks = lax.fori_loop(low, whole, lambda j, p: put(j, 2, True, p), peaks)
        peaks = lax.fori_loop(jnp.maximum(low, whole), i - 1, lambda j, p: put(j, 2, False, p), peaks)
        tops = [jnp.max(peak, axis=0, keepdims=True) for peak in peaks]

        def mix(j, carry):
            sums, total = carry
            value = turned[j]
            new = []
            both = []
            for head in range(2):
                weight = jnp.exp(scores[head, j] - tops[head])
                new.append(sums[head] + _fold(weight, jnp.add))
                both.append(_dot(value[64 * head:64 * head + 64], weight.astype(jnp.bfloat16), ((1,), (0,))))
            return tuple(new), total + jnp.concatenate(both)

        nothing = jnp.zeros((8, rows), jnp.float32)
        sums, total = lax.fori_loop(low, i + 1, mix, ((nothing, nothing), jnp.zeros((128, rows), jnp.float32)))
        sums = [jnp.sum(s, axis=0, keepdims=True) for s in sums]
        total = total / jnp.where(upper, sums[0], sums[1])
        wide_ref[i] = total
        for head in range(2):
            log_ref[i, head:head + 1, :] = tops[head] + jnp.log(sums[head])
        mixed[i] = jnp.transpose(total).astype(jnp.bfloat16)
        return 0

    lax.fori_loop(0, peers, one_row, 0)
    for slot in range(peers):
        outs[slot][...] = mixed[me ^ slot]

def attend(meta, far, line, parts, items):
    peers = len(parts)
    rows = parts[0].shape[1]
    smem = pl.BlockSpec(memory_space=pltpu.SMEM)
    vmem = pl.BlockSpec(memory_space=pltpu.VMEM)
    shapes = [jax.ShapeDtypeStruct((rows, 128), jnp.bfloat16)] * peers + [
        jax.ShapeDtypeStruct((peers, 128, rows), jnp.float32),
        jax.ShapeDtypeStruct((peers, 8, rows), jnp.float32),
    ]
    res = pl.pallas_call(
        partial(attend_kernel, peers, items, rows),
        out_shape=shapes,
        in_specs=[smem, smem] + [vmem] * (peers + 1),
        out_specs=[vmem] * (peers + 2),
        scratch_shapes=[
            pltpu.VMEM((peers, 3, rows, 128), jnp.bfloat16),
            pltpu.VMEM((peers, 128, rows), jnp.bfloat16),
            pltpu.VMEM((2, rows, 2 * rows), jnp.float32),
            pltpu.VMEM((2, peers, rows, rows), jnp.float32),
            pltpu.VMEM((peers, rows, 128), jnp.bfloat16),
        ],
        compiler_params=pltpu.CompilerParams(vmem_limit_bytes=40 * 2**20),
        cost_estimate=pl.CostEstimate(flops=8 * 10**9, bytes_accessed=4 * 2**20, transcendentals=3 * 10**6),
        name="attend",
    )(meta, far, line, *parts)
    return res[:peers], res[peers], res[peers + 1]

def attend_back_kernel(peers, items, rows, meta_ref, far_ref, line_ref, wide_ref, log_ref, *refs):
    parts = refs[:peers]
    grads = refs[peers:2 * peers]
    outs = refs[2 * peers:3 * peers]
    all_ref, table_ref = refs[3 * peers:3 * peers + 2]
    qkv, cot, turned, bias, near, far_sum, dkey, dvalue = refs[3 * peers + 2:]
    me = meta_ref[0]
    for slot in range(peers):
        qkv[me ^ slot] = parts[slot][...]
        cot[me ^ slot] = grads[slot][...]
        turned[me ^ slot] = _turned(parts[slot][1]).astype(jnp.bfloat16)
    _put_bias(bias, line_ref, rows)
    near[...] = jnp.zeros_like(near)
    far_sum[...] = jnp.zeros_like(far_sum)
    dkey[...] = jnp.zeros_like(dkey)
    dvalue[...] = jnp.zeros_like(dvalue)

    def one_row(i, _):
        low = meta_ref[1 + i]
        whole = jnp.minimum(meta_ref[1 + peers + i], i - 1)
        queries = _split(qkv[i, 0].astype(jnp.float32) * 0.125)
        grad = cot[i]
        grads_ = _split(grad)
        product = _turned(grad) * wide_ref[i]
        dots = [jnp.sum(product[64 * head:64 * head + 64], axis=0, keepdims=True) for head in range(2)]
        logs = [log_ref[i, head:head + 1, :] for head in range(2)]

        def step(j, which, masked, dquery):
            key = qkv[j, 1]
            value = qkv[j, 2]
            across = turned[j]
            if masked:
                allowed = _allowed(meta_ref, peers, items, rows, i, j, which == 0)
            dk = jnp.zeros((rows, 128), jnp.float32)
            dv = jnp.zeros((rows, 128), jnp.float32)
            both = []
            for head in range(2):
                raw = _biased(_dot(key, queries[head], ((1,), (1,))), bias, far_ref, head, which, rows)
                if masked:
                    raw = jnp.where(allowed, raw, masked_score)
                weight = jnp.exp(raw - logs[head])
                dweight = _dot(value, grads_[head], ((1,), (1,)))
                dscore = weight * (dweight - dots[head])
                low_score = dscore.astype(jnp.bfloat16)
                if which == 0:
                    near[head, :, :rows] += dscore
                elif which == 1:
                    near[head, :, rows:] += dscore
                else:
                    far_sum[head] += _fold(dscore, jnp.add)
                both.append(_dot(across[64 * head:64 * head + 64], low_score, ((1,), (0,))))
                dk = dk + _dot(low_score, queries[head], ((1,), (0,)))
                dv = dv + _dot(weight.astype(jnp.bfloat16), grads_[head], ((1,), (0,)))
            dkey[j] += dk
            dvalue[j] += dv
            return dquery + jnp.concatenate(both)

        dquery = step(i, 0, True, jnp.zeros((128, rows), jnp.float32))
        dquery = lax.cond(low < i, lambda d: step(i - 1, 1, True, d), lambda d: d, dquery)
        dquery = lax.fori_loop(low, whole, lambda j, d: step(j, 2, True, d), dquery)
        dquery = lax.fori_loop(jnp.maximum(low, whole), i - 1, lambda j, d: step(j, 2, False, d), dquery)
        all_ref[i, 0] = (jnp.transpose(dquery) * 0.125).astype(jnp.bfloat16)
        return 0

    lax.fori_loop(0, peers, one_row, 0)
    for i in range(peers):
        all_ref[i, 1] = dkey[i].astype(jnp.bfloat16)
        all_ref[i, 2] = dvalue[i].astype(jnp.bfloat16)
    for slot in range(peers):
        outs[slot][...] = all_ref[me ^ slot]
    wide = 2 * rows
    sub = lax.broadcasted_iota(jnp.int32, (8, wide), 0)
    for head in range(2):
        part = near[head]
        count = rows
        while count > 8:
            count //= 2
            part = part[:count] + pltpu.roll(part[count:], wide - count, 1)
        for bit in (4, 2, 1):
            part = jnp.where((sub & bit) != 0, pltpu.roll(part, wide - bit, 1), part)
        total = far_sum[head]
        table_ref[head, :, :rows] = part[:, :rows]
        table_ref[head, :, rows:] = part[:, rows:] + jnp.concatenate([jnp.zeros((8, rows - 128), jnp.float32), total[:, :128] + total[:, 128:]], axis=1)

def attend_back(meta, far, line, wide, logs, parts, grads, items):
    peers = len(parts)
    rows = parts[0].shape[1]
    smem = pl.BlockSpec(memory_space=pltpu.SMEM)
    vmem = pl.BlockSpec(memory_space=pltpu.VMEM)
    shapes = [jax.ShapeDtypeStruct((3, rows, 128), jnp.bfloat16)] * peers + [
        jax.ShapeDtypeStruct((peers, 3, rows, 128), jnp.bfloat16),
        jax.ShapeDtypeStruct((2, 8, 2 * rows), jnp.float32),
    ]
    res = pl.pallas_call(
        partial(attend_back_kernel, peers, items, rows),
        out_shape=shapes,
        in_specs=[smem, smem] + [vmem] * (2 * peers + 3),
        out_specs=[vmem] * (peers + 2),
        scratch_shapes=[
            pltpu.VMEM((peers, 3, rows, 128), jnp.bfloat16),
            pltpu.VMEM((peers, rows, 128), jnp.bfloat16),
            pltpu.VMEM((peers, 128, rows), jnp.bfloat16),
            pltpu.VMEM((2, rows, 2 * rows), jnp.float32),
            pltpu.VMEM((2, rows, 2 * rows), jnp.float32),
            pltpu.VMEM((2, 8, rows), jnp.float32),
            pltpu.VMEM((peers, rows, 128), jnp.float32),
            pltpu.VMEM((peers, rows, 128), jnp.float32),
        ],
        compiler_params=pltpu.CompilerParams(vmem_limit_bytes=40 * 2**20),
        cost_estimate=pl.CostEstimate(flops=20 * 10**9, bytes_accessed=8 * 2**20, transcendentals=3 * 10**6),
        name="attend_back",
    )(meta, far, line, wide, logs, *parts, *grads)
    return res[:peers], res[peers], jnp.sum(res[peers + 1], axis=1)

def plan(lengths, me, peers, rows):
    ends = jnp.cumsum(lengths)
    items = lengths.shape[0]
    place = jnp.arange(peers, dtype=jnp.int32)
    first = jnp.sum((place[:, None] * rows >= ends[None]).astype(jnp.int32), axis=1)
    last = jnp.sum((place[:, None] * rows + rows - 1 >= ends[None]).astype(jnp.int32), axis=1)
    low = jnp.sum((last[None, :] < first[:, None]).astype(jnp.int32), axis=1)
    low = jnp.where(first < items, jnp.minimum(low, place), place)
    whole = jnp.sum((first[None, :] < last[:, None]).astype(jnp.int32), axis=1)
    return jnp.concatenate([me[None].astype(jnp.int32), low, whole, ends.astype(jnp.int32)])
def bucket_lines(rows, buckets):
    k = jnp.arange(2 * rows, dtype=jnp.int32)
    return (bucket_of(k)[None, :] == jnp.arange(buckets, dtype=jnp.int32)[:, None]).astype(jnp.float32)


def _unit(value):
    mean = jnp.mean(value, axis=-1, keepdims=True)
    centred = value - mean
    variance = jnp.mean(centred * centred, axis=-1, keepdims=True)
    scale = lax.rsqrt(variance + epsilon)
    return centred * scale, scale


def _norm_back(grad, unit, scale, gain, sums_ref):
    inner = grad * gain
    first = jnp.mean(inner, axis=-1, keepdims=True)
    second = jnp.mean(inner * unit, axis=-1, keepdims=True)
    sums_ref[0:1, :] = jnp.sum(grad * unit, axis=0, keepdims=True)
    sums_ref[1:2, :] = jnp.sum(grad, axis=0, keepdims=True)
    return scale * (inner - first - unit * second)


def _lanes(index):
    return pl.ds(pl.multiple_of(index * 128, 128), 128)


def _specs(*kinds):
    places = {"s": pltpu.SMEM, "v": pltpu.VMEM, "a": pl.ANY}
    return [pl.BlockSpec(memory_space=places[kind]) for word in kinds for kind in word]


def _params(**more):
    return pltpu.CompilerParams(vmem_limit_bytes=44 * 2**20, **more)


def project_kernel(peers, meta_ref, tokens_ref, gain_ref, shift_ref, weight_ref, *refs):
    outs, act_ref, held, arrived = refs[:peers], refs[peers], refs[peers + 1], refs[peers + 2]
    me = meta_ref[0]
    copies = []
    for slot in range(peers):
        for block in range(3):
            columns = _lanes(block * peers + (me ^ slot))
            copies.append(pltpu.make_async_copy(weight_ref.at[:, columns], held.at[slot, block], arrived.at[slot, block]))
            copies[-1].start()
    unit, _ = _unit(tokens_ref[...].astype(jnp.float32))
    act = (unit * gain_ref[...] + shift_ref[...]).astype(jnp.bfloat16)
    act_ref[...] = act
    for slot in range(peers):
        for block in range(3):
            copies[3 * slot + block].wait()
            outs[slot][block] = _dot(act, held[slot, block], ((1,), (0,))).astype(jnp.bfloat16)


def project(meta, tokens, gain, shift, weight, peers):
    rows, width = tokens.shape
    return pl.pallas_call(
        partial(project_kernel, peers),
        out_shape=[jax.ShapeDtypeStruct((3, rows, 128), jnp.bfloat16)] * peers + [jax.ShapeDtypeStruct((rows, width), jnp.bfloat16)],
        in_specs=_specs("svvva"),
        out_specs=_specs("v" * (peers + 1)),
        scratch_shapes=[pltpu.VMEM((peers, 3, width, 128), jnp.bfloat16), pltpu.SemaphoreType.DMA((peers, 3))],
        compiler_params=_params(),
        cost_estimate=pl.CostEstimate(flops=4 * 10**9, bytes_accessed=8 * 2**20, transcendentals=0),
        name="project",
    )(meta, tokens, gain, shift, weight)


def merge_kernel(peers, meta_ref, tokens_ref, gain_ref, shift_ref, weight_ref, *refs):
    parts = refs[:peers]
    low_ref, middle_ref, act_ref = refs[peers:]
    me = meta_ref[0]
    for slot in range(peers):
        low_ref[:, _lanes(me ^ slot)] = parts[slot][...]
    middle = tokens_ref[...].astype(jnp.float32) + _dot(low_ref[...], weight_ref[...], ((1,), (0,)))
    middle_ref[...] = middle
    unit, _ = _unit(middle)
    act_ref[...] = (unit * gain_ref[...] + shift_ref[...]).astype(jnp.bfloat16)


def merge(meta, tokens, gain, shift, weight, parts):
    shape, peers = tokens.shape, len(parts)
    return pl.pallas_call(
        partial(merge_kernel, peers),
        out_shape=[jax.ShapeDtypeStruct(shape, t) for t in (jnp.bfloat16, jnp.float32, jnp.bfloat16)],
        in_specs=_specs("svvvv", "v" * peers),
        out_specs=_specs("vvv"),
        compiler_params=_params(),
        cost_estimate=pl.CostEstimate(flops=10**9, bytes_accessed=5 * 2**20, transcendentals=0),
        name="merge",
    )(meta, tokens, gain, shift, weight, *parts)


def feed_kernel(
    peers, rows, part, meta_ref, act_mine, act_other, grad_mine, grad_other, expand_ref, contract_ref,
    out_keep, out_send, in_keep, in_send, c_one_keep, c_one_send, c_two_keep, c_two_send,
    e_one_keep, e_one_send, e_two_keep, e_two_send, acts, grads, out_total, in_total, block_grad,
):
    step = pl.program_id(0)
    x, y = meta_ref[1], meta_ref[2]
    cut = c_one_keep.shape[2]
    group = block_grad.shape[1]
    half = group // 2

    @pl.when(step == 0)
    def _():
        acts[:rows] = act_mine[...]
        acts[rows:] = act_other[...]
        grads[:rows] = grad_mine[...]
        grads[rows:] = grad_other[...]

    before = _dot(acts[...], expand_ref[...], ((1,), (0,)))
    pulled = _dot(grads[...], contract_ref[...], ((1,), (1,)))
    rate = 0.5 * (1.0 + lax.erf(before * math.sqrt(0.5)))
    low = (before * rate).astype(jnp.bfloat16)
    slope = rate + before * jnp.exp(-0.5 * before * before) * (1.0 / math.sqrt(2.0 * math.pi))
    back = (pulled * slope).astype(jnp.bfloat16)
    out_part = _dot(low, contract_ref[...], ((1,), (0,)))
    in_part = _dot(back, expand_ref[...], ((1,), (1,)))

    @pl.when(step == 0)
    def _():
        out_total[...] = out_part
        in_total[...] = in_part

    @pl.when(step > 0)
    def _():
        out_total[...] += out_part
        in_total[...] += in_part

    contract_grad = _dot(low, grads[...], ((0,), (0,))).astype(jnp.bfloat16)
    level = step // 2

    @pl.when(step % 2 == x)
    def _():
        c_one_keep[level] = contract_grad[:, :cut]

    @pl.when(step % 2 != x)
    def _():
        c_one_send[level] = contract_grad[:, :cut]

    @pl.when(y == 0)
    def _():
        c_two_keep[step] = contract_grad[: part // 2, cut:]
        c_two_send[step] = contract_grad[part // 2 :, cut:]

    @pl.when(y != 0)
    def _():
        c_two_keep[step] = contract_grad[part // 2 :, cut:]
        c_two_send[step] = contract_grad[: part // 2, cut:]

    expand_grad = _dot(acts[...], back, ((0,), (0,))).astype(jnp.bfloat16)
    block_grad[...] = expand_grad.reshape(peers, group, part)
    near = peers // 2

    @pl.when(step < near)
    def _():
        columns = pl.ds(pl.multiple_of(step * part, part), part)
        for place in range(near):
            e_one_keep[place, :, columns] = block_grad[2 * place + x]
            e_one_send[place, :, columns] = block_grad[2 * place + 1 - x]

    @pl.when(step >= near)
    def _():
        columns = pl.ds(pl.multiple_of((step - near) * part, part), part)
        for place in range(peers):
            e_two_keep[place, :, columns] = block_grad[place, pl.ds(pl.multiple_of(y * half, half), half), :]
            e_two_send[place, :, columns] = block_grad[place, pl.ds(pl.multiple_of((1 - y) * half, half), half), :]

    @pl.when(step == peers - 1)
    def _():
        out_keep[...] = out_total[:rows]
        out_send[...] = out_total[rows:].astype(jnp.bfloat16)
        in_keep[...] = in_total[:rows]
        in_send[...] = in_total[rows:]


def feed(meta, act_mine, act_other, grad_mine, grad_other, expand_weight, contract_weight, peers):
    rows, width = act_mine.shape
    part = expand_weight.shape[1] // (2 * peers)
    group, cut = width // peers, width // 2
    whole = lambda *shape: pl.BlockSpec(shape, lambda step, meta_ref: (0,) * len(shape))
    shapes = [
        ((rows, width), jnp.float32),
        ((rows, width), jnp.bfloat16),
        ((rows, width), jnp.float32),
        ((rows, width), jnp.float32),
        ((peers // 2, part, cut), jnp.bfloat16),
        ((peers // 2, part, cut), jnp.bfloat16),
        ((peers, part // 2, cut), jnp.bfloat16),
        ((peers, part // 2, cut), jnp.bfloat16),
        ((peers // 2, group, part * peers // 2), jnp.bfloat16),
        ((peers // 2, group, part * peers // 2), jnp.bfloat16),
        ((peers, group // 2, part * peers // 2), jnp.bfloat16),
        ((peers, group // 2, part * peers // 2), jnp.bfloat16),
    ]
    return pl.pallas_call(
        partial(feed_kernel, peers, rows, part),
        out_shape=[jax.ShapeDtypeStruct(*shape) for shape in shapes],
        grid_spec=pltpu.PrefetchScalarGridSpec(
            num_scalar_prefetch=1,
            grid=(peers,),
            in_specs=[whole(rows, width)] * 4
            + [
                pl.BlockSpec((width, part), lambda step, meta_ref: (0, 2 * step + meta_ref[3])),
                pl.BlockSpec((part, width), lambda step, meta_ref: (2 * step + meta_ref[3], 0)),
            ],
            out_specs=[whole(*shape) for shape, _ in shapes],
            scratch_shapes=[
                pltpu.VMEM((2 * rows, width), jnp.bfloat16),
                pltpu.VMEM((2 * rows, width), jnp.bfloat16),
                pltpu.VMEM((2 * rows, width), jnp.float32),
                pltpu.VMEM((2 * rows, width), jnp.float32),
                pltpu.VMEM((peers, group, part), jnp.bfloat16),
            ],
        ),
        compiler_params=_params(),
        cost_estimate=pl.CostEstimate(flops=13 * 10**9, bytes_accessed=24 * 2**20, transcendentals=2 * 10**6),
        name="feed",
    )(meta, act_mine, act_other, grad_mine, grad_other, expand_weight, contract_weight)


def turn_kernel(peers, meta_ref, in_mine, in_other, middle_ref, grad_ref, gain_ref, weight_ref, *refs):
    outs = refs[:peers]
    total_ref, keep_ref, send_ref, sums_ref, held = refs[peers:]
    me, core = meta_ref[0], meta_ref[3]
    half = keep_ref.shape[1]
    unit, scale = _unit(middle_ref[...])
    total = grad_ref[...].astype(jnp.float32) + _norm_back(in_mine[...] + in_other[...], unit, scale, gain_ref[...], sums_ref)
    total_ref[...] = total
    low = total.astype(jnp.bfloat16)

    @pl.when(core == 0)
    def _():
        keep_ref[...] = low[:, :half]
        send_ref[...] = low[:, half:]

    @pl.when(core != 0)
    def _():
        keep_ref[...] = low[:, half:]
        send_ref[...] = low[:, :half]

    held[...] = _dot(low, weight_ref[...], ((1,), (1,))).astype(jnp.bfloat16)
    for slot in range(peers):
        outs[slot][...] = held[:, _lanes(me ^ slot)]


def turn(meta, in_mine, in_other, middle, grad, gain, weight, peers):
    rows, width = middle.shape
    shapes = [((rows, 128), jnp.bfloat16)] * peers + [
        ((rows, width), jnp.float32),
        ((rows, width // 2), jnp.bfloat16),
        ((rows, width // 2), jnp.bfloat16),
        ((2, width), jnp.float32),
    ]
    return pl.pallas_call(
        partial(turn_kernel, peers),
        out_shape=[jax.ShapeDtypeStruct(*shape) for shape in shapes],
        in_specs=_specs("svvvvvv"),
        out_specs=_specs("v" * len(shapes)),
        scratch_shapes=[pltpu.VMEM((rows, width), jnp.bfloat16)],
        compiler_params=_params(),
        cost_estimate=pl.CostEstimate(flops=10**9, bytes_accessed=8 * 2**20, transcendentals=0),
        name="turn",
    )(meta, in_mine, in_other, middle, grad, gain, weight)


def close_kernel(peers, meta_ref, tokens_ref, grad_ref, gain_ref, weight_ref, *refs):
    parts = refs[:peers]
    out_ref, sums_ref, held = refs[peers:]
    me = meta_ref[0]
    for slot in range(peers):
        for block in range(3):
            held[:, _lanes(block * peers + (me ^ slot))] = parts[slot][block]
    back = _dot(held[...], weight_ref[...], ((1,), (1,)))
    unit, scale = _unit(tokens_ref[...].astype(jnp.float32))
    out_ref[...] = grad_ref[...] + _norm_back(back, unit, scale, gain_ref[...], sums_ref)


def close(meta, tokens, grad, gain, weight, parts):
    rows, width = tokens.shape
    peers = len(parts)
    return pl.pallas_call(
        partial(close_kernel, peers),
        out_shape=[jax.ShapeDtypeStruct((rows, width), jnp.float32), jax.ShapeDtypeStruct((2, width), jnp.float32)],
        in_specs=_specs("svvvv", "v" * peers),
        out_specs=_specs("vv"),
        scratch_shapes=[pltpu.VMEM((rows, 3 * width), jnp.bfloat16)],
        compiler_params=_params(),
        cost_estimate=pl.CostEstimate(flops=2 * 10**9, bytes_accessed=10 * 2**20, transcendentals=0),
        name="close",
    )(meta, tokens, grad, gain, weight, *parts)


def flipped(array, axis, mask):
    peers = lax.axis_size(axis)
    return lax.ppermute(array, axis, [(i, i ^ mask) for i in range(peers)])


def pick(array, index, axis):
    return lax.dynamic_index_in_dim(array, index, axis, keepdims=False)


def added(a, b):
    return (a.astype(jnp.float32) + b.astype(jnp.float32)).astype(jnp.bfloat16)


def in_order(mine, other, bit, axis):
    lower = jnp.where(bit == 0, mine, other)
    upper = jnp.where(bit == 0, other, mine)
    return jnp.concatenate([lower, upper], axis=axis)


def over_chips(one_keep, one_send, two_keep, two_send, place):
    z, x, y = place
    levels, rows, cut = one_keep.shape
    half = rows // 2
    one_got = flipped(one_send, "blk", 1)
    two_got = flipped(two_send, "seq", 2)

    def sums(keep, got, shape, index, axis):
        return added(pick(keep.reshape(shape), index, axis), pick(got.reshape(shape), index, axis))

    tall, wide = (levels, 2, half, cut), (levels, 2, half, cut)
    one_next = flipped(sums(one_keep, one_got, tall, 1 - y, 1), "seq", 2)
    two_next = flipped(sums(two_keep, two_got, wide, 1 - x, 1), "blk", 1)
    one = added(sums(one_keep, one_got, tall, y, 1), one_next)
    two = added(sums(two_keep, two_got, wide, x, 1), two_next)
    both = jnp.concatenate([one, two], axis=-1)
    total = pick(both, z, 0).astype(jnp.float32)
    for step in range(1, levels):
        total = total + flipped(pick(both, z ^ step, 0), "blk", 2 * step).astype(jnp.float32)
    return total.astype(jnp.bfloat16)


def local_by_heads(
    tokens,
    lengths,
    attend_weight,
    merge_weight,
    expand_weight,
    contract_weight,
    gain_first,
    shift_first,
    gain_second,
    shift_second,
    bias_table,
    cotangent,
):
    rows, width = tokens.shape[1], tokens.shape[2]
    buckets, heads = bias_table.shape
    hidden = expand_weight.shape[1]
    items = lengths.shape[1]
    peers = lax.axis_size("blk")
    levels = peers // 2
    group = width // peers
    part = hidden // (2 * peers)
    me, line_of = lax.axis_index("blk"), lax.axis_index("seq")
    z, x, y, core = me // 2, me % 2, line_of // 2, line_of % 2
    place = (z, x, y)
    here = jnp.stack([me, x, y, core]).astype(jnp.int32)
    gain_first, shift_first, gain_second, shift_second = (
        v.reshape(1, width) for v in (gain_first, shift_first, gain_second, shift_second)
    )

    own, grad_out = tokens[0], cotangent[0]
    grad_other = flipped(grad_out, "seq", 1)
    meta = plan(lengths[0], me, peers, rows)
    hot = bucket_lines(rows, buckets)
    table_mine = lax.dynamic_slice_in_dim(bias_table, 2 * me, 2, 1)
    lines = jnp.dot(table_mine.T, hot, precision=highest)
    far = table_mine[buckets - 1]

    def exchanged(parts):
        return [parts[0]] + [flipped(parts[step], "blk", step) for step in range(1, peers)]

    def ordered(parts):
        stack = jnp.stack(parts)
        return jnp.stack([pick(stack, me ^ peer, 0) for peer in range(peers)])

    *parts, act_first = project(here, own, gain_first, shift_first, attend_weight, peers)
    parts = exchanged(parts)
    act_all = lax.all_gather(act_first, "blk", axis=0, tiled=True)
    mixed, wide, logs = attend(meta, far, lines, parts, items)
    attn_low, middle, act_second = merge(here, own, gain_second, shift_second, merge_weight, exchanged(mixed))
    act_other = flipped(act_second, "seq", 1)
    out_keep, out_send, in_keep, in_send, *grads = feed(
        here, act_second, act_other, grad_out, grad_other, expand_weight, contract_weight, peers
    )
    *grad_heads, grad_middle, keep_low, send_low, sums_second = turn(
        here, in_keep, flipped(in_send, "seq", 1), middle, grad_out, gain_second, merge_weight, peers
    )
    back_parts, back_all, line_grad = attend_back(meta, far, lines, wide, logs, parts, exchanged(grad_heads), items)
    tokens_grad, sums_first = close(here, own, grad_middle, gain_first, attend_weight, exchanged(back_parts))
    output = (middle + out_keep + flipped(out_send, "seq", 1).astype(jnp.float32)).astype(jnp.bfloat16)

    contract_grad = over_chips(*grads[:4], place)
    expand_grad = over_chips(*grads[4:], place)
    attn_both = jnp.concatenate([attn_low, flipped(attn_low, "seq", 1)])
    merge_right = jnp.concatenate([keep_low, flipped(send_low, "seq", 1)])
    merge_grad = jnp.einsum("td,te->de", attn_both, merge_right, preferred_element_type=jnp.float32).astype(jnp.bfloat16)
    merge_grad = merge_grad.reshape(levels, 2, group, width // 2)
    one, two = merge_grad[..., : width // 4], merge_grad[..., width // 4 :].reshape(levels, 2, 2, group // 2, width // 4)
    merge_grad = over_chips(pick(one, x, 1), pick(one, 1 - x, 1), pick(two, y, 2), pick(two, 1 - y, 2), place)
    attend_grad = jnp.einsum(
        "td,te->de",
        act_all,
        back_all.transpose(0, 2, 1, 3).reshape(peers * rows, 3 * group),
        preferred_element_type=jnp.float32,
    ).astype(jnp.bfloat16)
    attend_grad = attend_grad.reshape(peers, 2, group // 2, 3 * group)
    attend_grad = added(pick(attend_grad, core, 1), flipped(pick(attend_grad, 1 - core, 1), "seq", 1))
    attend_grad = attend_grad.reshape(peers, 2, group // 4, 3 * group)
    attend_grad = added(pick(attend_grad, y, 1), flipped(pick(attend_grad, 1 - y, 1), "seq", 2))
    attend_grad = ordered(exchanged([pick(attend_grad, me ^ slot, 0) for slot in range(peers)]))

    contract_grad = in_order(contract_grad, flipped(contract_grad, "seq", 2), y, 0)
    contract_grad = in_order(contract_grad, flipped(contract_grad, "seq", 1), core, 0).astype(jnp.float32)
    expand_grad = in_order(expand_grad, flipped(expand_grad, "seq", 2), y, 0)
    expand_other = flipped(expand_grad, "seq", 1)
    expand_halves = [jnp.where(core == side, expand_grad, expand_other) for side in range(2)]
    expand_grad = jnp.concatenate(
        [expand_halves[side][:, part * peer : part * (peer + 1)] for peer in range(peers) for side in range(2)], axis=1
    ).astype(jnp.float32)
    merge_grad = in_order(merge_grad, flipped(merge_grad, "seq", 2), y, 0)
    merge_grad = in_order(merge_grad, flipped(merge_grad, "seq", 1), core, 1).astype(jnp.float32)
    attend_grad = in_order(attend_grad, flipped(attend_grad, "seq", 2), y, 1)
    attend_grad = in_order(attend_grad, flipped(attend_grad, "seq", 1), core, 1)
    attend_grad = attend_grad.reshape(peers, group, 3, group).transpose(1, 2, 0, 3).reshape(group, 3 * width).astype(jnp.float32)

    table_mine = jnp.dot(hot, line_grad.T, precision=highest)
    table_local = lax.dynamic_update_slice(jnp.zeros((buckets, heads), jnp.float32), table_mine, (0, 2 * me))
    table_row = jnp.pad(table_local.reshape(1, buckets * heads), ((0, 0), (0, width - buckets * heads)))
    small = jnp.concatenate([sums_first, sums_second, table_row])
    for axis, mask in (("seq", 1), ("seq", 2), ("blk", 1), ("blk", 2), ("blk", 4)):
        small = small + flipped(small, axis, mask)
    table_grad = small[4, : buckets * heads].reshape(buckets, heads)
    vectors = lax.dynamic_slice_in_dim(small, me * group, group, 1)
    return (
        output[None],
        tokens_grad[None],
        attend_grad,
        merge_grad,
        expand_grad,
        contract_grad,
        vectors[0],
        vectors[1],
        vectors[2],
        vectors[3],
        table_grad,
    )


def local(*arguments):
    heads = arguments[10].shape[1]
    rows = arguments[0].shape[1]
    peers = lax.axis_size("blk")
    if peers == 8 and lax.axis_size("seq") == 4 and heads == 2 * peers and rows == 256:
        return local_by_heads(*arguments)
    return local_by_runs(*arguments)


def solution(mesh):
    in_specs = (
        P("seq", "blk", None),
        P("seq", None),
        P(),
        P(),
        P(),
        P(),
        P(),
        P(),
        P(),
        P(),
        P(),
        P("seq", "blk", None),
    )
    out_specs = (
        P("seq", "blk", None),
        P("seq", "blk", None),
        P("blk", None),
        P("blk", None),
        P("blk", None),
        P("blk", None),
        P("blk"),
        P("blk"),
        P("blk"),
        P("blk"),
        P(),
    )
    return jax.shard_map(local, mesh=mesh, in_specs=in_specs, out_specs=out_specs, check_vma=False)
```

```python
from functools import partial
import math

import jax
import jax.numpy as jnp
from jax import lax
from jax.experimental import pallas as pl
from jax.experimental.pallas import tpu as pltpu
from jax.sharding import PartitionSpec as P

HOPS = 6


epsilon = 1e-05
masked_score = -1e30
highest = lax.Precision.HIGHEST
bucket_edges = [math.ceil(16 * 8 ** (t / 16)) for t in range(1, 16)]


def shifted(array, axis, by):
    peers = lax.axis_size(axis)
    pairs = [(i, i + by) for i in range(peers) if 0 <= i + by < peers]
    return lax.ppermute(array, axis, pairs)


def shortened(array):

    def short(part):
        return part.astype(jnp.bfloat16) if part.dtype == jnp.float32 else part

    return jax.tree.map(short, array)


def bucket_of(distance):
    total = jnp.minimum(jnp.maximum(distance, 0), 16)
    for edge in bucket_edges:
        total = total + (distance >= edge).astype(jnp.int32)
    return total


def segment_of(position, ends):
    return jnp.sum((position[:, None] >= ends[None, :]).astype(jnp.int32), axis=1)


def layer_norm(value, gain, shift):
    mean = jnp.mean(value, axis=-1, keepdims=True)
    centred = value - mean
    variance = jnp.mean(centred * centred, axis=-1, keepdims=True)
    return centred * lax.rsqrt(variance + epsilon) * gain + shift


def diagonal_sums(grid, count):
    heads = grid.shape[0]
    padded = jnp.pad(jnp.flip(grid, axis=-1), ((0, 0), (0, 0), (0, count)))
    flat = padded.reshape(heads, 2 * count * count)[:, : count * (2 * count - 1)]
    return jnp.sum(flat.reshape(heads, count, 2 * count - 1), axis=1)


def band_matrix(line, count):
    heads = line.shape[0]
    flipped = jnp.flip(line, axis=-1)
    tiled = jnp.tile(flipped, (1, count))
    window = tiled[:, count - 1 : count - 1 + count * (2 * count - 2)]
    return window.reshape(heads, count, 2 * count - 2)[:, :, :count]


def fetch_earlier(block):
    earlier = []
    moving = block
    for hop in range(HOPS):
        moving = shifted(moving, "blk", 1)
        earlier.append(moving)
    return earlier


def return_parts(parts):
    carried = jnp.zeros_like(parts[0])
    for hop in range(HOPS, 0, -1):
        carried = shifted(shortened(carried + parts[hop - 1]), "blk", -1)
    return carried


def local_by_runs(
    tokens,
    lengths,
    attend_weight,
    merge_weight,
    expand_weight,
    contract_weight,
    gain_first,
    shift_first,
    gain_second,
    shift_second,
    bias_table,
    cotangent,
):
    rows = tokens.shape[1]
    width = tokens.shape[2]
    heads = bias_table.shape[1]
    buckets = bias_table.shape[0]
    head_size = width // heads
    items = lengths.shape[1]
    start = lax.axis_index("blk") * rows
    query_pos = start + jnp.arange(rows, dtype=jnp.int32)
    ends = jnp.cumsum(lengths[0])
    query_seg = segment_of(query_pos, ends)
    band = jnp.arange(2 * rows - 1, dtype=jnp.int32) - (rows - 1)
    bucket_ids = jnp.arange(buckets, dtype=jnp.int32)

    def pair_setup(hop):
        key_pos = query_pos - hop * rows
        key_seg = segment_of(key_pos, ends)
        key_valid = (key_pos >= 0) & (key_seg < items)
        same = key_pos[None, :] == query_pos[:, None]
        allowed = (
            (query_seg[:, None] == key_seg[None, :])
            & (key_pos[None, :] <= query_pos[:, None])
            & (key_valid[None, :] | same)
        )
        onehot = (bucket_of(hop * rows + band)[:, None] == bucket_ids[None, :]).astype(jnp.float32)
        band_bias = jnp.dot(onehot, bias_table, precision=highest).T
        bias = band_matrix(band_bias, rows)
        additive = jnp.where(allowed[None], bias, masked_score)
        return (jnp.any(allowed), onehot, additive)

    pairs = [pair_setup(hop) for hop in range(HOPS + 1)]
    residual = tokens[0].astype(jnp.float32)
    normed_first, norm_first_pull = jax.vjp(layer_norm, residual, gain_first, shift_first)
    act_first = normed_first.astype(jnp.bfloat16)
    projected = jnp.dot(act_first, attend_weight, preferred_element_type=jnp.float32).astype(
        jnp.bfloat16
    )
    query = projected[:, :width].reshape(rows, heads, head_size)
    keys_values = jnp.stack([projected[:, width : 2 * width], projected[:, 2 * width :]])
    blocks = [keys_values] + fetch_earlier(keys_values)

    def scores_of(block, pair):
        key = block[0].reshape(rows, heads, head_size)
        raw = jnp.einsum("qhe,khe->hqk", query, key, preferred_element_type=jnp.float32) * 0.125
        return raw + pair[2]

    def empty_total():
        return jnp.full((heads, rows), masked_score, jnp.float32)

    def empty_scores():
        return jnp.full((heads, rows, rows), masked_score, jnp.float32)

    log_total = empty_total()
    kept_scores = []
    for block, pair in zip(blocks, pairs):

        def part_total(block=block, pair=pair):
            scores = scores_of(block, pair)
            peak = jnp.max(scores, axis=-1)
            return (peak + jnp.log(jnp.sum(jnp.exp(scores - peak[..., None]), axis=-1)), scores)

        def skip_total():
            return (empty_total(), empty_scores())

        part_log, scores = lax.cond(pair[0], part_total, skip_total)
        log_total = jnp.logaddexp(log_total, part_log)
        kept_scores.append(scores)

    def empty_heads():
        return jnp.zeros((rows, heads, head_size), jnp.float32)

    attended = empty_heads()
    for block, pair, scores in zip(blocks, pairs, kept_scores):

        def part_mix(block=block, scores=scores):
            weights = jnp.exp(scores - log_total[..., None]).astype(jnp.bfloat16)
            value = block[1].reshape(rows, heads, head_size)
            return jnp.einsum("hqk,khe->qhe", weights, value, preferred_element_type=jnp.float32)

        attended = attended + lax.cond(pair[0], part_mix, empty_heads)
    attn_low = attended.reshape(rows, width).astype(jnp.bfloat16)
    middle = residual + jnp.dot(attn_low, merge_weight, preferred_element_type=jnp.float32)
    normed_second, norm_second_pull = jax.vjp(layer_norm, middle, gain_second, shift_second)
    act_second = normed_second.astype(jnp.bfloat16)
    hidden_pre = jnp.dot(act_second, expand_weight, preferred_element_type=jnp.float32)
    hidden, gelu_pull = jax.vjp(partial(jax.nn.gelu, approximate=False), hidden_pre)
    hidden_low = hidden.astype(jnp.bfloat16)
    output = (
        middle + jnp.dot(hidden_low, contract_weight, preferred_element_type=jnp.float32)
    ).astype(jnp.bfloat16)
    grad_out = cotangent[0]
    contract_grad = jnp.einsum(
        "tf,td->fd", hidden_low, grad_out, preferred_element_type=jnp.float32
    )
    grad_hidden = jnp.einsum(
        "td,fd->tf", grad_out, contract_weight, preferred_element_type=jnp.float32
    )
    grad_pre = gelu_pull(grad_hidden)[0].astype(jnp.bfloat16)
    expand_grad = jnp.einsum("td,tf->df", act_second, grad_pre, preferred_element_type=jnp.float32)
    grad_second = jnp.einsum(
        "tf,df->td", grad_pre, expand_weight, preferred_element_type=jnp.float32
    )
    grad_middle_norm, gain_second_grad, shift_second_grad = norm_second_pull(grad_second)
    grad_middle = grad_out.astype(jnp.float32) + grad_middle_norm
    grad_middle_low = grad_middle.astype(jnp.bfloat16)
    merge_grad = jnp.einsum(
        "td,te->de", attn_low, grad_middle_low, preferred_element_type=jnp.float32
    )
    grad_heads = (
        jnp.einsum("te,de->td", grad_middle_low, merge_weight, preferred_element_type=jnp.float32)
        .astype(jnp.bfloat16)
        .reshape(rows, heads, head_size)
    )
    row_dot = jnp.sum(grad_heads.astype(jnp.float32) * attended, axis=-1).T
    back_blocks = [keys_values] + fetch_earlier(keys_values)

    def empty_grads():
        return (
            empty_heads(),
            jnp.zeros((2, rows, width), jnp.float32),
            jnp.zeros((buckets, heads), jnp.float32),
        )

    grad_query = empty_heads()
    table_local = jnp.zeros((buckets, heads), jnp.float32)
    parts = []
    for block, pair in zip(back_blocks, pairs):

        def part_grads(block=block, pair=pair):
            key = block[0].reshape(rows, heads, head_size)
            value = block[1].reshape(rows, heads, head_size)
            weights = jnp.exp(scores_of(block, pair) - log_total[..., None])
            weights_low = weights.astype(jnp.bfloat16)
            grad_weights = jnp.einsum(
                "qhe,khe->hqk", grad_heads, value, preferred_element_type=jnp.float32
            )
            grad_scores = (weights * (grad_weights - row_dot[..., None])).astype(jnp.bfloat16)
            query_part = (
                jnp.einsum("hqk,khe->qhe", grad_scores, key, preferred_element_type=jnp.float32)
                * 0.125
            )
            key_part = (
                jnp.einsum("hqk,qhe->khe", grad_scores, query, preferred_element_type=jnp.float32)
                * 0.125
            )
            value_part = jnp.einsum(
                "hqk,qhe->khe", weights_low, grad_heads, preferred_element_type=jnp.float32
            )
            line_grad = diagonal_sums(grad_scores.astype(jnp.float32), rows)
            table_part = jnp.dot(pair[1].T, line_grad.T, precision=highest)
            return (
                query_part,
                jnp.stack([key_part.reshape(rows, width), value_part.reshape(rows, width)]),
                table_part,
            )

        query_part, pair_part, table_part = lax.cond(pair[0], part_grads, empty_grads)
        grad_query = grad_query + query_part
        table_local = table_local + table_part
        parts.append(pair_part)
    owned = (parts[0] + return_parts(parts[1:])).astype(jnp.bfloat16)
    grad_project = jnp.concatenate(
        [grad_query.reshape(rows, width).astype(jnp.bfloat16), owned[0], owned[1]], axis=1
    )
    attend_grad = jnp.einsum(
        "td,te->de", act_first, grad_project, preferred_element_type=jnp.float32
    )
    grad_first = jnp.einsum(
        "te,de->td", grad_project, attend_weight, preferred_element_type=jnp.float32
    )
    grad_input_norm, gain_first_grad, shift_first_grad = norm_first_pull(grad_first)
    tokens_grad = grad_middle + grad_input_norm
    results = (
        lax.psum_scatter(attend_grad, "blk", scatter_dimension=0, tiled=True),
        lax.psum_scatter(merge_grad, "blk", scatter_dimension=0, tiled=True),
        lax.psum_scatter(expand_grad, "blk", scatter_dimension=0, tiled=True),
        lax.psum_scatter(contract_grad, "blk", scatter_dimension=0, tiled=True),
        lax.psum_scatter(gain_first_grad, "blk", scatter_dimension=0, tiled=True),
        lax.psum_scatter(shift_first_grad, "blk", scatter_dimension=0, tiled=True),
        lax.psum_scatter(gain_second_grad, "blk", scatter_dimension=0, tiled=True),
        lax.psum_scatter(shift_second_grad, "blk", scatter_dimension=0, tiled=True),
    )
    results = (
        lax.psum(results[0].astype(jnp.bfloat16), "seq").astype(jnp.float32),
        lax.psum(results[1].astype(jnp.bfloat16), "seq").astype(jnp.float32),
        lax.psum(results[2].astype(jnp.bfloat16), "seq").astype(jnp.float32),
        lax.psum(results[3].astype(jnp.bfloat16), "seq").astype(jnp.float32),
        lax.psum(results[4].astype(jnp.bfloat16), "seq").astype(jnp.float32),
        lax.psum(results[5].astype(jnp.bfloat16), "seq").astype(jnp.float32),
        lax.psum(results[6].astype(jnp.bfloat16), "seq").astype(jnp.float32),
        lax.psum(results[7].astype(jnp.bfloat16), "seq").astype(jnp.float32),
    )
    table_grad = lax.psum(table_local, ("seq", "blk"))
    return (
        output[None],
        tokens_grad[None],
        results[0],
        results[1],
        results[2],
        results[3],
        results[4],
        results[5],
        results[6],
        results[7],
        table_grad,
    )


def _segments(position, meta_ref, first, items):
    total = jnp.zeros(position.shape, jnp.int32)
    for item in range(items):
        total = total + (position >= meta_ref[first + item]).astype(jnp.int32)
    return total

def _allowed(meta_ref, peers, items, rows, i, j, diagonal):
    first = 1 + 2 * peers
    q_seg = _segments(i * rows + lax.broadcasted_iota(jnp.int32, (1, rows), 1), meta_ref, first, items)
    k_seg = _segments(j * rows + lax.broadcasted_iota(jnp.int32, (rows, 1), 0), meta_ref, first, items)
    k_seg = jnp.where(k_seg < items, k_seg, -1)
    same = q_seg == k_seg
    if diagonal:
        key = lax.broadcasted_iota(jnp.int32, (rows, rows), 0)
        query = lax.broadcasted_iota(jnp.int32, (rows, rows), 1)
        return (same & (key < query)) | (key == query)
    return same

def _dot(a, b, dims):
    return lax.dot_general(a, b, (dims, ((), ())), preferred_element_type=jnp.float32)

def _turned(array):
    return jnp.transpose(array.astype(jnp.float32))

def _split(array, axis=1):
    wide = array.astype(jnp.float32)
    left = lax.broadcasted_iota(jnp.int32, array.shape, axis) < 64
    return jnp.where(left, wide, 0.0).astype(jnp.bfloat16), jnp.where(left, 0.0, wide).astype(jnp.bfloat16)

def _fold(value, op):
    while value.shape[0] > 8:
        half = value.shape[0] // 2
        value = op(value[:half], value[half:])
    return value

def _put_bias(bias, line_ref, rows):
    for head in range(2):
        line = jnp.broadcast_to(line_ref[head:head + 1, :], (rows, 2 * rows))
        bias[head] = pltpu.roll(line, 0, 1, stride=1, stride_axis=0)

def _biased(raw, bias, far_ref, head, which, rows):
    if which == 0:
        return raw + bias[head, :, :rows]
    if which == 1:
        return raw + bias[head, :, rows:]
    return raw + far_ref[head]

def attend_kernel(peers, items, rows, meta_ref, far_ref, line_ref, *refs):
    parts = refs[:peers]
    mixed, wide_ref, log_ref, qkv, turned, bias, scores = refs[peers:]
    me = meta_ref[0]
    for slot in range(peers):
        qkv[me ^ slot] = parts[slot][...]
        turned[me ^ slot] = _turned(parts[slot][2]).astype(jnp.bfloat16)
    _put_bias(bias, line_ref, rows)
    upper = lax.broadcasted_iota(jnp.int32, (128, rows), 0) < 64

    def one_row(i, _):
        low = meta_ref[1 + i]
        whole = jnp.minimum(meta_ref[1 + peers + i], i - 1)
        queries = _split(qkv[i, 0].astype(jnp.float32) * 0.125)

        def put(j, which, masked, peaks):
            key = qkv[j, 1]
            if masked:
                allowed = _allowed(meta_ref, peers, items, rows, i, j, which == 0)
            new = []
            for head in range(2):
                raw = _biased(_dot(key, queries[head], ((1,), (1,))), bias, far_ref, head, which, rows)
                if masked:
                    raw = jnp.where(allowed, raw, masked_score)
                scores[head, j] = raw
                new.append(jnp.maximum(peaks[head], _fold(raw, jnp.maximum)))
            return tuple(new)

        start = jnp.full((8, rows), masked_score, jnp.float32)
        peaks = put(i, 0, True, (start, start))
        peaks = lax.cond(low < i, lambda p: put(i - 1, 1, True, p), lambda p: p, peaks)
        peaks = lax.fori_loop(low, whole, lambda j, p: put(j, 2, True, p), peaks)
        peaks = lax.fori_loop(jnp.maximum(low, whole), i - 1, lambda j, p: put(j, 2, False, p), peaks)
        tops = [jnp.max(peak, axis=0, keepdims=True) for peak in peaks]

        def mix(j, carry):
            sums, total = carry
            value = turned[j]
            new = []
            both = []
            for head in range(2):
                weight = jnp.exp(scores[head, j] - tops[head])
                new.append(sums[head] + _fold(weight, jnp.add))
                both.append(_dot(value[64 * head:64 * head + 64], weight.astype(jnp.bfloat16), ((1,), (0,))))
            return tuple(new), total + jnp.concatenate(both)

        nothing = jnp.zeros((8, rows), jnp.float32)
        sums, total = lax.fori_loop(low, i + 1, mix, ((nothing, nothing), jnp.zeros((128, rows), jnp.float32)))
        sums = [jnp.sum(s, axis=0, keepdims=True) for s in sums]
        total = total / jnp.where(upper, sums[0], sums[1])
        wide_ref[i] = total
        for head in range(2):
            log_ref[i, head:head + 1, :] = tops[head] + jnp.log(sums[head])
        mixed[i] = jnp.transpose(total).astype(jnp.bfloat16)
        return 0

    lax.fori_loop(0, peers, one_row, 0)

def attend(meta, far, line, parts, items):
    peers = len(parts)
    rows = parts[0].shape[1]
    smem = pl.BlockSpec(memory_space=pltpu.SMEM)
    vmem = pl.BlockSpec(memory_space=pltpu.VMEM)
    shapes = [
        jax.ShapeDtypeStruct((peers, rows, 128), jnp.bfloat16),
        jax.ShapeDtypeStruct((peers, 128, rows), jnp.float32),
        jax.ShapeDtypeStruct((peers, 8, rows), jnp.float32),
    ]
    res = pl.pallas_call(
        partial(attend_kernel, peers, items, rows),
        out_shape=shapes,
        in_specs=[smem, smem] + [vmem] * (peers + 1),
        out_specs=[vmem] * 3,
        scratch_shapes=[
            pltpu.VMEM((peers, 3, rows, 128), jnp.bfloat16),
            pltpu.VMEM((peers, 128, rows), jnp.bfloat16),
            pltpu.VMEM((2, rows, 2 * rows), jnp.float32),
            pltpu.VMEM((2, peers, rows, rows), jnp.float32),
        ],
        compiler_params=pltpu.CompilerParams(vmem_limit_bytes=24 * 2**20),
        cost_estimate=pl.CostEstimate(flops=8 * 10**9, bytes_accessed=4 * 2**20, transcendentals=3 * 10**6),
        name="attend",
    )(meta, far, line, *parts)
    return res

def attend_back_kernel(peers, items, rows, meta_ref, far_ref, line_ref, wide_ref, log_ref, cot, *refs):
    parts = refs[:peers]
    all_ref, table_ref, qkv, turned, bias, near, far_sum, dkey, dvalue = refs[peers:]
    me = meta_ref[0]
    for slot in range(peers):
        qkv[me ^ slot] = parts[slot][...]
        turned[me ^ slot] = _turned(parts[slot][1]).astype(jnp.bfloat16)
    _put_bias(bias, line_ref, rows)
    near[...] = jnp.zeros_like(near)
    far_sum[...] = jnp.zeros_like(far_sum)
    dkey[...] = jnp.zeros_like(dkey)
    dvalue[...] = jnp.zeros_like(dvalue)

    def one_row(i, _):
        low = meta_ref[1 + i]
        whole = jnp.minimum(meta_ref[1 + peers + i], i - 1)
        queries = _split(qkv[i, 0].astype(jnp.float32) * 0.125)
        grad = cot[i]
        grads_ = _split(grad)
        product = _turned(grad) * wide_ref[i]
        dots = [jnp.sum(product[64 * head:64 * head + 64], axis=0, keepdims=True) for head in range(2)]
        logs = [log_ref[i, head:head + 1, :] for head in range(2)]

        def step(j, which, masked, dquery):
            key = qkv[j, 1]
            value = qkv[j, 2]
            across = turned[j]
            if masked:
                allowed = _allowed(meta_ref, peers, items, rows, i, j, which == 0)
            dk = jnp.zeros((rows, 128), jnp.float32)
            dv = jnp.zeros((rows, 128), jnp.float32)
            both = []
            for head in range(2):
                raw = _biased(_dot(key, queries[head], ((1,), (1,))), bias, far_ref, head, which, rows)
                if masked:
                    raw = jnp.where(allowed, raw, masked_score)
                weight = jnp.exp(raw - logs[head])
                dweight = _dot(value, grads_[head], ((1,), (1,)))
                dscore = weight * (dweight - dots[head])
                low_score = dscore.astype(jnp.bfloat16)
                if which == 0:
                    near[head, :, :rows] += dscore
                elif which == 1:
                    near[head, :, rows:] += dscore
                else:
                    far_sum[head] += _fold(dscore, jnp.add)
                both.append(_dot(across[64 * head:64 * head + 64], low_score, ((1,), (0,))))
                dk = dk + _dot(low_score, queries[head], ((1,), (0,)))
                dv = dv + _dot(weight.astype(jnp.bfloat16), grads_[head], ((1,), (0,)))
            dkey[j] += dk
            dvalue[j] += dv
            return dquery + jnp.concatenate(both)

        dquery = step(i, 0, True, jnp.zeros((128, rows), jnp.float32))
        dquery = lax.cond(low < i, lambda d: step(i - 1, 1, True, d), lambda d: d, dquery)
        dquery = lax.fori_loop(low, whole, lambda j, d: step(j, 2, True, d), dquery)
        dquery = lax.fori_loop(jnp.maximum(low, whole), i - 1, lambda j, d: step(j, 2, False, d), dquery)
        all_ref[i, 0] = (jnp.transpose(dquery) * 0.125).astype(jnp.bfloat16)
        return 0

    lax.fori_loop(0, peers, one_row, 0)
    for i in range(peers):
        all_ref[i, 1] = dkey[i].astype(jnp.bfloat16)
        all_ref[i, 2] = dvalue[i].astype(jnp.bfloat16)
    wide = 2 * rows
    sub = lax.broadcasted_iota(jnp.int32, (8, wide), 0)
    for head in range(2):
        part = near[head]
        count = rows
        while count > 8:
            count //= 2
            part = part[:count] + pltpu.roll(part[count:], wide - count, 1)
        for bit in (4, 2, 1):
            part = jnp.where((sub & bit) != 0, pltpu.roll(part, wide - bit, 1), part)
        total = far_sum[head]
        table_ref[head, :, :rows] = part[:, :rows]
        table_ref[head, :, rows:] = part[:, rows:] + jnp.concatenate([jnp.zeros((8, rows - 128), jnp.float32), total[:, :128] + total[:, 128:]], axis=1)

def attend_back(meta, far, line, wide, logs, parts, grads, items):
    peers = len(parts)
    rows = parts[0].shape[1]
    smem = pl.BlockSpec(memory_space=pltpu.SMEM)
    vmem = pl.BlockSpec(memory_space=pltpu.VMEM)
    shapes = [
        jax.ShapeDtypeStruct((peers, 3, rows, 128), jnp.bfloat16),
        jax.ShapeDtypeStruct((2, 8, 2 * rows), jnp.float32),
    ]
    res = pl.pallas_call(
        partial(attend_back_kernel, peers, items, rows),
        out_shape=shapes,
        in_specs=[smem, smem] + [vmem] * (peers + 4),
        out_specs=[vmem] * 2,
        scratch_shapes=[
            pltpu.VMEM((peers, 3, rows, 128), jnp.bfloat16),
            pltpu.VMEM((peers, 128, rows), jnp.bfloat16),
            pltpu.VMEM((2, rows, 2 * rows), jnp.float32),
            pltpu.VMEM((2, rows, 2 * rows), jnp.float32),
            pltpu.VMEM((2, 8, rows), jnp.float32),
            pltpu.VMEM((peers, rows, 128), jnp.float32),
            pltpu.VMEM((peers, rows, 128), jnp.float32),
        ],
        compiler_params=pltpu.CompilerParams(vmem_limit_bytes=24 * 2**20),
        cost_estimate=pl.CostEstimate(flops=20 * 10**9, bytes_accessed=8 * 2**20, transcendentals=3 * 10**6),
        name="attend_back",
    )(meta, far, line, wide, logs, grads, *parts)
    return res[0], jnp.sum(res[1], axis=1)

def plan(lengths, me, peers, rows):
    ends = jnp.cumsum(lengths)
    items = lengths.shape[0]
    place = jnp.arange(peers, dtype=jnp.int32)
    first = jnp.sum((place[:, None] * rows >= ends[None]).astype(jnp.int32), axis=1)
    last = jnp.sum((place[:, None] * rows + rows - 1 >= ends[None]).astype(jnp.int32), axis=1)
    low = jnp.sum((last[None, :] < first[:, None]).astype(jnp.int32), axis=1)
    low = jnp.where(first < items, jnp.minimum(low, place), place)
    whole = jnp.sum((first[None, :] < last[:, None]).astype(jnp.int32), axis=1)
    return jnp.concatenate([me[None].astype(jnp.int32), low, whole, ends.astype(jnp.int32)])
def bucket_lines(rows, buckets):
    k = jnp.arange(2 * rows, dtype=jnp.int32)
    return (bucket_of(k)[None, :] == jnp.arange(buckets, dtype=jnp.int32)[:, None]).astype(jnp.float32)


def _unit(value):
    mean = jnp.mean(value, axis=-1, keepdims=True)
    centred = value - mean
    variance = jnp.mean(centred * centred, axis=-1, keepdims=True)
    scale = lax.rsqrt(variance + epsilon)
    return centred * scale, scale


def _norm_back(grad, unit, scale, gain, sums_ref):
    inner = grad * gain
    first = jnp.mean(inner, axis=-1, keepdims=True)
    second = jnp.mean(inner * unit, axis=-1, keepdims=True)
    sums_ref[0:1, :] = jnp.sum(grad * unit, axis=0, keepdims=True)
    sums_ref[1:2, :] = jnp.sum(grad, axis=0, keepdims=True)
    return scale * (inner - first - unit * second)


def _lanes(index):
    return pl.ds(pl.multiple_of(index * 128, 128), 128)


def _specs(*kinds):
    places = {"s": pltpu.SMEM, "v": pltpu.VMEM, "h": pltpu.HBM}
    return [pl.BlockSpec(memory_space=places[kind]) for word in kinds for kind in word]


def _params(mebibytes):
    return pltpu.CompilerParams(vmem_limit_bytes=mebibytes * 2**20)


def project_kernel(peers, meta_ref, tokens_ref, gain_ref, shift_ref, weight_ref, *refs):
    outs, act_ref, held, done, arrived = refs[:peers], refs[peers], refs[peers + 1], refs[peers + 2], refs[peers + 3]
    me = meta_ref[0]
    pieces, _, span = held.shape
    copies = []
    for piece in range(pieces):
        copies.append(pltpu.make_async_copy(weight_ref.at[:, pl.ds(piece * span, span)], held.at[piece], arrived.at[piece]))
        copies[-1].start()
    unit, _ = _unit(tokens_ref[...].astype(jnp.float32))
    act = (unit * gain_ref[...] + shift_ref[...]).astype(jnp.bfloat16)
    act_ref[...] = act
    for piece in range(pieces):
        copies[piece].wait()
        got = _dot(act, held[piece], ((1,), (0,))).astype(jnp.bfloat16)
        for block in range(span // 128):
            done[piece * (span // 128) + block] = got[:, 128 * block : 128 * block + 128]
    for slot in range(peers):
        for block in range(3):
            outs[slot][block] = done[block * peers + (me ^ slot)]


def project(meta, tokens, gain, shift, weight, peers):
    rows, width = tokens.shape
    span = 512
    pieces = weight.shape[1] // span
    return pl.pallas_call(
        partial(project_kernel, peers),
        out_shape=[jax.ShapeDtypeStruct((3, rows, 128), jnp.bfloat16)] * peers + [jax.ShapeDtypeStruct((rows, width), jnp.bfloat16)],
        in_specs=_specs("svvvh"),
        out_specs=_specs("v" * (peers + 1)),
        scratch_shapes=[
            pltpu.VMEM((pieces, width, span), jnp.bfloat16),
            pltpu.VMEM((3 * peers, rows, 128), jnp.bfloat16),
            pltpu.SemaphoreType.DMA((pieces,)),
        ],
        compiler_params=_params(60),
        cost_estimate=pl.CostEstimate(flops=4 * 10**9, bytes_accessed=8 * 2**20, transcendentals=0),
        name="project",
    )(meta, tokens, gain, shift, weight)


def merge_kernel(parts_ref, tokens_ref, gain_ref, shift_ref, weight_ref, low_ref, middle_ref, act_ref):
    for part in range(parts_ref.shape[0]):
        low_ref[:, 128 * part : 128 * part + 128] = parts_ref[part]
    middle = tokens_ref[...].astype(jnp.float32) + _dot(low_ref[...], weight_ref[...], ((1,), (0,)))
    middle_ref[...] = middle
    unit, _ = _unit(middle)
    act_ref[...] = (unit * gain_ref[...] + shift_ref[...]).astype(jnp.bfloat16)


def merge(parts, tokens, gain, shift, weight):
    return pl.pallas_call(
        merge_kernel,
        out_shape=[jax.ShapeDtypeStruct(tokens.shape, t) for t in (jnp.bfloat16, jnp.float32, jnp.bfloat16)],
        in_specs=_specs("vvvvv"),
        out_specs=_specs("vvv"),
        compiler_params=_params(16),
        cost_estimate=pl.CostEstimate(flops=10**9, bytes_accessed=5 * 2**20, transcendentals=0),
        name="merge",
    )(parts, tokens, gain, shift, weight)


def _both(ref, mine, other):
    rows = mine.shape[0]
    ref[:rows] = mine[...]
    ref[rows:] = other[...]


def _whole(*shape):
    return pl.BlockSpec(shape, lambda step, meta_ref: (0,) * len(shape))


def _across(rows, columns):
    return pl.BlockSpec((rows, columns), lambda step, meta_ref: (0, step))


def pull_kernel(meta_ref, mine, other, contract_ref, out_ref, grads):
    @pl.when(pl.program_id(0) == 0)
    def _():
        _both(grads, mine, other)

    out_ref[...] = _dot(grads[...], contract_ref[...], ((1,), (1,)))


def pull(meta, mine, other, contract_weight, peers):
    rows, width = mine.shape
    part = contract_weight.shape[0] // (2 * peers)
    return pl.pallas_call(
        pull_kernel,
        out_shape=jax.ShapeDtypeStruct((2 * rows, peers * part), jnp.float32),
        grid_spec=pltpu.PrefetchScalarGridSpec(
            num_scalar_prefetch=1,
            grid=(peers,),
            in_specs=[_whole(rows, width)] * 2 + [pl.BlockSpec((part, width), lambda step, meta_ref: (2 * step + meta_ref[3], 0))],
            out_specs=_across(2 * rows, part),
            scratch_shapes=[pltpu.VMEM((2 * rows, width), jnp.bfloat16)],
        ),
        compiler_params=_params(16),
        cost_estimate=pl.CostEstimate(flops=3 * 10**9, bytes_accessed=9 * 2**20, transcendentals=0),
        name="pull",
    )(meta, mine, other, contract_weight)


def feed_kernel(
    rows, part, meta_ref, act_mine, act_other, grad_mine, grad_other, pulled_ref, expand_ref,
    in_keep, in_send, low_ref, back_ref, one_keep, one_send, two_keep, two_send, acts, grads, total,
):
    step = pl.program_id(0)
    x, y = meta_ref[1], meta_ref[2]
    cut, half = one_keep.shape[2], part // 2

    @pl.when(step == 0)
    def _():
        _both(acts, act_mine, act_other)
        _both(grads, grad_mine, grad_other)
        total[...] = jnp.zeros_like(total)

    before = _dot(acts[...], expand_ref[...], ((1,), (0,)))
    rate = 0.5 * (1.0 + lax.erf(before * math.sqrt(0.5)))
    low = (before * rate).astype(jnp.bfloat16)
    low_ref[...] = low
    contract_grad = _dot(low, grads[...], ((0,), (0,))).astype(jnp.bfloat16)
    slope = rate + before * jnp.exp(-0.5 * before * before) * (1.0 / math.sqrt(2.0 * math.pi))
    back = (pulled_ref[...] * slope).astype(jnp.bfloat16)
    back_ref[...] = back
    total[...] += _dot(back, expand_ref[...], ((1,), (1,)))
    level = step // 2

    @pl.when(step % 2 == x)
    def _():
        one_keep[level] = contract_grad[:, :cut]

    @pl.when(step % 2 != x)
    def _():
        one_send[level] = contract_grad[:, :cut]

    @pl.when(y == 0)
    def _():
        two_keep[step] = contract_grad[:half, cut:]
        two_send[step] = contract_grad[half:, cut:]

    @pl.when(y != 0)
    def _():
        two_keep[step] = contract_grad[half:, cut:]
        two_send[step] = contract_grad[:half, cut:]

    @pl.when(step == pl.num_programs(0) - 1)
    def _():
        in_keep[...] = total[:rows]
        in_send[...] = total[rows:]


def feed(meta, act_mine, act_other, grad_mine, grad_other, pulled, expand_weight, peers):
    rows, width = act_mine.shape
    part = expand_weight.shape[1] // (2 * peers)
    cut = width // 2
    shapes = [
        ((rows, width), jnp.float32),
        ((rows, width), jnp.float32),
        ((2 * rows, peers * part), jnp.bfloat16),
        ((2 * rows, peers * part), jnp.bfloat16),
        ((peers // 2, part, cut), jnp.bfloat16),
        ((peers // 2, part, cut), jnp.bfloat16),
        ((peers, part // 2, cut), jnp.bfloat16),
        ((peers, part // 2, cut), jnp.bfloat16),
    ]
    return pl.pallas_call(
        partial(feed_kernel, rows, part),
        out_shape=[jax.ShapeDtypeStruct(*shape) for shape in shapes],
        grid_spec=pltpu.PrefetchScalarGridSpec(
            num_scalar_prefetch=1,
            grid=(peers,),
            in_specs=[_whole(rows, width)] * 4
            + [_across(2 * rows, part), pl.BlockSpec((width, part), lambda step, meta_ref: (0, 2 * step + meta_ref[3]))],
            out_specs=[_whole(rows, width)] * 2 + [_across(2 * rows, part)] * 2 + [_whole(*shape) for shape, _ in shapes[4:]],
            scratch_shapes=[
                pltpu.VMEM((2 * rows, width), jnp.bfloat16),
                pltpu.VMEM((2 * rows, width), jnp.bfloat16),
                pltpu.VMEM((2 * rows, width), jnp.float32),
            ],
        ),
        compiler_params=_params(40),
        cost_estimate=pl.CostEstimate(flops=10 * 10**9, bytes_accessed=20 * 2**20, transcendentals=2 * 10**6),
        name="feed",
    )(meta, act_mine, act_other, grad_mine, grad_other, pulled, expand_weight)


def weigh_kernel(
    peers, rows, part, meta_ref, act_mine, act_other, mix_mine, mix_other, right_mine, right_other, low_ref, back_ref, contract_ref,
    out_keep, out_send, one_keep, one_send, two_keep, two_send, turned, total, block_grad,
):
    step = pl.program_id(0)
    x, y = meta_ref[1], meta_ref[2]
    group = block_grad.shape[1]
    half, near = group // 2, peers // 2

    def over_x(columns):
        for place in range(near):
            one_keep[place, :, columns] = block_grad[2 * place + x]
            one_send[place, :, columns] = block_grad[2 * place + 1 - x]

    def over_y(columns):
        for place in range(peers):
            two_keep[place, :, columns] = block_grad[place, pl.ds(pl.multiple_of(y * half, half), half), :]
            two_send[place, :, columns] = block_grad[place, pl.ds(pl.multiple_of((1 - y) * half, half), half), :]

    @pl.when(step == 0)
    def _():
        turned[:, :rows] = _turned(mix_mine[...]).astype(jnp.bfloat16)
        turned[:, rows:] = _turned(mix_other[...]).astype(jnp.bfloat16)
        right = jnp.concatenate([right_mine[...], right_other[...]])
        grad = _dot(turned[...], right, ((1,), (0,))).astype(jnp.bfloat16)
        tail = pl.ds(near * part, part)
        block_grad[...] = grad[:, :part].reshape(peers, group, part)
        over_x(tail)
        block_grad[...] = grad[:, part:].reshape(peers, group, part)
        over_y(tail)
        turned[:, :rows] = _turned(act_mine[...]).astype(jnp.bfloat16)
        turned[:, rows:] = _turned(act_other[...]).astype(jnp.bfloat16)
        total[...] = jnp.zeros_like(total)

    total[...] += _dot(low_ref[...], contract_ref[...], ((1,), (0,)))
    block_grad[...] = _dot(turned[...], back_ref[...], ((1,), (0,))).astype(jnp.bfloat16).reshape(peers, group, part)

    @pl.when(step < near)
    def _():
        over_x(pl.ds(pl.multiple_of(step * part, part), part))

    @pl.when(step >= near)
    def _():
        over_y(pl.ds(pl.multiple_of((step - near) * part, part), part))

    @pl.when(step == peers - 1)
    def _():
        out_keep[...] = total[:rows]
        out_send[...] = total[rows:].astype(jnp.bfloat16)


def weigh(meta, act_mine, act_other, mix_mine, mix_other, right_mine, right_other, low, back, contract_weight, peers):
    rows, width = act_mine.shape
    part = contract_weight.shape[0] // (2 * peers)
    group, span = width // peers, part * (peers // 2 + 1)
    shapes = [
        ((rows, width), jnp.float32),
        ((rows, width), jnp.bfloat16),
        ((peers // 2, group, span), jnp.bfloat16),
        ((peers // 2, group, span), jnp.bfloat16),
        ((peers, group // 2, span), jnp.bfloat16),
        ((peers, group // 2, span), jnp.bfloat16),
    ]
    return pl.pallas_call(
        partial(weigh_kernel, peers, rows, part),
        out_shape=[jax.ShapeDtypeStruct(*shape) for shape in shapes],
        grid_spec=pltpu.PrefetchScalarGridSpec(
            num_scalar_prefetch=1,
            grid=(peers,),
            in_specs=[_whole(rows, width)] * 4
            + [_whole(rows, width // 2)] * 2
            + [_across(2 * rows, part)] * 2
            + [pl.BlockSpec((part, width), lambda step, meta_ref: (2 * step + meta_ref[3], 0))],
            out_specs=[_whole(*shape) for shape, _ in shapes],
            scratch_shapes=[
                pltpu.VMEM((width, 2 * rows), jnp.bfloat16),
                pltpu.VMEM((2 * rows, width), jnp.float32),
                pltpu.VMEM((peers, group, part), jnp.bfloat16),
            ],
        ),
        compiler_params=_params(36),
        cost_estimate=pl.CostEstimate(flops=8 * 10**9, bytes_accessed=20 * 2**20, transcendentals=0),
        name="weigh",
    )(meta, act_mine, act_other, mix_mine, mix_other, right_mine, right_other, low, back, contract_weight)


def turn_kernel(meta_ref, in_mine, in_other, middle_ref, grad_ref, gain_ref, weight_ref, heads_ref, total_ref, keep_ref, send_ref, sums_ref):
    core = meta_ref[3]
    half = keep_ref.shape[1]
    unit, scale = _unit(middle_ref[...])
    total = grad_ref[...].astype(jnp.float32) + _norm_back(in_mine[...] + in_other[...], unit, scale, gain_ref[...], sums_ref)
    total_ref[...] = total
    low = total.astype(jnp.bfloat16)

    @pl.when(core == 0)
    def _():
        keep_ref[...] = low[:, :half]
        send_ref[...] = low[:, half:]

    @pl.when(core != 0)
    def _():
        keep_ref[...] = low[:, half:]
        send_ref[...] = low[:, :half]

    heads = _dot(low, weight_ref[...], ((1,), (1,))).astype(jnp.bfloat16)
    for part in range(heads_ref.shape[0]):
        heads_ref[part] = heads[:, 128 * part : 128 * part + 128]


def turn(meta, in_mine, in_other, middle, grad, gain, weight, peers):
    rows, width = middle.shape
    shapes = [
        ((peers, rows, width // peers), jnp.bfloat16),
        ((rows, width), jnp.float32),
        ((rows, width // 2), jnp.bfloat16),
        ((rows, width // 2), jnp.bfloat16),
        ((2, width), jnp.float32),
    ]
    return pl.pallas_call(
        turn_kernel,
        out_shape=[jax.ShapeDtypeStruct(*shape) for shape in shapes],
        in_specs=_specs("svvvvvv"),
        out_specs=_specs("v" * len(shapes)),
        compiler_params=_params(20),
        cost_estimate=pl.CostEstimate(flops=10**9, bytes_accessed=8 * 2**20, transcendentals=0),
        name="turn",
    )(meta, in_mine, in_other, middle, grad, gain, weight)


def close_kernel(parts_ref, tokens_ref, grad_ref, gain_ref, weight_ref, out_ref, sums_ref, held):
    peers = parts_ref.shape[0]
    for peer in range(peers):
        for block in range(3):
            at = 128 * (block * peers + peer)
            held[:, at : at + 128] = parts_ref[peer, block]
    back = _dot(held[...], weight_ref[...], ((1,), (1,)))
    unit, scale = _unit(tokens_ref[...].astype(jnp.float32))
    out_ref[...] = grad_ref[...] + _norm_back(back, unit, scale, gain_ref[...], sums_ref)


def close(parts, tokens, grad, gain, weight):
    rows, width = tokens.shape
    return pl.pallas_call(
        close_kernel,
        out_shape=[jax.ShapeDtypeStruct((rows, width), jnp.float32), jax.ShapeDtypeStruct((2, width), jnp.float32)],
        in_specs=_specs("vvvvv"),
        out_specs=_specs("vv"),
        scratch_shapes=[pltpu.VMEM((rows, 3 * width), jnp.bfloat16)],
        compiler_params=_params(24),
        cost_estimate=pl.CostEstimate(flops=2 * 10**9, bytes_accessed=10 * 2**20, transcendentals=0),
        name="close",
    )(parts, tokens, grad, gain, weight)


def attend_weigh_kernel(meta_ref, act_ref, back_ref, keep_ref, send_ref, held):
    core = meta_ref[3]
    peers, _, half, _ = held.shape
    for block in range(3):
        back = jnp.concatenate([back_ref[peer, block] for peer in range(peers)])
        grad = jnp.transpose(_dot(back, act_ref[...], ((0,), (0,)))).astype(jnp.bfloat16)
        held[:, :, :, 128 * block : 128 * block + 128] = grad.reshape(peers, 2, half, 128)
    for peer in range(peers):
        keep_ref[peer] = held[peer, core]
        send_ref[peer] = held[peer, 1 - core]


def attend_weigh(meta, act, back):
    peers = back.shape[0]
    shape = (peers, act.shape[1] // (2 * peers), 3 * back.shape[3])
    return pl.pallas_call(
        attend_weigh_kernel,
        out_shape=[jax.ShapeDtypeStruct(shape, jnp.bfloat16)] * 2,
        in_specs=_specs("svv"),
        out_specs=_specs("vv"),
        scratch_shapes=[pltpu.VMEM((peers, 2) + shape[1:], jnp.bfloat16)],
        compiler_params=_params(20),
        cost_estimate=pl.CostEstimate(flops=3 * 10**9, bytes_accessed=7 * 2**20, transcendentals=0),
        name="attend_weigh",
    )(meta, act, back)


def flipped(array, axis, mask):
    peers = lax.axis_size(axis)
    return lax.ppermute(array, axis, [(i, i ^ mask) for i in range(peers)])


def pick(array, index, axis):
    return lax.dynamic_index_in_dim(array, index, axis, keepdims=False)


def added(a, b):
    return (a.astype(jnp.float32) + b.astype(jnp.float32)).astype(jnp.bfloat16)


def in_order(mine, other, bit, axis):
    lower = jnp.where(bit == 0, mine, other)
    upper = jnp.where(bit == 0, other, mine)
    return jnp.concatenate([lower, upper], axis=axis)


def after(value, *others):
    return lax.optimization_barrier((value, others))[0]


def over_first(one_keep, one_send, two_keep, two_send):
    return one_keep, flipped(one_send, "blk", 1), two_keep, flipped(two_send, "seq", 2)


def over_second(place, one_keep, one_got, two_keep, two_got):
    _, x, y = place
    levels, rows, cut = one_keep.shape
    shape = (levels, 2, rows // 2, cut)

    def sums(keep, got, index):
        return added(pick(keep.reshape(shape), index, 1), pick(got.reshape(shape), index, 1))

    one_next = flipped(sums(one_keep, one_got, 1 - y), "seq", 2)
    two_next = flipped(sums(two_keep, two_got, 1 - x), "blk", 1)
    return sums(one_keep, one_got, y), one_next, sums(two_keep, two_got, x), two_next


def over_near(place, one, one_next, two, two_next):
    side = place[0] % 2
    levels = one.shape[0]
    shape = (levels // 2, 2) + one.shape[1:]

    def of(index):
        parts = [(pick(a.reshape(shape), index, 1), pick(b.reshape(shape), index, 1)) for a, b in ((one, one_next), (two, two_next))]
        return jnp.concatenate([added(a, b) for a, b in parts], axis=-1)

    return of(side), flipped(of(1 - side), "blk", 2)


def over_far(place, keep, got):
    upper = place[0] // 2

    def of(index):
        return added(pick(keep, index, 0), pick(got, index, 0))

    return of(upper), flipped(of(1 - upper), "blk", 4)


def local_by_heads(
    tokens,
    lengths,
    attend_weight,
    merge_weight,
    expand_weight,
    contract_weight,
    gain_first,
    shift_first,
    gain_second,
    shift_second,
    bias_table,
    cotangent,
):
    rows, width = tokens.shape[1], tokens.shape[2]
    buckets, heads = bias_table.shape
    hidden = expand_weight.shape[1]
    items = lengths.shape[1]
    peers = lax.axis_size("blk")
    levels = peers // 2
    group = width // peers
    part = hidden // (2 * peers)
    me, line_of = lax.axis_index("blk"), lax.axis_index("seq")
    z, x, y, core = me // 2, me % 2, line_of // 2, line_of % 2
    place = (z, x, y)
    here = jnp.stack([me, x, y, core]).astype(jnp.int32)
    gain_first, shift_first, gain_second, shift_second = (
        v.reshape(1, width) for v in (gain_first, shift_first, gain_second, shift_second)
    )

    own, grad_out = tokens[0], cotangent[0]
    grad_other = flipped(grad_out, "seq", 1)
    meta = plan(lengths[0], me, peers, rows)
    hot = bucket_lines(rows, buckets)
    table_mine = lax.dynamic_slice_in_dim(bias_table, 2 * me, 2, 1)
    lines = jnp.dot(table_mine.T, hot, precision=highest)
    far = table_mine[buckets - 1]

    def to_all(array):
        return lax.all_to_all(array, "blk", split_axis=0, concat_axis=0, tiled=True)

    *parts, act_first = project(here, own, gain_first, shift_first, attend_weight, peers)
    parts = [parts[0]] + [flipped(parts[step], "blk", step) for step in range(1, peers)]
    pulled = pull(here, grad_out, grad_other, contract_weight, peers)
    mixed, wide, logs = attend(meta, after(far, pulled), lines, parts, items)
    act_all = lax.all_gather(after(act_first, mixed), "blk", axis=0, tiled=True)
    attn_low, middle, act_second = merge(to_all(mixed), own, gain_second, shift_second, merge_weight)
    act_other = flipped(act_second, "seq", 1)
    attn_other = flipped(attn_low, "seq", 1)
    in_keep, in_send, hidden_low, hidden_back, *contract_parts = feed(
        here, act_second, act_other, grad_out, grad_other, pulled, expand_weight, peers
    )
    grad_heads, grad_middle, keep_low, send_low, sums_second = turn(
        here, in_keep, flipped(in_send, "seq", 1), middle, grad_out, gain_second, merge_weight, peers
    )
    contract_parts = over_first(*contract_parts)
    out_keep, out_send, *expand_parts = weigh(
        here, act_second, act_other, attn_low, attn_other, keep_low, flipped(send_low, "seq", 1), hidden_low, hidden_back, contract_weight, peers
    )
    expand_parts = over_first(*expand_parts)

    grad_heads, out_send, *contract_parts = lax.optimization_barrier((to_all(grad_heads), out_send, *contract_parts))
    contract_parts = over_second(place, *contract_parts)
    back_all, line_grad = attend_back(meta, far, lines, wide, logs, parts, grad_heads, items)
    act_all, back_all, *sums = lax.optimization_barrier((act_all, back_all, *contract_parts, *expand_parts))
    contract_parts = over_near(place, *sums[:4])
    expand_parts = over_second(place, *sums[4:])
    attend_keep, attend_send = attend_weigh(here, act_all, back_all)
    owned, attend_keep, attend_send, *sums = lax.optimization_barrier((to_all(back_all), attend_keep, attend_send, *contract_parts, *expand_parts))
    contract_parts = over_far(place, *sums[:2])
    expand_parts = over_near(place, *sums[2:])
    output = (middle + out_keep + flipped(out_send, "seq", 1).astype(jnp.float32)).astype(jnp.bfloat16)
    tokens_grad, sums_first = close(owned, own, grad_middle, gain_first, attend_weight)
    contract_grad = added(*contract_parts)
    expand_grad = added(*over_far(place, *expand_parts))
    attend_keep = added(attend_keep, flipped(attend_send, "seq", 1)).reshape(peers, 2, group // 4, 3 * group)
    attend_keep, attend_send = pick(attend_keep, y, 1), pick(attend_keep, 1 - y, 1)

    attend_grad = to_all(added(attend_keep, flipped(attend_send, "seq", 2)))

    contract_grad = in_order(contract_grad, flipped(contract_grad, "seq", 2), y, 0)
    contract_grad = in_order(contract_grad, flipped(contract_grad, "seq", 1), core, 0).astype(jnp.float32)
    span = part * (peers // 2 + 1)
    expand_grad = in_order(expand_grad, flipped(expand_grad, "seq", 2), y, 0)
    expand_other = flipped(expand_grad, "seq", 1)
    halves = [jnp.where(core == side, expand_grad, expand_other).astype(jnp.float32) for side in range(2)]
    at = [part * peer if peer < peers // 2 else part * (peer + 1) for peer in range(peers)]
    expand_grad = jnp.concatenate([halves[side][:, start : start + part] for start in at for side in range(2)], axis=1)
    merge_grad = jnp.concatenate([halves[side][:, start - part : start] for side in range(2) for start in (span, 2 * span)], axis=1)
    attend_grad = in_order(attend_grad, flipped(attend_grad, "seq", 2), y, 1)
    attend_grad = in_order(attend_grad, flipped(attend_grad, "seq", 1), core, 1)
    attend_grad = attend_grad.reshape(peers, group, 3, group).transpose(1, 2, 0, 3).reshape(group, 3 * width).astype(jnp.float32)

    table_mine = jnp.dot(hot, line_grad.T, precision=highest)
    table_local = lax.dynamic_update_slice(jnp.zeros((buckets, heads), jnp.float32), table_mine, (0, 2 * me))
    table_row = jnp.pad(table_local.reshape(1, buckets * heads), ((0, 0), (0, width - buckets * heads)))
    small = jnp.concatenate([sums_first, sums_second, table_row])
    for axis, mask in (("seq", 1), ("seq", 2), ("blk", 1), ("blk", 2), ("blk", 4)):
        small = small + flipped(small, axis, mask)
    table_grad = small[4, : buckets * heads].reshape(buckets, heads)
    vectors = lax.dynamic_slice_in_dim(small, me * group, group, 1)
    return (
        output[None],
        tokens_grad[None],
        attend_grad,
        merge_grad,
        expand_grad,
        contract_grad,
        vectors[0],
        vectors[1],
        vectors[2],
        vectors[3],
        table_grad,
    )


def local(*arguments):
    heads = arguments[10].shape[1]
    rows = arguments[0].shape[1]
    peers = lax.axis_size("blk")
    if peers == 8 and lax.axis_size("seq") == 4 and heads == 2 * peers and rows == 256:
        return local_by_heads(*arguments)
    return local_by_runs(*arguments)


def solution(mesh):
    in_specs = (
        P("seq", "blk", None),
        P("seq", None),
        P(),
        P(),
        P(),
        P(),
        P(),
        P(),
        P(),
        P(),
        P(),
        P("seq", "blk", None),
    )
    out_specs = (
        P("seq", "blk", None),
        P("seq", "blk", None),
        P("blk", None),
        P("blk", None),
        P("blk", None),
        P("blk", None),
        P("blk"),
        P("blk"),
        P("blk"),
        P("blk"),
        P(),
    )
    return jax.shard_map(local, mesh=mesh, in_specs=in_specs, out_specs=out_specs, check_vma=False)
```

```python
from functools import partial
import math

import jax
import jax.numpy as jnp
from jax import lax
from jax.experimental import pallas as pl
from jax.experimental.pallas import tpu as pltpu
from jax.sharding import PartitionSpec as P

HOPS = 6


epsilon = 1e-05
masked_score = -1e30
highest = lax.Precision.HIGHEST
bucket_edges = [math.ceil(16 * 8 ** (t / 16)) for t in range(1, 16)]


def shifted(array, axis, by):
    peers = lax.axis_size(axis)
    pairs = [(i, i + by) for i in range(peers) if 0 <= i + by < peers]
    return lax.ppermute(array, axis, pairs)


def shortened(array):

    def short(part):
        return part.astype(jnp.bfloat16) if part.dtype == jnp.float32 else part

    return jax.tree.map(short, array)


def bucket_of(distance):
    total = jnp.minimum(jnp.maximum(distance, 0), 16)
    for edge in bucket_edges:
        total = total + (distance >= edge).astype(jnp.int32)
    return total


def segment_of(position, ends):
    return jnp.sum((position[:, None] >= ends[None, :]).astype(jnp.int32), axis=1)


def layer_norm(value, gain, shift):
    mean = jnp.mean(value, axis=-1, keepdims=True)
    centred = value - mean
    variance = jnp.mean(centred * centred, axis=-1, keepdims=True)
    return centred * lax.rsqrt(variance + epsilon) * gain + shift


def diagonal_sums(grid, count):
    heads = grid.shape[0]
    padded = jnp.pad(jnp.flip(grid, axis=-1), ((0, 0), (0, 0), (0, count)))
    flat = padded.reshape(heads, 2 * count * count)[:, : count * (2 * count - 1)]
    return jnp.sum(flat.reshape(heads, count, 2 * count - 1), axis=1)


def band_matrix(line, count):
    heads = line.shape[0]
    flipped = jnp.flip(line, axis=-1)
    tiled = jnp.tile(flipped, (1, count))
    window = tiled[:, count - 1 : count - 1 + count * (2 * count - 2)]
    return window.reshape(heads, count, 2 * count - 2)[:, :, :count]


def fetch_earlier(block):
    earlier = []
    moving = block
    for hop in range(HOPS):
        moving = shifted(moving, "blk", 1)
        earlier.append(moving)
    return earlier


def return_parts(parts):
    carried = jnp.zeros_like(parts[0])
    for hop in range(HOPS, 0, -1):
        carried = shifted(shortened(carried + parts[hop - 1]), "blk", -1)
    return carried


def local_by_runs(
    tokens,
    lengths,
    attend_weight,
    merge_weight,
    expand_weight,
    contract_weight,
    gain_first,
    shift_first,
    gain_second,
    shift_second,
    bias_table,
    cotangent,
):
    rows = tokens.shape[1]
    width = tokens.shape[2]
    heads = bias_table.shape[1]
    buckets = bias_table.shape[0]
    head_size = width // heads
    items = lengths.shape[1]
    start = lax.axis_index("blk") * rows
    query_pos = start + jnp.arange(rows, dtype=jnp.int32)
    ends = jnp.cumsum(lengths[0])
    query_seg = segment_of(query_pos, ends)
    band = jnp.arange(2 * rows - 1, dtype=jnp.int32) - (rows - 1)
    bucket_ids = jnp.arange(buckets, dtype=jnp.int32)

    def pair_setup(hop):
        key_pos = query_pos - hop * rows
        key_seg = segment_of(key_pos, ends)
        key_valid = (key_pos >= 0) & (key_seg < items)
        same = key_pos[None, :] == query_pos[:, None]
        allowed = (
            (query_seg[:, None] == key_seg[None, :])
            & (key_pos[None, :] <= query_pos[:, None])
            & (key_valid[None, :] | same)
        )
        onehot = (bucket_of(hop * rows + band)[:, None] == bucket_ids[None, :]).astype(jnp.float32)
        band_bias = jnp.dot(onehot, bias_table, precision=highest).T
        bias = band_matrix(band_bias, rows)
        additive = jnp.where(allowed[None], bias, masked_score)
        return (jnp.any(allowed), onehot, additive)

    pairs = [pair_setup(hop) for hop in range(HOPS + 1)]
    residual = tokens[0].astype(jnp.float32)
    normed_first, norm_first_pull = jax.vjp(layer_norm, residual, gain_first, shift_first)
    act_first = normed_first.astype(jnp.bfloat16)
    projected = jnp.dot(act_first, attend_weight, preferred_element_type=jnp.float32).astype(
        jnp.bfloat16
    )
    query = projected[:, :width].reshape(rows, heads, head_size)
    keys_values = jnp.stack([projected[:, width : 2 * width], projected[:, 2 * width :]])
    blocks = [keys_values] + fetch_earlier(keys_values)

    def scores_of(block, pair):
        key = block[0].reshape(rows, heads, head_size)
        raw = jnp.einsum("qhe,khe->hqk", query, key, preferred_element_type=jnp.float32) * 0.125
        return raw + pair[2]

    def empty_total():
        return jnp.full((heads, rows), masked_score, jnp.float32)

    def empty_scores():
        return jnp.full((heads, rows, rows), masked_score, jnp.float32)

    log_total = empty_total()
    kept_scores = []
    for block, pair in zip(blocks, pairs):

        def part_total(block=block, pair=pair):
            scores = scores_of(block, pair)
            peak = jnp.max(scores, axis=-1)
            return (peak + jnp.log(jnp.sum(jnp.exp(scores - peak[..., None]), axis=-1)), scores)

        def skip_total():
            return (empty_total(), empty_scores())

        part_log, scores = lax.cond(pair[0], part_total, skip_total)
        log_total = jnp.logaddexp(log_total, part_log)
        kept_scores.append(scores)

    def empty_heads():
        return jnp.zeros((rows, heads, head_size), jnp.float32)

    attended = empty_heads()
    for block, pair, scores in zip(blocks, pairs, kept_scores):

        def part_mix(block=block, scores=scores):
            weights = jnp.exp(scores - log_total[..., None]).astype(jnp.bfloat16)
            value = block[1].reshape(rows, heads, head_size)
            return jnp.einsum("hqk,khe->qhe", weights, value, preferred_element_type=jnp.float32)

        attended = attended + lax.cond(pair[0], part_mix, empty_heads)
    attn_low = attended.reshape(rows, width).astype(jnp.bfloat16)
    middle = residual + jnp.dot(attn_low, merge_weight, preferred_element_type=jnp.float32)
    normed_second, norm_second_pull = jax.vjp(layer_norm, middle, gain_second, shift_second)
    act_second = normed_second.astype(jnp.bfloat16)
    hidden_pre = jnp.dot(act_second, expand_weight, preferred_element_type=jnp.float32)
    hidden, gelu_pull = jax.vjp(partial(jax.nn.gelu, approximate=False), hidden_pre)
    hidden_low = hidden.astype(jnp.bfloat16)
    output = (
        middle + jnp.dot(hidden_low, contract_weight, preferred_element_type=jnp.float32)
    ).astype(jnp.bfloat16)
    grad_out = cotangent[0]
    contract_grad = jnp.einsum(
        "tf,td->fd", hidden_low, grad_out, preferred_element_type=jnp.float32
    )
    grad_hidden = jnp.einsum(
        "td,fd->tf", grad_out, contract_weight, preferred_element_type=jnp.float32
    )
    grad_pre = gelu_pull(grad_hidden)[0].astype(jnp.bfloat16)
    expand_grad = jnp.einsum("td,tf->df", act_second, grad_pre, preferred_element_type=jnp.float32)
    grad_second = jnp.einsum(
        "tf,df->td", grad_pre, expand_weight, preferred_element_type=jnp.float32
    )
    grad_middle_norm, gain_second_grad, shift_second_grad = norm_second_pull(grad_second)
    grad_middle = grad_out.astype(jnp.float32) + grad_middle_norm
    grad_middle_low = grad_middle.astype(jnp.bfloat16)
    merge_grad = jnp.einsum(
        "td,te->de", attn_low, grad_middle_low, preferred_element_type=jnp.float32
    )
    grad_heads = (
        jnp.einsum("te,de->td", grad_middle_low, merge_weight, preferred_element_type=jnp.float32)
        .astype(jnp.bfloat16)
        .reshape(rows, heads, head_size)
    )
    row_dot = jnp.sum(grad_heads.astype(jnp.float32) * attended, axis=-1).T
    back_blocks = [keys_values] + fetch_earlier(keys_values)

    def empty_grads():
        return (
            empty_heads(),
            jnp.zeros((2, rows, width), jnp.float32),
            jnp.zeros((buckets, heads), jnp.float32),
        )

    grad_query = empty_heads()
    table_local = jnp.zeros((buckets, heads), jnp.float32)
    parts = []
    for block, pair in zip(back_blocks, pairs):

        def part_grads(block=block, pair=pair):
            key = block[0].reshape(rows, heads, head_size)
            value = block[1].reshape(rows, heads, head_size)
            weights = jnp.exp(scores_of(block, pair) - log_total[..., None])
            weights_low = weights.astype(jnp.bfloat16)
            grad_weights = jnp.einsum(
                "qhe,khe->hqk", grad_heads, value, preferred_element_type=jnp.float32
            )
            grad_scores = (weights * (grad_weights - row_dot[..., None])).astype(jnp.bfloat16)
            query_part = (
                jnp.einsum("hqk,khe->qhe", grad_scores, key, preferred_element_type=jnp.float32)
                * 0.125
            )
            key_part = (
                jnp.einsum("hqk,qhe->khe", grad_scores, query, preferred_element_type=jnp.float32)
                * 0.125
            )
            value_part = jnp.einsum(
                "hqk,qhe->khe", weights_low, grad_heads, preferred_element_type=jnp.float32
            )
            line_grad = diagonal_sums(grad_scores.astype(jnp.float32), rows)
            table_part = jnp.dot(pair[1].T, line_grad.T, precision=highest)
            return (
                query_part,
                jnp.stack([key_part.reshape(rows, width), value_part.reshape(rows, width)]),
                table_part,
            )

        query_part, pair_part, table_part = lax.cond(pair[0], part_grads, empty_grads)
        grad_query = grad_query + query_part
        table_local = table_local + table_part
        parts.append(pair_part)
    owned = (parts[0] + return_parts(parts[1:])).astype(jnp.bfloat16)
    grad_project = jnp.concatenate(
        [grad_query.reshape(rows, width).astype(jnp.bfloat16), owned[0], owned[1]], axis=1
    )
    attend_grad = jnp.einsum(
        "td,te->de", act_first, grad_project, preferred_element_type=jnp.float32
    )
    grad_first = jnp.einsum(
        "te,de->td", grad_project, attend_weight, preferred_element_type=jnp.float32
    )
    grad_input_norm, gain_first_grad, shift_first_grad = norm_first_pull(grad_first)
    tokens_grad = grad_middle + grad_input_norm
    results = (
        lax.psum_scatter(attend_grad, "blk", scatter_dimension=0, tiled=True),
        lax.psum_scatter(merge_grad, "blk", scatter_dimension=0, tiled=True),
        lax.psum_scatter(expand_grad, "blk", scatter_dimension=0, tiled=True),
        lax.psum_scatter(contract_grad, "blk", scatter_dimension=0, tiled=True),
        lax.psum_scatter(gain_first_grad, "blk", scatter_dimension=0, tiled=True),
        lax.psum_scatter(shift_first_grad, "blk", scatter_dimension=0, tiled=True),
        lax.psum_scatter(gain_second_grad, "blk", scatter_dimension=0, tiled=True),
        lax.psum_scatter(shift_second_grad, "blk", scatter_dimension=0, tiled=True),
    )
    results = (
        lax.psum(results[0].astype(jnp.bfloat16), "seq").astype(jnp.float32),
        lax.psum(results[1].astype(jnp.bfloat16), "seq").astype(jnp.float32),
        lax.psum(results[2].astype(jnp.bfloat16), "seq").astype(jnp.float32),
        lax.psum(results[3].astype(jnp.bfloat16), "seq").astype(jnp.float32),
        lax.psum(results[4].astype(jnp.bfloat16), "seq").astype(jnp.float32),
        lax.psum(results[5].astype(jnp.bfloat16), "seq").astype(jnp.float32),
        lax.psum(results[6].astype(jnp.bfloat16), "seq").astype(jnp.float32),
        lax.psum(results[7].astype(jnp.bfloat16), "seq").astype(jnp.float32),
    )
    table_grad = lax.psum(table_local, ("seq", "blk"))
    return (
        output[None],
        tokens_grad[None],
        results[0],
        results[1],
        results[2],
        results[3],
        results[4],
        results[5],
        results[6],
        results[7],
        table_grad,
    )


def _segments(position, meta_ref, first, items):
    total = jnp.zeros(position.shape, jnp.int32)
    for item in range(items):
        total = total + (position >= meta_ref[first + item]).astype(jnp.int32)
    return total

def _allowed(meta_ref, peers, items, rows, i, j, diagonal):
    first = 1 + 2 * peers
    q_seg = _segments(i * rows + lax.broadcasted_iota(jnp.int32, (1, rows), 1), meta_ref, first, items)
    k_seg = _segments(j * rows + lax.broadcasted_iota(jnp.int32, (rows, 1), 0), meta_ref, first, items)
    k_seg = jnp.where(k_seg < items, k_seg, -1)
    same = q_seg == k_seg
    if diagonal:
        key = lax.broadcasted_iota(jnp.int32, (rows, rows), 0)
        query = lax.broadcasted_iota(jnp.int32, (rows, rows), 1)
        return (same & (key < query)) | (key == query)
    return same

def _dot(a, b, dims):
    return lax.dot_general(a, b, (dims, ((), ())), preferred_element_type=jnp.float32)

def _turned(array):
    return jnp.transpose(array.astype(jnp.float32))

def _split(array, axis=1):
    wide = array.astype(jnp.float32)
    left = lax.broadcasted_iota(jnp.int32, array.shape, axis) < 64
    return jnp.where(left, wide, 0.0).astype(jnp.bfloat16), jnp.where(left, 0.0, wide).astype(jnp.bfloat16)

def _fold(value, op):
    while value.shape[0] > 8:
        half = value.shape[0] // 2
        value = op(value[:half], value[half:])
    return value

def _put_bias(bias, line_ref, rows):
    for head in range(2):
        line = jnp.broadcast_to(line_ref[head:head + 1, :], (rows, 2 * rows))
        bias[head] = pltpu.roll(line, 0, 1, stride=1, stride_axis=0)

def _biased(raw, bias, far_ref, head, which, rows):
    if which == 0:
        return raw + bias[head, :, :rows]
    if which == 1:
        return raw + bias[head, :, rows:]
    return raw + far_ref[head]

def attend_kernel(peers, items, rows, meta_ref, far_ref, line_ref, *refs):
    parts = refs[:peers]
    mixed, wide_ref, log_ref, qkv, turned, bias, scores = refs[peers:]
    me = meta_ref[0]
    for slot in range(peers):
        qkv[me ^ slot] = parts[slot][...]
        turned[me ^ slot] = _turned(parts[slot][2]).astype(jnp.bfloat16)
    _put_bias(bias, line_ref, rows)
    upper = lax.broadcasted_iota(jnp.int32, (128, rows), 0) < 64

    def one_row(i, _):
        low = meta_ref[1 + i]
        whole = jnp.minimum(meta_ref[1 + peers + i], i - 1)
        queries = _split(qkv[i, 0].astype(jnp.float32) * 0.125)

        def put(j, which, masked, peaks):
            key = qkv[j, 1]
            if masked:
                allowed = _allowed(meta_ref, peers, items, rows, i, j, which == 0)
            new = []
            for head in range(2):
                raw = _biased(_dot(key, queries[head], ((1,), (1,))), bias, far_ref, head, which, rows)
                if masked:
                    raw = jnp.where(allowed, raw, masked_score)
                scores[head, j] = raw
                new.append(jnp.maximum(peaks[head], _fold(raw, jnp.maximum)))
            return tuple(new)

        start = jnp.full((8, rows), masked_score, jnp.float32)
        peaks = put(i, 0, True, (start, start))
        peaks = lax.cond(low < i, lambda p: put(i - 1, 1, True, p), lambda p: p, peaks)
        peaks = lax.fori_loop(low, whole, lambda j, p: put(j, 2, True, p), peaks)
        peaks = lax.fori_loop(jnp.maximum(low, whole), i - 1, lambda j, p: put(j, 2, False, p), peaks)
        tops = [jnp.max(peak, axis=0, keepdims=True) for peak in peaks]

        def mix(j, carry):
            sums, total = carry
            value = turned[j]
            new = []
            both = []
            for head in range(2):
                weight = jnp.exp(scores[head, j] - tops[head])
                new.append(sums[head] + _fold(weight, jnp.add))
                both.append(_dot(value[64 * head:64 * head + 64], weight.astype(jnp.bfloat16), ((1,), (0,))))
            return tuple(new), total + jnp.concatenate(both)

        nothing = jnp.zeros((8, rows), jnp.float32)
        sums, total = lax.fori_loop(low, i + 1, mix, ((nothing, nothing), jnp.zeros((128, rows), jnp.float32)))
        sums = [jnp.sum(s, axis=0, keepdims=True) for s in sums]
        total = total / jnp.where(upper, sums[0], sums[1])
        wide_ref[i] = total
        for head in range(2):
            log_ref[i, head:head + 1, :] = tops[head] + jnp.log(sums[head])
        mixed[i] = jnp.transpose(total).astype(jnp.bfloat16)
        return 0

    lax.fori_loop(0, peers, one_row, 0)

def attend(meta, far, line, parts, items):
    peers = len(parts)
    rows = parts[0].shape[1]
    smem = pl.BlockSpec(memory_space=pltpu.SMEM)
    vmem = pl.BlockSpec(memory_space=pltpu.VMEM)
    shapes = [
        jax.ShapeDtypeStruct((peers, rows, 128), jnp.bfloat16),
        jax.ShapeDtypeStruct((peers, 128, rows), jnp.float32),
        jax.ShapeDtypeStruct((peers, 8, rows), jnp.float32),
        jax.ShapeDtypeStruct((peers, 3, rows, 128), jnp.bfloat16),
    ]
    res = pl.pallas_call(
        partial(attend_kernel, peers, items, rows),
        out_shape=shapes,
        in_specs=[smem, smem] + [vmem] * (peers + 1),
        out_specs=[vmem] * 4,
        scratch_shapes=[
            pltpu.VMEM((peers, 128, rows), jnp.bfloat16),
            pltpu.VMEM((2, rows, 2 * rows), jnp.float32),
            pltpu.VMEM((2, peers, rows, rows), jnp.float32),
        ],
        compiler_params=pltpu.CompilerParams(vmem_limit_bytes=18 * 2**20),
        cost_estimate=pl.CostEstimate(flops=8 * 10**9, bytes_accessed=4 * 2**20, transcendentals=3 * 10**6),
        name="attend",
    )(meta, far, line, *parts)
    return res

def attend_back_kernel(peers, items, rows, meta_ref, far_ref, line_ref, wide_ref, log_ref, cot, qkv, *refs):
    all_ref, table_ref, turned, bias, near, far_sum, dkey, dvalue = refs
    for peer in range(peers):
        turned[peer] = _turned(qkv[peer, 1]).astype(jnp.bfloat16)
    _put_bias(bias, line_ref, rows)
    near[...] = jnp.zeros_like(near)
    far_sum[...] = jnp.zeros_like(far_sum)
    dkey[...] = jnp.zeros_like(dkey)
    dvalue[...] = jnp.zeros_like(dvalue)

    def one_row(i, _):
        low = meta_ref[1 + i]
        whole = jnp.minimum(meta_ref[1 + peers + i], i - 1)
        queries = _split(qkv[i, 0].astype(jnp.float32) * 0.125)
        grad = cot[i]
        grads_ = _split(grad)
        product = _turned(grad) * wide_ref[i]
        dots = [jnp.sum(product[64 * head:64 * head + 64], axis=0, keepdims=True) for head in range(2)]
        logs = [log_ref[i, head:head + 1, :] for head in range(2)]

        def step(j, which, masked, dquery):
            key = qkv[j, 1]
            value = qkv[j, 2]
            across = turned[j]
            if masked:
                allowed = _allowed(meta_ref, peers, items, rows, i, j, which == 0)
            dk = jnp.zeros((rows, 128), jnp.float32)
            dv = jnp.zeros((rows, 128), jnp.float32)
            both = []
            for head in range(2):
                raw = _biased(_dot(key, queries[head], ((1,), (1,))), bias, far_ref, head, which, rows)
                if masked:
                    raw = jnp.where(allowed, raw, masked_score)
                weight = jnp.exp(raw - logs[head])
                dweight = _dot(value, grads_[head], ((1,), (1,)))
                dscore = weight * (dweight - dots[head])
                low_score = dscore.astype(jnp.bfloat16)
                if which == 0:
                    near[head, :, :rows] += dscore
                elif which == 1:
                    near[head, :, rows:] += dscore
                else:
                    far_sum[head] += _fold(dscore, jnp.add)
                both.append(_dot(across[64 * head:64 * head + 64], low_score, ((1,), (0,))))
                dk = dk + _dot(low_score, queries[head], ((1,), (0,)))
                dv = dv + _dot(weight.astype(jnp.bfloat16), grads_[head], ((1,), (0,)))
            dkey[j] += dk
            dvalue[j] += dv
            return dquery + jnp.concatenate(both)

        dquery = step(i, 0, True, jnp.zeros((128, rows), jnp.float32))
        dquery = lax.cond(low < i, lambda d: step(i - 1, 1, True, d), lambda d: d, dquery)
        dquery = lax.fori_loop(low, whole, lambda j, d: step(j, 2, True, d), dquery)
        dquery = lax.fori_loop(jnp.maximum(low, whole), i - 1, lambda j, d: step(j, 2, False, d), dquery)
        all_ref[i, 0] = (jnp.transpose(dquery) * 0.125).astype(jnp.bfloat16)
        return 0

    lax.fori_loop(0, peers, one_row, 0)
    for i in range(peers):
        all_ref[i, 1] = dkey[i].astype(jnp.bfloat16)
        all_ref[i, 2] = dvalue[i].astype(jnp.bfloat16)
    wide = 2 * rows
    sub = lax.broadcasted_iota(jnp.int32, (8, wide), 0)
    for head in range(2):
        part = near[head]
        count = rows
        while count > 8:
            count //= 2
            part = part[:count] + pltpu.roll(part[count:], wide - count, 1)
        for bit in (4, 2, 1):
            part = jnp.where((sub & bit) != 0, pltpu.roll(part, wide - bit, 1), part)
        total = far_sum[head]
        table_ref[head, :, :rows] = part[:, :rows]
        table_ref[head, :, rows:] = part[:, rows:] + jnp.concatenate([jnp.zeros((8, rows - 128), jnp.float32), total[:, :128] + total[:, 128:]], axis=1)

def attend_back(meta, far, line, wide, logs, qkv, grads, items):
    peers, _, rows, _ = qkv.shape
    smem = pl.BlockSpec(memory_space=pltpu.SMEM)
    vmem = pl.BlockSpec(memory_space=pltpu.VMEM)
    shapes = [
        jax.ShapeDtypeStruct((peers, 3, rows, 128), jnp.bfloat16),
        jax.ShapeDtypeStruct((2, 8, 2 * rows), jnp.float32),
    ]
    res = pl.pallas_call(
        partial(attend_back_kernel, peers, items, rows),
        out_shape=shapes,
        in_specs=[smem, smem] + [vmem] * 5,
        out_specs=[vmem] * 2,
        scratch_shapes=[
            pltpu.VMEM((peers, 128, rows), jnp.bfloat16),
            pltpu.VMEM((2, rows, 2 * rows), jnp.float32),
            pltpu.VMEM((2, rows, 2 * rows), jnp.float32),
            pltpu.VMEM((2, 8, rows), jnp.float32),
            pltpu.VMEM((peers, rows, 128), jnp.float32),
            pltpu.VMEM((peers, rows, 128), jnp.float32),
        ],
        compiler_params=pltpu.CompilerParams(vmem_limit_bytes=18 * 2**20),
        cost_estimate=pl.CostEstimate(flops=20 * 10**9, bytes_accessed=8 * 2**20, transcendentals=3 * 10**6),
        name="attend_back",
    )(meta, far, line, wide, logs, grads, qkv)
    return res[0], jnp.sum(res[1], axis=1)

def plan(lengths, me, peers, rows):
    ends = jnp.cumsum(lengths)
    items = lengths.shape[0]
    place = jnp.arange(peers, dtype=jnp.int32)
    first = jnp.sum((place[:, None] * rows >= ends[None]).astype(jnp.int32), axis=1)
    last = jnp.sum((place[:, None] * rows + rows - 1 >= ends[None]).astype(jnp.int32), axis=1)
    low = jnp.sum((last[None, :] < first[:, None]).astype(jnp.int32), axis=1)
    low = jnp.where(first < items, jnp.minimum(low, place), place)
    whole = jnp.sum((first[None, :] < last[:, None]).astype(jnp.int32), axis=1)
    return jnp.concatenate([me[None].astype(jnp.int32), low, whole, ends.astype(jnp.int32)])
def bucket_lines(rows, buckets):
    k = jnp.arange(2 * rows, dtype=jnp.int32)
    return (bucket_of(k)[None, :] == jnp.arange(buckets, dtype=jnp.int32)[:, None]).astype(jnp.float32)


def _unit(value):
    mean = jnp.mean(value, axis=-1, keepdims=True)
    centred = value - mean
    variance = jnp.mean(centred * centred, axis=-1, keepdims=True)
    scale = lax.rsqrt(variance + epsilon)
    return centred * scale, scale


def _norm_back(grad, unit, scale, gain, sums_ref):
    inner = grad * gain
    first = jnp.mean(inner, axis=-1, keepdims=True)
    second = jnp.mean(inner * unit, axis=-1, keepdims=True)
    sums_ref[0:1, :] = jnp.sum(grad * unit, axis=0, keepdims=True)
    sums_ref[1:2, :] = jnp.sum(grad, axis=0, keepdims=True)
    return scale * (inner - first - unit * second)


def _lanes(index):
    return pl.ds(pl.multiple_of(index * 128, 128), 128)


def _specs(*kinds):
    places = {"s": pltpu.SMEM, "v": pltpu.VMEM, "h": pltpu.HBM}
    return [pl.BlockSpec(memory_space=places[kind]) for word in kinds for kind in word]


def _params(mebibytes):
    return pltpu.CompilerParams(vmem_limit_bytes=mebibytes * 2**20)


def project_kernel(peers, meta_ref, tokens_ref, gain_ref, shift_ref, weight_ref, *refs):
    outs, act_ref, held, done, arrived = refs[:peers], refs[peers], refs[peers + 1], refs[peers + 2], refs[peers + 3]
    me = meta_ref[0]
    pieces, _, span = held.shape
    copies = []
    for piece in range(pieces):
        copies.append(pltpu.make_async_copy(weight_ref.at[:, pl.ds(piece * span, span)], held.at[piece], arrived.at[piece]))
        copies[-1].start()
    unit, _ = _unit(tokens_ref[...].astype(jnp.float32))
    act = (unit * gain_ref[...] + shift_ref[...]).astype(jnp.bfloat16)
    act_ref[...] = act
    for piece in range(pieces):
        copies[piece].wait()
        got = _dot(act, held[piece], ((1,), (0,))).astype(jnp.bfloat16)
        for block in range(span // 128):
            done[piece * (span // 128) + block] = got[:, 128 * block : 128 * block + 128]
    for slot in range(peers):
        for block in range(3):
            outs[slot][block] = done[block * peers + (me ^ slot)]


def project(meta, tokens, gain, shift, weight, peers):
    rows, width = tokens.shape
    span = 512
    pieces = weight.shape[1] // span
    return pl.pallas_call(
        partial(project_kernel, peers),
        out_shape=[jax.ShapeDtypeStruct((3, rows, 128), jnp.bfloat16)] * peers + [jax.ShapeDtypeStruct((rows, width), jnp.bfloat16)],
        in_specs=_specs("svvvh"),
        out_specs=_specs("v" * (peers + 1)),
        scratch_shapes=[
            pltpu.VMEM((pieces, width, span), jnp.bfloat16),
            pltpu.VMEM((3 * peers, rows, 128), jnp.bfloat16),
            pltpu.SemaphoreType.DMA((pieces,)),
        ],
        compiler_params=_params(60),
        cost_estimate=pl.CostEstimate(flops=4 * 10**9, bytes_accessed=8 * 2**20, transcendentals=0),
        name="project",
    )(meta, tokens, gain, shift, weight)


def merge_kernel(parts_ref, tokens_ref, gain_ref, shift_ref, weight_ref, low_ref, middle_ref, act_ref):
    for part in range(parts_ref.shape[0]):
        low_ref[:, 128 * part : 128 * part + 128] = parts_ref[part]
    middle = tokens_ref[...].astype(jnp.float32) + _dot(low_ref[...], weight_ref[...], ((1,), (0,)))
    middle_ref[...] = middle
    unit, _ = _unit(middle)
    act_ref[...] = (unit * gain_ref[...] + shift_ref[...]).astype(jnp.bfloat16)


def merge(parts, tokens, gain, shift, weight):
    return pl.pallas_call(
        merge_kernel,
        out_shape=[jax.ShapeDtypeStruct(tokens.shape, t) for t in (jnp.bfloat16, jnp.float32, jnp.bfloat16)],
        in_specs=_specs("vvvvv"),
        out_specs=_specs("vvv"),
        compiler_params=_params(16),
        cost_estimate=pl.CostEstimate(flops=10**9, bytes_accessed=5 * 2**20, transcendentals=0),
        name="merge",
    )(parts, tokens, gain, shift, weight)


def _both(ref, mine, other):
    rows = mine.shape[0]
    ref[:rows] = mine[...]
    ref[rows:] = other[...]


def _whole(*shape):
    return pl.BlockSpec(shape, lambda step, meta_ref: (0,) * len(shape))


def _across(rows, columns):
    return pl.BlockSpec((rows, columns), lambda step, meta_ref: (0, step))


def pull_kernel(meta_ref, mine, other, contract_ref, out_ref, grads):
    @pl.when(pl.program_id(0) == 0)
    def _():
        _both(grads, mine, other)

    out_ref[...] = _dot(grads[...], contract_ref[...], ((1,), (1,)))


def pull(meta, mine, other, contract_weight, peers):
    rows, width = mine.shape
    part = contract_weight.shape[0] // (2 * peers)
    return pl.pallas_call(
        pull_kernel,
        out_shape=jax.ShapeDtypeStruct((2 * rows, peers * part), jnp.float32),
        grid_spec=pltpu.PrefetchScalarGridSpec(
            num_scalar_prefetch=1,
            grid=(peers,),
            in_specs=[_whole(rows, width)] * 2 + [pl.BlockSpec((part, width), lambda step, meta_ref: (2 * step + meta_ref[3], 0))],
            out_specs=_across(2 * rows, part),
            scratch_shapes=[pltpu.VMEM((2 * rows, width), jnp.bfloat16)],
        ),
        compiler_params=_params(16),
        cost_estimate=pl.CostEstimate(flops=3 * 10**9, bytes_accessed=9 * 2**20, transcendentals=0),
        name="pull",
    )(meta, mine, other, contract_weight)


def feed_kernel(
    rows, part, meta_ref, act_mine, act_other, pulled_ref, expand_ref, in_keep, in_send, low_ref, back_ref, acts, weights, total, arrived
):
    core = meta_ref[3]
    pieces = weights.shape[1] // part
    copies = []
    for piece in range(pieces):
        columns = pl.ds(pl.multiple_of((2 * piece + core) * part, part), part)
        here = weights.at[:, pl.ds(piece * part, part)]
        copies.append(pltpu.make_async_copy(expand_ref.at[:, columns], here, arrived.at[piece]))
        copies[-1].start()
    _both(acts, act_mine, act_other)

    def before(piece):
        copies[piece].wait()
        return _dot(acts[...], weights[:, piece * part : (piece + 1) * part], ((1,), (0,)))

    now = before(0)
    for piece in range(pieces):
        later = before(piece + 1) if piece + 1 < pieces else None
        span = slice(piece * part, (piece + 1) * part)
        rate = 0.5 * (1.0 + lax.erf(now * math.sqrt(0.5)))
        low_ref[:, span] = (now * rate).astype(jnp.bfloat16)
        slope = rate + now * jnp.exp(-0.5 * now * now) * (1.0 / math.sqrt(2.0 * math.pi))
        back_ref[:, span] = (pulled_ref[:, span] * slope).astype(jnp.bfloat16)
        if piece % 2 == 1:
            pair = slice((piece - 1) * part, (piece + 1) * part)
            got = _dot(back_ref[:, pair], weights[:, pair], ((1,), (1,)))
            if piece == 1:
                total[...] = got
            elif piece + 1 < pieces:
                total[...] += got
            else:
                in_keep[...] = total[:rows] + got[:rows]
                in_send[...] = total[rows:] + got[rows:]
        now = later


def feed(meta, act_mine, act_other, pulled, expand_weight, peers):
    rows, width = act_mine.shape
    part = expand_weight.shape[1] // (2 * peers)
    shapes = [
        ((rows, width), jnp.float32),
        ((rows, width), jnp.float32),
        ((2 * rows, peers * part), jnp.bfloat16),
        ((2 * rows, peers * part), jnp.bfloat16),
    ]
    return pl.pallas_call(
        partial(feed_kernel, rows, part),
        out_shape=[jax.ShapeDtypeStruct(*shape) for shape in shapes],
        in_specs=_specs("svvvh"),
        out_specs=_specs("vvvv"),
        scratch_shapes=[
            pltpu.VMEM((2 * rows, width), jnp.bfloat16),
            pltpu.VMEM((width, peers * part), jnp.bfloat16),
            pltpu.VMEM((2 * rows, width), jnp.float32),
            pltpu.SemaphoreType.DMA((peers,)),
        ],
        compiler_params=_params(40),
        cost_estimate=pl.CostEstimate(flops=8 * 10**9, bytes_accessed=20 * 2**20, transcendentals=2 * 10**6),
        name="feed",
    )(meta, act_mine, act_other, pulled, expand_weight)


def contract_weigh_kernel(part, meta_ref, grad_mine, grad_other, low_ref, one_keep, one_send, two_keep, two_send, grads):
    step = pl.program_id(0)
    x, y = meta_ref[1], meta_ref[2]
    cut, half = one_keep.shape[2], part // 2

    @pl.when(step == 0)
    def _():
        _both(grads, grad_mine, grad_other)

    grad = _dot(low_ref[...], grads[...], ((0,), (0,))).astype(jnp.bfloat16)
    level = step // 2

    @pl.when(step % 2 == x)
    def _():
        one_keep[level] = grad[:, :cut]

    @pl.when(step % 2 != x)
    def _():
        one_send[level] = grad[:, :cut]

    @pl.when(y == 0)
    def _():
        two_keep[step] = grad[:half, cut:]
        two_send[step] = grad[half:, cut:]

    @pl.when(y != 0)
    def _():
        two_keep[step] = grad[half:, cut:]
        two_send[step] = grad[:half, cut:]


def contract_weigh(meta, grad_mine, grad_other, low, peers):
    rows, width = grad_mine.shape
    part, cut = low.shape[1] // peers, width // 2
    shapes = [(peers // 2, part, cut), (peers // 2, part, cut), (peers, part // 2, cut), (peers, part // 2, cut)]
    return pl.pallas_call(
        partial(contract_weigh_kernel, part),
        out_shape=[jax.ShapeDtypeStruct(shape, jnp.bfloat16) for shape in shapes],
        grid_spec=pltpu.PrefetchScalarGridSpec(
            num_scalar_prefetch=1,
            grid=(peers,),
            in_specs=[_whole(rows, width)] * 2 + [_across(2 * rows, part)],
            out_specs=[_whole(*shape) for shape in shapes],
            scratch_shapes=[pltpu.VMEM((2 * rows, width), jnp.bfloat16)],
        ),
        compiler_params=_params(12),
        cost_estimate=pl.CostEstimate(flops=10**8, bytes_accessed=2**20, transcendentals=0),
        name="contract_weigh",
    )(meta, grad_mine, grad_other, low)


def weigh_kernel(
    peers, rows, part, meta_ref, act_mine, act_other, mix_mine, mix_other, right_mine, right_other, low_ref, back_ref, contract_ref,
    out_keep, out_send, one_keep, one_send, two_keep, two_send, turned, total, block_grad,
):
    step = pl.program_id(0)
    x, y = meta_ref[1], meta_ref[2]
    group = block_grad.shape[1]
    half, near = group // 2, peers // 2

    def over_x(columns):
        for place in range(near):
            one_keep[place, :, columns] = block_grad[2 * place + x]
            one_send[place, :, columns] = block_grad[2 * place + 1 - x]

    def over_y(columns):
        for place in range(peers):
            two_keep[place, :, columns] = block_grad[place, pl.ds(pl.multiple_of(y * half, half), half), :]
            two_send[place, :, columns] = block_grad[place, pl.ds(pl.multiple_of((1 - y) * half, half), half), :]

    @pl.when(step == 0)
    def _():
        turned[:, :rows] = _turned(mix_mine[...]).astype(jnp.bfloat16)
        turned[:, rows:] = _turned(mix_other[...]).astype(jnp.bfloat16)
        right = jnp.concatenate([right_mine[...], right_other[...]])
        grad = _dot(turned[...], right, ((1,), (0,))).astype(jnp.bfloat16)
        tail = pl.ds(near * part, part)
        block_grad[...] = grad[:, :part].reshape(peers, group, part)
        over_x(tail)
        block_grad[...] = grad[:, part:].reshape(peers, group, part)
        over_y(tail)
        turned[:, :rows] = _turned(act_mine[...]).astype(jnp.bfloat16)
        turned[:, rows:] = _turned(act_other[...]).astype(jnp.bfloat16)
        total[...] = jnp.zeros_like(total)

    total[...] += _dot(low_ref[...], contract_ref[...], ((1,), (0,)))
    block_grad[...] = _dot(turned[...], back_ref[...], ((1,), (0,))).astype(jnp.bfloat16).reshape(peers, group, part)

    @pl.when(step < near)
    def _():
        over_x(pl.ds(pl.multiple_of(step * part, part), part))

    @pl.when(step >= near)
    def _():
        over_y(pl.ds(pl.multiple_of((step - near) * part, part), part))

    @pl.when(step == peers - 1)
    def _():
        out_keep[...] = total[:rows]
        out_send[...] = total[rows:].astype(jnp.bfloat16)


def weigh(meta, act_mine, act_other, mix_mine, mix_other, right_mine, right_other, low, back, contract_weight, peers):
    rows, width = act_mine.shape
    part = contract_weight.shape[0] // (2 * peers)
    group, span = width // peers, part * (peers // 2 + 1)
    shapes = [
        ((rows, width), jnp.float32),
        ((rows, width), jnp.bfloat16),
        ((peers // 2, group, span), jnp.bfloat16),
        ((peers // 2, group, span), jnp.bfloat16),
        ((peers, group // 2, span), jnp.bfloat16),
        ((peers, group // 2, span), jnp.bfloat16),
    ]
    return pl.pallas_call(
        partial(weigh_kernel, peers, rows, part),
        out_shape=[jax.ShapeDtypeStruct(*shape) for shape in shapes],
        grid_spec=pltpu.PrefetchScalarGridSpec(
            num_scalar_prefetch=1,
            grid=(peers,),
            in_specs=[_whole(rows, width)] * 4
            + [_whole(rows, width // 2)] * 2
            + [_across(2 * rows, part)] * 2
            + [pl.BlockSpec((part, width), lambda step, meta_ref: (2 * step + meta_ref[3], 0))],
            out_specs=[_whole(*shape) for shape, _ in shapes],
            scratch_shapes=[
                pltpu.VMEM((width, 2 * rows), jnp.bfloat16),
                pltpu.VMEM((2 * rows, width), jnp.float32),
                pltpu.VMEM((peers, group, part), jnp.bfloat16),
            ],
        ),
        compiler_params=_params(28),
        cost_estimate=pl.CostEstimate(flops=10**8, bytes_accessed=2**20, transcendentals=0),
        name="weigh",
    )(meta, act_mine, act_other, mix_mine, mix_other, right_mine, right_other, low, back, contract_weight)


def turn_kernel(meta_ref, in_mine, in_other, middle_ref, grad_ref, gain_ref, weight_ref, heads_ref, total_ref, keep_ref, send_ref, sums_ref):
    core = meta_ref[3]
    half = keep_ref.shape[1]
    unit, scale = _unit(middle_ref[...])
    total = grad_ref[...].astype(jnp.float32) + _norm_back(in_mine[...] + in_other[...], unit, scale, gain_ref[...], sums_ref)
    total_ref[...] = total
    low = total.astype(jnp.bfloat16)

    @pl.when(core == 0)
    def _():
        keep_ref[...] = low[:, :half]
        send_ref[...] = low[:, half:]

    @pl.when(core != 0)
    def _():
        keep_ref[...] = low[:, half:]
        send_ref[...] = low[:, :half]

    heads = _dot(low, weight_ref[...], ((1,), (1,))).astype(jnp.bfloat16)
    for part in range(heads_ref.shape[0]):
        heads_ref[part] = heads[:, 128 * part : 128 * part + 128]


def turn(meta, in_mine, in_other, middle, grad, gain, weight, peers):
    rows, width = middle.shape
    shapes = [
        ((peers, rows, width // peers), jnp.bfloat16),
        ((rows, width), jnp.float32),
        ((rows, width // 2), jnp.bfloat16),
        ((rows, width // 2), jnp.bfloat16),
        ((2, width), jnp.float32),
    ]
    return pl.pallas_call(
        turn_kernel,
        out_shape=[jax.ShapeDtypeStruct(*shape) for shape in shapes],
        in_specs=_specs("svvvvvv"),
        out_specs=_specs("v" * len(shapes)),
        compiler_params=_params(14),
        cost_estimate=pl.CostEstimate(flops=10**9, bytes_accessed=8 * 2**20, transcendentals=0),
        name="turn",
    )(meta, in_mine, in_other, middle, grad, gain, weight)


def close_kernel(parts_ref, tokens_ref, grad_ref, gain_ref, weight_ref, out_ref, sums_ref, held):
    peers = parts_ref.shape[0]
    for peer in range(peers):
        for block in range(3):
            at = 128 * (block * peers + peer)
            held[:, at : at + 128] = parts_ref[peer, block]
    back = _dot(held[...], weight_ref[...], ((1,), (1,)))
    unit, scale = _unit(tokens_ref[...].astype(jnp.float32))
    out_ref[...] = grad_ref[...] + _norm_back(back, unit, scale, gain_ref[...], sums_ref)


def close(parts, tokens, grad, gain, weight):
    rows, width = tokens.shape
    return pl.pallas_call(
        close_kernel,
        out_shape=[jax.ShapeDtypeStruct((rows, width), jnp.float32), jax.ShapeDtypeStruct((2, width), jnp.float32)],
        in_specs=_specs("vvvvv"),
        out_specs=_specs("vv"),
        scratch_shapes=[pltpu.VMEM((rows, 3 * width), jnp.bfloat16)],
        compiler_params=_params(20),
        cost_estimate=pl.CostEstimate(flops=2 * 10**9, bytes_accessed=10 * 2**20, transcendentals=0),
        name="close",
    )(parts, tokens, grad, gain, weight)


def _plus(a, b):
    return (a.astype(jnp.float32) + b.astype(jnp.float32)).astype(jnp.bfloat16)


def second_kernel(meta_ref, one_keep, one_got, two_keep, two_got, one_left, one_send, two_left, two_send):
    x, y = meta_ref[1], meta_ref[2]
    levels, half, _ = one_left.shape
    mine = pl.ds(pl.multiple_of(y * half, half), half)
    other = pl.ds(pl.multiple_of((1 - y) * half, half), half)
    for level in range(levels):
        one_left[level] = _plus(one_keep[level, mine], one_got[level, mine])
        one_send[level] = _plus(one_keep[level, other], one_got[level, other])
        two_left[level] = _plus(two_keep[2 * level + x], two_got[2 * level + x])
        two_send[level] = _plus(two_keep[2 * level + 1 - x], two_got[2 * level + 1 - x])


def near_kernel(meta_ref, one_keep, one_got, two_keep, two_got, left, send):
    side = (meta_ref[0] >> 1) & 1
    cut = one_keep.shape[2]
    for level in range(left.shape[0]):
        for out, at in ((left, 2 * level + side), (send, 2 * level + 1 - side)):
            out[level, :, :cut] = _plus(one_keep[at], one_got[at])
            out[level, :, cut:] = _plus(two_keep[at], two_got[at])


def far_kernel(meta_ref, keep, got, left, send):
    upper = meta_ref[0] >> 2
    left[...] = _plus(keep[upper], got[upper])
    send[...] = _plus(keep[1 - upper], got[1 - upper])


def last_kernel(keep, got, out):
    out[...] = _plus(keep[...], got[...])


def _small_call(kernel, name, shapes, kind, *arguments):
    size = sum(2 * math.prod(a.shape) for a in arguments[-4:])
    return pl.pallas_call(
        kernel,
        out_shape=[jax.ShapeDtypeStruct(shape, kind) for shape in shapes],
        in_specs=_specs(*("s" if a.dtype == jnp.int32 else "v" for a in arguments)),
        out_specs=_specs("v" * len(shapes)),
        compiler_params=_params(24),
        cost_estimate=pl.CostEstimate(flops=size, bytes_accessed=3 * size, transcendentals=0),
        name=name,
    )(*arguments)


def _places(meta_ref, half):
    y, core = meta_ref[2], meta_ref[3]
    return [(c, pl.ds(pl.multiple_of(h * half, half), half)) for c in (core, 1 - core) for h in (y, 1 - y)]


def finish_contract_kernel(meta_ref, *refs):
    half = refs[0].shape[0]
    y, core = meta_ref[2], meta_ref[3]
    starts = [(2 * c + h) * half for c in (core, 1 - core) for h in (y, 1 - y)]
    for part, start in zip(refs[:4], starts):
        refs[4][pl.ds(pl.multiple_of(start, half), half), :] = part[...].astype(jnp.float32)


def finish_expand_kernel(part, meta_ref, *refs):
    expand_ref, merge_ref = refs[4:]
    half, span = refs[0].shape[0], refs[0].shape[1] // 2
    near = span // part - 1
    for source, (core, rows) in zip(refs[:4], _places(meta_ref, half)):
        for side in range(2):
            for block in range(near):
                at = pl.multiple_of((2 * (side * near + block) + core) * part, part)
                start = side * span + block * part
                expand_ref[rows, pl.ds(at, part)] = source[:, start : start + part].astype(jnp.float32)
            at = pl.multiple_of((2 * core + side) * part, part)
            start = side * span + near * part
            merge_ref[rows, pl.ds(at, part)] = source[:, start : start + part].astype(jnp.float32)


def finish_attend_kernel(meta_ref, *refs):
    half, wide = refs[0].shape
    span = wide // 3
    for source, (core, rows) in zip(refs[:4], _places(meta_ref, half)):
        for block in range(3):
            at = pl.multiple_of((2 * block + core) * span, span)
            refs[4][rows, pl.ds(at, span)] = source[:, block * span : (block + 1) * span].astype(jnp.float32)


def attend_weigh_kernel(
    meta_ref, act_mine, act_other, owned_ref, other_ref, one_keep, one_send, two_keep, two_send, acts, right, held
):
    x, y, core = meta_ref[1], meta_ref[2], meta_ref[3]
    count, blocks, rows, _ = other_ref.shape
    peers, group, cut = held.shape
    half = group // 2
    _both(acts, act_mine, act_other)
    for block in range(blocks):
        for place in range(count):
            at = 128 * (block * count + place)
            right[:rows, at : at + 128] = owned_ref[core * count + place, block]
            right[rows:, at : at + 128] = other_ref[place, block]
    for side in range(2):
        grad = _dot(acts[...], right[:, side * cut : (side + 1) * cut], ((0,), (0,))).astype(jnp.bfloat16)
        held[...] = grad.reshape(peers, group, cut)
        if side == 0:
            for place in range(peers // 2):
                one_keep[place] = held[2 * place + x]
                one_send[place] = held[2 * place + 1 - x]
        else:
            for place in range(peers):
                two_keep[place] = held[place, pl.ds(pl.multiple_of(y * half, half), half), :]
                two_send[place] = held[place, pl.ds(pl.multiple_of((1 - y) * half, half), half), :]


def attend_weigh(meta, act_mine, act_other, owned, other):
    peers, blocks, rows, _ = owned.shape
    width = act_mine.shape[1]
    group, span = width // peers, blocks * width // 2
    cut = span // 2
    shapes = [(peers // 2, group, cut), (peers // 2, group, cut), (peers, group // 2, cut), (peers, group // 2, cut)]
    return pl.pallas_call(
        attend_weigh_kernel,
        out_shape=[jax.ShapeDtypeStruct(shape, jnp.bfloat16) for shape in shapes],
        in_specs=_specs("svvvv"),
        out_specs=_specs("vvvv"),
        scratch_shapes=[
            pltpu.VMEM((2 * rows, width), jnp.bfloat16),
            pltpu.VMEM((2 * rows, span), jnp.bfloat16),
            pltpu.VMEM((peers, group, cut), jnp.bfloat16),
        ],
        compiler_params=_params(20),
        cost_estimate=pl.CostEstimate(flops=2 * 10**9, bytes_accessed=7 * 2**20, transcendentals=0),
        name="attend_weigh",
    )(meta, act_mine, act_other, owned, other)


def flipped(array, axis, mask):
    peers = lax.axis_size(axis)
    return lax.ppermute(array, axis, [(i, i ^ mask) for i in range(peers)])


def pick(array, index, axis):
    return lax.dynamic_index_in_dim(array, index, axis, keepdims=False)


def added(a, b):
    return (a.astype(jnp.float32) + b.astype(jnp.float32)).astype(jnp.bfloat16)


def in_order(mine, other, bit, axis):
    lower = jnp.where(bit == 0, mine, other)
    upper = jnp.where(bit == 0, other, mine)
    return jnp.concatenate([lower, upper], axis=axis)


def after(value, *others):
    return lax.optimization_barrier((value, others))[0]


def over_first(one_keep, one_send, two_keep, two_send):
    return one_keep, flipped(one_send, "blk", 1), two_keep, flipped(two_send, "seq", 2)


def over_second(here, one_keep, one_got, two_keep, two_got):
    levels, rows, cut = one_keep.shape
    shape = (levels, rows // 2, cut)
    return _small_call(second_kernel, "second", [shape] * 4, jnp.bfloat16, here, one_keep, one_got, two_keep, two_got)


def send_second(one_left, one_send, two_left, two_send):
    return one_left, flipped(one_send, "seq", 2), two_left, flipped(two_send, "blk", 1)


def over_near(here, one_keep, one_got, two_keep, two_got):
    levels, half, cut = one_keep.shape
    left, send = _small_call(
        near_kernel, "near", [(levels // 2, half, 2 * cut)] * 2, jnp.bfloat16, here, one_keep, one_got, two_keep, two_got
    )
    return left, flipped(send, "blk", 2)


def over_far(here, keep, got):
    left, send = _small_call(far_kernel, "far", [keep.shape[1:]] * 2, jnp.bfloat16, here, keep, got)
    return left, flipped(send, "blk", 4)


def over_all(keep, got):
    return _small_call(last_kernel, "last", [keep.shape], jnp.bfloat16, keep, got)[0]


def of_all(own):
    across = flipped(own, "seq", 2)
    return own, across, flipped(own, "seq", 1), flipped(across, "seq", 1)


def local_by_heads(
    tokens,
    lengths,
    attend_weight,
    merge_weight,
    expand_weight,
    contract_weight,
    gain_first,
    shift_first,
    gain_second,
    shift_second,
    bias_table,
    cotangent,
):
    rows, width = tokens.shape[1], tokens.shape[2]
    buckets, heads = bias_table.shape
    hidden = expand_weight.shape[1]
    items = lengths.shape[1]
    peers = lax.axis_size("blk")
    levels = peers // 2
    group = width // peers
    part = hidden // (2 * peers)
    me, line_of = lax.axis_index("blk"), lax.axis_index("seq")
    z, x, y, core = me // 2, me % 2, line_of // 2, line_of % 2
    place = (z, x, y)
    here = jnp.stack([me, x, y, core]).astype(jnp.int32)
    gain_first, shift_first, gain_second, shift_second = (
        v.reshape(1, width) for v in (gain_first, shift_first, gain_second, shift_second)
    )

    own, grad_out = tokens[0], cotangent[0]
    grad_other = flipped(grad_out, "seq", 1)
    meta = plan(lengths[0], me, peers, rows)
    hot = bucket_lines(rows, buckets)
    table_mine = lax.dynamic_slice_in_dim(bias_table, 2 * me, 2, 1)
    lines = jnp.dot(table_mine.T, hot, precision=highest)
    far = table_mine[buckets - 1]

    def to_all(array):
        return lax.all_to_all(array, "blk", split_axis=0, concat_axis=0, tiled=True)

    *parts, act_first = project(here, own, gain_first, shift_first, attend_weight, peers)
    parts = [parts[0]] + [flipped(parts[step], "blk", step) for step in range(1, peers)]
    pulled = pull(here, grad_out, grad_other, contract_weight, peers)
    mixed, wide, logs, qkv = attend(meta, after(far, pulled), lines, parts, items)
    first_other = flipped(act_first, "seq", 1)
    attn_low, middle, act_second = merge(to_all(mixed), own, gain_second, shift_second, merge_weight)
    act_other = flipped(act_second, "seq", 1)
    attn_other = flipped(attn_low, "seq", 1)
    in_keep, in_send, hidden_low, hidden_back = feed(here, act_second, act_other, pulled, expand_weight, peers)
    grad_heads, grad_middle, keep_low, send_low, sums_second = turn(
        here, in_keep, flipped(in_send, "seq", 1), middle, grad_out, gain_second, merge_weight, peers
    )
    contract_parts = over_first(*contract_weigh(here, grad_out, grad_other, after(hidden_low, grad_heads), peers))
    out_keep, out_send, *expand_parts = weigh(
        here, act_second, act_other, attn_low, attn_other, keep_low, flipped(send_low, "seq", 1), hidden_low, hidden_back, contract_weight, peers
    )
    expand_parts = over_first(*expand_parts)

    grad_heads, out_send = lax.optimization_barrier((to_all(grad_heads), out_send))
    back_all, line_grad = attend_back(meta, far, lines, wide, logs, qkv, grad_heads, items)
    back_all, *sums = lax.optimization_barrier((back_all, *contract_parts, *expand_parts))
    owned = to_all(back_all)
    contract_parts = over_near(here, *send_second(*over_second(here, *sums[:4])))
    expand_parts = send_second(*over_second(here, *sums[4:]))
    owned, *sums = lax.optimization_barrier((owned, *contract_parts, *expand_parts))
    contract_parts = over_far(here, *sums[:2])
    expand_parts = over_near(here, *sums[2:])
    owned_send = pick(owned.reshape(2, levels, 3, rows, group), 1 - core, 0)
    attend_parts = over_first(*attend_weigh(here, act_first, first_other, owned, flipped(owned_send, "seq", 1)))
    output = (middle + out_keep + flipped(out_send, "seq", 1).astype(jnp.float32)).astype(jnp.bfloat16)
    tokens_grad, sums_first = close(owned, own, grad_middle, gain_first, attend_weight)
    table_mine = jnp.dot(hot, line_grad.T, precision=highest).reshape(1, 2 * buckets)
    table_row = jnp.broadcast_to(jnp.pad(table_mine, ((0, 0), (0, group - 2 * buckets)))[:, None], (1, peers, group))
    small = jnp.concatenate([sums_first.reshape(2, peers, group), sums_second.reshape(2, peers, group), table_row]).transpose(1, 0, 2)
    small = jnp.pad(small, ((0, 0), (0, 3), (0, 0)))

    sums = lax.optimization_barrier((*attend_parts, *contract_parts, *expand_parts))
    attend_parts = send_second(*over_second(here, *sums[:4]))
    contract_own = over_all(*sums[4:6])
    contract_across = flipped(contract_own, "seq", 2)
    expand_parts = over_far(here, *sums[6:])
    small, *sums = lax.optimization_barrier((small, *attend_parts, contract_across, *expand_parts))
    attend_parts = over_near(here, *sums[:4])
    contract_grad = (contract_own, sums[4], flipped(contract_own, "seq", 1), flipped(sums[4], "seq", 1))
    small = small + flipped(small, "seq", 1)
    expand_own = over_all(*sums[5:])
    expand_across = flipped(expand_own, "seq", 2)
    small, expand_across, *attend_parts = lax.optimization_barrier((small, expand_across, *attend_parts))
    attend_parts = over_far(here, *attend_parts)
    small = small + flipped(small, "seq", 2)
    expand_grad = (expand_own, expand_across, flipped(expand_own, "seq", 1), flipped(expand_across, "seq", 1))
    small = to_all(small)
    contract_grad = _small_call(finish_contract_kernel, "finish_contract", [(2 * part, width)], jnp.float32, here, *contract_grad)[0]
    expand_grad, merge_grad = _small_call(
        partial(finish_expand_kernel, part), "finish_expand", [(group, hidden), (group, width)], jnp.float32, here, *expand_grad
    )
    attend_grad = of_all(over_all(*attend_parts))
    attend_grad = _small_call(finish_attend_kernel, "finish_attend", [(group, 3 * width)], jnp.float32, here, *attend_grad)[0]
    table_grad = small[:, 4, : 2 * buckets].reshape(peers, buckets, 2).transpose(1, 0, 2).reshape(buckets, heads)
    vectors = jnp.sum(small[:, :4], axis=0)
    return (
        output[None],
        tokens_grad[None],
        attend_grad,
        merge_grad,
        expand_grad,
        contract_grad,
        vectors[0],
        vectors[1],
        vectors[2],
        vectors[3],
        table_grad,
    )


def local(*arguments):
    heads = arguments[10].shape[1]
    rows = arguments[0].shape[1]
    peers = lax.axis_size("blk")
    if peers == 8 and lax.axis_size("seq") == 4 and heads == 2 * peers and rows == 256:
        return local_by_heads(*arguments)
    return local_by_runs(*arguments)


def solution(mesh):
    in_specs = (
        P("seq", "blk", None),
        P("seq", None),
        P(),
        P(),
        P(),
        P(),
        P(),
        P(),
        P(),
        P(),
        P(),
        P("seq", "blk", None),
    )
    out_specs = (
        P("seq", "blk", None),
        P("seq", "blk", None),
        P("blk", None),
        P("blk", None),
        P("blk", None),
        P("blk", None),
        P("blk"),
        P("blk"),
        P("blk"),
        P("blk"),
        P(),
    )
    return jax.shard_map(local, mesh=mesh, in_specs=in_specs, out_specs=out_specs, check_vma=False)
```

```python
from functools import partial
import math

import jax
import jax.numpy as jnp
from jax import lax
from jax.experimental import pallas as pl
from jax.experimental.pallas import tpu as pltpu
from jax.sharding import PartitionSpec as P

HOPS = 6


epsilon = 1e-05
masked_score = -1e30
highest = lax.Precision.HIGHEST
bucket_edges = [math.ceil(16 * 8 ** (t / 16)) for t in range(1, 16)]


def shifted(array, axis, by):
    peers = lax.axis_size(axis)
    pairs = [(i, i + by) for i in range(peers) if 0 <= i + by < peers]
    return lax.ppermute(array, axis, pairs)


def shortened(array):

    def short(part):
        return part.astype(jnp.bfloat16) if part.dtype == jnp.float32 else part

    return jax.tree.map(short, array)


def bucket_of(distance):
    total = jnp.minimum(jnp.maximum(distance, 0), 16)
    for edge in bucket_edges:
        total = total + (distance >= edge).astype(jnp.int32)
    return total


def segment_of(position, ends):
    return jnp.sum((position[:, None] >= ends[None, :]).astype(jnp.int32), axis=1)


def layer_norm(value, gain, shift):
    mean = jnp.mean(value, axis=-1, keepdims=True)
    centred = value - mean
    variance = jnp.mean(centred * centred, axis=-1, keepdims=True)
    return centred * lax.rsqrt(variance + epsilon) * gain + shift


def diagonal_sums(grid, count):
    heads = grid.shape[0]
    padded = jnp.pad(jnp.flip(grid, axis=-1), ((0, 0), (0, 0), (0, count)))
    flat = padded.reshape(heads, 2 * count * count)[:, : count * (2 * count - 1)]
    return jnp.sum(flat.reshape(heads, count, 2 * count - 1), axis=1)


def band_matrix(line, count):
    heads = line.shape[0]
    flipped = jnp.flip(line, axis=-1)
    tiled = jnp.tile(flipped, (1, count))
    window = tiled[:, count - 1 : count - 1 + count * (2 * count - 2)]
    return window.reshape(heads, count, 2 * count - 2)[:, :, :count]


def fetch_earlier(block):
    earlier = []
    moving = block
    for hop in range(HOPS):
        moving = shifted(moving, "blk", 1)
        earlier.append(moving)
    return earlier


def return_parts(parts):
    carried = jnp.zeros_like(parts[0])
    for hop in range(HOPS, 0, -1):
        carried = shifted(shortened(carried + parts[hop - 1]), "blk", -1)
    return carried


def local_by_runs(
    tokens,
    lengths,
    attend_weight,
    merge_weight,
    expand_weight,
    contract_weight,
    gain_first,
    shift_first,
    gain_second,
    shift_second,
    bias_table,
    cotangent,
):
    rows = tokens.shape[1]
    width = tokens.shape[2]
    heads = bias_table.shape[1]
    buckets = bias_table.shape[0]
    head_size = width // heads
    items = lengths.shape[1]
    start = lax.axis_index("blk") * rows
    query_pos = start + jnp.arange(rows, dtype=jnp.int32)
    ends = jnp.cumsum(lengths[0])
    query_seg = segment_of(query_pos, ends)
    band = jnp.arange(2 * rows - 1, dtype=jnp.int32) - (rows - 1)
    bucket_ids = jnp.arange(buckets, dtype=jnp.int32)

    def pair_setup(hop):
        key_pos = query_pos - hop * rows
        key_seg = segment_of(key_pos, ends)
        key_valid = (key_pos >= 0) & (key_seg < items)
        same = key_pos[None, :] == query_pos[:, None]
        allowed = (
            (query_seg[:, None] == key_seg[None, :])
            & (key_pos[None, :] <= query_pos[:, None])
            & (key_valid[None, :] | same)
        )
        onehot = (bucket_of(hop * rows + band)[:, None] == bucket_ids[None, :]).astype(jnp.float32)
        band_bias = jnp.dot(onehot, bias_table, precision=highest).T
        bias = band_matrix(band_bias, rows)
        additive = jnp.where(allowed[None], bias, masked_score)
        return (jnp.any(allowed), onehot, additive)

    pairs = [pair_setup(hop) for hop in range(HOPS + 1)]
    residual = tokens[0].astype(jnp.float32)
    normed_first, norm_first_pull = jax.vjp(layer_norm, residual, gain_first, shift_first)
    act_first = normed_first.astype(jnp.bfloat16)
    projected = jnp.dot(act_first, attend_weight, preferred_element_type=jnp.float32).astype(
        jnp.bfloat16
    )
    query = projected[:, :width].reshape(rows, heads, head_size)
    keys_values = jnp.stack([projected[:, width : 2 * width], projected[:, 2 * width :]])
    blocks = [keys_values] + fetch_earlier(keys_values)

    def scores_of(block, pair):
        key = block[0].reshape(rows, heads, head_size)
        raw = jnp.einsum("qhe,khe->hqk", query, key, preferred_element_type=jnp.float32) * 0.125
        return raw + pair[2]

    def empty_total():
        return jnp.full((heads, rows), masked_score, jnp.float32)

    def empty_scores():
        return jnp.full((heads, rows, rows), masked_score, jnp.float32)

    log_total = empty_total()
    kept_scores = []
    for block, pair in zip(blocks, pairs):

        def part_total(block=block, pair=pair):
            scores = scores_of(block, pair)
            peak = jnp.max(scores, axis=-1)
            return (peak + jnp.log(jnp.sum(jnp.exp(scores - peak[..., None]), axis=-1)), scores)

        def skip_total():
            return (empty_total(), empty_scores())

        part_log, scores = lax.cond(pair[0], part_total, skip_total)
        log_total = jnp.logaddexp(log_total, part_log)
        kept_scores.append(scores)

    def empty_heads():
        return jnp.zeros((rows, heads, head_size), jnp.float32)

    attended = empty_heads()
    for block, pair, scores in zip(blocks, pairs, kept_scores):

        def part_mix(block=block, scores=scores):
            weights = jnp.exp(scores - log_total[..., None]).astype(jnp.bfloat16)
            value = block[1].reshape(rows, heads, head_size)
            return jnp.einsum("hqk,khe->qhe", weights, value, preferred_element_type=jnp.float32)

        attended = attended + lax.cond(pair[0], part_mix, empty_heads)
    attn_low = attended.reshape(rows, width).astype(jnp.bfloat16)
    middle = residual + jnp.dot(attn_low, merge_weight, preferred_element_type=jnp.float32)
    normed_second, norm_second_pull = jax.vjp(layer_norm, middle, gain_second, shift_second)
    act_second = normed_second.astype(jnp.bfloat16)
    hidden_pre = jnp.dot(act_second, expand_weight, preferred_element_type=jnp.float32)
    hidden, gelu_pull = jax.vjp(partial(jax.nn.gelu, approximate=False), hidden_pre)
    hidden_low = hidden.astype(jnp.bfloat16)
    output = (
        middle + jnp.dot(hidden_low, contract_weight, preferred_element_type=jnp.float32)
    ).astype(jnp.bfloat16)
    grad_out = cotangent[0]
    contract_grad = jnp.einsum(
        "tf,td->fd", hidden_low, grad_out, preferred_element_type=jnp.float32
    )
    grad_hidden = jnp.einsum(
        "td,fd->tf", grad_out, contract_weight, preferred_element_type=jnp.float32
    )
    grad_pre = gelu_pull(grad_hidden)[0].astype(jnp.bfloat16)
    expand_grad = jnp.einsum("td,tf->df", act_second, grad_pre, preferred_element_type=jnp.float32)
    grad_second = jnp.einsum(
        "tf,df->td", grad_pre, expand_weight, preferred_element_type=jnp.float32
    )
    grad_middle_norm, gain_second_grad, shift_second_grad = norm_second_pull(grad_second)
    grad_middle = grad_out.astype(jnp.float32) + grad_middle_norm
    grad_middle_low = grad_middle.astype(jnp.bfloat16)
    merge_grad = jnp.einsum(
        "td,te->de", attn_low, grad_middle_low, preferred_element_type=jnp.float32
    )
    grad_heads = (
        jnp.einsum("te,de->td", grad_middle_low, merge_weight, preferred_element_type=jnp.float32)
        .astype(jnp.bfloat16)
        .reshape(rows, heads, head_size)
    )
    row_dot = jnp.sum(grad_heads.astype(jnp.float32) * attended, axis=-1).T
    back_blocks = [keys_values] + fetch_earlier(keys_values)

    def empty_grads():
        return (
            empty_heads(),
            jnp.zeros((2, rows, width), jnp.float32),
            jnp.zeros((buckets, heads), jnp.float32),
        )

    grad_query = empty_heads()
    table_local = jnp.zeros((buckets, heads), jnp.float32)
    parts = []
    for block, pair in zip(back_blocks, pairs):

        def part_grads(block=block, pair=pair):
            key = block[0].reshape(rows, heads, head_size)
            value = block[1].reshape(rows, heads, head_size)
            weights = jnp.exp(scores_of(block, pair) - log_total[..., None])
            weights_low = weights.astype(jnp.bfloat16)
            grad_weights = jnp.einsum(
                "qhe,khe->hqk", grad_heads, value, preferred_element_type=jnp.float32
            )
            grad_scores = (weights * (grad_weights - row_dot[..., None])).astype(jnp.bfloat16)
            query_part = (
                jnp.einsum("hqk,khe->qhe", grad_scores, key, preferred_element_type=jnp.float32)
                * 0.125
            )
            key_part = (
                jnp.einsum("hqk,qhe->khe", grad_scores, query, preferred_element_type=jnp.float32)
                * 0.125
            )
            value_part = jnp.einsum(
                "hqk,qhe->khe", weights_low, grad_heads, preferred_element_type=jnp.float32
            )
            line_grad = diagonal_sums(grad_scores.astype(jnp.float32), rows)
            table_part = jnp.dot(pair[1].T, line_grad.T, precision=highest)
            return (
                query_part,
                jnp.stack([key_part.reshape(rows, width), value_part.reshape(rows, width)]),
                table_part,
            )

        query_part, pair_part, table_part = lax.cond(pair[0], part_grads, empty_grads)
        grad_query = grad_query + query_part
        table_local = table_local + table_part
        parts.append(pair_part)
    owned = (parts[0] + return_parts(parts[1:])).astype(jnp.bfloat16)
    grad_project = jnp.concatenate(
        [grad_query.reshape(rows, width).astype(jnp.bfloat16), owned[0], owned[1]], axis=1
    )
    attend_grad = jnp.einsum(
        "td,te->de", act_first, grad_project, preferred_element_type=jnp.float32
    )
    grad_first = jnp.einsum(
        "te,de->td", grad_project, attend_weight, preferred_element_type=jnp.float32
    )
    grad_input_norm, gain_first_grad, shift_first_grad = norm_first_pull(grad_first)
    tokens_grad = grad_middle + grad_input_norm
    results = (
        lax.psum_scatter(attend_grad, "blk", scatter_dimension=0, tiled=True),
        lax.psum_scatter(merge_grad, "blk", scatter_dimension=0, tiled=True),
        lax.psum_scatter(expand_grad, "blk", scatter_dimension=0, tiled=True),
        lax.psum_scatter(contract_grad, "blk", scatter_dimension=0, tiled=True),
        lax.psum_scatter(gain_first_grad, "blk", scatter_dimension=0, tiled=True),
        lax.psum_scatter(shift_first_grad, "blk", scatter_dimension=0, tiled=True),
        lax.psum_scatter(gain_second_grad, "blk", scatter_dimension=0, tiled=True),
        lax.psum_scatter(shift_second_grad, "blk", scatter_dimension=0, tiled=True),
    )
    results = (
        lax.psum(results[0].astype(jnp.bfloat16), "seq").astype(jnp.float32),
        lax.psum(results[1].astype(jnp.bfloat16), "seq").astype(jnp.float32),
        lax.psum(results[2].astype(jnp.bfloat16), "seq").astype(jnp.float32),
        lax.psum(results[3].astype(jnp.bfloat16), "seq").astype(jnp.float32),
        lax.psum(results[4].astype(jnp.bfloat16), "seq").astype(jnp.float32),
        lax.psum(results[5].astype(jnp.bfloat16), "seq").astype(jnp.float32),
        lax.psum(results[6].astype(jnp.bfloat16), "seq").astype(jnp.float32),
        lax.psum(results[7].astype(jnp.bfloat16), "seq").astype(jnp.float32),
    )
    table_grad = lax.psum(table_local, ("seq", "blk"))
    return (
        output[None],
        tokens_grad[None],
        results[0],
        results[1],
        results[2],
        results[3],
        results[4],
        results[5],
        results[6],
        results[7],
        table_grad,
    )


def _segments(position, meta_ref, first, items):
    total = jnp.zeros(position.shape, jnp.int32)
    for item in range(items):
        total = total + (position >= meta_ref[first + item]).astype(jnp.int32)
    return total

def _allowed(meta_ref, peers, items, rows, i, j, which, needed):
    first = 1 + 2 * peers
    q_seg = _segments(i * rows + lax.broadcasted_iota(jnp.int32, (1, rows), 1), meta_ref, first, items)
    k_seg = _segments(j * rows + lax.broadcasted_iota(jnp.int32, (rows, 1), 0), meta_ref, first, items)
    k_seg = jnp.where((k_seg < items) & needed if which == 1 else k_seg < items, k_seg, -1)
    same = q_seg == k_seg
    if which == 0:
        key = lax.broadcasted_iota(jnp.int32, (rows, rows), 0)
        query = lax.broadcasted_iota(jnp.int32, (rows, rows), 1)
        return (same & (key < query)) | (key == query)
    return same

def _dot(a, b, dims):
    return lax.dot_general(a, b, (dims, ((), ())), preferred_element_type=jnp.float32)

def _turned(array):
    return jnp.transpose(array.astype(jnp.float32))

def _split(array, axis=1):
    wide = array.astype(jnp.float32)
    left = lax.broadcasted_iota(jnp.int32, array.shape, axis) < 64
    return jnp.where(left, wide, 0.0).astype(jnp.bfloat16), jnp.where(left, 0.0, wide).astype(jnp.bfloat16)

def _fold(value, op):
    while value.shape[0] > 8:
        half = value.shape[0] // 2
        value = op(value[:half], value[half:])
    return value

def _put_bias(bias, line_ref, rows):
    for head in range(2):
        line = jnp.broadcast_to(line_ref[head:head + 1, :], (rows, 2 * rows))
        bias[head] = pltpu.roll(line, 0, 1, stride=1, stride_axis=0)

def _biased(raw, bias, far_ref, head, which, rows):
    if which == 0:
        return raw + bias[head, :, :rows]
    if which == 1:
        return raw + bias[head, :, rows:]
    return raw + far_ref[head]

def attend_kernel(peers, items, rows, meta_ref, far_ref, line_ref, *refs):
    parts = refs[:peers]
    mixed, wide_ref, log_ref, qkv, turned, bias, scores = refs[peers:]
    me = meta_ref[0]
    for slot in range(peers):
        qkv[me ^ slot] = parts[slot][...]
        turned[me ^ slot] = _turned(parts[slot][2]).astype(jnp.bfloat16)
    _put_bias(bias, line_ref, rows)
    upper = lax.broadcasted_iota(jnp.int32, (128, rows), 0) < 64

    def one_row(i, _):
        low = meta_ref[1 + i]
        whole = jnp.minimum(meta_ref[1 + peers + i], i - 1)
        queries = _split(qkv[i, 0].astype(jnp.float32) * 0.125)

        def put(j, slot, which, masked, peaks):
            key = qkv[j, 1]
            if masked:
                allowed = _allowed(meta_ref, peers, items, rows, i, j, which, low < i)
            new = []
            for head in range(2):
                raw = _biased(_dot(key, queries[head], ((1,), (1,))), bias, far_ref, head, which, rows)
                if masked:
                    raw = jnp.where(allowed, raw, masked_score)
                scores[head, slot] = raw
                new.append(jnp.maximum(peaks[head], _fold(raw, jnp.maximum)))
            return tuple(new)

        start = jnp.full((8, rows), masked_score, jnp.float32)
        before = jnp.maximum(i - 1, 0)
        peaks = put(i, peers, 0, True, (start, start))
        peaks = put(before, peers + 1, 1, True, peaks)
        peaks = lax.fori_loop(low, whole, lambda j, p: put(j, j, 2, True, p), peaks)
        peaks = lax.fori_loop(jnp.maximum(low, whole), i - 1, lambda j, p: put(j, j, 2, False, p), peaks)
        tops = [jnp.max(peak, axis=0, keepdims=True) for peak in peaks]

        def mix(j, slot, carry):
            sums, total = carry
            value = turned[j]
            new = []
            both = []
            for head in range(2):
                weight = jnp.exp(scores[head, slot] - tops[head])
                new.append(sums[head] + _fold(weight, jnp.add))
                both.append(_dot(value[64 * head:64 * head + 64], weight.astype(jnp.bfloat16), ((1,), (0,))))
            return tuple(new), total + jnp.concatenate(both)

        nothing = jnp.zeros((8, rows), jnp.float32)
        carry = ((nothing, nothing), jnp.zeros((128, rows), jnp.float32))
        carry = mix(before, peers + 1, mix(i, peers, carry))
        sums, total = lax.fori_loop(low, i - 1, lambda j, c: mix(j, j, c), carry)
        sums = [jnp.sum(s, axis=0, keepdims=True) for s in sums]
        total = total / jnp.where(upper, sums[0], sums[1])
        wide_ref[i] = total
        for head in range(2):
            log_ref[i, head:head + 1, :] = tops[head] + jnp.log(sums[head])
        mixed[i] = jnp.transpose(total).astype(jnp.bfloat16)
        return 0

    lax.fori_loop(0, peers, one_row, 0)

def attend(meta, far, line, parts, items):
    peers = len(parts)
    rows = parts[0].shape[1]
    smem = pl.BlockSpec(memory_space=pltpu.SMEM)
    vmem = pl.BlockSpec(memory_space=pltpu.VMEM)
    shapes = [
        jax.ShapeDtypeStruct((peers, rows, 128), jnp.bfloat16),
        jax.ShapeDtypeStruct((peers, 128, rows), jnp.float32),
        jax.ShapeDtypeStruct((peers, 8, rows), jnp.float32),
        jax.ShapeDtypeStruct((peers, 3, rows, 128), jnp.bfloat16),
    ]
    res = pl.pallas_call(
        partial(attend_kernel, peers, items, rows),
        out_shape=shapes,
        in_specs=[smem, smem] + [vmem] * (peers + 1),
        out_specs=[vmem] * 4,
        scratch_shapes=[
            pltpu.VMEM((peers, 128, rows), jnp.bfloat16),
            pltpu.VMEM((2, rows, 2 * rows), jnp.float32),
            pltpu.VMEM((2, peers + 2, rows, rows), jnp.float32),
        ],
        compiler_params=pltpu.CompilerParams(vmem_limit_bytes=18 * 2**20),
        cost_estimate=pl.CostEstimate(flops=8 * 10**9, bytes_accessed=4 * 2**20, transcendentals=3 * 10**6),
        name="attend",
    )(meta, far, line, *parts)
    return res

def attend_back_kernel(peers, items, rows, meta_ref, far_ref, line_ref, wide_ref, log_ref, cot, qkv, *refs):
    all_ref, table_ref, turned, bias, near, far_sum, dkey, dvalue = refs
    for peer in range(peers):
        turned[peer] = _turned(qkv[peer, 1]).astype(jnp.bfloat16)
    _put_bias(bias, line_ref, rows)
    near[...] = jnp.zeros_like(near)
    far_sum[...] = jnp.zeros_like(far_sum)
    dkey[...] = jnp.zeros_like(dkey)
    dvalue[...] = jnp.zeros_like(dvalue)

    def one_row(i, _):
        low = meta_ref[1 + i]
        whole = jnp.minimum(meta_ref[1 + peers + i], i - 1)
        queries = _split(qkv[i, 0].astype(jnp.float32) * 0.125)
        grad = cot[i]
        grads_ = _split(grad)
        product = _turned(grad) * wide_ref[i]
        dots = [jnp.sum(product[64 * head:64 * head + 64], axis=0, keepdims=True) for head in range(2)]
        logs = [log_ref[i, head:head + 1, :] for head in range(2)]

        def step(j, which, masked, dquery):
            key = qkv[j, 1]
            value = qkv[j, 2]
            across = turned[j]
            if masked:
                allowed = _allowed(meta_ref, peers, items, rows, i, j, which, low < i)
            dk = jnp.zeros((rows, 128), jnp.float32)
            dv = jnp.zeros((rows, 128), jnp.float32)
            both = []
            for head in range(2):
                raw = _biased(_dot(key, queries[head], ((1,), (1,))), bias, far_ref, head, which, rows)
                if masked:
                    raw = jnp.where(allowed, raw, masked_score)
                weight = jnp.exp(raw - logs[head])
                dweight = _dot(value, grads_[head], ((1,), (1,)))
                dscore = weight * (dweight - dots[head])
                low_score = dscore.astype(jnp.bfloat16)
                if which == 0:
                    near[head, :, :rows] += dscore
                elif which == 1:
                    near[head, :, rows:] += dscore
                else:
                    far_sum[head] += _fold(dscore, jnp.add)
                both.append(_dot(across[64 * head:64 * head + 64], low_score, ((1,), (0,))))
                dk = dk + _dot(low_score, queries[head], ((1,), (0,)))
                dv = dv + _dot(weight.astype(jnp.bfloat16), grads_[head], ((1,), (0,)))
            dkey[j] += dk
            dvalue[j] += dv
            return dquery + jnp.concatenate(both)

        dquery = step(i, 0, True, jnp.zeros((128, rows), jnp.float32))
        dquery = step(jnp.maximum(i - 1, 0), 1, True, dquery)
        dquery = lax.fori_loop(low, whole, lambda j, d: step(j, 2, True, d), dquery)
        dquery = lax.fori_loop(jnp.maximum(low, whole), i - 1, lambda j, d: step(j, 2, False, d), dquery)
        all_ref[i, 0] = (jnp.transpose(dquery) * 0.125).astype(jnp.bfloat16)
        return 0

    lax.fori_loop(0, peers, one_row, 0)
    for i in range(peers):
        all_ref[i, 1] = dkey[i].astype(jnp.bfloat16)
        all_ref[i, 2] = dvalue[i].astype(jnp.bfloat16)
    wide = 2 * rows
    sub = lax.broadcasted_iota(jnp.int32, (8, wide), 0)
    for head in range(2):
        part = near[head]
        count = rows
        while count > 8:
            count //= 2
            part = part[:count] + pltpu.roll(part[count:], wide - count, 1)
        for bit in (4, 2, 1):
            part = jnp.where((sub & bit) != 0, pltpu.roll(part, wide - bit, 1), part)
        total = far_sum[head]
        table_ref[head, :, :rows] = part[:, :rows]
        table_ref[head, :, rows:] = part[:, rows:] + jnp.concatenate([jnp.zeros((8, rows - 128), jnp.float32), total[:, :128] + total[:, 128:]], axis=1)

def attend_back(meta, far, line, wide, logs, qkv, grads, items):
    peers, _, rows, _ = qkv.shape
    smem = pl.BlockSpec(memory_space=pltpu.SMEM)
    vmem = pl.BlockSpec(memory_space=pltpu.VMEM)
    shapes = [
        jax.ShapeDtypeStruct((peers, 3, rows, 128), jnp.bfloat16),
        jax.ShapeDtypeStruct((2, 8, 2 * rows), jnp.float32),
    ]
    res = pl.pallas_call(
        partial(attend_back_kernel, peers, items, rows),
        out_shape=shapes,
        in_specs=[smem, smem] + [vmem] * 5,
        out_specs=[vmem] * 2,
        scratch_shapes=[
            pltpu.VMEM((peers, 128, rows), jnp.bfloat16),
            pltpu.VMEM((2, rows, 2 * rows), jnp.float32),
            pltpu.VMEM((2, rows, 2 * rows), jnp.float32),
            pltpu.VMEM((2, 8, rows), jnp.float32),
            pltpu.VMEM((peers, rows, 128), jnp.float32),
            pltpu.VMEM((peers, rows, 128), jnp.float32),
        ],
        compiler_params=pltpu.CompilerParams(vmem_limit_bytes=18 * 2**20),
        cost_estimate=pl.CostEstimate(flops=20 * 10**9, bytes_accessed=8 * 2**20, transcendentals=3 * 10**6),
        name="attend_back",
    )(meta, far, line, wide, logs, grads, qkv)
    return res[0], jnp.sum(res[1], axis=1)

def plan(lengths, me, peers, rows):
    ends = jnp.cumsum(lengths)
    items = lengths.shape[0]
    place = jnp.arange(peers, dtype=jnp.int32)
    first = jnp.sum((place[:, None] * rows >= ends[None]).astype(jnp.int32), axis=1)
    last = jnp.sum((place[:, None] * rows + rows - 1 >= ends[None]).astype(jnp.int32), axis=1)
    low = jnp.sum((last[None, :] < first[:, None]).astype(jnp.int32), axis=1)
    low = jnp.where(first < items, jnp.minimum(low, place), place)
    whole = jnp.sum((first[None, :] < last[:, None]).astype(jnp.int32), axis=1)
    return jnp.concatenate([me[None].astype(jnp.int32), low, whole, ends.astype(jnp.int32)])
def bucket_lines(rows, buckets):
    k = jnp.arange(2 * rows, dtype=jnp.int32)
    return (bucket_of(k)[None, :] == jnp.arange(buckets, dtype=jnp.int32)[:, None]).astype(jnp.float32)


def _unit(value):
    mean = jnp.mean(value, axis=-1, keepdims=True)
    centred = value - mean
    variance = jnp.mean(centred * centred, axis=-1, keepdims=True)
    scale = lax.rsqrt(variance + epsilon)
    return centred * scale, scale


def _norm_back(grad, unit, scale, gain, sums_ref):
    inner = grad * gain
    first = jnp.mean(inner, axis=-1, keepdims=True)
    second = jnp.mean(inner * unit, axis=-1, keepdims=True)
    sums_ref[0:1, :] = jnp.sum(grad * unit, axis=0, keepdims=True)
    sums_ref[1:2, :] = jnp.sum(grad, axis=0, keepdims=True)
    return scale * (inner - first - unit * second)


def _lanes(index):
    return pl.ds(pl.multiple_of(index * 128, 128), 128)


def _specs(*kinds):
    places = {"s": pltpu.SMEM, "v": pltpu.VMEM, "h": pltpu.HBM}
    return [pl.BlockSpec(memory_space=places[kind]) for word in kinds for kind in word]


def _params(mebibytes):
    return pltpu.CompilerParams(vmem_limit_bytes=mebibytes * 2**20)


def project_kernel(peers, meta_ref, tokens_ref, gain_ref, shift_ref, weight_ref, *refs):
    outs, act_ref, held, done, arrived = refs[:peers], refs[peers], refs[peers + 1], refs[peers + 2], refs[peers + 3]
    me = meta_ref[0]
    pieces, _, span = held.shape
    copies = []
    for piece in range(pieces):
        copies.append(pltpu.make_async_copy(weight_ref.at[:, pl.ds(piece * span, span)], held.at[piece], arrived.at[piece]))
        copies[-1].start()
    unit, _ = _unit(tokens_ref[...].astype(jnp.float32))
    act = (unit * gain_ref[...] + shift_ref[...]).astype(jnp.bfloat16)
    act_ref[...] = act
    for piece in range(pieces):
        copies[piece].wait()
        got = _dot(act, held[piece], ((1,), (0,))).astype(jnp.bfloat16)
        for block in range(span // 128):
            done[piece * (span // 128) + block] = got[:, 128 * block : 128 * block + 128]
    for slot in range(peers):
        for block in range(3):
            outs[slot][block] = done[block * peers + (me ^ slot)]


def project(meta, tokens, gain, shift, weight, peers):
    rows, width = tokens.shape
    span = 512
    pieces = weight.shape[1] // span
    return pl.pallas_call(
        partial(project_kernel, peers),
        out_shape=[jax.ShapeDtypeStruct((3, rows, 128), jnp.bfloat16)] * peers + [jax.ShapeDtypeStruct((rows, width), jnp.bfloat16)],
        in_specs=_specs("svvvh"),
        out_specs=_specs("v" * (peers + 1)),
        scratch_shapes=[
            pltpu.VMEM((pieces, width, span), jnp.bfloat16),
            pltpu.VMEM((3 * peers, rows, 128), jnp.bfloat16),
            pltpu.SemaphoreType.DMA((pieces,)),
        ],
        compiler_params=_params(60),
        cost_estimate=pl.CostEstimate(flops=4 * 10**9, bytes_accessed=8 * 2**20, transcendentals=0),
        name="project",
    )(meta, tokens, gain, shift, weight)


def merge_kernel(parts_ref, tokens_ref, gain_ref, shift_ref, weight_ref, low_ref, middle_ref, act_ref):
    for part in range(parts_ref.shape[0]):
        low_ref[:, 128 * part : 128 * part + 128] = parts_ref[part]
    middle = tokens_ref[...].astype(jnp.float32) + _dot(low_ref[...], weight_ref[...], ((1,), (0,)))
    middle_ref[...] = middle
    unit, _ = _unit(middle)
    act_ref[...] = (unit * gain_ref[...] + shift_ref[...]).astype(jnp.bfloat16)


def merge(parts, tokens, gain, shift, weight):
    return pl.pallas_call(
        merge_kernel,
        out_shape=[jax.ShapeDtypeStruct(tokens.shape, t) for t in (jnp.bfloat16, jnp.float32, jnp.bfloat16)],
        in_specs=_specs("vvvvv"),
        out_specs=_specs("vvv"),
        compiler_params=_params(16),
        cost_estimate=pl.CostEstimate(flops=10**9, bytes_accessed=5 * 2**20, transcendentals=0),
        name="merge",
    )(parts, tokens, gain, shift, weight)


def _both(ref, mine, other):
    rows = mine.shape[0]
    ref[:rows] = mine[...]
    ref[rows:] = other[...]


def _whole(*shape):
    return pl.BlockSpec(shape, lambda step, meta_ref: (0,) * len(shape))


def _across(rows, columns):
    return pl.BlockSpec((rows, columns), lambda step, meta_ref: (0, step))


def pull_kernel(meta_ref, mine, other, contract_ref, out_ref, grads):
    @pl.when(pl.program_id(0) == 0)
    def _():
        _both(grads, mine, other)

    out_ref[...] = _dot(grads[...], contract_ref[...], ((1,), (1,)))


def pull(meta, mine, other, contract_weight, peers):
    rows, width = mine.shape
    part = contract_weight.shape[0] // (2 * peers)
    return pl.pallas_call(
        pull_kernel,
        out_shape=jax.ShapeDtypeStruct((2 * rows, peers * part), jnp.float32),
        grid_spec=pltpu.PrefetchScalarGridSpec(
            num_scalar_prefetch=1,
            grid=(peers,),
            in_specs=[_whole(rows, width)] * 2 + [pl.BlockSpec((part, width), lambda step, meta_ref: (2 * step + meta_ref[3], 0))],
            out_specs=_across(2 * rows, part),
            scratch_shapes=[pltpu.VMEM((2 * rows, width), jnp.bfloat16)],
        ),
        compiler_params=_params(16),
        cost_estimate=pl.CostEstimate(flops=3 * 10**9, bytes_accessed=9 * 2**20, transcendentals=0),
        name="pull",
    )(meta, mine, other, contract_weight)


def feed_kernel(
    rows, part, meta_ref, act_mine, act_other, pulled_ref, expand_ref, in_keep, in_send, low_ref, back_ref, acts, weights, total, arrived
):
    core = meta_ref[3]
    pieces = weights.shape[1] // part
    copies = []
    for piece in range(pieces):
        columns = pl.ds(pl.multiple_of((2 * piece + core) * part, part), part)
        here = weights.at[:, pl.ds(piece * part, part)]
        copies.append(pltpu.make_async_copy(expand_ref.at[:, columns], here, arrived.at[piece]))
        copies[-1].start()
    _both(acts, act_mine, act_other)

    def before(piece):
        copies[piece].wait()
        return _dot(acts[...], weights[:, piece * part : (piece + 1) * part], ((1,), (0,)))

    now = before(0)
    for piece in range(pieces):
        later = before(piece + 1) if piece + 1 < pieces else None
        span = slice(piece * part, (piece + 1) * part)
        rate = 0.5 * (1.0 + lax.erf(now * math.sqrt(0.5)))
        low_ref[:, span] = (now * rate).astype(jnp.bfloat16)
        slope = rate + now * jnp.exp(-0.5 * now * now) * (1.0 / math.sqrt(2.0 * math.pi))
        back_ref[:, span] = (pulled_ref[:, span] * slope).astype(jnp.bfloat16)
        if piece % 2 == 1:
            pair = slice((piece - 1) * part, (piece + 1) * part)
            got = _dot(back_ref[:, pair], weights[:, pair], ((1,), (1,)))
            if piece == 1:
                total[...] = got
            elif piece + 1 < pieces:
                total[...] += got
            else:
                in_keep[...] = total[:rows] + got[:rows]
                in_send[...] = total[rows:] + got[rows:]
        now = later


def feed(meta, act_mine, act_other, pulled, expand_weight, peers):
    rows, width = act_mine.shape
    part = expand_weight.shape[1] // (2 * peers)
    shapes = [
        ((rows, width), jnp.float32),
        ((rows, width), jnp.float32),
        ((2 * rows, peers * part), jnp.bfloat16),
        ((2 * rows, peers * part), jnp.bfloat16),
    ]
    return pl.pallas_call(
        partial(feed_kernel, rows, part),
        out_shape=[jax.ShapeDtypeStruct(*shape) for shape in shapes],
        in_specs=_specs("svvvh"),
        out_specs=_specs("vvvv"),
        scratch_shapes=[
            pltpu.VMEM((2 * rows, width), jnp.bfloat16),
            pltpu.VMEM((width, peers * part), jnp.bfloat16),
            pltpu.VMEM((2 * rows, width), jnp.float32),
            pltpu.SemaphoreType.DMA((peers,)),
        ],
        compiler_params=_params(40),
        cost_estimate=pl.CostEstimate(flops=8 * 10**9, bytes_accessed=20 * 2**20, transcendentals=2 * 10**6),
        name="feed",
    )(meta, act_mine, act_other, pulled, expand_weight)


def _split_rows(held, x, y, one_keep, one_send, two_keep, two_send):
    peers, rows, _ = held.shape
    cut, half = one_keep.shape[2], rows // 2
    mine = pl.ds(pl.multiple_of(y * half, half), half)
    other = pl.ds(pl.multiple_of((1 - y) * half, half), half)
    for place in range(peers // 2):
        one_keep[place] = held[2 * place + x, :, :cut]
        one_send[place] = held[2 * place + 1 - x, :, :cut]
    for place in range(peers):
        two_keep[place] = held[place, mine, cut:]
        two_send[place] = held[place, other, cut:]


def contract_weigh_kernel(meta_ref, grad_mine, grad_other, low_ref, *refs):
    outs, grads, held = refs[:4], refs[4], refs[5]
    _both(grads, grad_mine, grad_other)
    part = held.shape[1]
    for piece in range(held.shape[0]):
        held[piece] = _dot(low_ref[:, piece * part : (piece + 1) * part], grads[...], ((0,), (0,))).astype(jnp.bfloat16)
    _split_rows(held, meta_ref[1], meta_ref[2], *outs)


def contract_weigh(meta, grad_mine, grad_other, low, peers):
    rows, width = grad_mine.shape
    part, cut = low.shape[1] // peers, width // 2
    shapes = [(peers // 2, part, cut), (peers // 2, part, cut), (peers, part // 2, cut), (peers, part // 2, cut)]
    return pl.pallas_call(
        contract_weigh_kernel,
        out_shape=[jax.ShapeDtypeStruct(shape, jnp.bfloat16) for shape in shapes],
        in_specs=_specs("svvv"),
        out_specs=_specs("vvvv"),
        scratch_shapes=[pltpu.VMEM((2 * rows, width), jnp.bfloat16), pltpu.VMEM((peers, part, width), jnp.bfloat16)],
        compiler_params=_params(14),
        cost_estimate=pl.CostEstimate(flops=10**8, bytes_accessed=2**20, transcendentals=0),
        name="contract_weigh",
    )(meta, grad_mine, grad_other, low)


def weigh_kernel(meta_ref, act_mine, act_other, mix_mine, mix_other, right_mine, right_other, back_ref, *refs):
    outs, left, held = refs[:4], refs[4], refs[5]
    peers, group, span = held.shape
    wide = back_ref.shape[1] // 2
    cut = span // 2
    _both(left, mix_mine, mix_other)
    right = jnp.concatenate([right_mine[...], right_other[...]])
    grad = _dot(left[...], right, ((0,), (0,))).astype(jnp.bfloat16)
    quarter = grad.shape[1] // 2
    held[:, :, wide:cut] = grad[:, :quarter].reshape(peers, group, quarter)
    held[:, :, cut + wide :] = grad[:, quarter:].reshape(peers, group, quarter)
    _both(left, act_mine, act_other)
    for side in range(2):
        grad = _dot(left[...], back_ref[:, side * wide : (side + 1) * wide], ((0,), (0,))).astype(jnp.bfloat16)
        held[:, :, side * cut : side * cut + wide] = grad.reshape(peers, group, wide)
    _split_rows(held, meta_ref[1], meta_ref[2], *outs)


def weigh(meta, act_mine, act_other, mix_mine, mix_other, right_mine, right_other, back, peers):
    rows, width = act_mine.shape
    group, cut = width // peers, back.shape[1] // 2 + width // 4
    shapes = [(peers // 2, group, cut), (peers // 2, group, cut), (peers, group // 2, cut), (peers, group // 2, cut)]
    return pl.pallas_call(
        weigh_kernel,
        out_shape=[jax.ShapeDtypeStruct(shape, jnp.bfloat16) for shape in shapes],
        in_specs=_specs("svvvvvvv"),
        out_specs=_specs("vvvv"),
        scratch_shapes=[pltpu.VMEM((2 * rows, width), jnp.bfloat16), pltpu.VMEM((peers, group, 2 * cut), jnp.bfloat16)],
        compiler_params=_params(20),
        cost_estimate=pl.CostEstimate(flops=10**8, bytes_accessed=2**20, transcendentals=0),
        name="weigh",
    )(meta, act_mine, act_other, mix_mine, mix_other, right_mine, right_other, back)


def emit_kernel(meta_ref, low_ref, contract_ref, keep_ref, send_ref, weights, arrived):
    core = meta_ref[3]
    rows, pieces = keep_ref.shape[0], arrived.shape[0]
    part = weights.shape[0] // pieces
    copies = []
    for piece in range(pieces):
        at = pl.ds(pl.multiple_of((2 * piece + core) * part, part), part)
        copies.append(pltpu.make_async_copy(contract_ref.at[at], weights.at[pl.ds(piece * part, part)], arrived.at[piece]))
        copies[-1].start()
    for copy in copies:
        copy.wait()
    keep_ref[...] = _dot(low_ref[:rows], weights[...], ((1,), (0,)))
    send_ref[...] = _dot(low_ref[rows:], weights[...], ((1,), (0,))).astype(jnp.bfloat16)


def emit(meta, low, contract_weight, peers):
    rows, width = low.shape[0] // 2, contract_weight.shape[1]
    return pl.pallas_call(
        emit_kernel,
        out_shape=[jax.ShapeDtypeStruct((rows, width), jnp.float32), jax.ShapeDtypeStruct((rows, width), jnp.bfloat16)],
        in_specs=_specs("svh"),
        out_specs=_specs("vv"),
        scratch_shapes=[pltpu.VMEM((low.shape[1], width), jnp.bfloat16), pltpu.SemaphoreType.DMA((peers,))],
        compiler_params=_params(30),
        cost_estimate=pl.CostEstimate(flops=2 * 10**9, bytes_accessed=8 * 2**20, transcendentals=0),
        name="emit",
    )(meta, low, contract_weight)


def turn_kernel(meta_ref, in_mine, in_other, middle_ref, grad_ref, gain_ref, weight_ref, heads_ref, total_ref, keep_ref, send_ref, sums_ref):
    core = meta_ref[3]
    half = keep_ref.shape[1]
    unit, scale = _unit(middle_ref[...])
    total = grad_ref[...].astype(jnp.float32) + _norm_back(in_mine[...] + in_other[...], unit, scale, gain_ref[...], sums_ref)
    total_ref[...] = total
    low = total.astype(jnp.bfloat16)

    @pl.when(core == 0)
    def _():
        keep_ref[...] = low[:, :half]
        send_ref[...] = low[:, half:]

    @pl.when(core != 0)
    def _():
        keep_ref[...] = low[:, half:]
        send_ref[...] = low[:, :half]

    heads = _dot(low, weight_ref[...], ((1,), (1,))).astype(jnp.bfloat16)
    for part in range(heads_ref.shape[0]):
        heads_ref[part] = heads[:, 128 * part : 128 * part + 128]


def turn(meta, in_mine, in_other, middle, grad, gain, weight, peers):
    rows, width = middle.shape
    shapes = [
        ((peers, rows, width // peers), jnp.bfloat16),
        ((rows, width), jnp.float32),
        ((rows, width // 2), jnp.bfloat16),
        ((rows, width // 2), jnp.bfloat16),
        ((2, width), jnp.float32),
    ]
    return pl.pallas_call(
        turn_kernel,
        out_shape=[jax.ShapeDtypeStruct(*shape) for shape in shapes],
        in_specs=_specs("svvvvvv"),
        out_specs=_specs("v" * len(shapes)),
        compiler_params=_params(14),
        cost_estimate=pl.CostEstimate(flops=10**9, bytes_accessed=8 * 2**20, transcendentals=0),
        name="turn",
    )(meta, in_mine, in_other, middle, grad, gain, weight)


def close_kernel(parts_ref, tokens_ref, grad_ref, gain_ref, weight_ref, out_ref, sums_ref, held):
    peers = parts_ref.shape[0]
    for peer in range(peers):
        for block in range(3):
            at = 128 * (block * peers + peer)
            held[:, at : at + 128] = parts_ref[peer, block]
    back = _dot(held[...], weight_ref[...], ((1,), (1,)))
    unit, scale = _unit(tokens_ref[...].astype(jnp.float32))
    out_ref[...] = grad_ref[...] + _norm_back(back, unit, scale, gain_ref[...], sums_ref)


def close(parts, tokens, grad, gain, weight):
    rows, width = tokens.shape
    return pl.pallas_call(
        close_kernel,
        out_shape=[jax.ShapeDtypeStruct((rows, width), jnp.float32), jax.ShapeDtypeStruct((2, width), jnp.float32)],
        in_specs=_specs("vvvvv"),
        out_specs=_specs("vv"),
        scratch_shapes=[pltpu.VMEM((rows, 3 * width), jnp.bfloat16)],
        compiler_params=_params(20),
        cost_estimate=pl.CostEstimate(flops=2 * 10**9, bytes_accessed=10 * 2**20, transcendentals=0),
        name="close",
    )(parts, tokens, grad, gain, weight)


def _plus(a, b):
    return (a.astype(jnp.float32) + b.astype(jnp.float32)).astype(jnp.bfloat16)


def second_kernel(meta_ref, one_keep, one_got, two_keep, two_got, one_left, one_send, two_left, two_send):
    x, y = meta_ref[1], meta_ref[2]
    levels, half, _ = one_left.shape
    mine = pl.ds(pl.multiple_of(y * half, half), half)
    other = pl.ds(pl.multiple_of((1 - y) * half, half), half)
    for level in range(levels):
        one_left[level] = _plus(one_keep[level, mine], one_got[level, mine])
        one_send[level] = _plus(one_keep[level, other], one_got[level, other])
        two_left[level] = _plus(two_keep[2 * level + x], two_got[2 * level + x])
        two_send[level] = _plus(two_keep[2 * level + 1 - x], two_got[2 * level + 1 - x])


def near_kernel(meta_ref, one_keep, one_got, two_keep, two_got, left, send):
    side = (meta_ref[0] >> 1) & 1
    cut = one_keep.shape[2]
    for level in range(left.shape[0]):
        for out, at in ((left, 2 * level + side), (send, 2 * level + 1 - side)):
            out[level, :, :cut] = _plus(one_keep[at], one_got[at])
            out[level, :, cut:] = _plus(two_keep[at], two_got[at])


def far_kernel(meta_ref, keep, got, left, send):
    upper = meta_ref[0] >> 2
    left[...] = _plus(keep[upper], got[upper])
    send[...] = _plus(keep[1 - upper], got[1 - upper])


def last_kernel(keep, got, out):
    out[...] = _plus(keep[...], got[...])


def _small_call(kernel, name, shapes, kind, *arguments):
    size = sum(2 * math.prod(a.shape) for a in arguments[-4:])
    return pl.pallas_call(
        kernel,
        out_shape=[jax.ShapeDtypeStruct(shape, kind) for shape in shapes],
        in_specs=_specs(*("s" if a.dtype == jnp.int32 else "v" for a in arguments)),
        out_specs=_specs("v" * len(shapes)),
        compiler_params=_params(24),
        cost_estimate=pl.CostEstimate(flops=size, bytes_accessed=3 * size, transcendentals=0),
        name=name,
    )(*arguments)


def _places(meta_ref, half):
    y, core = meta_ref[2], meta_ref[3]
    return [(c, pl.ds(pl.multiple_of(h * half, half), half)) for c in (core, 1 - core) for h in (y, 1 - y)]


def finish_contract_kernel(meta_ref, *refs):
    half = refs[0].shape[0]
    y, core = meta_ref[2], meta_ref[3]
    starts = [(2 * c + h) * half for c in (core, 1 - core) for h in (y, 1 - y)]
    for part, start in zip(refs[:4], starts):
        refs[4][pl.ds(pl.multiple_of(start, half), half), :] = part[...].astype(jnp.float32)


def finish_expand_kernel(part, meta_ref, *refs):
    expand_ref, merge_ref = refs[4:]
    half, span = refs[0].shape[0], refs[0].shape[1] // 2
    near = span // part - 1
    for source, (core, rows) in zip(refs[:4], _places(meta_ref, half)):
        for side in range(2):
            for block in range(near):
                at = pl.multiple_of((2 * (side * near + block) + core) * part, part)
                start = side * span + block * part
                expand_ref[rows, pl.ds(at, part)] = source[:, start : start + part].astype(jnp.float32)
            at = pl.multiple_of((2 * core + side) * part, part)
            start = side * span + near * part
            merge_ref[rows, pl.ds(at, part)] = source[:, start : start + part].astype(jnp.float32)


def finish_attend_kernel(meta_ref, *refs):
    half, wide = refs[0].shape
    span = wide // 3
    for source, (core, rows) in zip(refs[:4], _places(meta_ref, half)):
        for block in range(3):
            at = pl.multiple_of((2 * block + core) * span, span)
            refs[4][rows, pl.ds(at, span)] = source[:, block * span : (block + 1) * span].astype(jnp.float32)


def attend_weigh_kernel(
    meta_ref, act_mine, act_other, owned_ref, other_ref, one_keep, one_send, two_keep, two_send, acts, right, held
):
    x, y, core = meta_ref[1], meta_ref[2], meta_ref[3]
    count, blocks, rows, _ = other_ref.shape
    peers, group, cut = held.shape
    half = group // 2
    _both(acts, act_mine, act_other)
    for block in range(blocks):
        for place in range(count):
            at = 128 * (block * count + place)
            right[:rows, at : at + 128] = owned_ref[core * count + place, block]
            right[rows:, at : at + 128] = other_ref[place, block]
    for side in range(2):
        grad = _dot(acts[...], right[:, side * cut : (side + 1) * cut], ((0,), (0,))).astype(jnp.bfloat16)
        held[...] = grad.reshape(peers, group, cut)
        if side == 0:
            for place in range(peers // 2):
                one_keep[place] = held[2 * place + x]
                one_send[place] = held[2 * place + 1 - x]
        else:
            for place in range(peers):
                two_keep[place] = held[place, pl.ds(pl.multiple_of(y * half, half), half), :]
                two_send[place] = held[place, pl.ds(pl.multiple_of((1 - y) * half, half), half), :]


def attend_weigh(meta, act_mine, act_other, owned, other):
    peers, blocks, rows, _ = owned.shape
    width = act_mine.shape[1]
    group, span = width // peers, blocks * width // 2
    cut = span // 2
    shapes = [(peers // 2, group, cut), (peers // 2, group, cut), (peers, group // 2, cut), (peers, group // 2, cut)]
    return pl.pallas_call(
        attend_weigh_kernel,
        out_shape=[jax.ShapeDtypeStruct(shape, jnp.bfloat16) for shape in shapes],
        in_specs=_specs("svvvv"),
        out_specs=_specs("vvvv"),
        scratch_shapes=[
            pltpu.VMEM((2 * rows, width), jnp.bfloat16),
            pltpu.VMEM((2 * rows, span), jnp.bfloat16),
            pltpu.VMEM((peers, group, cut), jnp.bfloat16),
        ],
        compiler_params=_params(20),
        cost_estimate=pl.CostEstimate(flops=2 * 10**9, bytes_accessed=7 * 2**20, transcendentals=0),
        name="attend_weigh",
    )(meta, act_mine, act_other, owned, other)


def flipped(array, axis, mask):
    peers = lax.axis_size(axis)
    return lax.ppermute(array, axis, [(i, i ^ mask) for i in range(peers)])


def pick(array, index, axis):
    return lax.dynamic_index_in_dim(array, index, axis, keepdims=False)


def added(a, b):
    return (a.astype(jnp.float32) + b.astype(jnp.float32)).astype(jnp.bfloat16)


def in_order(mine, other, bit, axis):
    lower = jnp.where(bit == 0, mine, other)
    upper = jnp.where(bit == 0, other, mine)
    return jnp.concatenate([lower, upper], axis=axis)


def after(value, *others):
    return lax.optimization_barrier((value, others))[0]


def over_first(one_keep, one_send, two_keep, two_send):
    return one_keep, flipped(one_send, "blk", 1), two_keep, flipped(two_send, "seq", 2)


def over_second(here, one_keep, one_got, two_keep, two_got):
    levels, rows, cut = one_keep.shape
    shape = (levels, rows // 2, cut)
    return _small_call(second_kernel, "second", [shape] * 4, jnp.bfloat16, here, one_keep, one_got, two_keep, two_got)


def send_second(one_left, one_send, two_left, two_send):
    return one_left, flipped(one_send, "seq", 2), two_left, flipped(two_send, "blk", 1)


def over_near(here, one_keep, one_got, two_keep, two_got):
    levels, half, cut = one_keep.shape
    left, send = _small_call(
        near_kernel, "near", [(levels // 2, half, 2 * cut)] * 2, jnp.bfloat16, here, one_keep, one_got, two_keep, two_got
    )
    return left, flipped(send, "blk", 2)


def over_far(here, keep, got):
    left, send = _small_call(far_kernel, "far", [keep.shape[1:]] * 2, jnp.bfloat16, here, keep, got)
    return left, flipped(send, "blk", 4)


def over_all(keep, got):
    return _small_call(last_kernel, "last", [keep.shape], jnp.bfloat16, keep, got)[0]


def of_all(own):
    across = flipped(own, "seq", 2)
    return own, across, flipped(own, "seq", 1), flipped(across, "seq", 1)


def local_by_heads(
    tokens,
    lengths,
    attend_weight,
    merge_weight,
    expand_weight,
    contract_weight,
    gain_first,
    shift_first,
    gain_second,
    shift_second,
    bias_table,
    cotangent,
):
    rows, width = tokens.shape[1], tokens.shape[2]
    buckets, heads = bias_table.shape
    hidden = expand_weight.shape[1]
    items = lengths.shape[1]
    peers = lax.axis_size("blk")
    levels = peers // 2
    group = width // peers
    part = hidden // (2 * peers)
    me, line_of = lax.axis_index("blk"), lax.axis_index("seq")
    z, x, y, core = me // 2, me % 2, line_of // 2, line_of % 2
    place = (z, x, y)
    here = jnp.stack([me, x, y, core]).astype(jnp.int32)
    gain_first, shift_first, gain_second, shift_second = (
        v.reshape(1, width) for v in (gain_first, shift_first, gain_second, shift_second)
    )

    own, grad_out = tokens[0], cotangent[0]
    grad_other = flipped(grad_out, "seq", 1)
    meta = plan(lengths[0], me, peers, rows)
    hot = bucket_lines(rows, buckets)
    table_mine = lax.dynamic_slice_in_dim(bias_table, 2 * me, 2, 1)
    lines = jnp.dot(table_mine.T, hot, precision=highest)
    far = table_mine[buckets - 1]

    def to_all(array):
        return lax.all_to_all(array, "blk", split_axis=0, concat_axis=0, tiled=True)

    *parts, act_first = project(here, own, gain_first, shift_first, attend_weight, peers)
    parts = [parts[0]] + [flipped(parts[step], "blk", step) for step in range(1, peers)]
    pulled = pull(here, grad_out, grad_other, contract_weight, peers)
    mixed, wide, logs, qkv = attend(meta, after(far, pulled), lines, parts, items)
    first_other = flipped(act_first, "seq", 1)
    attn_low, middle, act_second = merge(to_all(mixed), own, gain_second, shift_second, merge_weight)
    act_other = flipped(act_second, "seq", 1)
    attn_other = flipped(attn_low, "seq", 1)
    in_keep, in_send, hidden_low, hidden_back = feed(here, act_second, act_other, pulled, expand_weight, peers)
    in_send = flipped(in_send, "seq", 1)
    contract_keep, *contract_parts = contract_weigh(here, grad_out, grad_other, hidden_low, peers)
    in_send, contract_keep, *contract_parts = lax.optimization_barrier((in_send, contract_keep, *contract_parts))
    contract_parts = over_first(contract_keep, *contract_parts)
    grad_heads, grad_middle, keep_low, send_low, sums_second = turn(
        here, in_keep, in_send, middle, grad_out, gain_second, merge_weight, peers
    )
    expand_parts = weigh(here, act_second, act_other, attn_low, attn_other, keep_low, flipped(send_low, "seq", 1), hidden_back, peers)
    expand_keep = expand_parts[0]
    _, *expand_parts = over_first(*expand_parts)

    grad_heads, expand_keep, *contract_parts = lax.optimization_barrier((to_all(grad_heads), expand_keep, *contract_parts))
    back_all, line_grad = attend_back(meta, far, lines, wide, logs, qkv, grad_heads, items)
    back_all, *sums = lax.optimization_barrier((back_all, *contract_parts, expand_keep, *expand_parts))
    owned = to_all(back_all)
    out_keep, out_send = emit(here, after(hidden_low, back_all), contract_weight, peers)
    contract_parts = over_near(here, *send_second(*over_second(here, *sums[:4])))
    expand_parts = send_second(*over_second(here, *sums[4:]))
    owned, out_keep, *sums = lax.optimization_barrier((owned, out_keep, *contract_parts, *expand_parts))
    contract_parts = over_far(here, *sums[:2])
    expand_parts = over_near(here, *sums[2:])
    owned_send = pick(owned.reshape(2, levels, 3, rows, group), 1 - core, 0)
    attend_parts = over_first(*attend_weigh(here, act_first, first_other, owned, flipped(owned_send, "seq", 1)))
    output = (middle + out_keep + flipped(out_send, "seq", 1).astype(jnp.float32)).astype(jnp.bfloat16)
    tokens_grad, sums_first = close(owned, own, grad_middle, gain_first, attend_weight)
    table_mine = jnp.dot(hot, line_grad.T, precision=highest).reshape(1, 2 * buckets)
    table_row = jnp.broadcast_to(jnp.pad(table_mine, ((0, 0), (0, group - 2 * buckets)))[:, None], (1, peers, group))
    small = jnp.concatenate([sums_first.reshape(2, peers, group), sums_second.reshape(2, peers, group), table_row]).transpose(1, 0, 2)
    small = jnp.pad(small, ((0, 0), (0, 3), (0, 0)))

    sums = lax.optimization_barrier((*attend_parts, *contract_parts, *expand_parts))
    attend_parts = send_second(*over_second(here, *sums[:4]))
    contract_own = over_all(*sums[4:6])
    contract_across = flipped(contract_own, "seq", 2)
    expand_parts = over_far(here, *sums[6:])
    small, *sums = lax.optimization_barrier((small, *attend_parts, contract_across, *expand_parts))
    attend_parts = over_near(here, *sums[:4])
    contract_grad = (contract_own, sums[4], flipped(contract_own, "seq", 1), flipped(sums[4], "seq", 1))
    small = small + flipped(small, "seq", 1)
    expand_own = over_all(*sums[5:])
    expand_across = flipped(expand_own, "seq", 2)
    small, expand_across, *attend_parts = lax.optimization_barrier((small, expand_across, *attend_parts))
    attend_parts = over_far(here, *attend_parts)
    small = small + flipped(small, "seq", 2)
    expand_grad = (expand_own, expand_across, flipped(expand_own, "seq", 1), flipped(expand_across, "seq", 1))
    small = to_all(small)
    contract_grad = _small_call(finish_contract_kernel, "finish_contract", [(2 * part, width)], jnp.float32, here, *contract_grad)[0]
    expand_grad, merge_grad = _small_call(
        partial(finish_expand_kernel, part), "finish_expand", [(group, hidden), (group, width)], jnp.float32, here, *expand_grad
    )
    attend_grad = of_all(over_all(*attend_parts))
    attend_grad = _small_call(finish_attend_kernel, "finish_attend", [(group, 3 * width)], jnp.float32, here, *attend_grad)[0]
    table_grad = small[:, 4, : 2 * buckets].reshape(peers, buckets, 2).transpose(1, 0, 2).reshape(buckets, heads)
    vectors = jnp.sum(small[:, :4], axis=0)
    return (
        output[None],
        tokens_grad[None],
        attend_grad,
        merge_grad,
        expand_grad,
        contract_grad,
        vectors[0],
        vectors[1],
        vectors[2],
        vectors[3],
        table_grad,
    )


def local(*arguments):
    heads = arguments[10].shape[1]
    rows = arguments[0].shape[1]
    peers = lax.axis_size("blk")
    if peers == 8 and lax.axis_size("seq") == 4 and heads == 2 * peers and rows == 256:
        return local_by_heads(*arguments)
    return local_by_runs(*arguments)


def solution(mesh):
    in_specs = (
        P("seq", "blk", None),
        P("seq", None),
        P(),
        P(),
        P(),
        P(),
        P(),
        P(),
        P(),
        P(),
        P(),
        P("seq", "blk", None),
    )
    out_specs = (
        P("seq", "blk", None),
        P("seq", "blk", None),
        P("blk", None),
        P("blk", None),
        P("blk", None),
        P("blk", None),
        P("blk"),
        P("blk"),
        P("blk"),
        P("blk"),
        P(),
    )
    return jax.shard_map(local, mesh=mesh, in_specs=in_specs, out_specs=out_specs, check_vma=False)
```

```python
from functools import partial
import math

import jax
import jax.numpy as jnp
from jax import lax
from jax.experimental import pallas as pl
from jax.experimental.pallas import tpu as pltpu
from jax.sharding import PartitionSpec as P

HOPS = 6


epsilon = 1e-05
masked_score = -1e30
highest = lax.Precision.HIGHEST
bucket_edges = [math.ceil(16 * 8 ** (t / 16)) for t in range(1, 16)]


def shifted(array, axis, by):
    peers = lax.axis_size(axis)
    pairs = [(i, i + by) for i in range(peers) if 0 <= i + by < peers]
    return lax.ppermute(array, axis, pairs)


def shortened(array):

    def short(part):
        return part.astype(jnp.bfloat16) if part.dtype == jnp.float32 else part

    return jax.tree.map(short, array)


def bucket_of(distance):
    total = jnp.minimum(jnp.maximum(distance, 0), 16)
    for edge in bucket_edges:
        total = total + (distance >= edge).astype(jnp.int32)
    return total


def segment_of(position, ends):
    return jnp.sum((position[:, None] >= ends[None, :]).astype(jnp.int32), axis=1)


def layer_norm(value, gain, shift):
    mean = jnp.mean(value, axis=-1, keepdims=True)
    centred = value - mean
    variance = jnp.mean(centred * centred, axis=-1, keepdims=True)
    return centred * lax.rsqrt(variance + epsilon) * gain + shift


def diagonal_sums(grid, count):
    heads = grid.shape[0]
    padded = jnp.pad(jnp.flip(grid, axis=-1), ((0, 0), (0, 0), (0, count)))
    flat = padded.reshape(heads, 2 * count * count)[:, : count * (2 * count - 1)]
    return jnp.sum(flat.reshape(heads, count, 2 * count - 1), axis=1)


def band_matrix(line, count):
    heads = line.shape[0]
    flipped = jnp.flip(line, axis=-1)
    tiled = jnp.tile(flipped, (1, count))
    window = tiled[:, count - 1 : count - 1 + count * (2 * count - 2)]
    return window.reshape(heads, count, 2 * count - 2)[:, :, :count]


def fetch_earlier(block):
    earlier = []
    moving = block
    for hop in range(HOPS):
        moving = shifted(moving, "blk", 1)
        earlier.append(moving)
    return earlier


def return_parts(parts):
    carried = jnp.zeros_like(parts[0])
    for hop in range(HOPS, 0, -1):
        carried = shifted(shortened(carried + parts[hop - 1]), "blk", -1)
    return carried


def local_by_runs(
    tokens,
    lengths,
    attend_weight,
    merge_weight,
    expand_weight,
    contract_weight,
    gain_first,
    shift_first,
    gain_second,
    shift_second,
    bias_table,
    cotangent,
):
    rows = tokens.shape[1]
    width = tokens.shape[2]
    heads = bias_table.shape[1]
    buckets = bias_table.shape[0]
    head_size = width // heads
    items = lengths.shape[1]
    start = lax.axis_index("blk") * rows
    query_pos = start + jnp.arange(rows, dtype=jnp.int32)
    ends = jnp.cumsum(lengths[0])
    query_seg = segment_of(query_pos, ends)
    band = jnp.arange(2 * rows - 1, dtype=jnp.int32) - (rows - 1)
    bucket_ids = jnp.arange(buckets, dtype=jnp.int32)

    def pair_setup(hop):
        key_pos = query_pos - hop * rows
        key_seg = segment_of(key_pos, ends)
        key_valid = (key_pos >= 0) & (key_seg < items)
        same = key_pos[None, :] == query_pos[:, None]
        allowed = (
            (query_seg[:, None] == key_seg[None, :])
            & (key_pos[None, :] <= query_pos[:, None])
            & (key_valid[None, :] | same)
        )
        onehot = (bucket_of(hop * rows + band)[:, None] == bucket_ids[None, :]).astype(jnp.float32)
        band_bias = jnp.dot(onehot, bias_table, precision=highest).T
        bias = band_matrix(band_bias, rows)
        additive = jnp.where(allowed[None], bias, masked_score)
        return (jnp.any(allowed), onehot, additive)

    pairs = [pair_setup(hop) for hop in range(HOPS + 1)]
    residual = tokens[0].astype(jnp.float32)
    normed_first, norm_first_pull = jax.vjp(layer_norm, residual, gain_first, shift_first)
    act_first = normed_first.astype(jnp.bfloat16)
    projected = jnp.dot(act_first, attend_weight, preferred_element_type=jnp.float32).astype(
        jnp.bfloat16
    )
    query = projected[:, :width].reshape(rows, heads, head_size)
    keys_values = jnp.stack([projected[:, width : 2 * width], projected[:, 2 * width :]])
    blocks = [keys_values] + fetch_earlier(keys_values)

    def scores_of(block, pair):
        key = block[0].reshape(rows, heads, head_size)
        raw = jnp.einsum("qhe,khe->hqk", query, key, preferred_element_type=jnp.float32) * 0.125
        return raw + pair[2]

    def empty_total():
        return jnp.full((heads, rows), masked_score, jnp.float32)

    def empty_scores():
        return jnp.full((heads, rows, rows), masked_score, jnp.float32)

    log_total = empty_total()
    kept_scores = []
    for block, pair in zip(blocks, pairs):

        def part_total(block=block, pair=pair):
            scores = scores_of(block, pair)
            peak = jnp.max(scores, axis=-1)
            return (peak + jnp.log(jnp.sum(jnp.exp(scores - peak[..., None]), axis=-1)), scores)

        def skip_total():
            return (empty_total(), empty_scores())

        part_log, scores = lax.cond(pair[0], part_total, skip_total)
        log_total = jnp.logaddexp(log_total, part_log)
        kept_scores.append(scores)

    def empty_heads():
        return jnp.zeros((rows, heads, head_size), jnp.float32)

    attended = empty_heads()
    for block, pair, scores in zip(blocks, pairs, kept_scores):

        def part_mix(block=block, scores=scores):
            weights = jnp.exp(scores - log_total[..., None]).astype(jnp.bfloat16)
            value = block[1].reshape(rows, heads, head_size)
            return jnp.einsum("hqk,khe->qhe", weights, value, preferred_element_type=jnp.float32)

        attended = attended + lax.cond(pair[0], part_mix, empty_heads)
    attn_low = attended.reshape(rows, width).astype(jnp.bfloat16)
    middle = residual + jnp.dot(attn_low, merge_weight, preferred_element_type=jnp.float32)
    normed_second, norm_second_pull = jax.vjp(layer_norm, middle, gain_second, shift_second)
    act_second = normed_second.astype(jnp.bfloat16)
    hidden_pre = jnp.dot(act_second, expand_weight, preferred_element_type=jnp.float32)
    hidden, gelu_pull = jax.vjp(partial(jax.nn.gelu, approximate=False), hidden_pre)
    hidden_low = hidden.astype(jnp.bfloat16)
    output = (
        middle + jnp.dot(hidden_low, contract_weight, preferred_element_type=jnp.float32)
    ).astype(jnp.bfloat16)
    grad_out = cotangent[0]
    contract_grad = jnp.einsum(
        "tf,td->fd", hidden_low, grad_out, preferred_element_type=jnp.float32
    )
    grad_hidden = jnp.einsum(
        "td,fd->tf", grad_out, contract_weight, preferred_element_type=jnp.float32
    )
    grad_pre = gelu_pull(grad_hidden)[0].astype(jnp.bfloat16)
    expand_grad = jnp.einsum("td,tf->df", act_second, grad_pre, preferred_element_type=jnp.float32)
    grad_second = jnp.einsum(
        "tf,df->td", grad_pre, expand_weight, preferred_element_type=jnp.float32
    )
    grad_middle_norm, gain_second_grad, shift_second_grad = norm_second_pull(grad_second)
    grad_middle = grad_out.astype(jnp.float32) + grad_middle_norm
    grad_middle_low = grad_middle.astype(jnp.bfloat16)
    merge_grad = jnp.einsum(
        "td,te->de", attn_low, grad_middle_low, preferred_element_type=jnp.float32
    )
    grad_heads = (
        jnp.einsum("te,de->td", grad_middle_low, merge_weight, preferred_element_type=jnp.float32)
        .astype(jnp.bfloat16)
        .reshape(rows, heads, head_size)
    )
    row_dot = jnp.sum(grad_heads.astype(jnp.float32) * attended, axis=-1).T
    back_blocks = [keys_values] + fetch_earlier(keys_values)

    def empty_grads():
        return (
            empty_heads(),
            jnp.zeros((2, rows, width), jnp.float32),
            jnp.zeros((buckets, heads), jnp.float32),
        )

    grad_query = empty_heads()
    table_local = jnp.zeros((buckets, heads), jnp.float32)
    parts = []
    for block, pair in zip(back_blocks, pairs):

        def part_grads(block=block, pair=pair):
            key = block[0].reshape(rows, heads, head_size)
            value = block[1].reshape(rows, heads, head_size)
            weights = jnp.exp(scores_of(block, pair) - log_total[..., None])
            weights_low = weights.astype(jnp.bfloat16)
            grad_weights = jnp.einsum(
                "qhe,khe->hqk", grad_heads, value, preferred_element_type=jnp.float32
            )
            grad_scores = (weights * (grad_weights - row_dot[..., None])).astype(jnp.bfloat16)
            query_part = (
                jnp.einsum("hqk,khe->qhe", grad_scores, key, preferred_element_type=jnp.float32)
                * 0.125
            )
            key_part = (
                jnp.einsum("hqk,qhe->khe", grad_scores, query, preferred_element_type=jnp.float32)
                * 0.125
            )
            value_part = jnp.einsum(
                "hqk,qhe->khe", weights_low, grad_heads, preferred_element_type=jnp.float32
            )
            line_grad = diagonal_sums(grad_scores.astype(jnp.float32), rows)
            table_part = jnp.dot(pair[1].T, line_grad.T, precision=highest)
            return (
                query_part,
                jnp.stack([key_part.reshape(rows, width), value_part.reshape(rows, width)]),
                table_part,
            )

        query_part, pair_part, table_part = lax.cond(pair[0], part_grads, empty_grads)
        grad_query = grad_query + query_part
        table_local = table_local + table_part
        parts.append(pair_part)
    owned = (parts[0] + return_parts(parts[1:])).astype(jnp.bfloat16)
    grad_project = jnp.concatenate(
        [grad_query.reshape(rows, width).astype(jnp.bfloat16), owned[0], owned[1]], axis=1
    )
    attend_grad = jnp.einsum(
        "td,te->de", act_first, grad_project, preferred_element_type=jnp.float32
    )
    grad_first = jnp.einsum(
        "te,de->td", grad_project, attend_weight, preferred_element_type=jnp.float32
    )
    grad_input_norm, gain_first_grad, shift_first_grad = norm_first_pull(grad_first)
    tokens_grad = grad_middle + grad_input_norm
    results = (
        lax.psum_scatter(attend_grad, "blk", scatter_dimension=0, tiled=True),
        lax.psum_scatter(merge_grad, "blk", scatter_dimension=0, tiled=True),
        lax.psum_scatter(expand_grad, "blk", scatter_dimension=0, tiled=True),
        lax.psum_scatter(contract_grad, "blk", scatter_dimension=0, tiled=True),
        lax.psum_scatter(gain_first_grad, "blk", scatter_dimension=0, tiled=True),
        lax.psum_scatter(shift_first_grad, "blk", scatter_dimension=0, tiled=True),
        lax.psum_scatter(gain_second_grad, "blk", scatter_dimension=0, tiled=True),
        lax.psum_scatter(shift_second_grad, "blk", scatter_dimension=0, tiled=True),
    )
    results = (
        lax.psum(results[0].astype(jnp.bfloat16), "seq").astype(jnp.float32),
        lax.psum(results[1].astype(jnp.bfloat16), "seq").astype(jnp.float32),
        lax.psum(results[2].astype(jnp.bfloat16), "seq").astype(jnp.float32),
        lax.psum(results[3].astype(jnp.bfloat16), "seq").astype(jnp.float32),
        lax.psum(results[4].astype(jnp.bfloat16), "seq").astype(jnp.float32),
        lax.psum(results[5].astype(jnp.bfloat16), "seq").astype(jnp.float32),
        lax.psum(results[6].astype(jnp.bfloat16), "seq").astype(jnp.float32),
        lax.psum(results[7].astype(jnp.bfloat16), "seq").astype(jnp.float32),
    )
    table_grad = lax.psum(table_local, ("seq", "blk"))
    return (
        output[None],
        tokens_grad[None],
        results[0],
        results[1],
        results[2],
        results[3],
        results[4],
        results[5],
        results[6],
        results[7],
        table_grad,
    )


def _segments(position, meta_ref, first, items):
    total = jnp.zeros(position.shape, jnp.int32)
    for item in range(items):
        total = total + (position >= meta_ref[first + item]).astype(jnp.int32)
    return total

def _allowed(meta_ref, peers, items, rows, i, j, which, needed):
    first = 1 + 2 * peers
    q_seg = _segments(i * rows + lax.broadcasted_iota(jnp.int32, (1, rows), 1), meta_ref, first, items)
    k_seg = _segments(j * rows + lax.broadcasted_iota(jnp.int32, (rows, 1), 0), meta_ref, first, items)
    k_seg = jnp.where((k_seg < items) & needed if which == 1 else k_seg < items, k_seg, -1)
    same = q_seg == k_seg
    if which == 0:
        key = lax.broadcasted_iota(jnp.int32, (rows, rows), 0)
        query = lax.broadcasted_iota(jnp.int32, (rows, rows), 1)
        return (same & (key < query)) | (key == query)
    return same

def _dot(a, b, dims):
    return lax.dot_general(a, b, (dims, ((), ())), preferred_element_type=jnp.float32)

def _turned(array):
    return jnp.transpose(array.astype(jnp.float32))

def _split(array, axis=1):
    wide = array.astype(jnp.float32)
    left = lax.broadcasted_iota(jnp.int32, array.shape, axis) < 64
    return jnp.where(left, wide, 0.0).astype(jnp.bfloat16), jnp.where(left, 0.0, wide).astype(jnp.bfloat16)

def _fold(value, op):
    while value.shape[0] > 8:
        half = value.shape[0] // 2
        value = op(value[:half], value[half:])
    return value

def _put_bias(bias, line_ref, rows):
    for head in range(2):
        line = jnp.broadcast_to(line_ref[head:head + 1, :], (rows, 2 * rows))
        bias[head] = pltpu.roll(line, 0, 1, stride=1, stride_axis=0)

def _biased(raw, bias, far_ref, head, which, rows):
    if which == 0:
        return raw + bias[head, :, :rows]
    if which == 1:
        return raw + bias[head, :, rows:]
    return raw + far_ref[head]

def attend_kernel(peers, items, rows, meta_ref, far_ref, line_ref, *refs):
    parts = refs[:peers]
    mixed, wide_ref, log_ref, qkv, turned, bias, scores = refs[peers:]
    me = meta_ref[0]
    for slot in range(peers):
        qkv[me ^ slot] = parts[slot][...]
        turned[me ^ slot] = _turned(parts[slot][2]).astype(jnp.bfloat16)
    _put_bias(bias, line_ref, rows)
    upper = lax.broadcasted_iota(jnp.int32, (128, rows), 0) < 64

    def one_row(i, _):
        low = meta_ref[1 + i]
        whole = jnp.minimum(meta_ref[1 + peers + i], i - 1)
        queries = _split(qkv[i, 0].astype(jnp.float32) * 0.125)

        def put(j, slot, which, masked, peaks):
            key = qkv[j, 1]
            if masked:
                allowed = _allowed(meta_ref, peers, items, rows, i, j, which, low < i)
            new = []
            for head in range(2):
                raw = _biased(_dot(key, queries[head], ((1,), (1,))), bias, far_ref, head, which, rows)
                if masked:
                    raw = jnp.where(allowed, raw, masked_score)
                scores[head, slot] = raw
                new.append(jnp.maximum(peaks[head], _fold(raw, jnp.maximum)))
            return tuple(new)

        start = jnp.full((8, rows), masked_score, jnp.float32)
        before = jnp.maximum(i - 1, 0)
        peaks = put(i, peers, 0, True, (start, start))
        peaks = put(before, peers + 1, 1, True, peaks)
        peaks = lax.fori_loop(low, whole, lambda j, p: put(j, j, 2, True, p), peaks)
        peaks = lax.fori_loop(jnp.maximum(low, whole), i - 1, lambda j, p: put(j, j, 2, False, p), peaks)
        tops = [jnp.max(peak, axis=0, keepdims=True) for peak in peaks]

        def mix(j, slot, carry):
            sums, total = carry
            value = turned[j]
            new = []
            both = []
            for head in range(2):
                weight = jnp.exp(scores[head, slot] - tops[head])
                new.append(sums[head] + _fold(weight, jnp.add))
                both.append(_dot(value[64 * head:64 * head + 64], weight.astype(jnp.bfloat16), ((1,), (0,))))
            return tuple(new), total + jnp.concatenate(both)

        nothing = jnp.zeros((8, rows), jnp.float32)
        carry = ((nothing, nothing), jnp.zeros((128, rows), jnp.float32))
        carry = mix(before, peers + 1, mix(i, peers, carry))
        sums, total = lax.fori_loop(low, i - 1, lambda j, c: mix(j, j, c), carry)
        sums = [jnp.sum(s, axis=0, keepdims=True) for s in sums]
        total = total / jnp.where(upper, sums[0], sums[1])
        wide_ref[i] = total
        for head in range(2):
            log_ref[i, head:head + 1, :] = tops[head] + jnp.log(sums[head])
        mixed[i] = jnp.transpose(total).astype(jnp.bfloat16)
        return 0

    lax.fori_loop(0, peers, one_row, 0)

def attend(meta, far, line, parts, items):
    peers = len(parts)
    rows = parts[0].shape[1]
    smem = pl.BlockSpec(memory_space=pltpu.SMEM)
    vmem = pl.BlockSpec(memory_space=pltpu.VMEM)
    shapes = [
        jax.ShapeDtypeStruct((peers, rows, 128), jnp.bfloat16),
        jax.ShapeDtypeStruct((peers, 128, rows), jnp.float32),
        jax.ShapeDtypeStruct((peers, 8, rows), jnp.float32),
        jax.ShapeDtypeStruct((peers, 3, rows, 128), jnp.bfloat16),
    ]
    res = pl.pallas_call(
        partial(attend_kernel, peers, items, rows),
        out_shape=shapes,
        in_specs=[smem, smem] + [vmem] * (peers + 1),
        out_specs=[vmem] * 4,
        scratch_shapes=[
            pltpu.VMEM((peers, 128, rows), jnp.bfloat16),
            pltpu.VMEM((2, rows, 2 * rows), jnp.float32),
            pltpu.VMEM((2, peers + 2, rows, rows), jnp.float32),
        ],
        compiler_params=pltpu.CompilerParams(vmem_limit_bytes=18 * 2**20),
        cost_estimate=pl.CostEstimate(flops=8 * 10**9, bytes_accessed=4 * 2**20, transcendentals=3 * 10**6),
        name="attend",
    )(meta, far, line, *parts)
    return res

def attend_back_kernel(peers, items, rows, meta_ref, far_ref, line_ref, wide_ref, log_ref, cot, qkv, *refs):
    all_ref, table_ref, turned, bias, near, far_sum, dkey, dvalue = refs
    for peer in range(peers):
        turned[peer] = _turned(qkv[peer, 1]).astype(jnp.bfloat16)
    _put_bias(bias, line_ref, rows)
    near[...] = jnp.zeros_like(near)
    far_sum[...] = jnp.zeros_like(far_sum)
    dkey[...] = jnp.zeros_like(dkey)
    dvalue[...] = jnp.zeros_like(dvalue)

    def one_row(i, _):
        low = meta_ref[1 + i]
        whole = jnp.minimum(meta_ref[1 + peers + i], i - 1)
        queries = _split(qkv[i, 0].astype(jnp.float32) * 0.125)
        grad = cot[i]
        grads_ = _split(grad)
        product = _turned(grad) * wide_ref[i]
        dots = [jnp.sum(product[64 * head:64 * head + 64], axis=0, keepdims=True) for head in range(2)]
        logs = [log_ref[i, head:head + 1, :] for head in range(2)]

        def step(j, which, masked, dquery):
            key = qkv[j, 1]
            value = qkv[j, 2]
            across = turned[j]
            if masked:
                allowed = _allowed(meta_ref, peers, items, rows, i, j, which, low < i)
            dk = jnp.zeros((rows, 128), jnp.float32)
            dv = jnp.zeros((rows, 128), jnp.float32)
            both = []
            for head in range(2):
                raw = _biased(_dot(key, queries[head], ((1,), (1,))), bias, far_ref, head, which, rows)
                if masked:
                    raw = jnp.where(allowed, raw, masked_score)
                weight = jnp.exp(raw - logs[head])
                dweight = _dot(value, grads_[head], ((1,), (1,)))
                dscore = weight * (dweight - dots[head])
                low_score = dscore.astype(jnp.bfloat16)
                if which == 0:
                    near[head, :, :rows] += dscore
                elif which == 1:
                    near[head, :, rows:] += dscore
                else:
                    far_sum[head] += _fold(dscore, jnp.add)
                both.append(_dot(across[64 * head:64 * head + 64], low_score, ((1,), (0,))))
                dk = dk + _dot(low_score, queries[head], ((1,), (0,)))
                dv = dv + _dot(weight.astype(jnp.bfloat16), grads_[head], ((1,), (0,)))
            dkey[j] += dk
            dvalue[j] += dv
            return dquery + jnp.concatenate(both)

        dquery = step(i, 0, True, jnp.zeros((128, rows), jnp.float32))
        dquery = step(jnp.maximum(i - 1, 0), 1, True, dquery)
        dquery = lax.fori_loop(low, whole, lambda j, d: step(j, 2, True, d), dquery)
        dquery = lax.fori_loop(jnp.maximum(low, whole), i - 1, lambda j, d: step(j, 2, False, d), dquery)
        all_ref[i, 0] = (jnp.transpose(dquery) * 0.125).astype(jnp.bfloat16)
        return 0

    lax.fori_loop(0, peers, one_row, 0)
    for i in range(peers):
        all_ref[i, 1] = dkey[i].astype(jnp.bfloat16)
        all_ref[i, 2] = dvalue[i].astype(jnp.bfloat16)
    wide = 2 * rows
    sub = lax.broadcasted_iota(jnp.int32, (8, wide), 0)
    for head in range(2):
        part = near[head]
        count = rows
        while count > 8:
            count //= 2
            part = part[:count] + pltpu.roll(part[count:], wide - count, 1)
        for bit in (4, 2, 1):
            part = jnp.where((sub & bit) != 0, pltpu.roll(part, wide - bit, 1), part)
        total = far_sum[head]
        table_ref[head, :, :rows] = part[:, :rows]
        table_ref[head, :, rows:] = part[:, rows:] + jnp.concatenate([jnp.zeros((8, rows - 128), jnp.float32), total[:, :128] + total[:, 128:]], axis=1)

def attend_back(meta, far, line, wide, logs, qkv, grads, items):
    peers, _, rows, _ = qkv.shape
    smem = pl.BlockSpec(memory_space=pltpu.SMEM)
    vmem = pl.BlockSpec(memory_space=pltpu.VMEM)
    shapes = [
        jax.ShapeDtypeStruct((peers, 3, rows, 128), jnp.bfloat16),
        jax.ShapeDtypeStruct((2, 8, 2 * rows), jnp.float32),
    ]
    res = pl.pallas_call(
        partial(attend_back_kernel, peers, items, rows),
        out_shape=shapes,
        in_specs=[smem, smem] + [vmem] * 5,
        out_specs=[vmem] * 2,
        scratch_shapes=[
            pltpu.VMEM((peers, 128, rows), jnp.bfloat16),
            pltpu.VMEM((2, rows, 2 * rows), jnp.float32),
            pltpu.VMEM((2, rows, 2 * rows), jnp.float32),
            pltpu.VMEM((2, 8, rows), jnp.float32),
            pltpu.VMEM((peers, rows, 128), jnp.float32),
            pltpu.VMEM((peers, rows, 128), jnp.float32),
        ],
        compiler_params=pltpu.CompilerParams(vmem_limit_bytes=18 * 2**20),
        cost_estimate=pl.CostEstimate(flops=20 * 10**9, bytes_accessed=8 * 2**20, transcendentals=3 * 10**6),
        name="attend_back",
    )(meta, far, line, wide, logs, grads, qkv)
    return res[0], jnp.sum(res[1], axis=1)

def plan(lengths, me, peers, rows):
    ends = jnp.cumsum(lengths)
    items = lengths.shape[0]
    place = jnp.arange(peers, dtype=jnp.int32)
    first = jnp.sum((place[:, None] * rows >= ends[None]).astype(jnp.int32), axis=1)
    last = jnp.sum((place[:, None] * rows + rows - 1 >= ends[None]).astype(jnp.int32), axis=1)
    low = jnp.sum((last[None, :] < first[:, None]).astype(jnp.int32), axis=1)
    low = jnp.where(first < items, jnp.minimum(low, place), place)
    whole = jnp.sum((first[None, :] < last[:, None]).astype(jnp.int32), axis=1)
    return jnp.concatenate([me[None].astype(jnp.int32), low, whole, ends.astype(jnp.int32)])
def bucket_lines(rows, buckets):
    k = jnp.arange(2 * rows, dtype=jnp.int32)
    return (bucket_of(k)[None, :] == jnp.arange(buckets, dtype=jnp.int32)[:, None]).astype(jnp.float32)


def _unit(value):
    mean = jnp.mean(value, axis=-1, keepdims=True)
    centred = value - mean
    variance = jnp.mean(centred * centred, axis=-1, keepdims=True)
    scale = lax.rsqrt(variance + epsilon)
    return centred * scale, scale


def _norm_back(grad, unit, scale, gain, sums_ref):
    inner = grad * gain
    first = jnp.mean(inner, axis=-1, keepdims=True)
    second = jnp.mean(inner * unit, axis=-1, keepdims=True)
    sums_ref[0:1, :] = jnp.sum(grad * unit, axis=0, keepdims=True)
    sums_ref[1:2, :] = jnp.sum(grad, axis=0, keepdims=True)
    return scale * (inner - first - unit * second)


def _lanes(index):
    return pl.ds(pl.multiple_of(index * 128, 128), 128)


def _specs(*kinds):
    places = {"s": pltpu.SMEM, "v": pltpu.VMEM, "h": pltpu.HBM}
    return [pl.BlockSpec(memory_space=places[kind]) for word in kinds for kind in word]


def _params(mebibytes):
    return pltpu.CompilerParams(vmem_limit_bytes=mebibytes * 2**20)


def project_kernel(peers, meta_ref, tokens_ref, gain_ref, shift_ref, weight_ref, *refs):
    outs, act_ref, held, done, arrived = refs[:peers], refs[peers], refs[peers + 1], refs[peers + 2], refs[peers + 3]
    me = meta_ref[0]
    pieces, _, span = held.shape
    copies = []
    for piece in range(pieces):
        copies.append(pltpu.make_async_copy(weight_ref.at[:, pl.ds(piece * span, span)], held.at[piece], arrived.at[piece]))
        copies[-1].start()
    unit, _ = _unit(tokens_ref[...].astype(jnp.float32))
    act = (unit * gain_ref[...] + shift_ref[...]).astype(jnp.bfloat16)
    act_ref[...] = act
    for piece in range(pieces):
        copies[piece].wait()
        got = _dot(act, held[piece], ((1,), (0,))).astype(jnp.bfloat16)
        for block in range(span // 128):
            done[piece * (span // 128) + block] = got[:, 128 * block : 128 * block + 128]
    for slot in range(peers):
        for block in range(3):
            outs[slot][block] = done[block * peers + (me ^ slot)]


def project(meta, tokens, gain, shift, weight, peers):
    rows, width = tokens.shape
    span = 512
    pieces = weight.shape[1] // span
    return pl.pallas_call(
        partial(project_kernel, peers),
        out_shape=[jax.ShapeDtypeStruct((3, rows, 128), jnp.bfloat16)] * peers + [jax.ShapeDtypeStruct((rows, width), jnp.bfloat16)],
        in_specs=_specs("svvvh"),
        out_specs=_specs("v" * (peers + 1)),
        scratch_shapes=[
            pltpu.VMEM((pieces, width, span), jnp.bfloat16),
            pltpu.VMEM((3 * peers, rows, 128), jnp.bfloat16),
            pltpu.SemaphoreType.DMA((pieces,)),
        ],
        compiler_params=_params(60),
        cost_estimate=pl.CostEstimate(flops=4 * 10**9, bytes_accessed=8 * 2**20, transcendentals=0),
        name="project",
    )(meta, tokens, gain, shift, weight)


def merge_kernel(parts_ref, tokens_ref, gain_ref, shift_ref, weight_ref, low_ref, middle_ref, act_ref):
    for part in range(parts_ref.shape[0]):
        low_ref[:, 128 * part : 128 * part + 128] = parts_ref[part]
    middle = tokens_ref[...].astype(jnp.float32) + _dot(low_ref[...], weight_ref[...], ((1,), (0,)))
    middle_ref[...] = middle
    unit, _ = _unit(middle)
    act_ref[...] = (unit * gain_ref[...] + shift_ref[...]).astype(jnp.bfloat16)


def merge(parts, tokens, gain, shift, weight):
    return pl.pallas_call(
        merge_kernel,
        out_shape=[jax.ShapeDtypeStruct(tokens.shape, t) for t in (jnp.bfloat16, jnp.float32, jnp.bfloat16)],
        in_specs=_specs("vvvvv"),
        out_specs=_specs("vvv"),
        compiler_params=_params(12),
        cost_estimate=pl.CostEstimate(flops=10**9, bytes_accessed=5 * 2**20, transcendentals=0),
        name="merge",
    )(parts, tokens, gain, shift, weight)


def _both(ref, mine, other):
    rows = mine.shape[0]
    ref[:rows] = mine[...]
    ref[rows:] = other[...]


def _whole(*shape):
    return pl.BlockSpec(shape, lambda step, meta_ref: (0,) * len(shape))


def _across(rows, columns):
    return pl.BlockSpec((rows, columns), lambda step, meta_ref: (0, step))


def pull_kernel(meta_ref, mine, other, contract_ref, out_ref, grads):
    @pl.when(pl.program_id(0) == 0)
    def _():
        _both(grads, mine, other)

    out_ref[...] = _dot(grads[...], contract_ref[...], ((1,), (1,)))


def pull(meta, mine, other, contract_weight, peers):
    rows, width = mine.shape
    part = contract_weight.shape[0] // (2 * peers)
    return pl.pallas_call(
        pull_kernel,
        out_shape=jax.ShapeDtypeStruct((2 * rows, peers * part), jnp.float32),
        grid_spec=pltpu.PrefetchScalarGridSpec(
            num_scalar_prefetch=1,
            grid=(peers,),
            in_specs=[_whole(rows, width)] * 2 + [pl.BlockSpec((part, width), lambda step, meta_ref: (2 * step + meta_ref[3], 0))],
            out_specs=_across(2 * rows, part),
            scratch_shapes=[pltpu.VMEM((2 * rows, width), jnp.bfloat16)],
        ),
        compiler_params=_params(16),
        cost_estimate=pl.CostEstimate(flops=3 * 10**9, bytes_accessed=9 * 2**20, transcendentals=0),
        name="pull",
    )(meta, mine, other, contract_weight)


def feed_kernel(
    rows, part, meta_ref, act_mine, act_other, pulled_ref, expand_ref, in_keep, in_send, low_ref, back_ref, acts, weights, total, arrived
):
    core = meta_ref[3]
    pieces = weights.shape[1] // part
    copies = []
    for piece in range(pieces):
        columns = pl.ds(pl.multiple_of((2 * piece + core) * part, part), part)
        here = weights.at[:, pl.ds(piece * part, part)]
        copies.append(pltpu.make_async_copy(expand_ref.at[:, columns], here, arrived.at[piece]))
        copies[-1].start()
    _both(acts, act_mine, act_other)

    def before(piece):
        copies[piece].wait()
        return _dot(acts[...], weights[:, piece * part : (piece + 1) * part], ((1,), (0,)))

    now = before(0)
    for piece in range(pieces):
        later = before(piece + 1) if piece + 1 < pieces else None
        span = slice(piece * part, (piece + 1) * part)
        rate = 0.5 * (1.0 + lax.erf(now * math.sqrt(0.5)))
        low_ref[:, span] = (now * rate).astype(jnp.bfloat16)
        slope = rate + now * jnp.exp(-0.5 * now * now) * (1.0 / math.sqrt(2.0 * math.pi))
        back_ref[:, span] = (pulled_ref[:, span] * slope).astype(jnp.bfloat16)
        if piece % 2 == 1:
            pair = slice((piece - 1) * part, (piece + 1) * part)
            got = _dot(back_ref[:, pair], weights[:, pair], ((1,), (1,)))
            if piece == 1:
                total[...] = got
            elif piece + 1 < pieces:
                total[...] += got
            else:
                in_keep[...] = total[:rows] + got[:rows]
                in_send[...] = total[rows:] + got[rows:]
        now = later


def feed(meta, act_mine, act_other, pulled, expand_weight, peers):
    rows, width = act_mine.shape
    part = expand_weight.shape[1] // (2 * peers)
    shapes = [
        ((rows, width), jnp.float32),
        ((rows, width), jnp.float32),
        ((2 * rows, peers * part), jnp.bfloat16),
        ((2 * rows, peers * part), jnp.bfloat16),
    ]
    return pl.pallas_call(
        partial(feed_kernel, rows, part),
        out_shape=[jax.ShapeDtypeStruct(*shape) for shape in shapes],
        in_specs=_specs("svvvh"),
        out_specs=_specs("vvvv"),
        scratch_shapes=[
            pltpu.VMEM((2 * rows, width), jnp.bfloat16),
            pltpu.VMEM((width, peers * part), jnp.bfloat16),
            pltpu.VMEM((2 * rows, width), jnp.float32),
            pltpu.SemaphoreType.DMA((peers,)),
        ],
        compiler_params=_params(40),
        cost_estimate=pl.CostEstimate(flops=8 * 10**9, bytes_accessed=20 * 2**20, transcendentals=2 * 10**6),
        name="feed",
    )(meta, act_mine, act_other, pulled, expand_weight)


def _split_rows(held, x, y, one_keep, one_send, two_keep, two_send):
    peers, rows, _ = held.shape
    cut, half = one_keep.shape[2], rows // 2
    mine = pl.ds(pl.multiple_of(y * half, half), half)
    other = pl.ds(pl.multiple_of((1 - y) * half, half), half)
    for place in range(peers // 2):
        one_keep[place] = held[2 * place + x, :, :cut]
        one_send[place] = held[2 * place + 1 - x, :, :cut]
    for place in range(peers):
        two_keep[place] = held[place, mine, cut:]
        two_send[place] = held[place, other, cut:]


def contract_weigh_kernel(meta_ref, grad_mine, grad_other, low_ref, *refs):
    outs, grads, held = refs[:4], refs[4], refs[5]
    _both(grads, grad_mine, grad_other)
    part = held.shape[1]
    for piece in range(held.shape[0]):
        held[piece] = _dot(low_ref[:, piece * part : (piece + 1) * part], grads[...], ((0,), (0,))).astype(jnp.bfloat16)
    _split_rows(held, meta_ref[1], meta_ref[2], *outs)


def contract_weigh(meta, grad_mine, grad_other, low, peers):
    rows, width = grad_mine.shape
    part, cut = low.shape[1] // peers, width // 2
    shapes = [(peers // 2, part, cut), (peers // 2, part, cut), (peers, part // 2, cut), (peers, part // 2, cut)]
    return pl.pallas_call(
        contract_weigh_kernel,
        out_shape=[jax.ShapeDtypeStruct(shape, jnp.bfloat16) for shape in shapes],
        in_specs=_specs("svvv"),
        out_specs=_specs("vvvv"),
        scratch_shapes=[pltpu.VMEM((2 * rows, width), jnp.bfloat16), pltpu.VMEM((peers, part, width), jnp.bfloat16)],
        compiler_params=_params(14),
        cost_estimate=pl.CostEstimate(flops=10**8, bytes_accessed=2**20, transcendentals=0),
        name="contract_weigh",
    )(meta, grad_mine, grad_other, low)


def weigh_kernel(meta_ref, act_mine, act_other, mix_mine, mix_other, right_mine, right_other, back_ref, *refs):
    outs, left, held = refs[:4], refs[4], refs[5]
    peers, group, span = held.shape
    wide = back_ref.shape[1] // 2
    cut = span // 2
    _both(left, mix_mine, mix_other)
    right = jnp.concatenate([right_mine[...], right_other[...]])
    grad = _dot(left[...], right, ((0,), (0,))).astype(jnp.bfloat16)
    quarter = grad.shape[1] // 2
    held[:, :, wide:cut] = grad[:, :quarter].reshape(peers, group, quarter)
    held[:, :, cut + wide :] = grad[:, quarter:].reshape(peers, group, quarter)
    _both(left, act_mine, act_other)
    for side in range(2):
        grad = _dot(left[...], back_ref[:, side * wide : (side + 1) * wide], ((0,), (0,))).astype(jnp.bfloat16)
        held[:, :, side * cut : side * cut + wide] = grad.reshape(peers, group, wide)
    _split_rows(held, meta_ref[1], meta_ref[2], *outs)


def weigh(meta, act_mine, act_other, mix_mine, mix_other, right_mine, right_other, back, peers):
    rows, width = act_mine.shape
    group, cut = width // peers, back.shape[1] // 2 + width // 4
    shapes = [(peers // 2, group, cut), (peers // 2, group, cut), (peers, group // 2, cut), (peers, group // 2, cut)]
    return pl.pallas_call(
        weigh_kernel,
        out_shape=[jax.ShapeDtypeStruct(shape, jnp.bfloat16) for shape in shapes],
        in_specs=_specs("svvvvvvv"),
        out_specs=_specs("vvvv"),
        scratch_shapes=[pltpu.VMEM((2 * rows, width), jnp.bfloat16), pltpu.VMEM((peers, group, 2 * cut), jnp.bfloat16)],
        compiler_params=_params(20),
        cost_estimate=pl.CostEstimate(flops=10**8, bytes_accessed=2**20, transcendentals=0),
        name="weigh",
    )(meta, act_mine, act_other, mix_mine, mix_other, right_mine, right_other, back)


def emit_kernel(meta_ref, low_ref, contract_ref, keep_ref, send_ref, weights, arrived):
    core = meta_ref[3]
    rows, pieces = keep_ref.shape[0], arrived.shape[0]
    part = weights.shape[0] // pieces
    copies = []
    for piece in range(pieces):
        at = pl.ds(pl.multiple_of((2 * piece + core) * part, part), part)
        copies.append(pltpu.make_async_copy(contract_ref.at[at], weights.at[pl.ds(piece * part, part)], arrived.at[piece]))
        copies[-1].start()
    for copy in copies:
        copy.wait()
    keep_ref[...] = _dot(low_ref[:rows], weights[...], ((1,), (0,)))
    send_ref[...] = _dot(low_ref[rows:], weights[...], ((1,), (0,))).astype(jnp.bfloat16)


def emit(meta, low, contract_weight, peers):
    rows, width = low.shape[0] // 2, contract_weight.shape[1]
    return pl.pallas_call(
        emit_kernel,
        out_shape=[jax.ShapeDtypeStruct((rows, width), jnp.float32), jax.ShapeDtypeStruct((rows, width), jnp.bfloat16)],
        in_specs=_specs("svh"),
        out_specs=_specs("vv"),
        scratch_shapes=[pltpu.VMEM((low.shape[1], width), jnp.bfloat16), pltpu.SemaphoreType.DMA((peers,))],
        compiler_params=_params(30),
        cost_estimate=pl.CostEstimate(flops=2 * 10**9, bytes_accessed=8 * 2**20, transcendentals=0),
        name="emit",
    )(meta, low, contract_weight)


def turn_kernel(meta_ref, in_mine, in_other, middle_ref, grad_ref, gain_ref, weight_ref, heads_ref, total_ref, keep_ref, send_ref, sums_ref):
    core = meta_ref[3]
    half = keep_ref.shape[1]
    unit, scale = _unit(middle_ref[...])
    total = grad_ref[...].astype(jnp.float32) + _norm_back(in_mine[...] + in_other[...], unit, scale, gain_ref[...], sums_ref)
    total_ref[...] = total
    low = total.astype(jnp.bfloat16)

    @pl.when(core == 0)
    def _():
        keep_ref[...] = low[:, :half]
        send_ref[...] = low[:, half:]

    @pl.when(core != 0)
    def _():
        keep_ref[...] = low[:, half:]
        send_ref[...] = low[:, :half]

    heads = _dot(low, weight_ref[...], ((1,), (1,))).astype(jnp.bfloat16)
    for part in range(heads_ref.shape[0]):
        heads_ref[part] = heads[:, 128 * part : 128 * part + 128]


def turn(meta, in_mine, in_other, middle, grad, gain, weight, peers):
    rows, width = middle.shape
    shapes = [
        ((peers, rows, width // peers), jnp.bfloat16),
        ((rows, width), jnp.float32),
        ((rows, width // 2), jnp.bfloat16),
        ((rows, width // 2), jnp.bfloat16),
        ((2, width), jnp.float32),
    ]
    return pl.pallas_call(
        turn_kernel,
        out_shape=[jax.ShapeDtypeStruct(*shape) for shape in shapes],
        in_specs=_specs("svvvvvv"),
        out_specs=_specs("v" * len(shapes)),
        compiler_params=_params(12),
        cost_estimate=pl.CostEstimate(flops=10**9, bytes_accessed=8 * 2**20, transcendentals=0),
        name="turn",
    )(meta, in_mine, in_other, middle, grad, gain, weight)


def close_kernel(parts_ref, tokens_ref, grad_ref, gain_ref, weight_ref, out_ref, sums_ref, held):
    peers = parts_ref.shape[0]
    for peer in range(peers):
        for block in range(3):
            at = 128 * (block * peers + peer)
            held[:, at : at + 128] = parts_ref[peer, block]
    back = _dot(held[...], weight_ref[...], ((1,), (1,)))
    unit, scale = _unit(tokens_ref[...].astype(jnp.float32))
    out_ref[...] = grad_ref[...] + _norm_back(back, unit, scale, gain_ref[...], sums_ref)


def close(parts, tokens, grad, gain, weight):
    rows, width = tokens.shape
    return pl.pallas_call(
        close_kernel,
        out_shape=[jax.ShapeDtypeStruct((rows, width), jnp.float32), jax.ShapeDtypeStruct((2, width), jnp.float32)],
        in_specs=_specs("vvvvv"),
        out_specs=_specs("vv"),
        scratch_shapes=[pltpu.VMEM((rows, 3 * width), jnp.bfloat16)],
        compiler_params=_params(16),
        cost_estimate=pl.CostEstimate(flops=2 * 10**9, bytes_accessed=10 * 2**20, transcendentals=0),
        name="close",
    )(parts, tokens, grad, gain, weight)


def _plus(a, b):
    return (a.astype(jnp.float32) + b.astype(jnp.float32)).astype(jnp.bfloat16)


def second_kernel(meta_ref, one_keep, one_got, two_keep, two_got, one_left, one_send, two_left, two_send):
    x, y = meta_ref[1], meta_ref[2]
    levels, half, _ = one_left.shape
    mine = pl.ds(pl.multiple_of(y * half, half), half)
    other = pl.ds(pl.multiple_of((1 - y) * half, half), half)
    for level in range(levels):
        one_left[level] = _plus(one_keep[level, mine], one_got[level, mine])
        one_send[level] = _plus(one_keep[level, other], one_got[level, other])
        two_left[level] = _plus(two_keep[2 * level + x], two_got[2 * level + x])
        two_send[level] = _plus(two_keep[2 * level + 1 - x], two_got[2 * level + 1 - x])


def near_kernel(meta_ref, one_keep, one_got, two_keep, two_got, left, send):
    side = (meta_ref[0] >> 1) & 1
    cut = one_keep.shape[2]
    for level in range(left.shape[0]):
        for out, at in ((left, 2 * level + side), (send, 2 * level + 1 - side)):
            out[level, :, :cut] = _plus(one_keep[at], one_got[at])
            out[level, :, cut:] = _plus(two_keep[at], two_got[at])


def far_kernel(meta_ref, keep, got, left, send):
    upper = meta_ref[0] >> 2
    left[...] = _plus(keep[upper], got[upper])
    send[...] = _plus(keep[1 - upper], got[1 - upper])


def last_kernel(keep, got, out):
    out[...] = _plus(keep[...], got[...])


def _small_call(kernel, name, shapes, kind, *arguments):
    size = sum(2 * math.prod(a.shape) for a in arguments[-4:])
    return pl.pallas_call(
        kernel,
        out_shape=[jax.ShapeDtypeStruct(shape, kind) for shape in shapes],
        in_specs=_specs(*("s" if a.dtype == jnp.int32 else "v" for a in arguments)),
        out_specs=_specs("v" * len(shapes)),
        compiler_params=_params(10),
        cost_estimate=pl.CostEstimate(flops=size, bytes_accessed=3 * size, transcendentals=0),
        name=name,
    )(*arguments)


def _places(meta_ref, half):
    y, core = meta_ref[2], meta_ref[3]
    return [(c, pl.ds(pl.multiple_of(h * half, half), half)) for c in (core, 1 - core) for h in (y, 1 - y)]


def finish_contract_kernel(meta_ref, *refs):
    half = refs[0].shape[0]
    y, core = meta_ref[2], meta_ref[3]
    starts = [(2 * c + h) * half for c in (core, 1 - core) for h in (y, 1 - y)]
    for part, start in zip(refs[:4], starts):
        refs[4][pl.ds(pl.multiple_of(start, half), half), :] = part[...].astype(jnp.float32)


def finish_expand_kernel(part, meta_ref, *refs):
    expand_ref, merge_ref = refs[4:]
    half, span = refs[0].shape[0], refs[0].shape[1] // 2
    near = span // part - 1
    for source, (core, rows) in zip(refs[:4], _places(meta_ref, half)):
        for side in range(2):
            for block in range(near):
                at = pl.multiple_of((2 * (side * near + block) + core) * part, part)
                start = side * span + block * part
                expand_ref[rows, pl.ds(at, part)] = source[:, start : start + part].astype(jnp.float32)
            at = pl.multiple_of((2 * core + side) * part, part)
            start = side * span + near * part
            merge_ref[rows, pl.ds(at, part)] = source[:, start : start + part].astype(jnp.float32)


def finish_attend_kernel(meta_ref, *refs):
    half, wide = refs[0].shape
    span = wide // 3
    for source, (core, rows) in zip(refs[:4], _places(meta_ref, half)):
        for block in range(3):
            at = pl.multiple_of((2 * block + core) * span, span)
            refs[4][rows, pl.ds(at, span)] = source[:, block * span : (block + 1) * span].astype(jnp.float32)


def attend_weigh_kernel(
    meta_ref, act_mine, act_other, owned_ref, other_ref, one_keep, one_send, two_keep, two_send, acts, right, held
):
    x, y, core = meta_ref[1], meta_ref[2], meta_ref[3]
    count, blocks, rows, _ = other_ref.shape
    peers, group, cut = held.shape
    half = group // 2
    _both(acts, act_mine, act_other)
    for block in range(blocks):
        for place in range(count):
            at = 128 * (block * count + place)
            right[:rows, at : at + 128] = owned_ref[core * count + place, block]
            right[rows:, at : at + 128] = other_ref[place, block]
    for side in range(2):
        grad = _dot(acts[...], right[:, side * cut : (side + 1) * cut], ((0,), (0,))).astype(jnp.bfloat16)
        held[...] = grad.reshape(peers, group, cut)
        if side == 0:
            for place in range(peers // 2):
                one_keep[place] = held[2 * place + x]
                one_send[place] = held[2 * place + 1 - x]
        else:
            for place in range(peers):
                two_keep[place] = held[place, pl.ds(pl.multiple_of(y * half, half), half), :]
                two_send[place] = held[place, pl.ds(pl.multiple_of((1 - y) * half, half), half), :]


def attend_weigh(meta, act_mine, act_other, owned, other):
    peers, blocks, rows, _ = owned.shape
    width = act_mine.shape[1]
    group, span = width // peers, blocks * width // 2
    cut = span // 2
    shapes = [(peers // 2, group, cut), (peers // 2, group, cut), (peers, group // 2, cut), (peers, group // 2, cut)]
    return pl.pallas_call(
        attend_weigh_kernel,
        out_shape=[jax.ShapeDtypeStruct(shape, jnp.bfloat16) for shape in shapes],
        in_specs=_specs("svvvv"),
        out_specs=_specs("vvvv"),
        scratch_shapes=[
            pltpu.VMEM((2 * rows, width), jnp.bfloat16),
            pltpu.VMEM((2 * rows, span), jnp.bfloat16),
            pltpu.VMEM((peers, group, cut), jnp.bfloat16),
        ],
        compiler_params=_params(12),
        cost_estimate=pl.CostEstimate(flops=2 * 10**9, bytes_accessed=7 * 2**20, transcendentals=0),
        name="attend_weigh",
    )(meta, act_mine, act_other, owned, other)


def flipped(array, axis, mask):
    peers = lax.axis_size(axis)
    return lax.ppermute(array, axis, [(i, i ^ mask) for i in range(peers)])


def pick(array, index, axis):
    return lax.dynamic_index_in_dim(array, index, axis, keepdims=False)


def added(a, b):
    return (a.astype(jnp.float32) + b.astype(jnp.float32)).astype(jnp.bfloat16)


def in_order(mine, other, bit, axis):
    lower = jnp.where(bit == 0, mine, other)
    upper = jnp.where(bit == 0, other, mine)
    return jnp.concatenate([lower, upper], axis=axis)


def after(value, *others):
    return lax.optimization_barrier((value, others))[0]


def over_first(one_keep, one_send, two_keep, two_send):
    return one_keep, flipped(one_send, "blk", 1), two_keep, flipped(two_send, "seq", 2)


def over_second(here, one_keep, one_got, two_keep, two_got):
    levels, rows, cut = one_keep.shape
    shape = (levels, rows // 2, cut)
    return _small_call(second_kernel, "second", [shape] * 4, jnp.bfloat16, here, one_keep, one_got, two_keep, two_got)


def send_second(one_left, one_send, two_left, two_send):
    return one_left, flipped(one_send, "seq", 2), two_left, flipped(two_send, "blk", 1)


def over_near(here, one_keep, one_got, two_keep, two_got):
    levels, half, cut = one_keep.shape
    left, send = _small_call(
        near_kernel, "near", [(levels // 2, half, 2 * cut)] * 2, jnp.bfloat16, here, one_keep, one_got, two_keep, two_got
    )
    return left, flipped(send, "blk", 2)


def over_far(here, keep, got):
    left, send = _small_call(far_kernel, "far", [keep.shape[1:]] * 2, jnp.bfloat16, here, keep, got)
    return left, flipped(send, "blk", 4)


def over_all(keep, got):
    return _small_call(last_kernel, "last", [keep.shape], jnp.bfloat16, keep, got)[0]


def of_all(own):
    across = flipped(own, "seq", 2)
    return own, across, flipped(own, "seq", 1), flipped(across, "seq", 1)


def local_by_heads(
    tokens,
    lengths,
    attend_weight,
    merge_weight,
    expand_weight,
    contract_weight,
    gain_first,
    shift_first,
    gain_second,
    shift_second,
    bias_table,
    cotangent,
):
    rows, width = tokens.shape[1], tokens.shape[2]
    buckets, heads = bias_table.shape
    hidden = expand_weight.shape[1]
    items = lengths.shape[1]
    peers = lax.axis_size("blk")
    levels = peers // 2
    group = width // peers
    part = hidden // (2 * peers)
    me, line_of = lax.axis_index("blk"), lax.axis_index("seq")
    z, x, y, core = me // 2, me % 2, line_of // 2, line_of % 2
    place = (z, x, y)
    here = jnp.stack([me, x, y, core]).astype(jnp.int32)
    gain_first, shift_first, gain_second, shift_second = (
        v.reshape(1, width) for v in (gain_first, shift_first, gain_second, shift_second)
    )

    own, grad_out = tokens[0], cotangent[0]
    grad_other = flipped(grad_out, "seq", 1)
    meta = plan(lengths[0], me, peers, rows)
    hot = bucket_lines(rows, buckets)
    table_mine = lax.dynamic_slice_in_dim(bias_table, 2 * me, 2, 1)
    lines = jnp.dot(table_mine.T, hot, precision=highest)
    far = table_mine[buckets - 1]

    def to_all(array):
        return lax.all_to_all(array, "blk", split_axis=0, concat_axis=0, tiled=True)

    *parts, act_first = project(here, own, gain_first, shift_first, attend_weight, peers)
    parts = [parts[0]] + [flipped(parts[step], "blk", step) for step in range(1, peers)]
    pulled = pull(here, grad_out, grad_other, contract_weight, peers)
    mixed, wide, logs, qkv = attend(meta, after(far, pulled), lines, parts, items)
    first_other = flipped(act_first, "seq", 1)
    attn_low, middle, act_second = merge(to_all(mixed), own, gain_second, shift_second, merge_weight)
    act_other = flipped(act_second, "seq", 1)
    attn_other = flipped(attn_low, "seq", 1)
    in_keep, in_send, hidden_low, hidden_back = feed(here, act_second, act_other, pulled, expand_weight, peers)
    in_send = flipped(in_send, "seq", 1)
    contract_keep, *contract_parts = contract_weigh(here, grad_out, grad_other, hidden_low, peers)
    in_send, contract_keep, *contract_parts = lax.optimization_barrier((in_send, contract_keep, *contract_parts))
    contract_parts = over_first(contract_keep, *contract_parts)
    grad_heads, grad_middle, keep_low, send_low, sums_second = turn(
        here, in_keep, in_send, middle, grad_out, gain_second, merge_weight, peers
    )
    expand_parts = weigh(here, act_second, act_other, attn_low, attn_other, keep_low, flipped(send_low, "seq", 1), hidden_back, peers)
    expand_keep = expand_parts[0]
    _, *expand_parts = over_first(*expand_parts)

    contract_parts = over_second(here, *contract_parts)
    grad_heads, expand_keep, *contract_parts = lax.optimization_barrier((to_all(grad_heads), expand_keep, *contract_parts))
    back_all, line_grad = attend_back(meta, far, lines, wide, logs, qkv, grad_heads, items)
    back_all, *sums = lax.optimization_barrier((back_all, *contract_parts, expand_keep, *expand_parts))
    owned = to_all(back_all)
    out_keep, out_send = emit(here, after(hidden_low, back_all), contract_weight, peers)
    contract_parts = over_near(here, *send_second(*sums[:4]))
    expand_parts = send_second(*over_second(here, *sums[4:]))
    owned, out_keep, *sums = lax.optimization_barrier((owned, out_keep, *contract_parts, *expand_parts))
    contract_parts = over_far(here, *sums[:2])
    expand_parts = over_near(here, *sums[2:])
    owned_send = pick(owned.reshape(2, levels, 3, rows, group), 1 - core, 0)
    attend_parts = over_first(*attend_weigh(here, act_first, first_other, owned, flipped(owned_send, "seq", 1)))
    output = (middle + out_keep + flipped(out_send, "seq", 1).astype(jnp.float32)).astype(jnp.bfloat16)
    tokens_grad, sums_first = close(owned, own, grad_middle, gain_first, attend_weight)
    table_mine = jnp.dot(hot, line_grad.T, precision=highest).reshape(1, 2 * buckets)
    table_row = jnp.broadcast_to(jnp.pad(table_mine, ((0, 0), (0, group - 2 * buckets)))[:, None], (1, peers, group))
    small = jnp.concatenate([sums_first.reshape(2, peers, group), sums_second.reshape(2, peers, group), table_row]).transpose(1, 0, 2)
    small = jnp.pad(small, ((0, 0), (0, 3), (0, 0)))

    sums = lax.optimization_barrier((*attend_parts, *contract_parts, *expand_parts))
    attend_parts = send_second(*over_second(here, *sums[:4]))
    contract_own = over_all(*sums[4:6])
    contract_across = flipped(contract_own, "seq", 2)
    expand_parts = over_far(here, *sums[6:])
    small, *sums = lax.optimization_barrier((small, *attend_parts, contract_across, *expand_parts))
    attend_parts = over_near(here, *sums[:4])
    contract_grad = (contract_own, sums[4], flipped(contract_own, "seq", 1), flipped(sums[4], "seq", 1))
    small = small + flipped(small, "seq", 1)
    expand_own = over_all(*sums[5:])
    expand_across = flipped(expand_own, "seq", 2)
    small, expand_across, *attend_parts = lax.optimization_barrier((small, expand_across, *attend_parts))
    attend_parts = over_far(here, *attend_parts)
    small = small + flipped(small, "seq", 2)
    expand_grad = (expand_own, expand_across, flipped(expand_own, "seq", 1), flipped(expand_across, "seq", 1))
    small = to_all(small)
    contract_grad = _small_call(finish_contract_kernel, "finish_contract", [(2 * part, width)], jnp.float32, here, *contract_grad)[0]
    expand_grad, merge_grad = _small_call(
        partial(finish_expand_kernel, part), "finish_expand", [(group, hidden), (group, width)], jnp.float32, here, *expand_grad
    )
    attend_grad = of_all(over_all(*attend_parts))
    attend_grad = _small_call(finish_attend_kernel, "finish_attend", [(group, 3 * width)], jnp.float32, here, *attend_grad)[0]
    table_grad = small[:, 4, : 2 * buckets].reshape(peers, buckets, 2).transpose(1, 0, 2).reshape(buckets, heads)
    vectors = jnp.sum(small[:, :4], axis=0)
    return (
        output[None],
        tokens_grad[None],
        attend_grad,
        merge_grad,
        expand_grad,
        contract_grad,
        vectors[0],
        vectors[1],
        vectors[2],
        vectors[3],
        table_grad,
    )


def local(*arguments):
    heads = arguments[10].shape[1]
    rows = arguments[0].shape[1]
    peers = lax.axis_size("blk")
    if peers == 8 and lax.axis_size("seq") == 4 and heads == 2 * peers and rows == 256:
        return local_by_heads(*arguments)
    return local_by_runs(*arguments)


def solution(mesh):
    in_specs = (
        P("seq", "blk", None),
        P("seq", None),
        P(),
        P(),
        P(),
        P(),
        P(),
        P(),
        P(),
        P(),
        P(),
        P("seq", "blk", None),
    )
    out_specs = (
        P("seq", "blk", None),
        P("seq", "blk", None),
        P("blk", None),
        P("blk", None),
        P("blk", None),
        P("blk", None),
        P("blk"),
        P("blk"),
        P("blk"),
        P("blk"),
        P(),
    )
    return jax.shard_map(local, mesh=mesh, in_specs=in_specs, out_specs=out_specs, check_vma=False)
```

```python
from functools import partial
import math

import jax
import jax.numpy as jnp
from jax import lax
from jax.experimental import pallas as pl
from jax.experimental.pallas import tpu as pltpu
from jax.sharding import PartitionSpec as P

HOPS = 6


epsilon = 1e-05
masked_score = -1e30
highest = lax.Precision.HIGHEST
bucket_edges = [math.ceil(16 * 8 ** (t / 16)) for t in range(1, 16)]


def shifted(array, axis, by):
    peers = lax.axis_size(axis)
    pairs = [(i, i + by) for i in range(peers) if 0 <= i + by < peers]
    return lax.ppermute(array, axis, pairs)


def shortened(array):

    def short(part):
        return part.astype(jnp.bfloat16) if part.dtype == jnp.float32 else part

    return jax.tree.map(short, array)


def bucket_of(distance):
    total = jnp.minimum(jnp.maximum(distance, 0), 16)
    for edge in bucket_edges:
        total = total + (distance >= edge).astype(jnp.int32)
    return total


def segment_of(position, ends):
    return jnp.sum((position[:, None] >= ends[None, :]).astype(jnp.int32), axis=1)


def layer_norm(value, gain, shift):
    mean = jnp.mean(value, axis=-1, keepdims=True)
    centred = value - mean
    variance = jnp.mean(centred * centred, axis=-1, keepdims=True)
    return centred * lax.rsqrt(variance + epsilon) * gain + shift


def diagonal_sums(grid, count):
    heads = grid.shape[0]
    padded = jnp.pad(jnp.flip(grid, axis=-1), ((0, 0), (0, 0), (0, count)))
    flat = padded.reshape(heads, 2 * count * count)[:, : count * (2 * count - 1)]
    return jnp.sum(flat.reshape(heads, count, 2 * count - 1), axis=1)


def band_matrix(line, count):
    heads = line.shape[0]
    flipped = jnp.flip(line, axis=-1)
    tiled = jnp.tile(flipped, (1, count))
    window = tiled[:, count - 1 : count - 1 + count * (2 * count - 2)]
    return window.reshape(heads, count, 2 * count - 2)[:, :, :count]


def fetch_earlier(block):
    earlier = []
    moving = block
    for hop in range(HOPS):
        moving = shifted(moving, "blk", 1)
        earlier.append(moving)
    return earlier


def return_parts(parts):
    carried = jnp.zeros_like(parts[0])
    for hop in range(HOPS, 0, -1):
        carried = shifted(shortened(carried + parts[hop - 1]), "blk", -1)
    return carried


def local_by_runs(
    tokens,
    lengths,
    attend_weight,
    merge_weight,
    expand_weight,
    contract_weight,
    gain_first,
    shift_first,
    gain_second,
    shift_second,
    bias_table,
    cotangent,
):
    rows = tokens.shape[1]
    width = tokens.shape[2]
    heads = bias_table.shape[1]
    buckets = bias_table.shape[0]
    head_size = width // heads
    items = lengths.shape[1]
    start = lax.axis_index("blk") * rows
    query_pos = start + jnp.arange(rows, dtype=jnp.int32)
    ends = jnp.cumsum(lengths[0])
    query_seg = segment_of(query_pos, ends)
    band = jnp.arange(2 * rows - 1, dtype=jnp.int32) - (rows - 1)
    bucket_ids = jnp.arange(buckets, dtype=jnp.int32)

    def pair_setup(hop):
        key_pos = query_pos - hop * rows
        key_seg = segment_of(key_pos, ends)
        key_valid = (key_pos >= 0) & (key_seg < items)
        same = key_pos[None, :] == query_pos[:, None]
        allowed = (
            (query_seg[:, None] == key_seg[None, :])
            & (key_pos[None, :] <= query_pos[:, None])
            & (key_valid[None, :] | same)
        )
        onehot = (bucket_of(hop * rows + band)[:, None] == bucket_ids[None, :]).astype(jnp.float32)
        band_bias = jnp.dot(onehot, bias_table, precision=highest).T
        bias = band_matrix(band_bias, rows)
        additive = jnp.where(allowed[None], bias, masked_score)
        return (jnp.any(allowed), onehot, additive)

    pairs = [pair_setup(hop) for hop in range(HOPS + 1)]
    residual = tokens[0].astype(jnp.float32)
    normed_first, norm_first_pull = jax.vjp(layer_norm, residual, gain_first, shift_first)
    act_first = normed_first.astype(jnp.bfloat16)
    projected = jnp.dot(act_first, attend_weight, preferred_element_type=jnp.float32).astype(
        jnp.bfloat16
    )
    query = projected[:, :width].reshape(rows, heads, head_size)
    keys_values = jnp.stack([projected[:, width : 2 * width], projected[:, 2 * width :]])
    blocks = [keys_values] + fetch_earlier(keys_values)

    def scores_of(block, pair):
        key = block[0].reshape(rows, heads, head_size)
        raw = jnp.einsum("qhe,khe->hqk", query, key, preferred_element_type=jnp.float32) * 0.125
        return raw + pair[2]

    def empty_total():
        return jnp.full((heads, rows), masked_score, jnp.float32)

    def empty_scores():
        return jnp.full((heads, rows, rows), masked_score, jnp.float32)

    log_total = empty_total()
    kept_scores = []
    for block, pair in zip(blocks, pairs):

        def part_total(block=block, pair=pair):
            scores = scores_of(block, pair)
            peak = jnp.max(scores, axis=-1)
            return (peak + jnp.log(jnp.sum(jnp.exp(scores - peak[..., None]), axis=-1)), scores)

        def skip_total():
            return (empty_total(), empty_scores())

        part_log, scores = lax.cond(pair[0], part_total, skip_total)
        log_total = jnp.logaddexp(log_total, part_log)
        kept_scores.append(scores)

    def empty_heads():
        return jnp.zeros((rows, heads, head_size), jnp.float32)

    attended = empty_heads()
    for block, pair, scores in zip(blocks, pairs, kept_scores):

        def part_mix(block=block, scores=scores):
            weights = jnp.exp(scores - log_total[..., None]).astype(jnp.bfloat16)
            value = block[1].reshape(rows, heads, head_size)
            return jnp.einsum("hqk,khe->qhe", weights, value, preferred_element_type=jnp.float32)

        attended = attended + lax.cond(pair[0], part_mix, empty_heads)
    attn_low = attended.reshape(rows, width).astype(jnp.bfloat16)
    middle = residual + jnp.dot(attn_low, merge_weight, preferred_element_type=jnp.float32)
    normed_second, norm_second_pull = jax.vjp(layer_norm, middle, gain_second, shift_second)
    act_second = normed_second.astype(jnp.bfloat16)
    hidden_pre = jnp.dot(act_second, expand_weight, preferred_element_type=jnp.float32)
    hidden, gelu_pull = jax.vjp(partial(jax.nn.gelu, approximate=False), hidden_pre)
    hidden_low = hidden.astype(jnp.bfloat16)
    output = (
        middle + jnp.dot(hidden_low, contract_weight, preferred_element_type=jnp.float32)
    ).astype(jnp.bfloat16)
    grad_out = cotangent[0]
    contract_grad = jnp.einsum(
        "tf,td->fd", hidden_low, grad_out, preferred_element_type=jnp.float32
    )
    grad_hidden = jnp.einsum(
        "td,fd->tf", grad_out, contract_weight, preferred_element_type=jnp.float32
    )
    grad_pre = gelu_pull(grad_hidden)[0].astype(jnp.bfloat16)
    expand_grad = jnp.einsum("td,tf->df", act_second, grad_pre, preferred_element_type=jnp.float32)
    grad_second = jnp.einsum(
        "tf,df->td", grad_pre, expand_weight, preferred_element_type=jnp.float32
    )
    grad_middle_norm, gain_second_grad, shift_second_grad = norm_second_pull(grad_second)
    grad_middle = grad_out.astype(jnp.float32) + grad_middle_norm
    grad_middle_low = grad_middle.astype(jnp.bfloat16)
    merge_grad = jnp.einsum(
        "td,te->de", attn_low, grad_middle_low, preferred_element_type=jnp.float32
    )
    grad_heads = (
        jnp.einsum("te,de->td", grad_middle_low, merge_weight, preferred_element_type=jnp.float32)
        .astype(jnp.bfloat16)
        .reshape(rows, heads, head_size)
    )
    row_dot = jnp.sum(grad_heads.astype(jnp.float32) * attended, axis=-1).T
    back_blocks = [keys_values] + fetch_earlier(keys_values)

    def empty_grads():
        return (
            empty_heads(),
            jnp.zeros((2, rows, width), jnp.float32),
            jnp.zeros((buckets, heads), jnp.float32),
        )

    grad_query = empty_heads()
    table_local = jnp.zeros((buckets, heads), jnp.float32)
    parts = []
    for block, pair in zip(back_blocks, pairs):

        def part_grads(block=block, pair=pair):
            key = block[0].reshape(rows, heads, head_size)
            value = block[1].reshape(rows, heads, head_size)
            weights = jnp.exp(scores_of(block, pair) - log_total[..., None])
            weights_low = weights.astype(jnp.bfloat16)
            grad_weights = jnp.einsum(
                "qhe,khe->hqk", grad_heads, value, preferred_element_type=jnp.float32
            )
            grad_scores = (weights * (grad_weights - row_dot[..., None])).astype(jnp.bfloat16)
            query_part = (
                jnp.einsum("hqk,khe->qhe", grad_scores, key, preferred_element_type=jnp.float32)
                * 0.125
            )
            key_part = (
                jnp.einsum("hqk,qhe->khe", grad_scores, query, preferred_element_type=jnp.float32)
                * 0.125
            )
            value_part = jnp.einsum(
                "hqk,qhe->khe", weights_low, grad_heads, preferred_element_type=jnp.float32
            )
            line_grad = diagonal_sums(grad_scores.astype(jnp.float32), rows)
            table_part = jnp.dot(pair[1].T, line_grad.T, precision=highest)
            return (
                query_part,
                jnp.stack([key_part.reshape(rows, width), value_part.reshape(rows, width)]),
                table_part,
            )

        query_part, pair_part, table_part = lax.cond(pair[0], part_grads, empty_grads)
        grad_query = grad_query + query_part
        table_local = table_local + table_part
        parts.append(pair_part)
    owned = (parts[0] + return_parts(parts[1:])).astype(jnp.bfloat16)
    grad_project = jnp.concatenate(
        [grad_query.reshape(rows, width).astype(jnp.bfloat16), owned[0], owned[1]], axis=1
    )
    attend_grad = jnp.einsum(
        "td,te->de", act_first, grad_project, preferred_element_type=jnp.float32
    )
    grad_first = jnp.einsum(
        "te,de->td", grad_project, attend_weight, preferred_element_type=jnp.float32
    )
    grad_input_norm, gain_first_grad, shift_first_grad = norm_first_pull(grad_first)
    tokens_grad = grad_middle + grad_input_norm
    results = (
        lax.psum_scatter(attend_grad, "blk", scatter_dimension=0, tiled=True),
        lax.psum_scatter(merge_grad, "blk", scatter_dimension=0, tiled=True),
        lax.psum_scatter(expand_grad, "blk", scatter_dimension=0, tiled=True),
        lax.psum_scatter(contract_grad, "blk", scatter_dimension=0, tiled=True),
        lax.psum_scatter(gain_first_grad, "blk", scatter_dimension=0, tiled=True),
        lax.psum_scatter(shift_first_grad, "blk", scatter_dimension=0, tiled=True),
        lax.psum_scatter(gain_second_grad, "blk", scatter_dimension=0, tiled=True),
        lax.psum_scatter(shift_second_grad, "blk", scatter_dimension=0, tiled=True),
    )
    results = (
        lax.psum(results[0].astype(jnp.bfloat16), "seq").astype(jnp.float32),
        lax.psum(results[1].astype(jnp.bfloat16), "seq").astype(jnp.float32),
        lax.psum(results[2].astype(jnp.bfloat16), "seq").astype(jnp.float32),
        lax.psum(results[3].astype(jnp.bfloat16), "seq").astype(jnp.float32),
        lax.psum(results[4].astype(jnp.bfloat16), "seq").astype(jnp.float32),
        lax.psum(results[5].astype(jnp.bfloat16), "seq").astype(jnp.float32),
        lax.psum(results[6].astype(jnp.bfloat16), "seq").astype(jnp.float32),
        lax.psum(results[7].astype(jnp.bfloat16), "seq").astype(jnp.float32),
    )
    table_grad = lax.psum(table_local, ("seq", "blk"))
    return (
        output[None],
        tokens_grad[None],
        results[0],
        results[1],
        results[2],
        results[3],
        results[4],
        results[5],
        results[6],
        results[7],
        table_grad,
    )


def _segments(position, meta_ref, first, items):
    total = jnp.zeros(position.shape, jnp.int32)
    for item in range(items):
        total = total + (position >= meta_ref[first + item]).astype(jnp.int32)
    return total

def _allowed(meta_ref, peers, items, rows, i, j, which, needed):
    first = 1 + 2 * peers
    q_seg = _segments(i * rows + lax.broadcasted_iota(jnp.int32, (1, rows), 1), meta_ref, first, items)
    k_seg = _segments(j * rows + lax.broadcasted_iota(jnp.int32, (rows, 1), 0), meta_ref, first, items)
    k_seg = jnp.where((k_seg < items) & needed if which == 1 else k_seg < items, k_seg, -1)
    same = q_seg == k_seg
    if which == 0:
        key = lax.broadcasted_iota(jnp.int32, (rows, rows), 0)
        query = lax.broadcasted_iota(jnp.int32, (rows, rows), 1)
        return (same & (key < query)) | (key == query)
    return same

def _dot(a, b, dims):
    return lax.dot_general(a, b, (dims, ((), ())), preferred_element_type=jnp.float32)

def _turned(array):
    return jnp.transpose(array.astype(jnp.float32))

def _split(array, axis=1):
    wide = array.astype(jnp.float32)
    left = lax.broadcasted_iota(jnp.int32, array.shape, axis) < 64
    return jnp.where(left, wide, 0.0).astype(jnp.bfloat16), jnp.where(left, 0.0, wide).astype(jnp.bfloat16)

def _fold(value, op):
    while value.shape[0] > 8:
        half = value.shape[0] // 2
        value = op(value[:half], value[half:])
    return value

def _put_bias(bias, line_ref, rows):
    for head in range(2):
        line = jnp.broadcast_to(line_ref[head:head + 1, :], (rows, 2 * rows))
        bias[head] = pltpu.roll(line, 0, 1, stride=1, stride_axis=0)

def _biased(raw, bias, far_ref, head, which, rows):
    if which == 0:
        return raw + bias[head, :, :rows]
    if which == 1:
        return raw + bias[head, :, rows:]
    return raw + far_ref[head]

def attend_kernel(peers, items, rows, meta_ref, far_ref, line_ref, *refs):
    parts = refs[:peers]
    mixed, wide_ref, log_ref, qkv, turned, bias, scores = refs[peers:]
    me = meta_ref[0]
    for slot in range(peers):
        qkv[me ^ slot] = parts[slot][...]
        turned[me ^ slot] = _turned(parts[slot][2]).astype(jnp.bfloat16)
    _put_bias(bias, line_ref, rows)
    upper = lax.broadcasted_iota(jnp.int32, (128, rows), 0) < 64

    def one_row(i, _):
        low = meta_ref[1 + i]
        whole = jnp.minimum(meta_ref[1 + peers + i], i - 1)
        queries = _split(qkv[i, 0].astype(jnp.float32) * 0.125)

        def put(j, slot, which, masked, peaks):
            key = qkv[j, 1]
            if masked:
                allowed = _allowed(meta_ref, peers, items, rows, i, j, which, low < i)
            new = []
            for head in range(2):
                raw = _biased(_dot(key, queries[head], ((1,), (1,))), bias, far_ref, head, which, rows)
                if masked:
                    raw = jnp.where(allowed, raw, masked_score)
                scores[head, slot] = raw
                new.append(jnp.maximum(peaks[head], _fold(raw, jnp.maximum)))
            return tuple(new)

        start = jnp.full((8, rows), masked_score, jnp.float32)
        before = jnp.maximum(i - 1, 0)
        peaks = put(i, peers, 0, True, (start, start))
        peaks = put(before, peers + 1, 1, True, peaks)
        peaks = lax.fori_loop(low, whole, lambda j, p: put(j, j, 2, True, p), peaks)
        peaks = lax.fori_loop(jnp.maximum(low, whole), i - 1, lambda j, p: put(j, j, 2, False, p), peaks)
        tops = [jnp.max(peak, axis=0, keepdims=True) for peak in peaks]

        def mix(j, slot, carry):
            sums, total = carry
            value = turned[j]
            new = []
            both = []
            for head in range(2):
                weight = jnp.exp(scores[head, slot] - tops[head])
                new.append(sums[head] + _fold(weight, jnp.add))
                both.append(_dot(value[64 * head:64 * head + 64], weight.astype(jnp.bfloat16), ((1,), (0,))))
            return tuple(new), total + jnp.concatenate(both)

        nothing = jnp.zeros((8, rows), jnp.float32)
        carry = ((nothing, nothing), jnp.zeros((128, rows), jnp.float32))
        carry = mix(before, peers + 1, mix(i, peers, carry))
        sums, total = lax.fori_loop(low, i - 1, lambda j, c: mix(j, j, c), carry)
        sums = [jnp.sum(s, axis=0, keepdims=True) for s in sums]
        total = total / jnp.where(upper, sums[0], sums[1])
        wide_ref[i] = total
        for head in range(2):
            log_ref[i, head:head + 1, :] = tops[head] + jnp.log(sums[head])
        mixed[i] = jnp.transpose(total).astype(jnp.bfloat16)
        return 0

    lax.fori_loop(0, peers, one_row, 0)

def attend(meta, far, line, parts, items):
    peers = len(parts)
    rows = parts[0].shape[1]
    smem = pl.BlockSpec(memory_space=pltpu.SMEM)
    vmem = pl.BlockSpec(memory_space=pltpu.VMEM)
    shapes = [
        jax.ShapeDtypeStruct((peers, rows, 128), jnp.bfloat16),
        jax.ShapeDtypeStruct((peers, 128, rows), jnp.float32),
        jax.ShapeDtypeStruct((peers, 8, rows), jnp.float32),
        jax.ShapeDtypeStruct((peers, 3, rows, 128), jnp.bfloat16),
    ]
    res = pl.pallas_call(
        partial(attend_kernel, peers, items, rows),
        out_shape=shapes,
        in_specs=[smem, smem] + [vmem] * (peers + 1),
        out_specs=[vmem] * 4,
        scratch_shapes=[
            pltpu.VMEM((peers, 128, rows), jnp.bfloat16),
            pltpu.VMEM((2, rows, 2 * rows), jnp.float32),
            pltpu.VMEM((2, peers + 2, rows, rows), jnp.float32),
        ],
        compiler_params=pltpu.CompilerParams(vmem_limit_bytes=18 * 2**20),
        cost_estimate=pl.CostEstimate(flops=8 * 10**9, bytes_accessed=4 * 2**20, transcendentals=3 * 10**6),
        name="attend",
    )(meta, far, line, *parts)
    return res

def attend_back_kernel(peers, items, rows, meta_ref, far_ref, line_ref, wide_ref, log_ref, cot, qkv, *refs):
    all_ref, table_ref, turned, bias, near, far_sum, dkey, dvalue = refs
    for peer in range(peers):
        turned[peer] = _turned(qkv[peer, 1]).astype(jnp.bfloat16)
    _put_bias(bias, line_ref, rows)
    near[...] = jnp.zeros_like(near)
    far_sum[...] = jnp.zeros_like(far_sum)
    dkey[...] = jnp.zeros_like(dkey)
    dvalue[...] = jnp.zeros_like(dvalue)

    def one_row(i, _):
        low = meta_ref[1 + i]
        whole = jnp.minimum(meta_ref[1 + peers + i], i - 1)
        queries = _split(qkv[i, 0].astype(jnp.float32) * 0.125)
        grad = cot[i]
        grads_ = _split(grad)
        product = _turned(grad) * wide_ref[i]
        dots = [jnp.sum(product[64 * head:64 * head + 64], axis=0, keepdims=True) for head in range(2)]
        logs = [log_ref[i, head:head + 1, :] for head in range(2)]

        def step(j, which, masked, dquery):
            key = qkv[j, 1]
            value = qkv[j, 2]
            across = turned[j]
            if masked:
                allowed = _allowed(meta_ref, peers, items, rows, i, j, which, low < i)
            dk = jnp.zeros((rows, 128), jnp.float32)
            dv = jnp.zeros((rows, 128), jnp.float32)
            both = []
            for head in range(2):
                raw = _biased(_dot(key, queries[head], ((1,), (1,))), bias, far_ref, head, which, rows)
                if masked:
                    raw = jnp.where(allowed, raw, masked_score)
                weight = jnp.exp(raw - logs[head])
                dweight = _dot(value, grads_[head], ((1,), (1,)))
                dscore = weight * (dweight - dots[head])
                low_score = dscore.astype(jnp.bfloat16)
                if which == 0:
                    near[head, :, :rows] += dscore
                elif which == 1:
                    near[head, :, rows:] += dscore
                else:
                    far_sum[head] += _fold(dscore, jnp.add)
                both.append(_dot(across[64 * head:64 * head + 64], low_score, ((1,), (0,))))
                dk = dk + _dot(low_score, queries[head], ((1,), (0,)))
                dv = dv + _dot(weight.astype(jnp.bfloat16), grads_[head], ((1,), (0,)))
            dkey[j] += dk
            dvalue[j] += dv
            return dquery + jnp.concatenate(both)

        dquery = step(i, 0, True, jnp.zeros((128, rows), jnp.float32))
        dquery = step(jnp.maximum(i - 1, 0), 1, True, dquery)
        dquery = lax.fori_loop(low, whole, lambda j, d: step(j, 2, True, d), dquery)
        dquery = lax.fori_loop(jnp.maximum(low, whole), i - 1, lambda j, d: step(j, 2, False, d), dquery)
        all_ref[i, 0] = (jnp.transpose(dquery) * 0.125).astype(jnp.bfloat16)
        return 0

    lax.fori_loop(0, peers, one_row, 0)
    for i in range(peers):
        all_ref[i, 1] = dkey[i].astype(jnp.bfloat16)
        all_ref[i, 2] = dvalue[i].astype(jnp.bfloat16)
    wide = 2 * rows
    sub = lax.broadcasted_iota(jnp.int32, (8, wide), 0)
    for head in range(2):
        part = near[head]
        count = rows
        while count > 8:
            count //= 2
            part = part[:count] + pltpu.roll(part[count:], wide - count, 1)
        for bit in (4, 2, 1):
            part = jnp.where((sub & bit) != 0, pltpu.roll(part, wide - bit, 1), part)
        total = far_sum[head]
        table_ref[head, :, :rows] = part[:, :rows]
        table_ref[head, :, rows:] = part[:, rows:] + jnp.concatenate([jnp.zeros((8, rows - 128), jnp.float32), total[:, :128] + total[:, 128:]], axis=1)

def attend_back(meta, far, line, wide, logs, qkv, grads, items):
    peers, _, rows, _ = qkv.shape
    smem = pl.BlockSpec(memory_space=pltpu.SMEM)
    vmem = pl.BlockSpec(memory_space=pltpu.VMEM)
    shapes = [
        jax.ShapeDtypeStruct((peers, 3, rows, 128), jnp.bfloat16),
        jax.ShapeDtypeStruct((2, 8, 2 * rows), jnp.float32),
    ]
    res = pl.pallas_call(
        partial(attend_back_kernel, peers, items, rows),
        out_shape=shapes,
        in_specs=[smem, smem] + [vmem] * 5,
        out_specs=[vmem] * 2,
        scratch_shapes=[
            pltpu.VMEM((peers, 128, rows), jnp.bfloat16),
            pltpu.VMEM((2, rows, 2 * rows), jnp.float32),
            pltpu.VMEM((2, rows, 2 * rows), jnp.float32),
            pltpu.VMEM((2, 8, rows), jnp.float32),
            pltpu.VMEM((peers, rows, 128), jnp.float32),
            pltpu.VMEM((peers, rows, 128), jnp.float32),
        ],
        compiler_params=pltpu.CompilerParams(vmem_limit_bytes=18 * 2**20),
        cost_estimate=pl.CostEstimate(flops=20 * 10**9, bytes_accessed=8 * 2**20, transcendentals=3 * 10**6),
        name="attend_back",
    )(meta, far, line, wide, logs, grads, qkv)
    return res[0], jnp.sum(res[1], axis=1)

def plan(lengths, me, peers, rows):
    ends = jnp.cumsum(lengths)
    items = lengths.shape[0]
    place = jnp.arange(peers, dtype=jnp.int32)
    first = jnp.sum((place[:, None] * rows >= ends[None]).astype(jnp.int32), axis=1)
    last = jnp.sum((place[:, None] * rows + rows - 1 >= ends[None]).astype(jnp.int32), axis=1)
    low = jnp.sum((last[None, :] < first[:, None]).astype(jnp.int32), axis=1)
    low = jnp.where(first < items, jnp.minimum(low, place), place)
    whole = jnp.sum((first[None, :] < last[:, None]).astype(jnp.int32), axis=1)
    return jnp.concatenate([me[None].astype(jnp.int32), low, whole, ends.astype(jnp.int32)])
def bucket_lines(rows, buckets):
    k = jnp.arange(2 * rows, dtype=jnp.int32)
    return (bucket_of(k)[None, :] == jnp.arange(buckets, dtype=jnp.int32)[:, None]).astype(jnp.float32)


def _unit(value):
    mean = jnp.mean(value, axis=-1, keepdims=True)
    centred = value - mean
    variance = jnp.mean(centred * centred, axis=-1, keepdims=True)
    scale = lax.rsqrt(variance + epsilon)
    return centred * scale, scale


def _norm_back(grad, unit, scale, gain, sums_ref):
    inner = grad * gain
    first = jnp.mean(inner, axis=-1, keepdims=True)
    second = jnp.mean(inner * unit, axis=-1, keepdims=True)
    sums_ref[0:1, :] = jnp.sum(grad * unit, axis=0, keepdims=True)
    sums_ref[1:2, :] = jnp.sum(grad, axis=0, keepdims=True)
    return scale * (inner - first - unit * second)


def _lanes(index):
    return pl.ds(pl.multiple_of(index * 128, 128), 128)


def _specs(*kinds):
    places = {"s": pltpu.SMEM, "v": pltpu.VMEM, "h": pltpu.HBM}
    return [pl.BlockSpec(memory_space=places[kind]) for word in kinds for kind in word]


def _params(mebibytes):
    return pltpu.CompilerParams(vmem_limit_bytes=mebibytes * 2**20)


def project_kernel(peers, meta_ref, tokens_ref, gain_ref, shift_ref, weight_ref, *refs):
    outs, act_ref, held, done, arrived = refs[:peers], refs[peers], refs[peers + 1], refs[peers + 2], refs[peers + 3]
    me = meta_ref[0]
    pieces, _, span = held.shape
    copies = []
    for piece in range(pieces):
        copies.append(pltpu.make_async_copy(weight_ref.at[:, pl.ds(piece * span, span)], held.at[piece], arrived.at[piece]))
        copies[-1].start()
    unit, _ = _unit(tokens_ref[...].astype(jnp.float32))
    act = (unit * gain_ref[...] + shift_ref[...]).astype(jnp.bfloat16)
    act_ref[...] = act
    for piece in range(pieces):
        copies[piece].wait()
        got = _dot(act, held[piece], ((1,), (0,))).astype(jnp.bfloat16)
        for block in range(span // 128):
            done[piece * (span // 128) + block] = got[:, 128 * block : 128 * block + 128]
    for slot in range(peers):
        for block in range(3):
            outs[slot][block] = done[block * peers + (me ^ slot)]


def project(meta, tokens, gain, shift, weight, peers):
    rows, width = tokens.shape
    span = 512
    pieces = weight.shape[1] // span
    return pl.pallas_call(
        partial(project_kernel, peers),
        out_shape=[jax.ShapeDtypeStruct((3, rows, 128), jnp.bfloat16)] * peers + [jax.ShapeDtypeStruct((rows, width), jnp.bfloat16)],
        in_specs=_specs("svvvh"),
        out_specs=_specs("v" * (peers + 1)),
        scratch_shapes=[
            pltpu.VMEM((pieces, width, span), jnp.bfloat16),
            pltpu.VMEM((3 * peers, rows, 128), jnp.bfloat16),
            pltpu.SemaphoreType.DMA((pieces,)),
        ],
        compiler_params=_params(60),
        cost_estimate=pl.CostEstimate(flops=4 * 10**9, bytes_accessed=8 * 2**20, transcendentals=0),
        name="project",
    )(meta, tokens, gain, shift, weight)


def merge_kernel(parts_ref, tokens_ref, gain_ref, shift_ref, weight_ref, low_ref, middle_ref, act_ref):
    for part in range(parts_ref.shape[0]):
        low_ref[:, 128 * part : 128 * part + 128] = parts_ref[part]
    middle = tokens_ref[...].astype(jnp.float32) + _dot(low_ref[...], weight_ref[...], ((1,), (0,)))
    middle_ref[...] = middle
    unit, _ = _unit(middle)
    act_ref[...] = (unit * gain_ref[...] + shift_ref[...]).astype(jnp.bfloat16)


def merge(parts, tokens, gain, shift, weight):
    return pl.pallas_call(
        merge_kernel,
        out_shape=[jax.ShapeDtypeStruct(tokens.shape, t) for t in (jnp.bfloat16, jnp.float32, jnp.bfloat16)],
        in_specs=_specs("vvvvv"),
        out_specs=_specs("vvv"),
        compiler_params=_params(12),
        cost_estimate=pl.CostEstimate(flops=10**9, bytes_accessed=5 * 2**20, transcendentals=0),
        name="merge",
    )(parts, tokens, gain, shift, weight)


def _both(ref, mine, other):
    rows = mine.shape[0]
    ref[:rows] = mine[...]
    ref[rows:] = other[...]


def _whole(*shape):
    return pl.BlockSpec(shape, lambda step, meta_ref: (0,) * len(shape))


def _across(rows, columns):
    return pl.BlockSpec((rows, columns), lambda step, meta_ref: (0, step))


def pull_kernel(meta_ref, mine, other, contract_ref, out_ref, grads):
    @pl.when(pl.program_id(0) == 0)
    def _():
        _both(grads, mine, other)

    out_ref[...] = _dot(grads[...], contract_ref[...], ((1,), (1,)))


def pull(meta, mine, other, contract_weight, peers):
    rows, width = mine.shape
    part = contract_weight.shape[0] // (2 * peers)
    return pl.pallas_call(
        pull_kernel,
        out_shape=jax.ShapeDtypeStruct((2 * rows, peers * part), jnp.float32),
        grid_spec=pltpu.PrefetchScalarGridSpec(
            num_scalar_prefetch=1,
            grid=(peers,),
            in_specs=[_whole(rows, width)] * 2 + [pl.BlockSpec((part, width), lambda step, meta_ref: (2 * step + meta_ref[3], 0))],
            out_specs=_across(2 * rows, part),
            scratch_shapes=[pltpu.VMEM((2 * rows, width), jnp.bfloat16)],
        ),
        compiler_params=_params(16),
        cost_estimate=pl.CostEstimate(flops=3 * 10**9, bytes_accessed=9 * 2**20, transcendentals=0),
        name="pull",
    )(meta, mine, other, contract_weight)


def feed_kernel(
    rows, part, meta_ref, act_mine, act_other, pulled_ref, expand_ref, in_keep, in_send, low_ref, back_ref, acts, weights, total, arrived
):
    core = meta_ref[3]
    pieces = weights.shape[1] // part
    copies = []
    for piece in range(pieces):
        columns = pl.ds(pl.multiple_of((2 * piece + core) * part, part), part)
        here = weights.at[:, pl.ds(piece * part, part)]
        copies.append(pltpu.make_async_copy(expand_ref.at[:, columns], here, arrived.at[piece]))
        copies[-1].start()
    _both(acts, act_mine, act_other)

    def before(piece):
        copies[piece].wait()
        return _dot(acts[...], weights[:, piece * part : (piece + 1) * part], ((1,), (0,)))

    now = before(0)
    for piece in range(pieces):
        later = before(piece + 1) if piece + 1 < pieces else None
        span = slice(piece * part, (piece + 1) * part)
        rate = 0.5 * (1.0 + lax.erf(now * math.sqrt(0.5)))
        low_ref[:, span] = (now * rate).astype(jnp.bfloat16)
        slope = rate + now * jnp.exp(-0.5 * now * now) * (1.0 / math.sqrt(2.0 * math.pi))
        back_ref[:, span] = (pulled_ref[:, span] * slope).astype(jnp.bfloat16)
        if piece % 2 == 1:
            pair = slice((piece - 1) * part, (piece + 1) * part)
            got = _dot(back_ref[:, pair], weights[:, pair], ((1,), (1,)))
            if piece == 1:
                total[...] = got
            elif piece + 1 < pieces:
                total[...] += got
            else:
                in_keep[...] = total[:rows] + got[:rows]
                in_send[...] = total[rows:] + got[rows:]
        now = later


def feed(meta, act_mine, act_other, pulled, expand_weight, peers):
    rows, width = act_mine.shape
    part = expand_weight.shape[1] // (2 * peers)
    shapes = [
        ((rows, width), jnp.float32),
        ((rows, width), jnp.float32),
        ((2 * rows, peers * part), jnp.bfloat16),
        ((2 * rows, peers * part), jnp.bfloat16),
    ]
    return pl.pallas_call(
        partial(feed_kernel, rows, part),
        out_shape=[jax.ShapeDtypeStruct(*shape) for shape in shapes],
        in_specs=_specs("svvvh"),
        out_specs=_specs("vvvv"),
        scratch_shapes=[
            pltpu.VMEM((2 * rows, width), jnp.bfloat16),
            pltpu.VMEM((width, peers * part), jnp.bfloat16),
            pltpu.VMEM((2 * rows, width), jnp.float32),
            pltpu.SemaphoreType.DMA((peers,)),
        ],
        compiler_params=_params(40),
        cost_estimate=pl.CostEstimate(flops=8 * 10**9, bytes_accessed=20 * 2**20, transcendentals=2 * 10**6),
        name="feed",
    )(meta, act_mine, act_other, pulled, expand_weight)


def _split_rows(held, x, y, one_keep, one_send, two_keep, two_send):
    peers, rows, _ = held.shape
    cut, half = one_keep.shape[2], rows // 2
    mine = pl.ds(pl.multiple_of(y * half, half), half)
    other = pl.ds(pl.multiple_of((1 - y) * half, half), half)
    for place in range(peers // 2):
        one_keep[place] = held[2 * place + x, :, :cut]
        one_send[place] = held[2 * place + 1 - x, :, :cut]
    for place in range(peers):
        two_keep[place] = held[place, mine, cut:]
        two_send[place] = held[place, other, cut:]


def contract_weigh_kernel(meta_ref, grad_mine, grad_other, low_ref, *refs):
    outs, grads, held = refs[:4], refs[4], refs[5]
    _both(grads, grad_mine, grad_other)
    part = held.shape[1]
    for piece in range(held.shape[0]):
        held[piece] = _dot(low_ref[:, piece * part : (piece + 1) * part], grads[...], ((0,), (0,))).astype(jnp.bfloat16)
    _split_rows(held, meta_ref[1], meta_ref[2], *outs)


def contract_weigh(meta, grad_mine, grad_other, low, peers):
    rows, width = grad_mine.shape
    part, cut = low.shape[1] // peers, width // 2
    shapes = [(peers // 2, part, cut), (peers // 2, part, cut), (peers, part // 2, cut), (peers, part // 2, cut)]
    return pl.pallas_call(
        contract_weigh_kernel,
        out_shape=[jax.ShapeDtypeStruct(shape, jnp.bfloat16) for shape in shapes],
        in_specs=_specs("svvv"),
        out_specs=_specs("vvvv"),
        scratch_shapes=[pltpu.VMEM((2 * rows, width), jnp.bfloat16), pltpu.VMEM((peers, part, width), jnp.bfloat16)],
        compiler_params=_params(14),
        cost_estimate=pl.CostEstimate(flops=10**8, bytes_accessed=2**20, transcendentals=0),
        name="contract_weigh",
    )(meta, grad_mine, grad_other, low)


def weigh_kernel(meta_ref, act_mine, act_other, mix_mine, mix_other, right_mine, right_other, back_ref, *refs):
    outs, left, held = refs[:4], refs[4], refs[5]
    peers, group, span = held.shape
    wide = back_ref.shape[1] // 2
    cut = span // 2
    _both(left, mix_mine, mix_other)
    right = jnp.concatenate([right_mine[...], right_other[...]])
    grad = _dot(left[...], right, ((0,), (0,))).astype(jnp.bfloat16)
    quarter = grad.shape[1] // 2
    held[:, :, wide:cut] = grad[:, :quarter].reshape(peers, group, quarter)
    held[:, :, cut + wide :] = grad[:, quarter:].reshape(peers, group, quarter)
    _both(left, act_mine, act_other)
    for side in range(2):
        grad = _dot(left[...], back_ref[:, side * wide : (side + 1) * wide], ((0,), (0,))).astype(jnp.bfloat16)
        held[:, :, side * cut : side * cut + wide] = grad.reshape(peers, group, wide)
    _split_rows(held, meta_ref[1], meta_ref[2], *outs)


def weigh(meta, act_mine, act_other, mix_mine, mix_other, right_mine, right_other, back, peers):
    rows, width = act_mine.shape
    group, cut = width // peers, back.shape[1] // 2 + width // 4
    shapes = [(peers // 2, group, cut), (peers // 2, group, cut), (peers, group // 2, cut), (peers, group // 2, cut)]
    return pl.pallas_call(
        weigh_kernel,
        out_shape=[jax.ShapeDtypeStruct(shape, jnp.bfloat16) for shape in shapes],
        in_specs=_specs("svvvvvvv"),
        out_specs=_specs("vvvv"),
        scratch_shapes=[pltpu.VMEM((2 * rows, width), jnp.bfloat16), pltpu.VMEM((peers, group, 2 * cut), jnp.bfloat16)],
        compiler_params=_params(20),
        cost_estimate=pl.CostEstimate(flops=10**8, bytes_accessed=2**20, transcendentals=0),
        name="weigh",
    )(meta, act_mine, act_other, mix_mine, mix_other, right_mine, right_other, back)


def emit_kernel(meta_ref, low_ref, contract_ref, keep_ref, send_ref, weights, arrived):
    core = meta_ref[3]
    rows, pieces = keep_ref.shape[0], arrived.shape[0]
    part = weights.shape[0] // pieces
    copies = []
    for piece in range(pieces):
        at = pl.ds(pl.multiple_of((2 * piece + core) * part, part), part)
        copies.append(pltpu.make_async_copy(contract_ref.at[at], weights.at[pl.ds(piece * part, part)], arrived.at[piece]))
        copies[-1].start()
    for copy in copies:
        copy.wait()
    keep_ref[...] = _dot(low_ref[:rows], weights[...], ((1,), (0,)))
    send_ref[...] = _dot(low_ref[rows:], weights[...], ((1,), (0,))).astype(jnp.bfloat16)


def emit(meta, low, contract_weight, peers):
    rows, width = low.shape[0] // 2, contract_weight.shape[1]
    return pl.pallas_call(
        emit_kernel,
        out_shape=[jax.ShapeDtypeStruct((rows, width), jnp.float32), jax.ShapeDtypeStruct((rows, width), jnp.bfloat16)],
        in_specs=_specs("svh"),
        out_specs=_specs("vv"),
        scratch_shapes=[pltpu.VMEM((low.shape[1], width), jnp.bfloat16), pltpu.SemaphoreType.DMA((peers,))],
        compiler_params=_params(30),
        cost_estimate=pl.CostEstimate(flops=2 * 10**9, bytes_accessed=8 * 2**20, transcendentals=0),
        name="emit",
    )(meta, low, contract_weight)


def turn_kernel(meta_ref, in_mine, in_other, middle_ref, grad_ref, gain_ref, weight_ref, heads_ref, total_ref, keep_ref, send_ref, sums_ref):
    core = meta_ref[3]
    half = keep_ref.shape[1]
    unit, scale = _unit(middle_ref[...])
    total = grad_ref[...].astype(jnp.float32) + _norm_back(in_mine[...] + in_other[...], unit, scale, gain_ref[...], sums_ref)
    total_ref[...] = total
    low = total.astype(jnp.bfloat16)

    @pl.when(core == 0)
    def _():
        keep_ref[...] = low[:, :half]
        send_ref[...] = low[:, half:]

    @pl.when(core != 0)
    def _():
        keep_ref[...] = low[:, half:]
        send_ref[...] = low[:, :half]

    heads = _dot(low, weight_ref[...], ((1,), (1,))).astype(jnp.bfloat16)
    for part in range(heads_ref.shape[0]):
        heads_ref[part] = heads[:, 128 * part : 128 * part + 128]


def turn(meta, in_mine, in_other, middle, grad, gain, weight, peers):
    rows, width = middle.shape
    shapes = [
        ((peers, rows, width // peers), jnp.bfloat16),
        ((rows, width), jnp.float32),
        ((rows, width // 2), jnp.bfloat16),
        ((rows, width // 2), jnp.bfloat16),
        ((2, width), jnp.float32),
    ]
    return pl.pallas_call(
        turn_kernel,
        out_shape=[jax.ShapeDtypeStruct(*shape) for shape in shapes],
        in_specs=_specs("svvvvvv"),
        out_specs=_specs("v" * len(shapes)),
        compiler_params=_params(12),
        cost_estimate=pl.CostEstimate(flops=10**9, bytes_accessed=8 * 2**20, transcendentals=0),
        name="turn",
    )(meta, in_mine, in_other, middle, grad, gain, weight)


def close_kernel(parts_ref, tokens_ref, grad_ref, gain_ref, weight_ref, out_ref, sums_ref, held):
    peers = parts_ref.shape[0]
    for peer in range(peers):
        for block in range(3):
            at = 128 * (block * peers + peer)
            held[:, at : at + 128] = parts_ref[peer, block]
    back = _dot(held[...], weight_ref[...], ((1,), (1,)))
    unit, scale = _unit(tokens_ref[...].astype(jnp.float32))
    out_ref[...] = grad_ref[...] + _norm_back(back, unit, scale, gain_ref[...], sums_ref)


def close(parts, tokens, grad, gain, weight):
    rows, width = tokens.shape
    return pl.pallas_call(
        close_kernel,
        out_shape=[jax.ShapeDtypeStruct((rows, width), jnp.float32), jax.ShapeDtypeStruct((2, width), jnp.float32)],
        in_specs=_specs("vvvvv"),
        out_specs=_specs("vv"),
        scratch_shapes=[pltpu.VMEM((rows, 3 * width), jnp.bfloat16)],
        compiler_params=_params(16),
        cost_estimate=pl.CostEstimate(flops=2 * 10**9, bytes_accessed=10 * 2**20, transcendentals=0),
        name="close",
    )(parts, tokens, grad, gain, weight)


def _plus(a, b):
    return (a.astype(jnp.float32) + b.astype(jnp.float32)).astype(jnp.bfloat16)


def second_kernel(meta_ref, one_keep, one_got, two_keep, two_got, one_left, one_send, two_left, two_send):
    x, y = meta_ref[1], meta_ref[2]
    levels, half, _ = one_left.shape
    mine = pl.ds(pl.multiple_of(y * half, half), half)
    other = pl.ds(pl.multiple_of((1 - y) * half, half), half)
    for level in range(levels):
        one_left[level] = _plus(one_keep[level, mine], one_got[level, mine])
        one_send[level] = _plus(one_keep[level, other], one_got[level, other])
        two_left[level] = _plus(two_keep[2 * level + x], two_got[2 * level + x])
        two_send[level] = _plus(two_keep[2 * level + 1 - x], two_got[2 * level + 1 - x])


def near_kernel(meta_ref, one_keep, one_got, two_keep, two_got, left, send):
    side = (meta_ref[0] >> 1) & 1
    cut = one_keep.shape[2]
    for level in range(left.shape[0]):
        for out, at in ((left, 2 * level + side), (send, 2 * level + 1 - side)):
            out[level, :, :cut] = _plus(one_keep[at], one_got[at])
            out[level, :, cut:] = _plus(two_keep[at], two_got[at])


def far_kernel(meta_ref, keep, got, left, send):
    upper = meta_ref[0] >> 2
    left[...] = _plus(keep[upper], got[upper])
    send[...] = _plus(keep[1 - upper], got[1 - upper])


def last_kernel(keep, got, out):
    out[...] = _plus(keep[...], got[...])


def _small_call(kernel, name, shapes, kind, *arguments):
    size = sum(2 * math.prod(a.shape) for a in arguments[-4:])
    return pl.pallas_call(
        kernel,
        out_shape=[jax.ShapeDtypeStruct(shape, kind) for shape in shapes],
        in_specs=_specs(*("s" if a.dtype == jnp.int32 else "v" for a in arguments)),
        out_specs=_specs("v" * len(shapes)),
        compiler_params=_params(10),
        cost_estimate=pl.CostEstimate(flops=size, bytes_accessed=3 * size, transcendentals=0),
        name=name,
    )(*arguments)


def _places(meta_ref, half):
    y, core = meta_ref[2], meta_ref[3]
    return [(c, pl.ds(pl.multiple_of(h * half, half), half)) for c in (core, 1 - core) for h in (y, 1 - y)]


def finish_contract_kernel(meta_ref, *refs):
    half = refs[0].shape[0]
    y, core = meta_ref[2], meta_ref[3]
    starts = [(2 * c + h) * half for c in (core, 1 - core) for h in (y, 1 - y)]
    for part, start in zip(refs[:4], starts):
        refs[4][pl.ds(pl.multiple_of(start, half), half), :] = part[...].astype(jnp.float32)


def finish_expand_kernel(part, meta_ref, *refs):
    expand_ref, merge_ref = refs[4:]
    half, span = refs[0].shape[0], refs[0].shape[1] // 2
    near = span // part - 1
    for source, (core, rows) in zip(refs[:4], _places(meta_ref, half)):
        for side in range(2):
            for block in range(near):
                at = pl.multiple_of((2 * (side * near + block) + core) * part, part)
                start = side * span + block * part
                expand_ref[rows, pl.ds(at, part)] = source[:, start : start + part].astype(jnp.float32)
            at = pl.multiple_of((2 * core + side) * part, part)
            start = side * span + near * part
            merge_ref[rows, pl.ds(at, part)] = source[:, start : start + part].astype(jnp.float32)


def finish_attend_kernel(meta_ref, *refs):
    half, wide = refs[0].shape
    span = wide // 3
    for source, (core, rows) in zip(refs[:4], _places(meta_ref, half)):
        for block in range(3):
            at = pl.multiple_of((2 * block + core) * span, span)
            refs[4][rows, pl.ds(at, span)] = source[:, block * span : (block + 1) * span].astype(jnp.float32)


def attend_weigh_kernel(
    meta_ref, act_mine, act_other, owned_ref, other_ref, one_keep, one_send, two_keep, two_send, acts, right, held
):
    x, y, core = meta_ref[1], meta_ref[2], meta_ref[3]
    count, blocks, rows, _ = other_ref.shape
    peers, group, cut = held.shape
    half = group // 2
    _both(acts, act_mine, act_other)
    for block in range(blocks):
        for place in range(count):
            at = 128 * (block * count + place)
            right[:rows, at : at + 128] = owned_ref[core * count + place, block]
            right[rows:, at : at + 128] = other_ref[place, block]
    for side in range(2):
        grad = _dot(acts[...], right[:, side * cut : (side + 1) * cut], ((0,), (0,))).astype(jnp.bfloat16)
        held[...] = grad.reshape(peers, group, cut)
        if side == 0:
            for place in range(peers // 2):
                one_keep[place] = held[2 * place + x]
                one_send[place] = held[2 * place + 1 - x]
        else:
            for place in range(peers):
                two_keep[place] = held[place, pl.ds(pl.multiple_of(y * half, half), half), :]
                two_send[place] = held[place, pl.ds(pl.multiple_of((1 - y) * half, half), half), :]


def attend_weigh(meta, act_mine, act_other, owned, other):
    peers, blocks, rows, _ = owned.shape
    width = act_mine.shape[1]
    group, span = width // peers, blocks * width // 2
    cut = span // 2
    shapes = [(peers // 2, group, cut), (peers // 2, group, cut), (peers, group // 2, cut), (peers, group // 2, cut)]
    return pl.pallas_call(
        attend_weigh_kernel,
        out_shape=[jax.ShapeDtypeStruct(shape, jnp.bfloat16) for shape in shapes],
        in_specs=_specs("svvvv"),
        out_specs=_specs("vvvv"),
        scratch_shapes=[
            pltpu.VMEM((2 * rows, width), jnp.bfloat16),
            pltpu.VMEM((2 * rows, span), jnp.bfloat16),
            pltpu.VMEM((peers, group, cut), jnp.bfloat16),
        ],
        compiler_params=_params(12),
        cost_estimate=pl.CostEstimate(flops=2 * 10**9, bytes_accessed=7 * 2**20, transcendentals=0),
        name="attend_weigh",
    )(meta, act_mine, act_other, owned, other)


def flipped(array, axis, mask):
    peers = lax.axis_size(axis)
    return lax.ppermute(array, axis, [(i, i ^ mask) for i in range(peers)])


def pick(array, index, axis):
    return lax.dynamic_index_in_dim(array, index, axis, keepdims=False)


def added(a, b):
    return (a.astype(jnp.float32) + b.astype(jnp.float32)).astype(jnp.bfloat16)


def in_order(mine, other, bit, axis):
    lower = jnp.where(bit == 0, mine, other)
    upper = jnp.where(bit == 0, other, mine)
    return jnp.concatenate([lower, upper], axis=axis)


def after(value, *others):
    return lax.optimization_barrier((value, others))[0]


def over_first(one_keep, one_send, two_keep, two_send):
    return one_keep, flipped(one_send, "blk", 1), two_keep, flipped(two_send, "seq", 2)


def over_second(here, one_keep, one_got, two_keep, two_got):
    levels, rows, cut = one_keep.shape
    shape = (levels, rows // 2, cut)
    return _small_call(second_kernel, "second", [shape] * 4, jnp.bfloat16, here, one_keep, one_got, two_keep, two_got)


def send_second(one_left, one_send, two_left, two_send):
    return one_left, flipped(one_send, "seq", 2), two_left, flipped(two_send, "blk", 1)


def near_sums(here, one_keep, one_got, two_keep, two_got):
    levels, half, cut = one_keep.shape
    return _small_call(
        near_kernel, "near", [(levels // 2, half, 2 * cut)] * 2, jnp.bfloat16, here, one_keep, one_got, two_keep, two_got
    )


def over_near(here, *parts):
    left, send = near_sums(here, *parts)
    return left, flipped(send, "blk", 2)


def over_far(here, keep, got):
    left, send = _small_call(far_kernel, "far", [keep.shape[1:]] * 2, jnp.bfloat16, here, keep, got)
    return left, flipped(send, "blk", 4)


def over_all(keep, got):
    return _small_call(last_kernel, "last", [keep.shape], jnp.bfloat16, keep, got)[0]


def of_all(own):
    across = flipped(own, "seq", 2)
    return own, across, flipped(own, "seq", 1), flipped(across, "seq", 1)


def local_by_heads(
    tokens,
    lengths,
    attend_weight,
    merge_weight,
    expand_weight,
    contract_weight,
    gain_first,
    shift_first,
    gain_second,
    shift_second,
    bias_table,
    cotangent,
):
    rows, width = tokens.shape[1], tokens.shape[2]
    buckets, heads = bias_table.shape
    hidden = expand_weight.shape[1]
    items = lengths.shape[1]
    peers = lax.axis_size("blk")
    levels = peers // 2
    group = width // peers
    part = hidden // (2 * peers)
    me, line_of = lax.axis_index("blk"), lax.axis_index("seq")
    z, x, y, core = me // 2, me % 2, line_of // 2, line_of % 2
    place = (z, x, y)
    here = jnp.stack([me, x, y, core]).astype(jnp.int32)
    gain_first, shift_first, gain_second, shift_second = (
        v.reshape(1, width) for v in (gain_first, shift_first, gain_second, shift_second)
    )

    own, grad_out = tokens[0], cotangent[0]
    grad_other = flipped(grad_out, "seq", 1)
    meta = plan(lengths[0], me, peers, rows)
    hot = bucket_lines(rows, buckets)
    table_mine = lax.dynamic_slice_in_dim(bias_table, 2 * me, 2, 1)
    lines = jnp.dot(table_mine.T, hot, precision=highest)
    far = table_mine[buckets - 1]

    def to_all(array):
        return lax.all_to_all(array, "blk", split_axis=0, concat_axis=0, tiled=True)

    *parts, act_first = project(here, own, gain_first, shift_first, attend_weight, peers)
    parts = [parts[0]] + [flipped(parts[step], "blk", step) for step in range(1, peers)]
    pulled = pull(here, grad_out, grad_other, contract_weight, peers)
    mixed, wide, logs, qkv = attend(meta, after(far, pulled), lines, parts, items)
    first_other = flipped(act_first, "seq", 1)
    attn_low, middle, act_second = merge(to_all(mixed), own, gain_second, shift_second, merge_weight)
    act_other = flipped(act_second, "seq", 1)
    attn_other = flipped(attn_low, "seq", 1)
    in_keep, in_send, hidden_low, hidden_back = feed(here, act_second, act_other, pulled, expand_weight, peers)
    in_send = flipped(in_send, "seq", 1)
    contract_keep, *contract_parts = contract_weigh(here, grad_out, grad_other, hidden_low, peers)
    in_send, contract_keep, *contract_parts = lax.optimization_barrier((in_send, contract_keep, *contract_parts))
    contract_parts = over_first(contract_keep, *contract_parts)
    grad_heads, grad_middle, keep_low, send_low, sums_second = turn(
        here, in_keep, in_send, middle, grad_out, gain_second, merge_weight, peers
    )
    expand_parts = weigh(here, act_second, act_other, attn_low, attn_other, keep_low, flipped(send_low, "seq", 1), hidden_back, peers)
    expand_keep = expand_parts[0]
    _, *expand_parts = over_first(*expand_parts)

    contract_parts = over_second(here, *contract_parts)
    grad_heads, expand_keep, *contract_parts = lax.optimization_barrier((to_all(grad_heads), expand_keep, *contract_parts))
    back_all, line_grad = attend_back(meta, far, lines, wide, logs, qkv, grad_heads, items)
    back_all, *sums = lax.optimization_barrier((back_all, *contract_parts, expand_keep, *expand_parts))
    owned = to_all(back_all)
    out_keep, out_send = emit(here, after(hidden_low, back_all), contract_weight, peers)
    contract_parts = over_near(here, *send_second(*sums[:4]))
    expand_parts = send_second(*over_second(here, *sums[4:]))
    expand_left, expand_send = near_sums(here, *expand_parts)
    owned, out_keep, expand_left, expand_send, *sums = lax.optimization_barrier((owned, out_keep, expand_left, expand_send, *contract_parts))
    expand_parts = expand_left, flipped(expand_send, "blk", 2)
    contract_parts = over_far(here, *sums)
    owned_send = pick(owned.reshape(2, levels, 3, rows, group), 1 - core, 0)
    attend_parts = over_first(*attend_weigh(here, act_first, first_other, owned, flipped(owned_send, "seq", 1)))
    output = (middle + out_keep + flipped(out_send, "seq", 1).astype(jnp.float32)).astype(jnp.bfloat16)
    tokens_grad, sums_first = close(owned, own, grad_middle, gain_first, attend_weight)
    table_mine = jnp.dot(hot, line_grad.T, precision=highest).reshape(1, 2 * buckets)
    table_row = jnp.broadcast_to(jnp.pad(table_mine, ((0, 0), (0, group - 2 * buckets)))[:, None], (1, peers, group))
    small = jnp.concatenate([sums_first.reshape(2, peers, group), sums_second.reshape(2, peers, group), table_row]).transpose(1, 0, 2)
    small = jnp.pad(small, ((0, 0), (0, 3), (0, 0)))

    sums = lax.optimization_barrier((*attend_parts, *contract_parts, *expand_parts))
    attend_parts = send_second(*over_second(here, *sums[:4]))
    contract_own = over_all(*sums[4:6])
    contract_across = flipped(contract_own, "seq", 2)
    expand_parts = over_far(here, *sums[6:])
    small, *sums = lax.optimization_barrier((small, *attend_parts, contract_across, *expand_parts))
    attend_parts = over_near(here, *sums[:4])
    contract_grad = (contract_own, sums[4], flipped(contract_own, "seq", 1), flipped(sums[4], "seq", 1))
    small = small + flipped(small, "seq", 1)
    expand_own = over_all(*sums[5:])
    expand_across = flipped(expand_own, "seq", 2)
    small, expand_across, *attend_parts = lax.optimization_barrier((small, expand_across, *attend_parts))
    attend_parts = over_far(here, *attend_parts)
    small = small + flipped(small, "seq", 2)
    expand_grad = (expand_own, expand_across, flipped(expand_own, "seq", 1), flipped(expand_across, "seq", 1))
    small = to_all(small)
    contract_grad = _small_call(finish_contract_kernel, "finish_contract", [(2 * part, width)], jnp.float32, here, *contract_grad)[0]
    expand_grad, merge_grad = _small_call(
        partial(finish_expand_kernel, part), "finish_expand", [(group, hidden), (group, width)], jnp.float32, here, *expand_grad
    )
    attend_grad = of_all(over_all(*attend_parts))
    attend_grad = _small_call(finish_attend_kernel, "finish_attend", [(group, 3 * width)], jnp.float32, here, *attend_grad)[0]
    table_grad = small[:, 4, : 2 * buckets].reshape(peers, buckets, 2).transpose(1, 0, 2).reshape(buckets, heads)
    vectors = jnp.sum(small[:, :4], axis=0)
    return (
        output[None],
        tokens_grad[None],
        attend_grad,
        merge_grad,
        expand_grad,
        contract_grad,
        vectors[0],
        vectors[1],
        vectors[2],
        vectors[3],
        table_grad,
    )


def local(*arguments):
    heads = arguments[10].shape[1]
    rows = arguments[0].shape[1]
    peers = lax.axis_size("blk")
    if peers == 8 and lax.axis_size("seq") == 4 and heads == 2 * peers and rows == 256:
        return local_by_heads(*arguments)
    return local_by_runs(*arguments)


def solution(mesh):
    in_specs = (
        P("seq", "blk", None),
        P("seq", None),
        P(),
        P(),
        P(),
        P(),
        P(),
        P(),
        P(),
        P(),
        P(),
        P("seq", "blk", None),
    )
    out_specs = (
        P("seq", "blk", None),
        P("seq", "blk", None),
        P("blk", None),
        P("blk", None),
        P("blk", None),
        P("blk", None),
        P("blk"),
        P("blk"),
        P("blk"),
        P("blk"),
        P(),
    )
    return jax.shard_map(local, mesh=mesh, in_specs=in_specs, out_specs=out_specs, check_vma=False)
```

```python
from functools import partial
import math

import jax
import jax.numpy as jnp
from jax import lax
from jax.experimental import pallas as pl
from jax.experimental.pallas import tpu as pltpu
from jax.sharding import PartitionSpec as P

HOPS = 6


epsilon = 1e-05
masked_score = -1e30
highest = lax.Precision.HIGHEST
bucket_edges = [math.ceil(16 * 8 ** (t / 16)) for t in range(1, 16)]


def shifted(array, axis, by):
    peers = lax.axis_size(axis)
    pairs = [(i, i + by) for i in range(peers) if 0 <= i + by < peers]
    return lax.ppermute(array, axis, pairs)


def shortened(array):

    def short(part):
        return part.astype(jnp.bfloat16) if part.dtype == jnp.float32 else part

    return jax.tree.map(short, array)


def bucket_of(distance):
    total = jnp.minimum(jnp.maximum(distance, 0), 16)
    for edge in bucket_edges:
        total = total + (distance >= edge).astype(jnp.int32)
    return total


def segment_of(position, ends):
    return jnp.sum((position[:, None] >= ends[None, :]).astype(jnp.int32), axis=1)


def layer_norm(value, gain, shift):
    mean = jnp.mean(value, axis=-1, keepdims=True)
    centred = value - mean
    variance = jnp.mean(centred * centred, axis=-1, keepdims=True)
    return centred * lax.rsqrt(variance + epsilon) * gain + shift


def diagonal_sums(grid, count):
    heads = grid.shape[0]
    padded = jnp.pad(jnp.flip(grid, axis=-1), ((0, 0), (0, 0), (0, count)))
    flat = padded.reshape(heads, 2 * count * count)[:, : count * (2 * count - 1)]
    return jnp.sum(flat.reshape(heads, count, 2 * count - 1), axis=1)


def band_matrix(line, count):
    heads = line.shape[0]
    flipped = jnp.flip(line, axis=-1)
    tiled = jnp.tile(flipped, (1, count))
    window = tiled[:, count - 1 : count - 1 + count * (2 * count - 2)]
    return window.reshape(heads, count, 2 * count - 2)[:, :, :count]


def fetch_earlier(block):
    earlier = []
    moving = block
    for hop in range(HOPS):
        moving = shifted(moving, "blk", 1)
        earlier.append(moving)
    return earlier


def return_parts(parts):
    carried = jnp.zeros_like(parts[0])
    for hop in range(HOPS, 0, -1):
        carried = shifted(shortened(carried + parts[hop - 1]), "blk", -1)
    return carried


def local_by_runs(
    tokens,
    lengths,
    attend_weight,
    merge_weight,
    expand_weight,
    contract_weight,
    gain_first,
    shift_first,
    gain_second,
    shift_second,
    bias_table,
    cotangent,
):
    rows = tokens.shape[1]
    width = tokens.shape[2]
    heads = bias_table.shape[1]
    buckets = bias_table.shape[0]
    head_size = width // heads
    items = lengths.shape[1]
    start = lax.axis_index("blk") * rows
    query_pos = start + jnp.arange(rows, dtype=jnp.int32)
    ends = jnp.cumsum(lengths[0])
    query_seg = segment_of(query_pos, ends)
    band = jnp.arange(2 * rows - 1, dtype=jnp.int32) - (rows - 1)
    bucket_ids = jnp.arange(buckets, dtype=jnp.int32)

    def pair_setup(hop):
        key_pos = query_pos - hop * rows
        key_seg = segment_of(key_pos, ends)
        key_valid = (key_pos >= 0) & (key_seg < items)
        same = key_pos[None, :] == query_pos[:, None]
        allowed = (
            (query_seg[:, None] == key_seg[None, :])
            & (key_pos[None, :] <= query_pos[:, None])
            & (key_valid[None, :] | same)
        )
        onehot = (bucket_of(hop * rows + band)[:, None] == bucket_ids[None, :]).astype(jnp.float32)
        band_bias = jnp.dot(onehot, bias_table, precision=highest).T
        bias = band_matrix(band_bias, rows)
        additive = jnp.where(allowed[None], bias, masked_score)
        return (jnp.any(allowed), onehot, additive)

    pairs = [pair_setup(hop) for hop in range(HOPS + 1)]
    residual = tokens[0].astype(jnp.float32)
    normed_first, norm_first_pull = jax.vjp(layer_norm, residual, gain_first, shift_first)
    act_first = normed_first.astype(jnp.bfloat16)
    projected = jnp.dot(act_first, attend_weight, preferred_element_type=jnp.float32).astype(
        jnp.bfloat16
    )
    query = projected[:, :width].reshape(rows, heads, head_size)
    keys_values = jnp.stack([projected[:, width : 2 * width], projected[:, 2 * width :]])
    blocks = [keys_values] + fetch_earlier(keys_values)

    def scores_of(block, pair):
        key = block[0].reshape(rows, heads, head_size)
        raw = jnp.einsum("qhe,khe->hqk", query, key, preferred_element_type=jnp.float32) * 0.125
        return raw + pair[2]

    def empty_total():
        return jnp.full((heads, rows), masked_score, jnp.float32)

    def empty_scores():
        return jnp.full((heads, rows, rows), masked_score, jnp.float32)

    log_total = empty_total()
    kept_scores = []
    for block, pair in zip(blocks, pairs):

        def part_total(block=block, pair=pair):
            scores = scores_of(block, pair)
            peak = jnp.max(scores, axis=-1)
            return (peak + jnp.log(jnp.sum(jnp.exp(scores - peak[..., None]), axis=-1)), scores)

        def skip_total():
            return (empty_total(), empty_scores())

        part_log, scores = lax.cond(pair[0], part_total, skip_total)
        log_total = jnp.logaddexp(log_total, part_log)
        kept_scores.append(scores)

    def empty_heads():
        return jnp.zeros((rows, heads, head_size), jnp.float32)

    attended = empty_heads()
    for block, pair, scores in zip(blocks, pairs, kept_scores):

        def part_mix(block=block, scores=scores):
            weights = jnp.exp(scores - log_total[..., None]).astype(jnp.bfloat16)
            value = block[1].reshape(rows, heads, head_size)
            return jnp.einsum("hqk,khe->qhe", weights, value, preferred_element_type=jnp.float32)

        attended = attended + lax.cond(pair[0], part_mix, empty_heads)
    attn_low = attended.reshape(rows, width).astype(jnp.bfloat16)
    middle = residual + jnp.dot(attn_low, merge_weight, preferred_element_type=jnp.float32)
    normed_second, norm_second_pull = jax.vjp(layer_norm, middle, gain_second, shift_second)
    act_second = normed_second.astype(jnp.bfloat16)
    hidden_pre = jnp.dot(act_second, expand_weight, preferred_element_type=jnp.float32)
    hidden, gelu_pull = jax.vjp(partial(jax.nn.gelu, approximate=False), hidden_pre)
    hidden_low = hidden.astype(jnp.bfloat16)
    output = (
        middle + jnp.dot(hidden_low, contract_weight, preferred_element_type=jnp.float32)
    ).astype(jnp.bfloat16)
    grad_out = cotangent[0]
    contract_grad = jnp.einsum(
        "tf,td->fd", hidden_low, grad_out, preferred_element_type=jnp.float32
    )
    grad_hidden = jnp.einsum(
        "td,fd->tf", grad_out, contract_weight, preferred_element_type=jnp.float32
    )
    grad_pre = gelu_pull(grad_hidden)[0].astype(jnp.bfloat16)
    expand_grad = jnp.einsum("td,tf->df", act_second, grad_pre, preferred_element_type=jnp.float32)
    grad_second = jnp.einsum(
        "tf,df->td", grad_pre, expand_weight, preferred_element_type=jnp.float32
    )
    grad_middle_norm, gain_second_grad, shift_second_grad = norm_second_pull(grad_second)
    grad_middle = grad_out.astype(jnp.float32) + grad_middle_norm
    grad_middle_low = grad_middle.astype(jnp.bfloat16)
    merge_grad = jnp.einsum(
        "td,te->de", attn_low, grad_middle_low, preferred_element_type=jnp.float32
    )
    grad_heads = (
        jnp.einsum("te,de->td", grad_middle_low, merge_weight, preferred_element_type=jnp.float32)
        .astype(jnp.bfloat16)
        .reshape(rows, heads, head_size)
    )
    row_dot = jnp.sum(grad_heads.astype(jnp.float32) * attended, axis=-1).T
    back_blocks = [keys_values] + fetch_earlier(keys_values)

    def empty_grads():
        return (
            empty_heads(),
            jnp.zeros((2, rows, width), jnp.float32),
            jnp.zeros((buckets, heads), jnp.float32),
        )

    grad_query = empty_heads()
    table_local = jnp.zeros((buckets, heads), jnp.float32)
    parts = []
    for block, pair in zip(back_blocks, pairs):

        def part_grads(block=block, pair=pair):
            key = block[0].reshape(rows, heads, head_size)
            value = block[1].reshape(rows, heads, head_size)
            weights = jnp.exp(scores_of(block, pair) - log_total[..., None])
            weights_low = weights.astype(jnp.bfloat16)
            grad_weights = jnp.einsum(
                "qhe,khe->hqk", grad_heads, value, preferred_element_type=jnp.float32
            )
            grad_scores = (weights * (grad_weights - row_dot[..., None])).astype(jnp.bfloat16)
            query_part = (
                jnp.einsum("hqk,khe->qhe", grad_scores, key, preferred_element_type=jnp.float32)
                * 0.125
            )
            key_part = (
                jnp.einsum("hqk,qhe->khe", grad_scores, query, preferred_element_type=jnp.float32)
                * 0.125
            )
            value_part = jnp.einsum(
                "hqk,qhe->khe", weights_low, grad_heads, preferred_element_type=jnp.float32
            )
            line_grad = diagonal_sums(grad_scores.astype(jnp.float32), rows)
            table_part = jnp.dot(pair[1].T, line_grad.T, precision=highest)
            return (
                query_part,
                jnp.stack([key_part.reshape(rows, width), value_part.reshape(rows, width)]),
                table_part,
            )

        query_part, pair_part, table_part = lax.cond(pair[0], part_grads, empty_grads)
        grad_query = grad_query + query_part
        table_local = table_local + table_part
        parts.append(pair_part)
    owned = (parts[0] + return_parts(parts[1:])).astype(jnp.bfloat16)
    grad_project = jnp.concatenate(
        [grad_query.reshape(rows, width).astype(jnp.bfloat16), owned[0], owned[1]], axis=1
    )
    attend_grad = jnp.einsum(
        "td,te->de", act_first, grad_project, preferred_element_type=jnp.float32
    )
    grad_first = jnp.einsum(
        "te,de->td", grad_project, attend_weight, preferred_element_type=jnp.float32
    )
    grad_input_norm, gain_first_grad, shift_first_grad = norm_first_pull(grad_first)
    tokens_grad = grad_middle + grad_input_norm
    results = (
        lax.psum_scatter(attend_grad, "blk", scatter_dimension=0, tiled=True),
        lax.psum_scatter(merge_grad, "blk", scatter_dimension=0, tiled=True),
        lax.psum_scatter(expand_grad, "blk", scatter_dimension=0, tiled=True),
        lax.psum_scatter(contract_grad, "blk", scatter_dimension=0, tiled=True),
        lax.psum_scatter(gain_first_grad, "blk", scatter_dimension=0, tiled=True),
        lax.psum_scatter(shift_first_grad, "blk", scatter_dimension=0, tiled=True),
        lax.psum_scatter(gain_second_grad, "blk", scatter_dimension=0, tiled=True),
        lax.psum_scatter(shift_second_grad, "blk", scatter_dimension=0, tiled=True),
    )
    results = (
        lax.psum(results[0].astype(jnp.bfloat16), "seq").astype(jnp.float32),
        lax.psum(results[1].astype(jnp.bfloat16), "seq").astype(jnp.float32),
        lax.psum(results[2].astype(jnp.bfloat16), "seq").astype(jnp.float32),
        lax.psum(results[3].astype(jnp.bfloat16), "seq").astype(jnp.float32),
        lax.psum(results[4].astype(jnp.bfloat16), "seq").astype(jnp.float32),
        lax.psum(results[5].astype(jnp.bfloat16), "seq").astype(jnp.float32),
        lax.psum(results[6].astype(jnp.bfloat16), "seq").astype(jnp.float32),
        lax.psum(results[7].astype(jnp.bfloat16), "seq").astype(jnp.float32),
    )
    table_grad = lax.psum(table_local, ("seq", "blk"))
    return (
        output[None],
        tokens_grad[None],
        results[0],
        results[1],
        results[2],
        results[3],
        results[4],
        results[5],
        results[6],
        results[7],
        table_grad,
    )


def _segments(position, meta_ref, first, items):
    total = jnp.zeros(position.shape, jnp.int32)
    for item in range(items):
        total = total + (position >= meta_ref[first + item]).astype(jnp.int32)
    return total

def _allowed(meta_ref, peers, items, rows, i, j, which, needed):
    first = 1 + 2 * peers
    q_seg = _segments(i * rows + lax.broadcasted_iota(jnp.int32, (1, rows), 1), meta_ref, first, items)
    k_seg = _segments(j * rows + lax.broadcasted_iota(jnp.int32, (rows, 1), 0), meta_ref, first, items)
    k_seg = jnp.where((k_seg < items) & needed if which == 1 else k_seg < items, k_seg, -1)
    same = q_seg == k_seg
    if which == 0:
        key = lax.broadcasted_iota(jnp.int32, (rows, rows), 0)
        query = lax.broadcasted_iota(jnp.int32, (rows, rows), 1)
        return (same & (key < query)) | (key == query)
    return same

def _dot(a, b, dims):
    return lax.dot_general(a, b, (dims, ((), ())), preferred_element_type=jnp.float32)

def _turned(array):
    return jnp.transpose(array.astype(jnp.float32))

def _split(array, axis=1):
    wide = array.astype(jnp.float32)
    left = lax.broadcasted_iota(jnp.int32, array.shape, axis) < 64
    return jnp.where(left, wide, 0.0).astype(jnp.bfloat16), jnp.where(left, 0.0, wide).astype(jnp.bfloat16)

def _fold(value, op):
    while value.shape[0] > 8:
        half = value.shape[0] // 2
        value = op(value[:half], value[half:])
    return value

def _put_bias(bias, line_ref, rows):
    for head in range(2):
        line = jnp.broadcast_to(line_ref[head:head + 1, :], (rows, 2 * rows))
        bias[head] = pltpu.roll(line, 0, 1, stride=1, stride_axis=0)

def _biased(raw, bias, far_ref, head, which, rows):
    if which == 0:
        return raw + bias[head, :, :rows]
    if which == 1:
        return raw + bias[head, :, rows:]
    return raw + far_ref[head]

def attend_kernel(peers, items, rows, meta_ref, far_ref, line_ref, *refs):
    parts = refs[:peers]
    mixed, wide_ref, log_ref, qkv, turned, bias, scores = refs[peers:]
    me = meta_ref[0]
    for slot in range(peers):
        qkv[me ^ slot] = parts[slot][...]
        turned[me ^ slot] = _turned(parts[slot][2]).astype(jnp.bfloat16)
    _put_bias(bias, line_ref, rows)
    upper = lax.broadcasted_iota(jnp.int32, (128, rows), 0) < 64

    def one_row(i, _):
        low = meta_ref[1 + i]
        whole = jnp.minimum(meta_ref[1 + peers + i], i - 1)
        queries = _split(qkv[i, 0].astype(jnp.float32) * 0.125)

        def put(j, slot, which, masked, peaks):
            key = qkv[j, 1]
            if masked:
                allowed = _allowed(meta_ref, peers, items, rows, i, j, which, low < i)
            new = []
            for head in range(2):
                raw = _biased(_dot(key, queries[head], ((1,), (1,))), bias, far_ref, head, which, rows)
                if masked:
                    raw = jnp.where(allowed, raw, masked_score)
                scores[head, slot] = raw
                new.append(jnp.maximum(peaks[head], _fold(raw, jnp.maximum)))
            return tuple(new)

        start = jnp.full((8, rows), masked_score, jnp.float32)
        before = jnp.maximum(i - 1, 0)
        peaks = put(i, peers, 0, True, (start, start))
        peaks = put(before, peers + 1, 1, True, peaks)
        peaks = lax.fori_loop(low, whole, lambda j, p: put(j, j, 2, True, p), peaks)
        peaks = lax.fori_loop(jnp.maximum(low, whole), i - 1, lambda j, p: put(j, j, 2, False, p), peaks)
        tops = [jnp.max(peak, axis=0, keepdims=True) for peak in peaks]

        def mix(j, slot, carry):
            sums, total = carry
            value = turned[j]
            new = []
            both = []
            for head in range(2):
                weight = jnp.exp(scores[head, slot] - tops[head])
                new.append(sums[head] + _fold(weight, jnp.add))
                both.append(_dot(value[64 * head:64 * head + 64], weight.astype(jnp.bfloat16), ((1,), (0,))))
            return tuple(new), total + jnp.concatenate(both)

        nothing = jnp.zeros((8, rows), jnp.float32)
        carry = ((nothing, nothing), jnp.zeros((128, rows), jnp.float32))
        carry = mix(before, peers + 1, mix(i, peers, carry))
        sums, total = lax.fori_loop(low, i - 1, lambda j, c: mix(j, j, c), carry)
        sums = [jnp.sum(s, axis=0, keepdims=True) for s in sums]
        total = total / jnp.where(upper, sums[0], sums[1])
        wide_ref[i] = total
        for head in range(2):
            log_ref[i, head:head + 1, :] = tops[head] + jnp.log(sums[head])
        mixed[i] = jnp.transpose(total).astype(jnp.bfloat16)
        return 0

    lax.fori_loop(0, peers, one_row, 0)

def attend(meta, far, line, parts, items):
    peers = len(parts)
    rows = parts[0].shape[1]
    smem = pl.BlockSpec(memory_space=pltpu.SMEM)
    vmem = pl.BlockSpec(memory_space=pltpu.VMEM)
    shapes = [
        jax.ShapeDtypeStruct((peers, rows, 128), jnp.bfloat16),
        jax.ShapeDtypeStruct((peers, 128, rows), jnp.float32),
        jax.ShapeDtypeStruct((peers, 8, rows), jnp.float32),
        jax.ShapeDtypeStruct((peers, 3, rows, 128), jnp.bfloat16),
    ]
    res = pl.pallas_call(
        partial(attend_kernel, peers, items, rows),
        out_shape=shapes,
        in_specs=[smem, smem] + [vmem] * (peers + 1),
        out_specs=[vmem] * 4,
        scratch_shapes=[
            pltpu.VMEM((peers, 128, rows), jnp.bfloat16),
            pltpu.VMEM((2, rows, 2 * rows), jnp.float32),
            pltpu.VMEM((2, peers + 2, rows, rows), jnp.float32),
        ],
        compiler_params=pltpu.CompilerParams(vmem_limit_bytes=18 * 2**20),
        cost_estimate=pl.CostEstimate(flops=8 * 10**9, bytes_accessed=4 * 2**20, transcendentals=3 * 10**6),
        name="attend",
    )(meta, far, line, *parts)
    return res

def attend_back_kernel(peers, items, rows, meta_ref, far_ref, line_ref, wide_ref, log_ref, cot, qkv, *refs):
    all_ref, table_ref, turned, bias, near, far_sum, dkey, dvalue = refs
    for peer in range(peers):
        turned[peer] = _turned(qkv[peer, 1]).astype(jnp.bfloat16)
    _put_bias(bias, line_ref, rows)
    near[...] = jnp.zeros_like(near)
    far_sum[...] = jnp.zeros_like(far_sum)
    dkey[...] = jnp.zeros_like(dkey)
    dvalue[...] = jnp.zeros_like(dvalue)

    def one_row(i, _):
        low = meta_ref[1 + i]
        whole = jnp.minimum(meta_ref[1 + peers + i], i - 1)
        queries = _split(qkv[i, 0].astype(jnp.float32) * 0.125)
        grad = cot[i]
        grads_ = _split(grad)
        product = _turned(grad) * wide_ref[i]
        dots = [jnp.sum(product[64 * head:64 * head + 64], axis=0, keepdims=True) for head in range(2)]
        logs = [log_ref[i, head:head + 1, :] for head in range(2)]

        def step(j, which, masked, dquery):
            key = qkv[j, 1]
            value = qkv[j, 2]
            across = turned[j]
            if masked:
                allowed = _allowed(meta_ref, peers, items, rows, i, j, which, low < i)
            dk = jnp.zeros((rows, 128), jnp.float32)
            dv = jnp.zeros((rows, 128), jnp.float32)
            both = []
            for head in range(2):
                raw = _biased(_dot(key, queries[head], ((1,), (1,))), bias, far_ref, head, which, rows)
                if masked:
                    raw = jnp.where(allowed, raw, masked_score)
                weight = jnp.exp(raw - logs[head])
                dweight = _dot(value, grads_[head], ((1,), (1,)))
                dscore = weight * (dweight - dots[head])
                low_score = dscore.astype(jnp.bfloat16)
                if which == 0:
                    near[head, :, :rows] += dscore
                elif which == 1:
                    near[head, :, rows:] += dscore
                else:
                    far_sum[head] += _fold(dscore, jnp.add)
                both.append(_dot(across[64 * head:64 * head + 64], low_score, ((1,), (0,))))
                dk = dk + _dot(low_score, queries[head], ((1,), (0,)))
                dv = dv + _dot(weight.astype(jnp.bfloat16), grads_[head], ((1,), (0,)))
            dkey[j] += dk
            dvalue[j] += dv
            return dquery + jnp.concatenate(both)

        dquery = step(i, 0, True, jnp.zeros((128, rows), jnp.float32))
        dquery = step(jnp.maximum(i - 1, 0), 1, True, dquery)
        dquery = lax.fori_loop(low, whole, lambda j, d: step(j, 2, True, d), dquery)
        dquery = lax.fori_loop(jnp.maximum(low, whole), i - 1, lambda j, d: step(j, 2, False, d), dquery)
        all_ref[i, 0] = (jnp.transpose(dquery) * 0.125).astype(jnp.bfloat16)
        return 0

    lax.fori_loop(0, peers, one_row, 0)
    for i in range(peers):
        all_ref[i, 1] = dkey[i].astype(jnp.bfloat16)
        all_ref[i, 2] = dvalue[i].astype(jnp.bfloat16)
    wide = 2 * rows
    sub = lax.broadcasted_iota(jnp.int32, (8, wide), 0)
    for head in range(2):
        part = near[head]
        count = rows
        while count > 8:
            count //= 2
            part = part[:count] + pltpu.roll(part[count:], wide - count, 1)
        for bit in (4, 2, 1):
            part = jnp.where((sub & bit) != 0, pltpu.roll(part, wide - bit, 1), part)
        total = far_sum[head]
        table_ref[head, :, :rows] = part[:, :rows]
        table_ref[head, :, rows:] = part[:, rows:] + jnp.concatenate([jnp.zeros((8, rows - 128), jnp.float32), total[:, :128] + total[:, 128:]], axis=1)

def attend_back(meta, far, line, wide, logs, qkv, grads, items):
    peers, _, rows, _ = qkv.shape
    smem = pl.BlockSpec(memory_space=pltpu.SMEM)
    vmem = pl.BlockSpec(memory_space=pltpu.VMEM)
    shapes = [
        jax.ShapeDtypeStruct((peers, 3, rows, 128), jnp.bfloat16),
        jax.ShapeDtypeStruct((2, 8, 2 * rows), jnp.float32),
    ]
    res = pl.pallas_call(
        partial(attend_back_kernel, peers, items, rows),
        out_shape=shapes,
        in_specs=[smem, smem] + [vmem] * 5,
        out_specs=[vmem] * 2,
        scratch_shapes=[
            pltpu.VMEM((peers, 128, rows), jnp.bfloat16),
            pltpu.VMEM((2, rows, 2 * rows), jnp.float32),
            pltpu.VMEM((2, rows, 2 * rows), jnp.float32),
            pltpu.VMEM((2, 8, rows), jnp.float32),
            pltpu.VMEM((peers, rows, 128), jnp.float32),
            pltpu.VMEM((peers, rows, 128), jnp.float32),
        ],
        compiler_params=pltpu.CompilerParams(vmem_limit_bytes=18 * 2**20),
        cost_estimate=pl.CostEstimate(flops=20 * 10**9, bytes_accessed=8 * 2**20, transcendentals=3 * 10**6),
        name="attend_back",
    )(meta, far, line, wide, logs, grads, qkv)
    return res[0], jnp.sum(res[1], axis=1)

def plan(lengths, me, peers, rows):
    ends = jnp.cumsum(lengths)
    items = lengths.shape[0]
    place = jnp.arange(peers, dtype=jnp.int32)
    first = jnp.sum((place[:, None] * rows >= ends[None]).astype(jnp.int32), axis=1)
    last = jnp.sum((place[:, None] * rows + rows - 1 >= ends[None]).astype(jnp.int32), axis=1)
    low = jnp.sum((last[None, :] < first[:, None]).astype(jnp.int32), axis=1)
    low = jnp.where(first < items, jnp.minimum(low, place), place)
    whole = jnp.sum((first[None, :] < last[:, None]).astype(jnp.int32), axis=1)
    return jnp.concatenate([me[None].astype(jnp.int32), low, whole, ends.astype(jnp.int32)])
def bucket_lines(rows, buckets):
    k = jnp.arange(2 * rows, dtype=jnp.int32)
    return (bucket_of(k)[None, :] == jnp.arange(buckets, dtype=jnp.int32)[:, None]).astype(jnp.float32)


def _unit(value):
    mean = jnp.mean(value, axis=-1, keepdims=True)
    centred = value - mean
    variance = jnp.mean(centred * centred, axis=-1, keepdims=True)
    scale = lax.rsqrt(variance + epsilon)
    return centred * scale, scale


def _norm_back(grad, unit, scale, gain, sums_ref):
    inner = grad * gain
    first = jnp.mean(inner, axis=-1, keepdims=True)
    second = jnp.mean(inner * unit, axis=-1, keepdims=True)
    sums_ref[0:1, :] = jnp.sum(grad * unit, axis=0, keepdims=True)
    sums_ref[1:2, :] = jnp.sum(grad, axis=0, keepdims=True)
    return scale * (inner - first - unit * second)


def _lanes(index):
    return pl.ds(pl.multiple_of(index * 128, 128), 128)


def _specs(*kinds):
    places = {"s": pltpu.SMEM, "v": pltpu.VMEM, "h": pltpu.HBM}
    return [pl.BlockSpec(memory_space=places[kind]) for word in kinds for kind in word]


def _params(mebibytes):
    return pltpu.CompilerParams(vmem_limit_bytes=mebibytes * 2**20)


def project_kernel(peers, meta_ref, tokens_ref, gain_ref, shift_ref, weight_ref, *refs):
    outs, act_ref, held, done, arrived = refs[:peers], refs[peers], refs[peers + 1], refs[peers + 2], refs[peers + 3]
    me = meta_ref[0]
    pieces, _, span = held.shape
    copies = []
    for piece in range(pieces):
        copies.append(pltpu.make_async_copy(weight_ref.at[:, pl.ds(piece * span, span)], held.at[piece], arrived.at[piece]))
        copies[-1].start()
    unit, _ = _unit(tokens_ref[...].astype(jnp.float32))
    act = (unit * gain_ref[...] + shift_ref[...]).astype(jnp.bfloat16)
    act_ref[...] = act
    for piece in range(pieces):
        copies[piece].wait()
        got = _dot(act, held[piece], ((1,), (0,))).astype(jnp.bfloat16)
        for block in range(span // 128):
            done[piece * (span // 128) + block] = got[:, 128 * block : 128 * block + 128]
    for slot in range(peers):
        for block in range(3):
            outs[slot][block] = done[block * peers + (me ^ slot)]


def project(meta, tokens, gain, shift, weight, peers):
    rows, width = tokens.shape
    span = 512
    pieces = weight.shape[1] // span
    return pl.pallas_call(
        partial(project_kernel, peers),
        out_shape=[jax.ShapeDtypeStruct((3, rows, 128), jnp.bfloat16)] * peers + [jax.ShapeDtypeStruct((rows, width), jnp.bfloat16)],
        in_specs=_specs("svvvh"),
        out_specs=_specs("v" * (peers + 1)),
        scratch_shapes=[
            pltpu.VMEM((pieces, width, span), jnp.bfloat16),
            pltpu.VMEM((3 * peers, rows, 128), jnp.bfloat16),
            pltpu.SemaphoreType.DMA((pieces,)),
        ],
        compiler_params=_params(60),
        cost_estimate=pl.CostEstimate(flops=4 * 10**9, bytes_accessed=8 * 2**20, transcendentals=0),
        name="project",
    )(meta, tokens, gain, shift, weight)


def merge_kernel(parts_ref, tokens_ref, gain_ref, shift_ref, weight_ref, low_ref, middle_ref, act_ref):
    for part in range(parts_ref.shape[0]):
        low_ref[:, 128 * part : 128 * part + 128] = parts_ref[part]
    middle = tokens_ref[...].astype(jnp.float32) + _dot(low_ref[...], weight_ref[...], ((1,), (0,)))
    middle_ref[...] = middle
    unit, _ = _unit(middle)
    act_ref[...] = (unit * gain_ref[...] + shift_ref[...]).astype(jnp.bfloat16)


def merge(parts, tokens, gain, shift, weight):
    return pl.pallas_call(
        merge_kernel,
        out_shape=[jax.ShapeDtypeStruct(tokens.shape, t) for t in (jnp.bfloat16, jnp.float32, jnp.bfloat16)],
        in_specs=_specs("vvvvv"),
        out_specs=_specs("vvv"),
        compiler_params=_params(12),
        cost_estimate=pl.CostEstimate(flops=10**9, bytes_accessed=5 * 2**20, transcendentals=0),
        name="merge",
    )(parts, tokens, gain, shift, weight)


def _both(ref, mine, other):
    rows = mine.shape[0]
    ref[:rows] = mine[...]
    ref[rows:] = other[...]


def _whole(*shape):
    return pl.BlockSpec(shape, lambda step, meta_ref: (0,) * len(shape))


def _across(rows, columns):
    return pl.BlockSpec((rows, columns), lambda step, meta_ref: (0, step))


def pull_kernel(meta_ref, mine, other, contract_ref, out_ref, grads):
    @pl.when(pl.program_id(0) == 0)
    def _():
        _both(grads, mine, other)

    out_ref[...] = _dot(grads[...], contract_ref[...], ((1,), (1,)))


def pull(meta, mine, other, contract_weight, peers):
    rows, width = mine.shape
    part = contract_weight.shape[0] // (2 * peers)
    return pl.pallas_call(
        pull_kernel,
        out_shape=jax.ShapeDtypeStruct((2 * rows, peers * part), jnp.float32),
        grid_spec=pltpu.PrefetchScalarGridSpec(
            num_scalar_prefetch=1,
            grid=(peers,),
            in_specs=[_whole(rows, width)] * 2 + [pl.BlockSpec((part, width), lambda step, meta_ref: (2 * step + meta_ref[3], 0))],
            out_specs=_across(2 * rows, part),
            scratch_shapes=[pltpu.VMEM((2 * rows, width), jnp.bfloat16)],
        ),
        compiler_params=_params(16),
        cost_estimate=pl.CostEstimate(flops=3 * 10**9, bytes_accessed=9 * 2**20, transcendentals=0),
        name="pull",
    )(meta, mine, other, contract_weight)


def feed_kernel(
    rows, part, meta_ref, act_mine, act_other, pulled_ref, expand_ref, in_keep, in_send, low_ref, back_ref, acts, weights, total, arrived
):
    core = meta_ref[3]
    pieces = weights.shape[1] // part
    copies = []
    for piece in range(pieces):
        columns = pl.ds(pl.multiple_of((2 * piece + core) * part, part), part)
        here = weights.at[:, pl.ds(piece * part, part)]
        copies.append(pltpu.make_async_copy(expand_ref.at[:, columns], here, arrived.at[piece]))
        copies[-1].start()
    _both(acts, act_mine, act_other)

    def before(piece):
        copies[piece].wait()
        return _dot(acts[...], weights[:, piece * part : (piece + 1) * part], ((1,), (0,)))

    now = before(0)
    for piece in range(pieces):
        later = before(piece + 1) if piece + 1 < pieces else None
        span = slice(piece * part, (piece + 1) * part)
        rate = 0.5 * (1.0 + lax.erf(now * math.sqrt(0.5)))
        low_ref[:, span] = (now * rate).astype(jnp.bfloat16)
        slope = rate + now * jnp.exp(-0.5 * now * now) * (1.0 / math.sqrt(2.0 * math.pi))
        back_ref[:, span] = (pulled_ref[:, span] * slope).astype(jnp.bfloat16)
        if piece % 2 == 1:
            pair = slice((piece - 1) * part, (piece + 1) * part)
            got = _dot(back_ref[:, pair], weights[:, pair], ((1,), (1,)))
            if piece == 1:
                total[...] = got
            elif piece + 1 < pieces:
                total[...] += got
            else:
                in_keep[...] = total[:rows] + got[:rows]
                in_send[...] = total[rows:] + got[rows:]
        now = later


def feed(meta, act_mine, act_other, pulled, expand_weight, peers):
    rows, width = act_mine.shape
    part = expand_weight.shape[1] // (2 * peers)
    shapes = [
        ((rows, width), jnp.float32),
        ((rows, width), jnp.float32),
        ((2 * rows, peers * part), jnp.bfloat16),
        ((2 * rows, peers * part), jnp.bfloat16),
    ]
    return pl.pallas_call(
        partial(feed_kernel, rows, part),
        out_shape=[jax.ShapeDtypeStruct(*shape) for shape in shapes],
        in_specs=_specs("svvvh"),
        out_specs=_specs("vvvv"),
        scratch_shapes=[
            pltpu.VMEM((2 * rows, width), jnp.bfloat16),
            pltpu.VMEM((width, peers * part), jnp.bfloat16),
            pltpu.VMEM((2 * rows, width), jnp.float32),
            pltpu.SemaphoreType.DMA((peers,)),
        ],
        compiler_params=_params(40),
        cost_estimate=pl.CostEstimate(flops=8 * 10**9, bytes_accessed=20 * 2**20, transcendentals=2 * 10**6),
        name="feed",
    )(meta, act_mine, act_other, pulled, expand_weight)


def _split_rows(held, x, y, one_keep, one_send, two_keep, two_send):
    peers, rows, _ = held.shape
    cut, half = one_keep.shape[2], rows // 2
    mine = pl.ds(pl.multiple_of(y * half, half), half)
    other = pl.ds(pl.multiple_of((1 - y) * half, half), half)
    for place in range(peers // 2):
        one_keep[place] = held[2 * place + x, :, :cut]
        one_send[place] = held[2 * place + 1 - x, :, :cut]
    for place in range(peers):
        two_keep[place] = held[place, mine, cut:]
        two_send[place] = held[place, other, cut:]


def contract_weigh_kernel(meta_ref, grad_mine, grad_other, low_ref, *refs):
    outs, grads, held = refs[:4], refs[4], refs[5]
    _both(grads, grad_mine, grad_other)
    part = held.shape[1]
    for piece in range(held.shape[0]):
        held[piece] = _dot(low_ref[:, piece * part : (piece + 1) * part], grads[...], ((0,), (0,))).astype(jnp.bfloat16)
    _split_rows(held, meta_ref[1], meta_ref[2], *outs)


def contract_weigh(meta, grad_mine, grad_other, low, peers):
    rows, width = grad_mine.shape
    part, cut = low.shape[1] // peers, width // 2
    shapes = [(peers // 2, part, cut), (peers // 2, part, cut), (peers, part // 2, cut), (peers, part // 2, cut)]
    return pl.pallas_call(
        contract_weigh_kernel,
        out_shape=[jax.ShapeDtypeStruct(shape, jnp.bfloat16) for shape in shapes],
        in_specs=_specs("svvv"),
        out_specs=_specs("vvvv"),
        scratch_shapes=[pltpu.VMEM((2 * rows, width), jnp.bfloat16), pltpu.VMEM((peers, part, width), jnp.bfloat16)],
        compiler_params=_params(14),
        cost_estimate=pl.CostEstimate(flops=10**8, bytes_accessed=2**20, transcendentals=0),
        name="contract_weigh",
    )(meta, grad_mine, grad_other, low)


def weigh_kernel(meta_ref, act_mine, act_other, mix_mine, mix_other, right_mine, right_other, back_ref, *refs):
    outs, left, held = refs[:4], refs[4], refs[5]
    peers, group, span = held.shape
    wide = back_ref.shape[1] // 2
    cut = span // 2
    _both(left, mix_mine, mix_other)
    right = jnp.concatenate([right_mine[...], right_other[...]])
    grad = _dot(left[...], right, ((0,), (0,))).astype(jnp.bfloat16)
    quarter = grad.shape[1] // 2
    held[:, :, wide:cut] = grad[:, :quarter].reshape(peers, group, quarter)
    held[:, :, cut + wide :] = grad[:, quarter:].reshape(peers, group, quarter)
    _both(left, act_mine, act_other)
    for side in range(2):
        grad = _dot(left[...], back_ref[:, side * wide : (side + 1) * wide], ((0,), (0,))).astype(jnp.bfloat16)
        held[:, :, side * cut : side * cut + wide] = grad.reshape(peers, group, wide)
    _split_rows(held, meta_ref[1], meta_ref[2], *outs)


def weigh(meta, act_mine, act_other, mix_mine, mix_other, right_mine, right_other, back, peers):
    rows, width = act_mine.shape
    group, cut = width // peers, back.shape[1] // 2 + width // 4
    shapes = [(peers // 2, group, cut), (peers // 2, group, cut), (peers, group // 2, cut), (peers, group // 2, cut)]
    return pl.pallas_call(
        weigh_kernel,
        out_shape=[jax.ShapeDtypeStruct(shape, jnp.bfloat16) for shape in shapes],
        in_specs=_specs("svvvvvvv"),
        out_specs=_specs("vvvv"),
        scratch_shapes=[pltpu.VMEM((2 * rows, width), jnp.bfloat16), pltpu.VMEM((peers, group, 2 * cut), jnp.bfloat16)],
        compiler_params=_params(20),
        cost_estimate=pl.CostEstimate(flops=10**8, bytes_accessed=2**20, transcendentals=0),
        name="weigh",
    )(meta, act_mine, act_other, mix_mine, mix_other, right_mine, right_other, back)


def emit_kernel(meta_ref, low_ref, contract_ref, keep_ref, send_ref, weights, arrived):
    core = meta_ref[3]
    rows, pieces = keep_ref.shape[0], arrived.shape[0]
    part = weights.shape[0] // pieces
    copies = []
    for piece in range(pieces):
        at = pl.ds(pl.multiple_of((2 * piece + core) * part, part), part)
        copies.append(pltpu.make_async_copy(contract_ref.at[at], weights.at[pl.ds(piece * part, part)], arrived.at[piece]))
        copies[-1].start()
    for copy in copies:
        copy.wait()
    keep_ref[...] = _dot(low_ref[:rows], weights[...], ((1,), (0,)))
    send_ref[...] = _dot(low_ref[rows:], weights[...], ((1,), (0,))).astype(jnp.bfloat16)


def emit(meta, low, contract_weight, peers):
    rows, width = low.shape[0] // 2, contract_weight.shape[1]
    return pl.pallas_call(
        emit_kernel,
        out_shape=[jax.ShapeDtypeStruct((rows, width), jnp.float32), jax.ShapeDtypeStruct((rows, width), jnp.bfloat16)],
        in_specs=_specs("svh"),
        out_specs=_specs("vv"),
        scratch_shapes=[pltpu.VMEM((low.shape[1], width), jnp.bfloat16), pltpu.SemaphoreType.DMA((peers,))],
        compiler_params=_params(30),
        cost_estimate=pl.CostEstimate(flops=2 * 10**9, bytes_accessed=8 * 2**20, transcendentals=0),
        name="emit",
    )(meta, low, contract_weight)


def turn_kernel(meta_ref, in_mine, in_other, middle_ref, grad_ref, gain_ref, weight_ref, heads_ref, total_ref, keep_ref, send_ref, sums_ref):
    core = meta_ref[3]
    half = keep_ref.shape[1]
    unit, scale = _unit(middle_ref[...])
    total = grad_ref[...].astype(jnp.float32) + _norm_back(in_mine[...] + in_other[...], unit, scale, gain_ref[...], sums_ref)
    total_ref[...] = total
    low = total.astype(jnp.bfloat16)

    @pl.when(core == 0)
    def _():
        keep_ref[...] = low[:, :half]
        send_ref[...] = low[:, half:]

    @pl.when(core != 0)
    def _():
        keep_ref[...] = low[:, half:]
        send_ref[...] = low[:, :half]

    heads = _dot(low, weight_ref[...], ((1,), (1,))).astype(jnp.bfloat16)
    for part in range(heads_ref.shape[0]):
        heads_ref[part] = heads[:, 128 * part : 128 * part + 128]


def turn(meta, in_mine, in_other, middle, grad, gain, weight, peers):
    rows, width = middle.shape
    shapes = [
        ((peers, rows, width // peers), jnp.bfloat16),
        ((rows, width), jnp.float32),
        ((rows, width // 2), jnp.bfloat16),
        ((rows, width // 2), jnp.bfloat16),
        ((2, width), jnp.float32),
    ]
    return pl.pallas_call(
        turn_kernel,
        out_shape=[jax.ShapeDtypeStruct(*shape) for shape in shapes],
        in_specs=_specs("svvvvvv"),
        out_specs=_specs("v" * len(shapes)),
        compiler_params=_params(12),
        cost_estimate=pl.CostEstimate(flops=10**9, bytes_accessed=8 * 2**20, transcendentals=0),
        name="turn",
    )(meta, in_mine, in_other, middle, grad, gain, weight)


def close_kernel(parts_ref, tokens_ref, grad_ref, gain_ref, weight_ref, out_ref, sums_ref, held):
    peers = parts_ref.shape[0]
    for peer in range(peers):
        for block in range(3):
            at = 128 * (block * peers + peer)
            held[:, at : at + 128] = parts_ref[peer, block]
    back = _dot(held[...], weight_ref[...], ((1,), (1,)))
    unit, scale = _unit(tokens_ref[...].astype(jnp.float32))
    out_ref[...] = grad_ref[...] + _norm_back(back, unit, scale, gain_ref[...], sums_ref)


def close(parts, tokens, grad, gain, weight):
    rows, width = tokens.shape
    return pl.pallas_call(
        close_kernel,
        out_shape=[jax.ShapeDtypeStruct((rows, width), jnp.float32), jax.ShapeDtypeStruct((2, width), jnp.float32)],
        in_specs=_specs("vvvvv"),
        out_specs=_specs("vv"),
        scratch_shapes=[pltpu.VMEM((rows, 3 * width), jnp.bfloat16)],
        compiler_params=_params(16),
        cost_estimate=pl.CostEstimate(flops=2 * 10**9, bytes_accessed=10 * 2**20, transcendentals=0),
        name="close",
    )(parts, tokens, grad, gain, weight)


def _plus(a, b):
    return (a.astype(jnp.float32) + b.astype(jnp.float32)).astype(jnp.bfloat16)


def second_kernel(meta_ref, one_keep, one_got, two_keep, two_got, one_left, one_send, two_left, two_send):
    x, y = meta_ref[1], meta_ref[2]
    levels, half, _ = one_left.shape
    mine = pl.ds(pl.multiple_of(y * half, half), half)
    other = pl.ds(pl.multiple_of((1 - y) * half, half), half)
    for level in range(levels):
        one_left[level] = _plus(one_keep[level, mine], one_got[level, mine])
        one_send[level] = _plus(one_keep[level, other], one_got[level, other])
        two_left[level] = _plus(two_keep[2 * level + x], two_got[2 * level + x])
        two_send[level] = _plus(two_keep[2 * level + 1 - x], two_got[2 * level + 1 - x])


def near_kernel(meta_ref, one_keep, one_got, two_keep, two_got, left, send):
    side = (meta_ref[0] >> 1) & 1
    cut = one_keep.shape[2]
    for level in range(left.shape[0]):
        for out, at in ((left, 2 * level + side), (send, 2 * level + 1 - side)):
            out[level, :, :cut] = _plus(one_keep[at], one_got[at])
            out[level, :, cut:] = _plus(two_keep[at], two_got[at])


def far_kernel(meta_ref, keep, got, left, send):
    upper = meta_ref[0] >> 2
    left[...] = _plus(keep[upper], got[upper])
    send[...] = _plus(keep[1 - upper], got[1 - upper])


def last_kernel(keep, got, out):
    out[...] = _plus(keep[...], got[...])


def _small_call(kernel, name, shapes, kind, *arguments):
    size = sum(2 * math.prod(a.shape) for a in arguments[-4:])
    return pl.pallas_call(
        kernel,
        out_shape=[jax.ShapeDtypeStruct(shape, kind) for shape in shapes],
        in_specs=_specs(*("s" if a.dtype == jnp.int32 else "v" for a in arguments)),
        out_specs=_specs("v" * len(shapes)),
        compiler_params=_params(10),
        cost_estimate=pl.CostEstimate(flops=size, bytes_accessed=3 * size, transcendentals=0),
        name=name,
    )(*arguments)


def _places(meta_ref, half):
    y, core = meta_ref[2], meta_ref[3]
    return [(c, pl.ds(pl.multiple_of(h * half, half), half)) for c in (core, 1 - core) for h in (y, 1 - y)]


def finish_contract_kernel(meta_ref, *refs):
    half = refs[0].shape[0]
    y, core = meta_ref[2], meta_ref[3]
    starts = [(2 * c + h) * half for c in (core, 1 - core) for h in (y, 1 - y)]
    for part, start in zip(refs[:4], starts):
        refs[4][pl.ds(pl.multiple_of(start, half), half), :] = part[...].astype(jnp.float32)


def finish_expand_kernel(part, meta_ref, *refs):
    expand_ref, merge_ref = refs[4:]
    half, span = refs[0].shape[0], refs[0].shape[1] // 2
    near = span // part - 1
    for source, (core, rows) in zip(refs[:4], _places(meta_ref, half)):
        for side in range(2):
            for block in range(near):
                at = pl.multiple_of((2 * (side * near + block) + core) * part, part)
                start = side * span + block * part
                expand_ref[rows, pl.ds(at, part)] = source[:, start : start + part].astype(jnp.float32)
            at = pl.multiple_of((2 * core + side) * part, part)
            start = side * span + near * part
            merge_ref[rows, pl.ds(at, part)] = source[:, start : start + part].astype(jnp.float32)


def finish_attend_kernel(meta_ref, *refs):
    half, wide = refs[0].shape
    span = wide // 3
    for source, (core, rows) in zip(refs[:4], _places(meta_ref, half)):
        for block in range(3):
            at = pl.multiple_of((2 * block + core) * span, span)
            refs[4][rows, pl.ds(at, span)] = source[:, block * span : (block + 1) * span].astype(jnp.float32)


def attend_weigh_kernel(
    meta_ref, act_mine, act_other, owned_ref, other_ref, one_keep, one_send, two_keep, two_send, acts, right, held
):
    x, y, core = meta_ref[1], meta_ref[2], meta_ref[3]
    count, blocks, rows, _ = other_ref.shape
    peers, group, cut = held.shape
    half = group // 2
    _both(acts, act_mine, act_other)
    for block in range(blocks):
        for place in range(count):
            at = 128 * (block * count + place)
            right[:rows, at : at + 128] = owned_ref[core * count + place, block]
            right[rows:, at : at + 128] = other_ref[place, block]
    for side in range(2):
        grad = _dot(acts[...], right[:, side * cut : (side + 1) * cut], ((0,), (0,))).astype(jnp.bfloat16)
        held[...] = grad.reshape(peers, group, cut)
        if side == 0:
            for place in range(peers // 2):
                one_keep[place] = held[2 * place + x]
                one_send[place] = held[2 * place + 1 - x]
        else:
            for place in range(peers):
                two_keep[place] = held[place, pl.ds(pl.multiple_of(y * half, half), half), :]
                two_send[place] = held[place, pl.ds(pl.multiple_of((1 - y) * half, half), half), :]


def attend_weigh(meta, act_mine, act_other, owned, other):
    peers, blocks, rows, _ = owned.shape
    width = act_mine.shape[1]
    group, span = width // peers, blocks * width // 2
    cut = span // 2
    shapes = [(peers // 2, group, cut), (peers // 2, group, cut), (peers, group // 2, cut), (peers, group // 2, cut)]
    return pl.pallas_call(
        attend_weigh_kernel,
        out_shape=[jax.ShapeDtypeStruct(shape, jnp.bfloat16) for shape in shapes],
        in_specs=_specs("svvvv"),
        out_specs=_specs("vvvv"),
        scratch_shapes=[
            pltpu.VMEM((2 * rows, width), jnp.bfloat16),
            pltpu.VMEM((2 * rows, span), jnp.bfloat16),
            pltpu.VMEM((peers, group, cut), jnp.bfloat16),
        ],
        compiler_params=_params(12),
        cost_estimate=pl.CostEstimate(flops=2 * 10**9, bytes_accessed=7 * 2**20, transcendentals=0),
        name="attend_weigh",
    )(meta, act_mine, act_other, owned, other)


def flipped(array, axis, mask):
    peers = lax.axis_size(axis)
    return lax.ppermute(array, axis, [(i, i ^ mask) for i in range(peers)])


def pick(array, index, axis):
    return lax.dynamic_index_in_dim(array, index, axis, keepdims=False)


def added(a, b):
    return (a.astype(jnp.float32) + b.astype(jnp.float32)).astype(jnp.bfloat16)


def in_order(mine, other, bit, axis):
    lower = jnp.where(bit == 0, mine, other)
    upper = jnp.where(bit == 0, other, mine)
    return jnp.concatenate([lower, upper], axis=axis)


def after(value, *others):
    return lax.optimization_barrier((value, others))[0]


def over_first(one_keep, one_send, two_keep, two_send):
    return one_keep, flipped(one_send, "blk", 1), two_keep, flipped(two_send, "seq", 2)


def over_second(here, one_keep, one_got, two_keep, two_got):
    levels, rows, cut = one_keep.shape
    shape = (levels, rows // 2, cut)
    return _small_call(second_kernel, "second", [shape] * 4, jnp.bfloat16, here, one_keep, one_got, two_keep, two_got)


def send_second(one_left, one_send, two_left, two_send):
    return one_left, flipped(one_send, "seq", 2), two_left, flipped(two_send, "blk", 1)


def near_sums(here, one_keep, one_got, two_keep, two_got):
    levels, half, cut = one_keep.shape
    return _small_call(
        near_kernel, "near", [(levels // 2, half, 2 * cut)] * 2, jnp.bfloat16, here, one_keep, one_got, two_keep, two_got
    )


def over_near(here, *parts):
    left, send = near_sums(here, *parts)
    return left, flipped(send, "blk", 2)


def over_far(here, keep, got):
    left, send = _small_call(far_kernel, "far", [keep.shape[1:]] * 2, jnp.bfloat16, here, keep, got)
    return left, flipped(send, "blk", 4)


def over_all(keep, got):
    return _small_call(last_kernel, "last", [keep.shape], jnp.bfloat16, keep, got)[0]


def of_all(own):
    across = flipped(own, "seq", 2)
    return own, across, flipped(own, "seq", 1), flipped(across, "seq", 1)


def local_by_heads(
    tokens,
    lengths,
    attend_weight,
    merge_weight,
    expand_weight,
    contract_weight,
    gain_first,
    shift_first,
    gain_second,
    shift_second,
    bias_table,
    cotangent,
):
    rows, width = tokens.shape[1], tokens.shape[2]
    buckets, heads = bias_table.shape
    hidden = expand_weight.shape[1]
    items = lengths.shape[1]
    peers = lax.axis_size("blk")
    levels = peers // 2
    group = width // peers
    part = hidden // (2 * peers)
    me, line_of = lax.axis_index("blk"), lax.axis_index("seq")
    z, x, y, core = me // 2, me % 2, line_of // 2, line_of % 2
    place = (z, x, y)
    here = jnp.stack([me, x, y, core]).astype(jnp.int32)
    gain_first, shift_first, gain_second, shift_second = (
        v.reshape(1, width) for v in (gain_first, shift_first, gain_second, shift_second)
    )

    own, grad_out = tokens[0], cotangent[0]
    grad_other = flipped(grad_out, "seq", 1)
    meta = plan(lengths[0], me, peers, rows)
    hot = bucket_lines(rows, buckets)
    table_mine = lax.dynamic_slice_in_dim(bias_table, 2 * me, 2, 1)
    lines = jnp.dot(table_mine.T, hot, precision=highest)
    far = table_mine[buckets - 1]

    def to_all(array):
        return lax.all_to_all(array, "blk", split_axis=0, concat_axis=0, tiled=True)

    *parts, act_first = project(here, own, gain_first, shift_first, attend_weight, peers)
    parts = [parts[0]] + [flipped(parts[step], "blk", step) for step in range(1, peers)]
    pulled = pull(here, grad_out, grad_other, contract_weight, peers)
    mixed, wide, logs, qkv = attend(meta, after(far, pulled), lines, parts, items)
    first_other = flipped(act_first, "seq", 1)
    attn_low, middle, act_second = merge(to_all(mixed), own, gain_second, shift_second, merge_weight)
    act_other = flipped(act_second, "seq", 1)
    attn_other = flipped(attn_low, "seq", 1)
    in_keep, in_send, hidden_low, hidden_back = feed(here, act_second, act_other, pulled, expand_weight, peers)
    in_send = flipped(in_send, "seq", 1)
    contract_keep, *contract_parts = contract_weigh(here, grad_out, grad_other, hidden_low, peers)
    in_send, contract_keep, *contract_parts = lax.optimization_barrier((in_send, contract_keep, *contract_parts))
    contract_parts = over_first(contract_keep, *contract_parts)
    grad_heads, grad_middle, keep_low, send_low, sums_second = turn(
        here, in_keep, in_send, middle, grad_out, gain_second, merge_weight, peers
    )
    expand_parts = weigh(here, act_second, act_other, attn_low, attn_other, keep_low, flipped(send_low, "seq", 1), hidden_back, peers)
    expand_keep = expand_parts[0]
    _, *expand_parts = over_first(*expand_parts)

    contract_parts = over_second(here, *contract_parts)
    grad_heads, expand_keep, *contract_parts = lax.optimization_barrier((to_all(grad_heads), expand_keep, *contract_parts))
    back_all, line_grad = attend_back(meta, far, lines, wide, logs, qkv, grad_heads, items)
    back_all, *sums = lax.optimization_barrier((back_all, *contract_parts, expand_keep, *expand_parts))
    owned = to_all(back_all)
    out_keep, out_send = emit(here, after(hidden_low, back_all), contract_weight, peers)
    contract_parts = over_near(here, *send_second(*sums[:4]))
    expand_parts = send_second(*over_second(here, *sums[4:]))
    expand_left, expand_send = near_sums(here, *expand_parts)
    owned, out_keep, expand_left, expand_send, *sums = lax.optimization_barrier((owned, out_keep, expand_left, expand_send, *contract_parts))
    expand_parts = expand_left, flipped(expand_send, "blk", 2)
    contract_parts = over_far(here, *sums)
    owned_send = pick(owned.reshape(2, levels, 3, rows, group), 1 - core, 0)
    attend_parts = over_first(*attend_weigh(here, act_first, first_other, owned, flipped(owned_send, "seq", 1)))
    output = (middle + out_keep + flipped(out_send, "seq", 1).astype(jnp.float32)).astype(jnp.bfloat16)
    tokens_grad, sums_first = close(owned, own, grad_middle, gain_first, attend_weight)
    table_mine = jnp.dot(hot, line_grad.T, precision=highest).reshape(1, 2 * buckets)
    table_row = jnp.broadcast_to(jnp.pad(table_mine, ((0, 0), (0, group - 2 * buckets)))[:, None], (1, peers, group))
    small = jnp.concatenate([sums_first.reshape(2, peers, group), sums_second.reshape(2, peers, group), table_row]).transpose(1, 0, 2)
    small = jnp.pad(small, ((0, 0), (0, 3), (0, 0)))

    sums = lax.optimization_barrier((*attend_parts, *contract_parts, *expand_parts))
    attend_parts = send_second(*over_second(here, *sums[:4]))
    contract_own = over_all(*sums[4:6])
    contract_across = flipped(contract_own, "seq", 2)
    expand_parts = over_far(here, *sums[6:])
    small, *sums = lax.optimization_barrier((small, *attend_parts, contract_across, *expand_parts))
    attend_parts = over_near(here, *sums[:4])
    contract_grad = (contract_own, sums[4], flipped(contract_own, "seq", 1), flipped(sums[4], "seq", 1))
    small = small + flipped(small, "seq", 1)
    expand_own = over_all(*sums[5:])
    expand_across = flipped(expand_own, "seq", 2)
    small, expand_across, *attend_parts = lax.optimization_barrier((small, expand_across, *attend_parts))
    attend_parts = over_far(here, *attend_parts)
    small = small + flipped(small, "seq", 2)
    expand_grad = (expand_own, expand_across, flipped(expand_own, "seq", 1), flipped(expand_across, "seq", 1))
    small = to_all(small)
    contract_grad = _small_call(finish_contract_kernel, "finish_contract", [(2 * part, width)], jnp.float32, here, *contract_grad)[0]
    expand_grad, merge_grad = _small_call(
        partial(finish_expand_kernel, part), "finish_expand", [(group, hidden), (group, width)], jnp.float32, here, *expand_grad
    )
    output, *attend_parts = lax.optimization_barrier((output, *attend_parts))
    attend_grad = of_all(over_all(*attend_parts))
    attend_grad = _small_call(finish_attend_kernel, "finish_attend", [(group, 3 * width)], jnp.float32, here, *attend_grad)[0]
    table_grad = small[:, 4, : 2 * buckets].reshape(peers, buckets, 2).transpose(1, 0, 2).reshape(buckets, heads)
    vectors = jnp.sum(small[:, :4], axis=0)
    return (
        output[None],
        tokens_grad[None],
        attend_grad,
        merge_grad,
        expand_grad,
        contract_grad,
        vectors[0],
        vectors[1],
        vectors[2],
        vectors[3],
        table_grad,
    )


def local(*arguments):
    heads = arguments[10].shape[1]
    rows = arguments[0].shape[1]
    peers = lax.axis_size("blk")
    if peers == 8 and lax.axis_size("seq") == 4 and heads == 2 * peers and rows == 256:
        return local_by_heads(*arguments)
    return local_by_runs(*arguments)


def solution(mesh):
    in_specs = (
        P("seq", "blk", None),
        P("seq", None),
        P(),
        P(),
        P(),
        P(),
        P(),
        P(),
        P(),
        P(),
        P(),
        P("seq", "blk", None),
    )
    out_specs = (
        P("seq", "blk", None),
        P("seq", "blk", None),
        P("blk", None),
        P("blk", None),
        P("blk", None),
        P("blk", None),
        P("blk"),
        P("blk"),
        P("blk"),
        P("blk"),
        P(),
    )
    return jax.shard_map(local, mesh=mesh, in_specs=in_specs, out_specs=out_specs, check_vma=False)
```

```python
from functools import partial
import math

import jax
import jax.numpy as jnp
from jax import lax
from jax.experimental import pallas as pl
from jax.experimental.pallas import tpu as pltpu
from jax.sharding import PartitionSpec as P

HOPS = 6


epsilon = 1e-05
masked_score = -1e30
highest = lax.Precision.HIGHEST
bucket_edges = [math.ceil(16 * 8 ** (t / 16)) for t in range(1, 16)]


def shifted(array, axis, by):
    peers = lax.axis_size(axis)
    pairs = [(i, i + by) for i in range(peers) if 0 <= i + by < peers]
    return lax.ppermute(array, axis, pairs)


def shortened(array):

    def short(part):
        return part.astype(jnp.bfloat16) if part.dtype == jnp.float32 else part

    return jax.tree.map(short, array)


def bucket_of(distance):
    total = jnp.minimum(jnp.maximum(distance, 0), 16)
    for edge in bucket_edges:
        total = total + (distance >= edge).astype(jnp.int32)
    return total


def segment_of(position, ends):
    return jnp.sum((position[:, None] >= ends[None, :]).astype(jnp.int32), axis=1)


def layer_norm(value, gain, shift):
    mean = jnp.mean(value, axis=-1, keepdims=True)
    centred = value - mean
    variance = jnp.mean(centred * centred, axis=-1, keepdims=True)
    return centred * lax.rsqrt(variance + epsilon) * gain + shift


def diagonal_sums(grid, count):
    heads = grid.shape[0]
    padded = jnp.pad(jnp.flip(grid, axis=-1), ((0, 0), (0, 0), (0, count)))
    flat = padded.reshape(heads, 2 * count * count)[:, : count * (2 * count - 1)]
    return jnp.sum(flat.reshape(heads, count, 2 * count - 1), axis=1)


def band_matrix(line, count):
    heads = line.shape[0]
    flipped = jnp.flip(line, axis=-1)
    tiled = jnp.tile(flipped, (1, count))
    window = tiled[:, count - 1 : count - 1 + count * (2 * count - 2)]
    return window.reshape(heads, count, 2 * count - 2)[:, :, :count]


def fetch_earlier(block):
    earlier = []
    moving = block
    for hop in range(HOPS):
        moving = shifted(moving, "blk", 1)
        earlier.append(moving)
    return earlier


def return_parts(parts):
    carried = jnp.zeros_like(parts[0])
    for hop in range(HOPS, 0, -1):
        carried = shifted(shortened(carried + parts[hop - 1]), "blk", -1)
    return carried


def local_by_runs(
    tokens,
    lengths,
    attend_weight,
    merge_weight,
    expand_weight,
    contract_weight,
    gain_first,
    shift_first,
    gain_second,
    shift_second,
    bias_table,
    cotangent,
):
    rows = tokens.shape[1]
    width = tokens.shape[2]
    heads = bias_table.shape[1]
    buckets = bias_table.shape[0]
    head_size = width // heads
    items = lengths.shape[1]
    start = lax.axis_index("blk") * rows
    query_pos = start + jnp.arange(rows, dtype=jnp.int32)
    ends = jnp.cumsum(lengths[0])
    query_seg = segment_of(query_pos, ends)
    band = jnp.arange(2 * rows - 1, dtype=jnp.int32) - (rows - 1)
    bucket_ids = jnp.arange(buckets, dtype=jnp.int32)

    def pair_setup(hop):
        key_pos = query_pos - hop * rows
        key_seg = segment_of(key_pos, ends)
        key_valid = (key_pos >= 0) & (key_seg < items)
        same = key_pos[None, :] == query_pos[:, None]
        allowed = (
            (query_seg[:, None] == key_seg[None, :])
            & (key_pos[None, :] <= query_pos[:, None])
            & (key_valid[None, :] | same)
        )
        onehot = (bucket_of(hop * rows + band)[:, None] == bucket_ids[None, :]).astype(jnp.float32)
        band_bias = jnp.dot(onehot, bias_table, precision=highest).T
        bias = band_matrix(band_bias, rows)
        additive = jnp.where(allowed[None], bias, masked_score)
        return (jnp.any(allowed), onehot, additive)

    pairs = [pair_setup(hop) for hop in range(HOPS + 1)]
    residual = tokens[0].astype(jnp.float32)
    normed_first, norm_first_pull = jax.vjp(layer_norm, residual, gain_first, shift_first)
    act_first = normed_first.astype(jnp.bfloat16)
    projected = jnp.dot(act_first, attend_weight, preferred_element_type=jnp.float32).astype(
        jnp.bfloat16
    )
    query = projected[:, :width].reshape(rows, heads, head_size)
    keys_values = jnp.stack([projected[:, width : 2 * width], projected[:, 2 * width :]])
    blocks = [keys_values] + fetch_earlier(keys_values)

    def scores_of(block, pair):
        key = block[0].reshape(rows, heads, head_size)
        raw = jnp.einsum("qhe,khe->hqk", query, key, preferred_element_type=jnp.float32) * 0.125
        return raw + pair[2]

    def empty_total():
        return jnp.full((heads, rows), masked_score, jnp.float32)

    def empty_scores():
        return jnp.full((heads, rows, rows), masked_score, jnp.float32)

    log_total = empty_total()
    kept_scores = []
    for block, pair in zip(blocks, pairs):

        def part_total(block=block, pair=pair):
            scores = scores_of(block, pair)
            peak = jnp.max(scores, axis=-1)
            return (peak + jnp.log(jnp.sum(jnp.exp(scores - peak[..., None]), axis=-1)), scores)

        def skip_total():
            return (empty_total(), empty_scores())

        part_log, scores = lax.cond(pair[0], part_total, skip_total)
        log_total = jnp.logaddexp(log_total, part_log)
        kept_scores.append(scores)

    def empty_heads():
        return jnp.zeros((rows, heads, head_size), jnp.float32)

    attended = empty_heads()
    for block, pair, scores in zip(blocks, pairs, kept_scores):

        def part_mix(block=block, scores=scores):
            weights = jnp.exp(scores - log_total[..., None]).astype(jnp.bfloat16)
            value = block[1].reshape(rows, heads, head_size)
            return jnp.einsum("hqk,khe->qhe", weights, value, preferred_element_type=jnp.float32)

        attended = attended + lax.cond(pair[0], part_mix, empty_heads)
    attn_low = attended.reshape(rows, width).astype(jnp.bfloat16)
    middle = residual + jnp.dot(attn_low, merge_weight, preferred_element_type=jnp.float32)
    normed_second, norm_second_pull = jax.vjp(layer_norm, middle, gain_second, shift_second)
    act_second = normed_second.astype(jnp.bfloat16)
    hidden_pre = jnp.dot(act_second, expand_weight, preferred_element_type=jnp.float32)
    hidden, gelu_pull = jax.vjp(partial(jax.nn.gelu, approximate=False), hidden_pre)
    hidden_low = hidden.astype(jnp.bfloat16)
    output = (
        middle + jnp.dot(hidden_low, contract_weight, preferred_element_type=jnp.float32)
    ).astype(jnp.bfloat16)
    grad_out = cotangent[0]
    contract_grad = jnp.einsum(
        "tf,td->fd", hidden_low, grad_out, preferred_element_type=jnp.float32
    )
    grad_hidden = jnp.einsum(
        "td,fd->tf", grad_out, contract_weight, preferred_element_type=jnp.float32
    )
    grad_pre = gelu_pull(grad_hidden)[0].astype(jnp.bfloat16)
    expand_grad = jnp.einsum("td,tf->df", act_second, grad_pre, preferred_element_type=jnp.float32)
    grad_second = jnp.einsum(
        "tf,df->td", grad_pre, expand_weight, preferred_element_type=jnp.float32
    )
    grad_middle_norm, gain_second_grad, shift_second_grad = norm_second_pull(grad_second)
    grad_middle = grad_out.astype(jnp.float32) + grad_middle_norm
    grad_middle_low = grad_middle.astype(jnp.bfloat16)
    merge_grad = jnp.einsum(
        "td,te->de", attn_low, grad_middle_low, preferred_element_type=jnp.float32
    )
    grad_heads = (
        jnp.einsum("te,de->td", grad_middle_low, merge_weight, preferred_element_type=jnp.float32)
        .astype(jnp.bfloat16)
        .reshape(rows, heads, head_size)
    )
    row_dot = jnp.sum(grad_heads.astype(jnp.float32) * attended, axis=-1).T
    back_blocks = [keys_values] + fetch_earlier(keys_values)

    def empty_grads():
        return (
            empty_heads(),
            jnp.zeros((2, rows, width), jnp.float32),
            jnp.zeros((buckets, heads), jnp.float32),
        )

    grad_query = empty_heads()
    table_local = jnp.zeros((buckets, heads), jnp.float32)
    parts = []
    for block, pair in zip(back_blocks, pairs):

        def part_grads(block=block, pair=pair):
            key = block[0].reshape(rows, heads, head_size)
            value = block[1].reshape(rows, heads, head_size)
            weights = jnp.exp(scores_of(block, pair) - log_total[..., None])
            weights_low = weights.astype(jnp.bfloat16)
            grad_weights = jnp.einsum(
                "qhe,khe->hqk", grad_heads, value, preferred_element_type=jnp.float32
            )
            grad_scores = (weights * (grad_weights - row_dot[..., None])).astype(jnp.bfloat16)
            query_part = (
                jnp.einsum("hqk,khe->qhe", grad_scores, key, preferred_element_type=jnp.float32)
                * 0.125
            )
            key_part = (
                jnp.einsum("hqk,qhe->khe", grad_scores, query, preferred_element_type=jnp.float32)
                * 0.125
            )
            value_part = jnp.einsum(
                "hqk,qhe->khe", weights_low, grad_heads, preferred_element_type=jnp.float32
            )
            line_grad = diagonal_sums(grad_scores.astype(jnp.float32), rows)
            table_part = jnp.dot(pair[1].T, line_grad.T, precision=highest)
            return (
                query_part,
                jnp.stack([key_part.reshape(rows, width), value_part.reshape(rows, width)]),
                table_part,
            )

        query_part, pair_part, table_part = lax.cond(pair[0], part_grads, empty_grads)
        grad_query = grad_query + query_part
        table_local = table_local + table_part
        parts.append(pair_part)
    owned = (parts[0] + return_parts(parts[1:])).astype(jnp.bfloat16)
    grad_project = jnp.concatenate(
        [grad_query.reshape(rows, width).astype(jnp.bfloat16), owned[0], owned[1]], axis=1
    )
    attend_grad = jnp.einsum(
        "td,te->de", act_first, grad_project, preferred_element_type=jnp.float32
    )
    grad_first = jnp.einsum(
        "te,de->td", grad_project, attend_weight, preferred_element_type=jnp.float32
    )
    grad_input_norm, gain_first_grad, shift_first_grad = norm_first_pull(grad_first)
    tokens_grad = grad_middle + grad_input_norm
    results = (
        lax.psum_scatter(attend_grad, "blk", scatter_dimension=0, tiled=True),
        lax.psum_scatter(merge_grad, "blk", scatter_dimension=0, tiled=True),
        lax.psum_scatter(expand_grad, "blk", scatter_dimension=0, tiled=True),
        lax.psum_scatter(contract_grad, "blk", scatter_dimension=0, tiled=True),
        lax.psum_scatter(gain_first_grad, "blk", scatter_dimension=0, tiled=True),
        lax.psum_scatter(shift_first_grad, "blk", scatter_dimension=0, tiled=True),
        lax.psum_scatter(gain_second_grad, "blk", scatter_dimension=0, tiled=True),
        lax.psum_scatter(shift_second_grad, "blk", scatter_dimension=0, tiled=True),
    )
    results = (
        lax.psum(results[0].astype(jnp.bfloat16), "seq").astype(jnp.float32),
        lax.psum(results[1].astype(jnp.bfloat16), "seq").astype(jnp.float32),
        lax.psum(results[2].astype(jnp.bfloat16), "seq").astype(jnp.float32),
        lax.psum(results[3].astype(jnp.bfloat16), "seq").astype(jnp.float32),
        lax.psum(results[4].astype(jnp.bfloat16), "seq").astype(jnp.float32),
        lax.psum(results[5].astype(jnp.bfloat16), "seq").astype(jnp.float32),
        lax.psum(results[6].astype(jnp.bfloat16), "seq").astype(jnp.float32),
        lax.psum(results[7].astype(jnp.bfloat16), "seq").astype(jnp.float32),
    )
    table_grad = lax.psum(table_local, ("seq", "blk"))
    return (
        output[None],
        tokens_grad[None],
        results[0],
        results[1],
        results[2],
        results[3],
        results[4],
        results[5],
        results[6],
        results[7],
        table_grad,
    )


def _segments(position, meta_ref, first, items):
    total = jnp.zeros(position.shape, jnp.int32)
    for item in range(items):
        total = total + (position >= meta_ref[first + item]).astype(jnp.int32)
    return total

def _allowed(meta_ref, peers, items, rows, i, j, which, needed):
    first = 1 + 2 * peers
    q_seg = _segments(i * rows + lax.broadcasted_iota(jnp.int32, (1, rows), 1), meta_ref, first, items)
    k_seg = _segments(j * rows + lax.broadcasted_iota(jnp.int32, (rows, 1), 0), meta_ref, first, items)
    k_seg = jnp.where((k_seg < items) & needed if which == 1 else k_seg < items, k_seg, -1)
    same = q_seg == k_seg
    if which == 0:
        key = lax.broadcasted_iota(jnp.int32, (rows, rows), 0)
        query = lax.broadcasted_iota(jnp.int32, (rows, rows), 1)
        return (same & (key < query)) | (key == query)
    return same

def _dot(a, b, dims):
    return lax.dot_general(a, b, (dims, ((), ())), preferred_element_type=jnp.float32)

def _turned(array):
    return jnp.transpose(array.astype(jnp.float32))

def _split(array, axis=1):
    wide = array.astype(jnp.float32)
    left = lax.broadcasted_iota(jnp.int32, array.shape, axis) < 64
    return jnp.where(left, wide, 0.0).astype(jnp.bfloat16), jnp.where(left, 0.0, wide).astype(jnp.bfloat16)

def _fold(value, op):
    while value.shape[0] > 8:
        half = value.shape[0] // 2
        value = op(value[:half], value[half:])
    return value

def _put_bias(bias, line_ref, rows):
    for head in range(2):
        line = jnp.broadcast_to(line_ref[head:head + 1, :], (rows, 2 * rows))
        bias[head] = pltpu.roll(line, 0, 1, stride=1, stride_axis=0)

def _biased(raw, bias, far_ref, head, which, rows):
    if which == 0:
        return raw + bias[head, :, :rows]
    if which == 1:
        return raw + bias[head, :, rows:]
    return raw + far_ref[head]

def attend_kernel(peers, items, rows, meta_ref, far_ref, line_ref, *refs):
    parts = refs[:peers]
    mixed, wide_ref, log_ref, qkv, turned, bias, scores = refs[peers:]
    me = meta_ref[0]
    for slot in range(peers):
        qkv[me ^ slot] = parts[slot][...]
        turned[me ^ slot] = _turned(parts[slot][2]).astype(jnp.bfloat16)
    _put_bias(bias, line_ref, rows)
    upper = lax.broadcasted_iota(jnp.int32, (128, rows), 0) < 64

    def one_row(i, _):
        low = meta_ref[1 + i]
        whole = jnp.minimum(meta_ref[1 + peers + i], i - 1)
        queries = _split(qkv[i, 0].astype(jnp.float32) * 0.125)

        def put(j, slot, which, masked, peaks):
            key = qkv[j, 1]
            if masked:
                allowed = _allowed(meta_ref, peers, items, rows, i, j, which, low < i)
            new = []
            for head in range(2):
                raw = _biased(_dot(key, queries[head], ((1,), (1,))), bias, far_ref, head, which, rows)
                if masked:
                    raw = jnp.where(allowed, raw, masked_score)
                scores[head, slot] = raw
                new.append(jnp.maximum(peaks[head], _fold(raw, jnp.maximum)))
            return tuple(new)

        start = jnp.full((8, rows), masked_score, jnp.float32)
        before = jnp.maximum(i - 1, 0)
        peaks = put(i, peers, 0, True, (start, start))
        peaks = put(before, peers + 1, 1, True, peaks)
        peaks = lax.fori_loop(low, whole, lambda j, p: put(j, j, 2, True, p), peaks)
        peaks = lax.fori_loop(jnp.maximum(low, whole), i - 1, lambda j, p: put(j, j, 2, False, p), peaks)
        tops = [jnp.max(peak, axis=0, keepdims=True) for peak in peaks]

        def mix(j, slot, carry):
            sums, total = carry
            value = turned[j]
            new = []
            both = []
            for head in range(2):
                weight = jnp.exp(scores[head, slot] - tops[head])
                new.append(sums[head] + _fold(weight, jnp.add))
                both.append(_dot(value[64 * head:64 * head + 64], weight.astype(jnp.bfloat16), ((1,), (0,))))
            return tuple(new), total + jnp.concatenate(both)

        nothing = jnp.zeros((8, rows), jnp.float32)
        carry = ((nothing, nothing), jnp.zeros((128, rows), jnp.float32))
        carry = mix(before, peers + 1, mix(i, peers, carry))
        sums, total = lax.fori_loop(low, i - 1, lambda j, c: mix(j, j, c), carry)
        sums = [jnp.sum(s, axis=0, keepdims=True) for s in sums]
        total = total / jnp.where(upper, sums[0], sums[1])
        wide_ref[i] = total
        for head in range(2):
            log_ref[i, head:head + 1, :] = tops[head] + jnp.log(sums[head])
        mixed[i] = jnp.transpose(total).astype(jnp.bfloat16)
        return 0

    lax.fori_loop(0, peers, one_row, 0)

def attend(meta, far, line, parts, items):
    peers = len(parts)
    rows = parts[0].shape[1]
    smem = pl.BlockSpec(memory_space=pltpu.SMEM)
    vmem = pl.BlockSpec(memory_space=pltpu.VMEM)
    shapes = [
        jax.ShapeDtypeStruct((peers, rows, 128), jnp.bfloat16),
        jax.ShapeDtypeStruct((peers, 128, rows), jnp.float32),
        jax.ShapeDtypeStruct((peers, 8, rows), jnp.float32),
        jax.ShapeDtypeStruct((peers, 3, rows, 128), jnp.bfloat16),
    ]
    res = pl.pallas_call(
        partial(attend_kernel, peers, items, rows),
        out_shape=shapes,
        in_specs=[smem, smem] + [vmem] * (peers + 1),
        out_specs=[vmem] * 4,
        scratch_shapes=[
            pltpu.VMEM((peers, 128, rows), jnp.bfloat16),
            pltpu.VMEM((2, rows, 2 * rows), jnp.float32),
            pltpu.VMEM((2, peers + 2, rows, rows), jnp.float32),
        ],
        compiler_params=pltpu.CompilerParams(vmem_limit_bytes=18 * 2**20),
        cost_estimate=pl.CostEstimate(flops=8 * 10**9, bytes_accessed=4 * 2**20, transcendentals=3 * 10**6),
        name="attend",
    )(meta, far, line, *parts)
    return res

def attend_back_kernel(peers, items, rows, meta_ref, far_ref, line_ref, wide_ref, log_ref, cot, qkv, *refs):
    all_ref, table_ref, turned, bias, near, far_sum, dkey, dvalue = refs
    for peer in range(peers):
        turned[peer] = _turned(qkv[peer, 1]).astype(jnp.bfloat16)
    _put_bias(bias, line_ref, rows)
    near[...] = jnp.zeros_like(near)
    far_sum[...] = jnp.zeros_like(far_sum)
    dkey[...] = jnp.zeros_like(dkey)
    dvalue[...] = jnp.zeros_like(dvalue)

    def one_row(i, _):
        low = meta_ref[1 + i]
        whole = jnp.minimum(meta_ref[1 + peers + i], i - 1)
        queries = _split(qkv[i, 0].astype(jnp.float32) * 0.125)
        grad = cot[i]
        grads_ = _split(grad)
        product = _turned(grad) * wide_ref[i]
        dots = [jnp.sum(product[64 * head:64 * head + 64], axis=0, keepdims=True) for head in range(2)]
        logs = [log_ref[i, head:head + 1, :] for head in range(2)]

        def step(j, which, masked, dquery):
            key = qkv[j, 1]
            value = qkv[j, 2]
            across = turned[j]
            if masked:
                allowed = _allowed(meta_ref, peers, items, rows, i, j, which, low < i)
            dk = jnp.zeros((rows, 128), jnp.float32)
            dv = jnp.zeros((rows, 128), jnp.float32)
            both = []
            for head in range(2):
                raw = _biased(_dot(key, queries[head], ((1,), (1,))), bias, far_ref, head, which, rows)
                if masked:
                    raw = jnp.where(allowed, raw, masked_score)
                weight = jnp.exp(raw - logs[head])
                dweight = _dot(value, grads_[head], ((1,), (1,)))
                dscore = weight * (dweight - dots[head])
                low_score = dscore.astype(jnp.bfloat16)
                if which == 0:
                    near[head, :, :rows] += dscore
                elif which == 1:
                    near[head, :, rows:] += dscore
                else:
                    far_sum[head] += _fold(dscore, jnp.add)
                both.append(_dot(across[64 * head:64 * head + 64], low_score, ((1,), (0,))))
                dk = dk + _dot(low_score, queries[head], ((1,), (0,)))
                dv = dv + _dot(weight.astype(jnp.bfloat16), grads_[head], ((1,), (0,)))
            dkey[j] += dk
            dvalue[j] += dv
            return dquery + jnp.concatenate(both)

        dquery = step(i, 0, True, jnp.zeros((128, rows), jnp.float32))
        dquery = step(jnp.maximum(i - 1, 0), 1, True, dquery)
        dquery = lax.fori_loop(low, whole, lambda j, d: step(j, 2, True, d), dquery)
        dquery = lax.fori_loop(jnp.maximum(low, whole), i - 1, lambda j, d: step(j, 2, False, d), dquery)
        all_ref[i, 0] = (jnp.transpose(dquery) * 0.125).astype(jnp.bfloat16)
        return 0

    lax.fori_loop(0, peers, one_row, 0)
    for i in range(peers):
        all_ref[i, 1] = dkey[i].astype(jnp.bfloat16)
        all_ref[i, 2] = dvalue[i].astype(jnp.bfloat16)
    wide = 2 * rows
    sub = lax.broadcasted_iota(jnp.int32, (8, wide), 0)
    for head in range(2):
        part = near[head]
        count = rows
        while count > 8:
            count //= 2
            part = part[:count] + pltpu.roll(part[count:], wide - count, 1)
        for bit in (4, 2, 1):
            part = jnp.where((sub & bit) != 0, pltpu.roll(part, wide - bit, 1), part)
        total = far_sum[head]
        table_ref[head, :, :rows] = part[:, :rows]
        table_ref[head, :, rows:] = part[:, rows:] + jnp.concatenate([jnp.zeros((8, rows - 128), jnp.float32), total[:, :128] + total[:, 128:]], axis=1)

def attend_back(meta, far, line, wide, logs, qkv, grads, items):
    peers, _, rows, _ = qkv.shape
    smem = pl.BlockSpec(memory_space=pltpu.SMEM)
    vmem = pl.BlockSpec(memory_space=pltpu.VMEM)
    shapes = [
        jax.ShapeDtypeStruct((peers, 3, rows, 128), jnp.bfloat16),
        jax.ShapeDtypeStruct((2, 8, 2 * rows), jnp.float32),
    ]
    res = pl.pallas_call(
        partial(attend_back_kernel, peers, items, rows),
        out_shape=shapes,
        in_specs=[smem, smem] + [vmem] * 5,
        out_specs=[vmem] * 2,
        scratch_shapes=[
            pltpu.VMEM((peers, 128, rows), jnp.bfloat16),
            pltpu.VMEM((2, rows, 2 * rows), jnp.float32),
            pltpu.VMEM((2, rows, 2 * rows), jnp.float32),
            pltpu.VMEM((2, 8, rows), jnp.float32),
            pltpu.VMEM((peers, rows, 128), jnp.float32),
            pltpu.VMEM((peers, rows, 128), jnp.float32),
        ],
        compiler_params=pltpu.CompilerParams(vmem_limit_bytes=18 * 2**20),
        cost_estimate=pl.CostEstimate(flops=20 * 10**9, bytes_accessed=8 * 2**20, transcendentals=3 * 10**6),
        name="attend_back",
    )(meta, far, line, wide, logs, grads, qkv)
    return res[0], jnp.sum(res[1], axis=1)

def plan(lengths, me, peers, rows):
    ends = jnp.cumsum(lengths)
    items = lengths.shape[0]
    place = jnp.arange(peers, dtype=jnp.int32)
    first = jnp.sum((place[:, None] * rows >= ends[None]).astype(jnp.int32), axis=1)
    last = jnp.sum((place[:, None] * rows + rows - 1 >= ends[None]).astype(jnp.int32), axis=1)
    low = jnp.sum((last[None, :] < first[:, None]).astype(jnp.int32), axis=1)
    low = jnp.where(first < items, jnp.minimum(low, place), place)
    whole = jnp.sum((first[None, :] < last[:, None]).astype(jnp.int32), axis=1)
    return jnp.concatenate([me[None].astype(jnp.int32), low, whole, ends.astype(jnp.int32)])
def bucket_lines(rows, buckets):
    k = jnp.arange(2 * rows, dtype=jnp.int32)
    return (bucket_of(k)[None, :] == jnp.arange(buckets, dtype=jnp.int32)[:, None]).astype(jnp.float32)


def _unit(value):
    mean = jnp.mean(value, axis=-1, keepdims=True)
    centred = value - mean
    variance = jnp.mean(centred * centred, axis=-1, keepdims=True)
    scale = lax.rsqrt(variance + epsilon)
    return centred * scale, scale


def _norm_back(grad, unit, scale, gain, sums_ref):
    inner = grad * gain
    first = jnp.mean(inner, axis=-1, keepdims=True)
    second = jnp.mean(inner * unit, axis=-1, keepdims=True)
    sums_ref[0:1, :] = jnp.sum(grad * unit, axis=0, keepdims=True)
    sums_ref[1:2, :] = jnp.sum(grad, axis=0, keepdims=True)
    return scale * (inner - first - unit * second)


def _lanes(index):
    return pl.ds(pl.multiple_of(index * 128, 128), 128)


def _specs(*kinds):
    places = {"s": pltpu.SMEM, "v": pltpu.VMEM, "h": pltpu.HBM}
    return [pl.BlockSpec(memory_space=places[kind]) for word in kinds for kind in word]


def _params(mebibytes):
    return pltpu.CompilerParams(vmem_limit_bytes=mebibytes * 2**20)


def project_kernel(peers, meta_ref, tokens_ref, gain_ref, shift_ref, weight_ref, *refs):
    outs, act_ref, held, done, arrived = refs[:peers], refs[peers], refs[peers + 1], refs[peers + 2], refs[peers + 3]
    me = meta_ref[0]
    pieces, _, span = held.shape
    copies = []
    for piece in range(pieces):
        copies.append(pltpu.make_async_copy(weight_ref.at[:, pl.ds(piece * span, span)], held.at[piece], arrived.at[piece]))
        copies[-1].start()
    unit, _ = _unit(tokens_ref[...].astype(jnp.float32))
    act = (unit * gain_ref[...] + shift_ref[...]).astype(jnp.bfloat16)
    act_ref[...] = act
    for piece in range(pieces):
        copies[piece].wait()
        got = _dot(act, held[piece], ((1,), (0,))).astype(jnp.bfloat16)
        for block in range(span // 128):
            done[piece * (span // 128) + block] = got[:, 128 * block : 128 * block + 128]
    for slot in range(peers):
        for block in range(3):
            outs[slot][block] = done[block * peers + (me ^ slot)]


def project(meta, tokens, gain, shift, weight, peers):
    rows, width = tokens.shape
    span = 512
    pieces = weight.shape[1] // span
    return pl.pallas_call(
        partial(project_kernel, peers),
        out_shape=[jax.ShapeDtypeStruct((3, rows, 128), jnp.bfloat16)] * peers + [jax.ShapeDtypeStruct((rows, width), jnp.bfloat16)],
        in_specs=_specs("svvvh"),
        out_specs=_specs("v" * (peers + 1)),
        scratch_shapes=[
            pltpu.VMEM((pieces, width, span), jnp.bfloat16),
            pltpu.VMEM((3 * peers, rows, 128), jnp.bfloat16),
            pltpu.SemaphoreType.DMA((pieces,)),
        ],
        compiler_params=_params(60),
        cost_estimate=pl.CostEstimate(flops=4 * 10**9, bytes_accessed=8 * 2**20, transcendentals=0),
        name="project",
    )(meta, tokens, gain, shift, weight)


def merge_kernel(parts_ref, tokens_ref, gain_ref, shift_ref, weight_ref, low_ref, middle_ref, act_ref):
    for part in range(parts_ref.shape[0]):
        low_ref[:, 128 * part : 128 * part + 128] = parts_ref[part]
    middle = tokens_ref[...].astype(jnp.float32) + _dot(low_ref[...], weight_ref[...], ((1,), (0,)))
    middle_ref[...] = middle
    unit, _ = _unit(middle)
    act_ref[...] = (unit * gain_ref[...] + shift_ref[...]).astype(jnp.bfloat16)


def merge(parts, tokens, gain, shift, weight):
    return pl.pallas_call(
        merge_kernel,
        out_shape=[jax.ShapeDtypeStruct(tokens.shape, t) for t in (jnp.bfloat16, jnp.float32, jnp.bfloat16)],
        in_specs=_specs("vvvvv"),
        out_specs=_specs("vvv"),
        compiler_params=_params(12),
        cost_estimate=pl.CostEstimate(flops=10**9, bytes_accessed=5 * 2**20, transcendentals=0),
        name="merge",
    )(parts, tokens, gain, shift, weight)


def _both(ref, mine, other):
    rows = mine.shape[0]
    ref[:rows] = mine[...]
    ref[rows:] = other[...]


def _whole(*shape):
    return pl.BlockSpec(shape, lambda step, meta_ref: (0,) * len(shape))


def _across(rows, columns):
    return pl.BlockSpec((rows, columns), lambda step, meta_ref: (0, step))


def pull_kernel(meta_ref, mine, other, contract_ref, out_ref, grads):
    @pl.when(pl.program_id(0) == 0)
    def _():
        _both(grads, mine, other)

    out_ref[...] = _dot(grads[...], contract_ref[...], ((1,), (1,)))


def pull(meta, mine, other, contract_weight, peers):
    rows, width = mine.shape
    part = contract_weight.shape[0] // (2 * peers)
    return pl.pallas_call(
        pull_kernel,
        out_shape=jax.ShapeDtypeStruct((2 * rows, peers * part), jnp.float32),
        grid_spec=pltpu.PrefetchScalarGridSpec(
            num_scalar_prefetch=1,
            grid=(peers,),
            in_specs=[_whole(rows, width)] * 2 + [pl.BlockSpec((part, width), lambda step, meta_ref: (2 * step + meta_ref[3], 0))],
            out_specs=_across(2 * rows, part),
            scratch_shapes=[pltpu.VMEM((2 * rows, width), jnp.bfloat16)],
        ),
        compiler_params=_params(16),
        cost_estimate=pl.CostEstimate(flops=3 * 10**9, bytes_accessed=9 * 2**20, transcendentals=0),
        name="pull",
    )(meta, mine, other, contract_weight)


def feed_kernel(
    rows, part, meta_ref, act_mine, act_other, pulled_ref, expand_ref, in_keep, in_send, low_ref, back_ref, acts, weights, total, arrived
):
    core = meta_ref[3]
    pieces = weights.shape[1] // part
    copies = []
    for piece in range(pieces):
        columns = pl.ds(pl.multiple_of((2 * piece + core) * part, part), part)
        here = weights.at[:, pl.ds(piece * part, part)]
        copies.append(pltpu.make_async_copy(expand_ref.at[:, columns], here, arrived.at[piece]))
        copies[-1].start()
    _both(acts, act_mine, act_other)

    def before(piece):
        copies[piece].wait()
        return _dot(acts[...], weights[:, piece * part : (piece + 1) * part], ((1,), (0,)))

    now = before(0)
    for piece in range(pieces):
        later = before(piece + 1) if piece + 1 < pieces else None
        span = slice(piece * part, (piece + 1) * part)
        rate = 0.5 * (1.0 + lax.erf(now * math.sqrt(0.5)))
        low_ref[:, span] = (now * rate).astype(jnp.bfloat16)
        slope = rate + now * jnp.exp(-0.5 * now * now) * (1.0 / math.sqrt(2.0 * math.pi))
        back_ref[:, span] = (pulled_ref[:, span] * slope).astype(jnp.bfloat16)
        if piece % 2 == 1:
            pair = slice((piece - 1) * part, (piece + 1) * part)
            got = _dot(back_ref[:, pair], weights[:, pair], ((1,), (1,)))
            if piece == 1:
                total[...] = got
            elif piece + 1 < pieces:
                total[...] += got
            else:
                in_keep[...] = total[:rows] + got[:rows]
                in_send[...] = total[rows:] + got[rows:]
        now = later


def feed(meta, act_mine, act_other, pulled, expand_weight, peers):
    rows, width = act_mine.shape
    part = expand_weight.shape[1] // (2 * peers)
    shapes = [
        ((rows, width), jnp.float32),
        ((rows, width), jnp.float32),
        ((2 * rows, peers * part), jnp.bfloat16),
        ((2 * rows, peers * part), jnp.bfloat16),
    ]
    return pl.pallas_call(
        partial(feed_kernel, rows, part),
        out_shape=[jax.ShapeDtypeStruct(*shape) for shape in shapes],
        in_specs=_specs("svvvh"),
        out_specs=_specs("vvvv"),
        scratch_shapes=[
            pltpu.VMEM((2 * rows, width), jnp.bfloat16),
            pltpu.VMEM((width, peers * part), jnp.bfloat16),
            pltpu.VMEM((2 * rows, width), jnp.float32),
            pltpu.SemaphoreType.DMA((peers,)),
        ],
        compiler_params=_params(40),
        cost_estimate=pl.CostEstimate(flops=8 * 10**9, bytes_accessed=20 * 2**20, transcendentals=2 * 10**6),
        name="feed",
    )(meta, act_mine, act_other, pulled, expand_weight)


def _split_rows(held, x, y, one_keep, one_send, two_keep, two_send):
    peers, rows, _ = held.shape
    cut, half = one_keep.shape[2], rows // 2
    mine = pl.ds(pl.multiple_of(y * half, half), half)
    other = pl.ds(pl.multiple_of((1 - y) * half, half), half)
    for place in range(peers // 2):
        one_keep[place] = held[2 * place + x, :, :cut]
        one_send[place] = held[2 * place + 1 - x, :, :cut]
    for place in range(peers):
        two_keep[place] = held[place, mine, cut:]
        two_send[place] = held[place, other, cut:]


def contract_weigh_kernel(meta_ref, grad_mine, grad_other, low_ref, *refs):
    outs, grads, held = refs[:4], refs[4], refs[5]
    _both(grads, grad_mine, grad_other)
    part = held.shape[1]
    for piece in range(held.shape[0]):
        held[piece] = _dot(low_ref[:, piece * part : (piece + 1) * part], grads[...], ((0,), (0,))).astype(jnp.bfloat16)
    _split_rows(held, meta_ref[1], meta_ref[2], *outs)


def contract_weigh(meta, grad_mine, grad_other, low, peers):
    rows, width = grad_mine.shape
    part, cut = low.shape[1] // peers, width // 2
    shapes = [(peers // 2, part, cut), (peers // 2, part, cut), (peers, part // 2, cut), (peers, part // 2, cut)]
    return pl.pallas_call(
        contract_weigh_kernel,
        out_shape=[jax.ShapeDtypeStruct(shape, jnp.bfloat16) for shape in shapes],
        in_specs=_specs("svvv"),
        out_specs=_specs("vvvv"),
        scratch_shapes=[pltpu.VMEM((2 * rows, width), jnp.bfloat16), pltpu.VMEM((peers, part, width), jnp.bfloat16)],
        compiler_params=_params(14),
        cost_estimate=pl.CostEstimate(flops=10**8, bytes_accessed=2**20, transcendentals=0),
        name="contract_weigh",
    )(meta, grad_mine, grad_other, low)


def weigh_kernel(meta_ref, act_mine, act_other, mix_mine, mix_other, right_mine, right_other, back_ref, *refs):
    outs, left, held = refs[:4], refs[4], refs[5]
    peers, group, span = held.shape
    wide = back_ref.shape[1] // 2
    cut = span // 2
    _both(left, mix_mine, mix_other)
    right = jnp.concatenate([right_mine[...], right_other[...]])
    grad = _dot(left[...], right, ((0,), (0,))).astype(jnp.bfloat16)
    quarter = grad.shape[1] // 2
    held[:, :, wide:cut] = grad[:, :quarter].reshape(peers, group, quarter)
    held[:, :, cut + wide :] = grad[:, quarter:].reshape(peers, group, quarter)
    _both(left, act_mine, act_other)
    for side in range(2):
        grad = _dot(left[...], back_ref[:, side * wide : (side + 1) * wide], ((0,), (0,))).astype(jnp.bfloat16)
        held[:, :, side * cut : side * cut + wide] = grad.reshape(peers, group, wide)
    _split_rows(held, meta_ref[1], meta_ref[2], *outs)


def weigh(meta, act_mine, act_other, mix_mine, mix_other, right_mine, right_other, back, peers):
    rows, width = act_mine.shape
    group, cut = width // peers, back.shape[1] // 2 + width // 4
    shapes = [(peers // 2, group, cut), (peers // 2, group, cut), (peers, group // 2, cut), (peers, group // 2, cut)]
    return pl.pallas_call(
        weigh_kernel,
        out_shape=[jax.ShapeDtypeStruct(shape, jnp.bfloat16) for shape in shapes],
        in_specs=_specs("svvvvvvv"),
        out_specs=_specs("vvvv"),
        scratch_shapes=[pltpu.VMEM((2 * rows, width), jnp.bfloat16), pltpu.VMEM((peers, group, 2 * cut), jnp.bfloat16)],
        compiler_params=_params(20),
        cost_estimate=pl.CostEstimate(flops=10**8, bytes_accessed=2**20, transcendentals=0),
        name="weigh",
    )(meta, act_mine, act_other, mix_mine, mix_other, right_mine, right_other, back)


def emit_kernel(meta_ref, low_ref, contract_ref, keep_ref, send_ref, weights, arrived):
    core = meta_ref[3]
    rows, pieces = keep_ref.shape[0], arrived.shape[0]
    part = weights.shape[0] // pieces
    copies = []
    for piece in range(pieces):
        at = pl.ds(pl.multiple_of((2 * piece + core) * part, part), part)
        copies.append(pltpu.make_async_copy(contract_ref.at[at], weights.at[pl.ds(piece * part, part)], arrived.at[piece]))
        copies[-1].start()
    for copy in copies:
        copy.wait()
    keep_ref[...] = _dot(low_ref[:rows], weights[...], ((1,), (0,)))
    send_ref[...] = _dot(low_ref[rows:], weights[...], ((1,), (0,))).astype(jnp.bfloat16)


def emit(meta, low, contract_weight, peers):
    rows, width = low.shape[0] // 2, contract_weight.shape[1]
    return pl.pallas_call(
        emit_kernel,
        out_shape=[jax.ShapeDtypeStruct((rows, width), jnp.float32), jax.ShapeDtypeStruct((rows, width), jnp.bfloat16)],
        in_specs=_specs("svh"),
        out_specs=_specs("vv"),
        scratch_shapes=[pltpu.VMEM((low.shape[1], width), jnp.bfloat16), pltpu.SemaphoreType.DMA((peers,))],
        compiler_params=_params(30),
        cost_estimate=pl.CostEstimate(flops=2 * 10**9, bytes_accessed=8 * 2**20, transcendentals=0),
        name="emit",
    )(meta, low, contract_weight)


def turn_kernel(meta_ref, in_mine, in_other, middle_ref, grad_ref, gain_ref, weight_ref, heads_ref, total_ref, keep_ref, send_ref, sums_ref):
    core = meta_ref[3]
    half = keep_ref.shape[1]
    unit, scale = _unit(middle_ref[...])
    total = grad_ref[...].astype(jnp.float32) + _norm_back(in_mine[...] + in_other[...], unit, scale, gain_ref[...], sums_ref)
    total_ref[...] = total
    low = total.astype(jnp.bfloat16)

    @pl.when(core == 0)
    def _():
        keep_ref[...] = low[:, :half]
        send_ref[...] = low[:, half:]

    @pl.when(core != 0)
    def _():
        keep_ref[...] = low[:, half:]
        send_ref[...] = low[:, :half]

    heads = _dot(low, weight_ref[...], ((1,), (1,))).astype(jnp.bfloat16)
    for part in range(heads_ref.shape[0]):
        heads_ref[part] = heads[:, 128 * part : 128 * part + 128]


def turn(meta, in_mine, in_other, middle, grad, gain, weight, peers):
    rows, width = middle.shape
    shapes = [
        ((peers, rows, width // peers), jnp.bfloat16),
        ((rows, width), jnp.float32),
        ((rows, width // 2), jnp.bfloat16),
        ((rows, width // 2), jnp.bfloat16),
        ((2, width), jnp.float32),
    ]
    return pl.pallas_call(
        turn_kernel,
        out_shape=[jax.ShapeDtypeStruct(*shape) for shape in shapes],
        in_specs=_specs("svvvvvv"),
        out_specs=_specs("v" * len(shapes)),
        compiler_params=_params(12),
        cost_estimate=pl.CostEstimate(flops=10**9, bytes_accessed=8 * 2**20, transcendentals=0),
        name="turn",
    )(meta, in_mine, in_other, middle, grad, gain, weight)


def close_kernel(parts_ref, tokens_ref, grad_ref, gain_ref, weight_ref, out_ref, sums_ref, held):
    peers = parts_ref.shape[0]
    for peer in range(peers):
        for block in range(3):
            at = 128 * (block * peers + peer)
            held[:, at : at + 128] = parts_ref[peer, block]
    back = _dot(held[...], weight_ref[...], ((1,), (1,)))
    unit, scale = _unit(tokens_ref[...].astype(jnp.float32))
    out_ref[...] = grad_ref[...] + _norm_back(back, unit, scale, gain_ref[...], sums_ref)


def close(parts, tokens, grad, gain, weight):
    rows, width = tokens.shape
    return pl.pallas_call(
        close_kernel,
        out_shape=[jax.ShapeDtypeStruct((rows, width), jnp.float32), jax.ShapeDtypeStruct((2, width), jnp.float32)],
        in_specs=_specs("vvvvv"),
        out_specs=_specs("vv"),
        scratch_shapes=[pltpu.VMEM((rows, 3 * width), jnp.bfloat16)],
        compiler_params=_params(16),
        cost_estimate=pl.CostEstimate(flops=2 * 10**9, bytes_accessed=10 * 2**20, transcendentals=0),
        name="close",
    )(parts, tokens, grad, gain, weight)


def _plus(a, b):
    return (a.astype(jnp.float32) + b.astype(jnp.float32)).astype(jnp.bfloat16)


def second_kernel(meta_ref, one_keep, one_got, two_keep, two_got, one_left, one_send, two_left, two_send):
    x, y = meta_ref[1], meta_ref[2]
    levels, half, _ = one_left.shape
    mine = pl.ds(pl.multiple_of(y * half, half), half)
    other = pl.ds(pl.multiple_of((1 - y) * half, half), half)
    for level in range(levels):
        one_left[level] = _plus(one_keep[level, mine], one_got[level, mine])
        one_send[level] = _plus(one_keep[level, other], one_got[level, other])
        two_left[level] = _plus(two_keep[2 * level + x], two_got[2 * level + x])
        two_send[level] = _plus(two_keep[2 * level + 1 - x], two_got[2 * level + 1 - x])


def near_kernel(meta_ref, one_keep, one_got, two_keep, two_got, left, send):
    side = (meta_ref[0] >> 1) & 1
    cut = one_keep.shape[2]
    for level in range(left.shape[0]):
        for out, at in ((left, 2 * level + side), (send, 2 * level + 1 - side)):
            out[level, :, :cut] = _plus(one_keep[at], one_got[at])
            out[level, :, cut:] = _plus(two_keep[at], two_got[at])


def far_kernel(meta_ref, keep, got, left, send):
    upper = meta_ref[0] >> 2
    left[...] = _plus(keep[upper], got[upper])
    send[...] = _plus(keep[1 - upper], got[1 - upper])


def last_kernel(keep, got, out):
    out[...] = _plus(keep[...], got[...])


def _small_call(kernel, name, shapes, kind, *arguments):
    size = sum(2 * math.prod(a.shape) for a in arguments[-4:])
    return pl.pallas_call(
        kernel,
        out_shape=[jax.ShapeDtypeStruct(shape, kind) for shape in shapes],
        in_specs=_specs(*("s" if a.dtype == jnp.int32 else "v" for a in arguments)),
        out_specs=_specs("v" * len(shapes)),
        compiler_params=_params(10),
        cost_estimate=pl.CostEstimate(flops=size, bytes_accessed=3 * size, transcendentals=0),
        name=name,
    )(*arguments)


def _places(meta_ref, half):
    y, core = meta_ref[2], meta_ref[3]
    return [(c, pl.ds(pl.multiple_of(h * half, half), half)) for c in (core, 1 - core) for h in (y, 1 - y)]


def finish_contract_kernel(meta_ref, *refs):
    half = refs[0].shape[0]
    y, core = meta_ref[2], meta_ref[3]
    starts = [(2 * c + h) * half for c in (core, 1 - core) for h in (y, 1 - y)]
    for part, start in zip(refs[:4], starts):
        refs[4][pl.ds(pl.multiple_of(start, half), half), :] = part[...].astype(jnp.float32)


def finish_expand_kernel(part, meta_ref, *refs):
    expand_ref, merge_ref = refs[4:]
    half, span = refs[0].shape[0], refs[0].shape[1] // 2
    near = span // part - 1
    for source, (core, rows) in zip(refs[:4], _places(meta_ref, half)):
        for side in range(2):
            for block in range(near):
                at = pl.multiple_of((2 * (side * near + block) + core) * part, part)
                start = side * span + block * part
                expand_ref[rows, pl.ds(at, part)] = source[:, start : start + part].astype(jnp.float32)
            at = pl.multiple_of((2 * core + side) * part, part)
            start = side * span + near * part
            merge_ref[rows, pl.ds(at, part)] = source[:, start : start + part].astype(jnp.float32)


def finish_attend_kernel(meta_ref, *refs):
    half, wide = refs[0].shape
    span = wide // 3
    for source, (core, rows) in zip(refs[:4], _places(meta_ref, half)):
        for block in range(3):
            at = pl.multiple_of((2 * block + core) * span, span)
            refs[4][rows, pl.ds(at, span)] = source[:, block * span : (block + 1) * span].astype(jnp.float32)


def attend_weigh_kernel(
    meta_ref, act_mine, act_other, owned_ref, other_ref, one_keep, one_send, two_keep, two_send, acts, right, held
):
    x, y, core = meta_ref[1], meta_ref[2], meta_ref[3]
    count, blocks, rows, _ = other_ref.shape
    peers, group, cut = held.shape
    half = group // 2
    _both(acts, act_mine, act_other)
    for block in range(blocks):
        for place in range(count):
            at = 128 * (block * count + place)
            right[:rows, at : at + 128] = owned_ref[core * count + place, block]
            right[rows:, at : at + 128] = other_ref[place, block]
    for side in range(2):
        grad = _dot(acts[...], right[:, side * cut : (side + 1) * cut], ((0,), (0,))).astype(jnp.bfloat16)
        held[...] = grad.reshape(peers, group, cut)
        if side == 0:
            for place in range(peers // 2):
                one_keep[place] = held[2 * place + x]
                one_send[place] = held[2 * place + 1 - x]
        else:
            for place in range(peers):
                two_keep[place] = held[place, pl.ds(pl.multiple_of(y * half, half), half), :]
                two_send[place] = held[place, pl.ds(pl.multiple_of((1 - y) * half, half), half), :]


def attend_weigh(meta, act_mine, act_other, owned, other):
    peers, blocks, rows, _ = owned.shape
    width = act_mine.shape[1]
    group, span = width // peers, blocks * width // 2
    cut = span // 2
    shapes = [(peers // 2, group, cut), (peers // 2, group, cut), (peers, group // 2, cut), (peers, group // 2, cut)]
    return pl.pallas_call(
        attend_weigh_kernel,
        out_shape=[jax.ShapeDtypeStruct(shape, jnp.bfloat16) for shape in shapes],
        in_specs=_specs("svvvv"),
        out_specs=_specs("vvvv"),
        scratch_shapes=[
            pltpu.VMEM((2 * rows, width), jnp.bfloat16),
            pltpu.VMEM((2 * rows, span), jnp.bfloat16),
            pltpu.VMEM((peers, group, cut), jnp.bfloat16),
        ],
        compiler_params=_params(12),
        cost_estimate=pl.CostEstimate(flops=2 * 10**9, bytes_accessed=7 * 2**20, transcendentals=0),
        name="attend_weigh",
    )(meta, act_mine, act_other, owned, other)


def flipped(array, axis, mask):
    peers = lax.axis_size(axis)
    return lax.ppermute(array, axis, [(i, i ^ mask) for i in range(peers)])


def pick(array, index, axis):
    return lax.dynamic_index_in_dim(array, index, axis, keepdims=False)


def added(a, b):
    return (a.astype(jnp.float32) + b.astype(jnp.float32)).astype(jnp.bfloat16)


def in_order(mine, other, bit, axis):
    lower = jnp.where(bit == 0, mine, other)
    upper = jnp.where(bit == 0, other, mine)
    return jnp.concatenate([lower, upper], axis=axis)


def after(value, *others):
    return lax.optimization_barrier((value, others))[0]


def over_first(one_keep, one_send, two_keep, two_send):
    return one_keep, flipped(one_send, "blk", 1), two_keep, flipped(two_send, "seq", 2)


def over_second(here, one_keep, one_got, two_keep, two_got):
    levels, rows, cut = one_keep.shape
    shape = (levels, rows // 2, cut)
    return _small_call(second_kernel, "second", [shape] * 4, jnp.bfloat16, here, one_keep, one_got, two_keep, two_got)


def send_second(one_left, one_send, two_left, two_send):
    return one_left, flipped(one_send, "seq", 2), two_left, flipped(two_send, "blk", 1)


def near_sums(here, one_keep, one_got, two_keep, two_got):
    levels, half, cut = one_keep.shape
    return _small_call(
        near_kernel, "near", [(levels // 2, half, 2 * cut)] * 2, jnp.bfloat16, here, one_keep, one_got, two_keep, two_got
    )


def over_near(here, *parts):
    left, send = near_sums(here, *parts)
    return left, flipped(send, "blk", 2)


def over_far(here, keep, got):
    left, send = _small_call(far_kernel, "far", [keep.shape[1:]] * 2, jnp.bfloat16, here, keep, got)
    return left, flipped(send, "blk", 4)


def over_all(keep, got):
    return _small_call(last_kernel, "last", [keep.shape], jnp.bfloat16, keep, got)[0]


def of_all(own):
    across = flipped(own, "seq", 2)
    return own, across, flipped(own, "seq", 1), flipped(across, "seq", 1)


def local_by_heads(
    tokens,
    lengths,
    attend_weight,
    merge_weight,
    expand_weight,
    contract_weight,
    gain_first,
    shift_first,
    gain_second,
    shift_second,
    bias_table,
    cotangent,
):
    rows, width = tokens.shape[1], tokens.shape[2]
    buckets, heads = bias_table.shape
    hidden = expand_weight.shape[1]
    items = lengths.shape[1]
    peers = lax.axis_size("blk")
    levels = peers // 2
    group = width // peers
    part = hidden // (2 * peers)
    me, line_of = lax.axis_index("blk"), lax.axis_index("seq")
    z, x, y, core = me // 2, me % 2, line_of // 2, line_of % 2
    place = (z, x, y)
    here = jnp.stack([me, x, y, core]).astype(jnp.int32)
    gain_first, shift_first, gain_second, shift_second = (
        v.reshape(1, width) for v in (gain_first, shift_first, gain_second, shift_second)
    )

    own, grad_out = tokens[0], cotangent[0]
    grad_other = flipped(grad_out, "seq", 1)
    meta = plan(lengths[0], me, peers, rows)
    hot = bucket_lines(rows, buckets)
    table_mine = lax.dynamic_slice_in_dim(bias_table, 2 * me, 2, 1)
    lines = jnp.dot(table_mine.T, hot, precision=highest)
    far = table_mine[buckets - 1]

    def to_all(array):
        return lax.all_to_all(array, "blk", split_axis=0, concat_axis=0, tiled=True)

    *parts, act_first = project(here, own, gain_first, shift_first, attend_weight, peers)
    parts = [parts[0]] + [flipped(parts[step], "blk", step) for step in range(1, peers)]
    pulled = pull(here, grad_out, grad_other, contract_weight, peers)
    mixed, wide, logs, qkv = attend(meta, after(far, pulled), lines, parts, items)
    first_other = flipped(act_first, "seq", 1)
    attn_low, middle, act_second = merge(to_all(mixed), own, gain_second, shift_second, merge_weight)
    act_other = flipped(act_second, "seq", 1)
    attn_other = flipped(attn_low, "seq", 1)
    in_keep, in_send, hidden_low, hidden_back = feed(here, act_second, act_other, pulled, expand_weight, peers)
    in_send = flipped(in_send, "seq", 1)
    contract_keep, *contract_parts = contract_weigh(here, grad_out, grad_other, hidden_low, peers)
    in_send, contract_keep, *contract_parts = lax.optimization_barrier((in_send, contract_keep, *contract_parts))
    contract_parts = over_first(contract_keep, *contract_parts)
    grad_heads, grad_middle, keep_low, send_low, sums_second = turn(
        here, in_keep, in_send, middle, grad_out, gain_second, merge_weight, peers
    )
    expand_parts = weigh(here, act_second, act_other, attn_low, attn_other, keep_low, flipped(send_low, "seq", 1), hidden_back, peers)
    expand_keep = expand_parts[0]
    _, *expand_parts = over_first(*expand_parts)

    contract_parts = over_second(here, *contract_parts)
    grad_heads, expand_keep, first_other, *contract_parts = lax.optimization_barrier(
        (to_all(grad_heads), expand_keep, first_other, *contract_parts)
    )
    back_all, line_grad = attend_back(meta, far, lines, wide, logs, qkv, grad_heads, items)
    back_all, *sums = lax.optimization_barrier((back_all, *contract_parts, expand_keep, *expand_parts))
    owned = to_all(back_all)
    out_keep, out_send = emit(here, after(hidden_low, back_all), contract_weight, peers)
    contract_parts = over_near(here, *send_second(*sums[:4]))
    expand_parts = send_second(*over_second(here, *sums[4:]))
    expand_left, expand_send = near_sums(here, *expand_parts)
    owned, out_keep, expand_left, expand_send, *sums = lax.optimization_barrier((owned, out_keep, expand_left, expand_send, *contract_parts))
    expand_parts = expand_left, flipped(expand_send, "blk", 2)
    contract_parts = over_far(here, *sums)
    owned_send = pick(owned.reshape(2, levels, 3, rows, group), 1 - core, 0)
    attend_parts = over_first(*attend_weigh(here, act_first, first_other, owned, flipped(owned_send, "seq", 1)))
    output = (middle + out_keep + flipped(out_send, "seq", 1).astype(jnp.float32)).astype(jnp.bfloat16)
    tokens_grad, sums_first = close(owned, own, grad_middle, gain_first, attend_weight)
    table_mine = jnp.dot(hot, line_grad.T, precision=highest).reshape(1, 2 * buckets)
    table_row = jnp.broadcast_to(jnp.pad(table_mine, ((0, 0), (0, group - 2 * buckets)))[:, None], (1, peers, group))
    small = jnp.concatenate([sums_first.reshape(2, peers, group), sums_second.reshape(2, peers, group), table_row]).transpose(1, 0, 2)
    small = jnp.pad(small, ((0, 0), (0, 3), (0, 0)))

    sums = lax.optimization_barrier((*attend_parts, *contract_parts, *expand_parts))
    attend_parts = send_second(*over_second(here, *sums[:4]))
    contract_own = over_all(*sums[4:6])
    contract_across = flipped(contract_own, "seq", 2)
    expand_parts = over_far(here, *sums[6:])
    small, *sums = lax.optimization_barrier((small, *attend_parts, contract_across, *expand_parts))
    attend_parts = over_near(here, *sums[:4])
    contract_grad = (contract_own, sums[4], flipped(contract_own, "seq", 1), flipped(sums[4], "seq", 1))
    small = small + flipped(small, "seq", 1)
    expand_own = over_all(*sums[5:])
    expand_across = flipped(expand_own, "seq", 2)
    small, expand_across, *attend_parts = lax.optimization_barrier((small, expand_across, *attend_parts))
    attend_parts = over_far(here, *attend_parts)
    small = small + flipped(small, "seq", 2)
    expand_grad = (expand_own, expand_across, flipped(expand_own, "seq", 1), flipped(expand_across, "seq", 1))
    small = to_all(small)
    contract_grad = _small_call(finish_contract_kernel, "finish_contract", [(2 * part, width)], jnp.float32, here, *contract_grad)[0]
    expand_grad, merge_grad = _small_call(
        partial(finish_expand_kernel, part), "finish_expand", [(group, hidden), (group, width)], jnp.float32, here, *expand_grad
    )
    output, *attend_parts = lax.optimization_barrier((output, *attend_parts))
    attend_grad = of_all(over_all(*attend_parts))
    attend_grad = _small_call(finish_attend_kernel, "finish_attend", [(group, 3 * width)], jnp.float32, here, *attend_grad)[0]
    table_grad = small[:, 4, : 2 * buckets].reshape(peers, buckets, 2).transpose(1, 0, 2).reshape(buckets, heads)
    vectors = jnp.sum(small[:, :4], axis=0)
    return (
        output[None],
        tokens_grad[None],
        attend_grad,
        merge_grad,
        expand_grad,
        contract_grad,
        vectors[0],
        vectors[1],
        vectors[2],
        vectors[3],
        table_grad,
    )


def local(*arguments):
    heads = arguments[10].shape[1]
    rows = arguments[0].shape[1]
    peers = lax.axis_size("blk")
    if peers == 8 and lax.axis_size("seq") == 4 and heads == 2 * peers and rows == 256:
        return local_by_heads(*arguments)
    return local_by_runs(*arguments)


def solution(mesh):
    in_specs = (
        P("seq", "blk", None),
        P("seq", None),
        P(),
        P(),
        P(),
        P(),
        P(),
        P(),
        P(),
        P(),
        P(),
        P("seq", "blk", None),
    )
    out_specs = (
        P("seq", "blk", None),
        P("seq", "blk", None),
        P("blk", None),
        P("blk", None),
        P("blk", None),
        P("blk", None),
        P("blk"),
        P("blk"),
        P("blk"),
        P("blk"),
        P(),
    )
    return jax.shard_map(local, mesh=mesh, in_specs=in_specs, out_specs=out_specs, check_vma=False)
```
